32 devices in a mesh: gx: 8 (over z, y), gy: 4 (over x, core).
Axes of the slice: x: 2, y: 2, z: 4, core: 2. Of those that a mesh axis runs over, the one named last changes fastest.
Arguments:
- adjoint_in: float32 [57, 4, 64, 512], P(None, None, 'gx', 'gy'), may hold values from -6 to 6
- populations_early: bfloat16 [57, 4, 64, 512], P(None, None, 'gx', 'gy'), may hold values from 0.019897461 to 0.099609375
- populations_late: bfloat16 [57, 4, 64, 512], P(None, None, 'gx', 'gy'), may hold values from 0.019897461 to 0.099609375
- dipoles_early: bfloat16 [3, 4, 64, 512], P(None, None, 'gx', 'gy'), may hold values from -4 to 4
- dipoles_late: bfloat16 [3, 4, 64, 512], P(None, None, 'gx', 'gy'), may hold values from -4 to 4
Outputs:
- adjoint_out: float32 [57, 4, 64, 512], P(None, None, 'gx', 'gy')
The draws below stay inside these ranges and needn't reach their ends.
All inputs are finite; a program needn't handle non-finite values.
Results may differ from the reference program's by a relative error of at most 0.0003.
Values sent between devices are 32-bit elements; how exact they have to be, the bound alone decides.
No kernel may reach another device: no remote copies, remote signals or barrier semaphores. Data moves between devices by JAX's collectives and lax.ppermute only.
A program may use at most 128 MiB of HBM per device.

```python
import jax
import jax.numpy as jnp
from jax import lax

POPS = 57
BX = 8
PLANES = 4
NX = 64
NY = 512


def levels(stream_key, dims, split, smallest, top_value):
    level = 1.0
    for axis_at, parts in split:
        draws = jax.random.uniform(jax.random.fold_in(jax.random.fold_in(stream_key, 6), axis_at), (parts,), jnp.float32, smallest / len(split), top_value / len(split))
        level = level * jnp.repeat(jnp.exp(draws), dims[axis_at] // parts).reshape((-1,) + (1,) * (len(dims) - 1 - axis_at))
    return level


def gaussian(own_key, dims, scale, limit, split=(), held_as=jnp.bfloat16):
    loudness = levels(own_key, dims, split, -0.22, 0.18) if split else 1.0
    values = jax.random.normal(own_key, dims, jnp.float32) * scale * loudness
    return jnp.minimum(jnp.maximum(values, -limit), limit).astype(held_as)


def setup_inputs(seed: int = 0) -> dict:
    key_of = jax.random.split(jax.random.key(seed), 6)
    adjoint_in = gaussian(key_of[0], (POPS, PLANES, NX, NY), 1.0, 6.0, ((2, 8), (3, 4)), jnp.float32)
    populations_early = jnp.clip(0.019897461 + 0.079711914 * jax.random.uniform(key_of[1], (POPS, PLANES, NX, NY), jnp.float32) ** levels(key_of[1], (POPS, PLANES, NX, NY), ((2, 8), (3, 4)), -0.2, 0.2), 0.019897461, 0.099609375).astype(jnp.bfloat16)
    populations_late = jnp.clip(0.019897461 + 0.079711914 * jax.random.uniform(key_of[2], (POPS, PLANES, NX, NY), jnp.float32) ** levels(key_of[2], (POPS, PLANES, NX, NY), ((2, 8), (3, 4)), -0.2, 0.2), 0.019897461, 0.099609375).astype(jnp.bfloat16)
    dipoles_early = gaussian(key_of[3], (3, PLANES, NX, NY), 1.0, 4.0, ((2, 8), (3, 4)))
    dipoles_late = gaussian(key_of[4], (3, PLANES, NX, NY), 1.0, 4.0, ((2, 8), (3, 4)))
    return dict(adjoint_in=adjoint_in, populations_early=populations_early, populations_late=populations_late, dipoles_early=dipoles_early, dipoles_late=dipoles_late)


VELOCITY = ((1, 0, 0), (-1, 0, 0), (0, 1, 0), (0, -1, 0), (1, 1, 0), (-1, -1, 0), (1, -1, 0), (-1, 1, 0), (1, 0, 1), (-1, 0, -1), (1, 0, -1), (-1, 0, 1), (0, 1, 1), (0, -1, -1), (0, 1, -1), (0, -1, 1), (0, 0, 0), (0, 0, 1), (0, 0, -1))
WEIGHT = (1.0 / 18.0,) * 4 + (1.0 / 36.0,) * 12 + (1.0 / 3.0, 1.0 / 18.0, 1.0 / 18.0)
RELAXATION = (1.0, 1.0, 1.25)
COUPLING = ((0.0, 1.2, -0.6), (1.2, 0.0, -0.6), (-0.6, -0.6, -0.3))
DIPOLE_COUPLING = 0.5
CHARGE = (1.0, -1.0)

def neighbour(padded, shift_x, shift_y, shift_z):
    row_count = padded.shape[2] - 2
    col_count = padded.shape[3] - 2
    window = padded[:, :, 1 + shift_x:1 + shift_x + row_count, 1 + shift_y:1 + shift_y + col_count]
    return jnp.roll(window, -shift_z, axis=1)

def stencils(field_pad):
    shape = (field_pad.shape[1], field_pad.shape[2] - 2, field_pad.shape[3] - 2)
    sums = [jnp.zeros(shape, jnp.float32)] * 21
    for q in range(19):
        if q == 16:
            continue
        c = VELOCITY[q]
        weight = WEIGHT[q]
        nearby = neighbour(field_pad, c[0], c[1], c[2])
        projected = c[0] * nearby[3] + c[1] * nearby[4] + c[2] * nearby[5]
        contrast = nearby[0] - nearby[1]
        for d in range(3):
            if c[d] == 0:
                continue
            for s in range(3):
                sums[3 * s + d] = sums[3 * s + d] + weight * c[d] * nearby[s]
            sums[9 + d] = sums[9 + d] + weight * c[d] * projected * nearby[2]
            for j in range(3):
                if c[j] != 0:
                    sums[12 + 3 * d + j] = sums[12 + 3 * d + j] + weight * c[d] * c[j] * contrast
    return jnp.stack(sums)

def forces(potential, dipole, coupled):
    pieces = []
    for s in range(3):
        for d in range(3):
            mixture = COUPLING[s][0] * coupled[d] + COUPLING[s][1] * coupled[3 + d] + COUPLING[s][2] * coupled[6 + d]
            amount = -potential[s] * mixture
            if s < 2:
                amount = amount - 2.0 * DIPOLE_COUPLING * CHARGE[s] * potential[s] * coupled[9 + d]
            else:
                turned = coupled[12 + 3 * d] * dipole[0] + coupled[13 + 3 * d] * dipole[1] + coupled[14 + 3 * d] * dipole[2]
                amount = amount + 2.0 * DIPOLE_COUPLING * potential[2] * turned
            pieces.append(amount)
    return jnp.stack(pieces)

def collide(populations, forcing):
    shaped = populations.reshape((3, 19) + populations.shape[1:])
    density = lax.optimization_barrier(jnp.sum(shaped, axis=1))
    density_sum = lax.optimization_barrier(jnp.sum(density, axis=0))
    flows = lax.optimization_barrier(jnp.sum(shaped, axis=0))
    momentum = []
    for d in range(3):
        amount = jnp.zeros_like(density_sum)
        for q in range(19):
            if VELOCITY[q][d] != 0:
                amount = amount + VELOCITY[q][d] * flows[q]
        momentum.append(amount / density_sum)
    collided = []
    for s in range(3):
        drifts = [momentum[d] + RELAXATION[s] * forcing[3 * s + d] / density[s] for d in range(3)]
        square = drifts[0] * drifts[0] + drifts[1] * drifts[1] + drifts[2] * drifts[2]
        for q in range(19):
            c = VELOCITY[q]
            projected = c[0] * drifts[0] + c[1] * drifts[1] + c[2] * drifts[2]
            equilibrium = WEIGHT[q] * density[s] * (1.0 + 3.0 * projected + 4.5 * projected * projected - 1.5 * square)
            collided.append(shaped[s, q] - (shaped[s, q] - equilibrium) / RELAXATION[s])
    return jnp.stack(collided)

def spread_back(cot_pad, dipole):
    returned = [jnp.zeros(dipole.shape[1:], jnp.float32)] * 3
    for q in range(19):
        if q == 16:
            continue
        c = VELOCITY[q]
        weight = WEIGHT[q]
        nearby = neighbour(cot_pad, -c[0], -c[1], -c[2])
        projected = c[0] * dipole[0] + c[1] * dipole[1] + c[2] * dipole[2]
        tensor = jnp.zeros(dipole.shape[1:], jnp.float32)
        for d in range(3):
            if c[d] == 0:
                continue
            for s in range(3):
                returned[s] = returned[s] + weight * c[d] * nearby[3 * s + d]
            returned[2] = returned[2] + weight * c[d] * projected * nearby[9 + d]
            for j in range(3):
                if c[j] != 0:
                    tensor = tensor + c[d] * c[j] * nearby[12 + 3 * d + j]
        returned[0] = returned[0] + weight * tensor
        returned[1] = returned[1] - weight * tensor
    return jnp.stack(returned)

def saved_field(saved_pops, dipole):
    populations = saved_pops.astype(jnp.float32)
    density = lax.optimization_barrier(jnp.sum(populations.reshape((3, 19) + populations.shape[1:]), axis=1))
    return jnp.concatenate([1.0 - jnp.exp(-density), dipole.astype(jnp.float32)], axis=0)

def pull_all(padded):
    pulled = []
    for s in range(3):
        for q in range(19):
            c = VELOCITY[q]
            pulled.append(neighbour(padded[s * 19 + q:s * 19 + q + 1], c[0], c[1], c[2])[0])
    return jnp.stack(pulled)

def local_adjoint(populations, potential, dipole, coupled, stream):

    def forward(population_arg, potential_arg, coupled_arg):
        return collide(population_arg, forces(potential_arg, dipole, coupled_arg))
    unused, pullback = jax.vjp(forward, populations, potential, coupled)
    return pullback(stream)

def combine(grad_pops, grad_potential, potential):
    grad_density = grad_potential * (1.0 - potential)
    shaped = grad_pops.reshape((3, 19) + grad_pops.shape[1:])
    return (shaped + grad_density[:, None]).reshape(grad_pops.shape)

def wrap_pad(array):
    return jnp.pad(array, ((0, 0), (0, 0), (1, 1), (1, 1)), mode='wrap')

def reverse_ref(adjoint, saved_pops, dipoles):
    stream = pull_all(wrap_pad(adjoint))
    field = saved_field(saved_pops, dipoles)
    coupled = stencils(wrap_pad(field))
    potential = field[:3]
    dipole = field[3:]

    def block_step(block_index, carry):
        offset = (block_index * BX).astype(jnp.int32)

        def slice_block(array):
            return lax.dynamic_slice_in_dim(array, offset, BX, axis=2)
        pieces = local_adjoint(slice_block(saved_pops).astype(jnp.float32), slice_block(potential), slice_block(dipole), slice_block(coupled), slice_block(stream))
        return tuple((lax.dynamic_update_slice_in_dim(whole_array, piece_array, offset, axis=2) for whole_array, piece_array in zip(carry, pieces)))
    initial = (jnp.zeros(stream.shape, jnp.float32), jnp.zeros(potential.shape, jnp.float32), jnp.zeros(coupled.shape, jnp.float32))
    grad_pops, grad_potential, grad_coupled = lax.fori_loop(0, NX // BX, block_step, initial)
    total_potential = grad_potential + spread_back(wrap_pad(grad_coupled), dipole)
    return combine(grad_pops, total_potential, potential)

def reference(adjoint_in, populations_early, populations_late, dipoles_early, dipoles_late):
    adjoint_mid = reverse_ref(adjoint_in, populations_late, dipoles_late)
    return reverse_ref(adjoint_mid, populations_early, dipoles_early)
```

```python
import jax
import jax.numpy as jnp
from jax import lax
from jax.experimental import pallas as pl
from jax.experimental.pallas import tpu as pltpu
from jax.sharding import PartitionSpec as P

VELOCITY = (
    (1, 0, 0),
    (-1, 0, 0),
    (0, 1, 0),
    (0, -1, 0),
    (1, 1, 0),
    (-1, -1, 0),
    (1, -1, 0),
    (-1, 1, 0),
    (1, 0, 1),
    (-1, 0, -1),
    (1, 0, -1),
    (-1, 0, 1),
    (0, 1, 1),
    (0, -1, -1),
    (0, 1, -1),
    (0, -1, 1),
    (0, 0, 0),
    (0, 0, 1),
    (0, 0, -1),
)
INDEX = {c: q for q, c in enumerate(VELOCITY)}
W1, W2, W0 = 1.0 / 18.0, 1.0 / 36.0, 1.0 / 3.0
RELAXATION = (1.0, 1.0, 1.25)
COUPLING = ((0.0, 1.2, -0.6), (1.2, 0.0, -0.6), (-0.6, -0.6, -0.3))
CROSS = ((0, 0), (1, 0), (-1, 0), (0, 1), (0, -1))
AHEAD = tuple(INDEX[(1,) + yz] for yz in CROSS)
BEHIND = tuple(INDEX[(-1,) + yz] for yz in CROSS)
SIDE = ((1, 0), (-1, 0), (0, 1), (0, -1), (1, 1), (-1, -1), (1, -1), (-1, 1))
F32 = jnp.float32
VMEM_BYTES = 40 * 1024 * 1024
HALO = 4


class Grid:
    def __init__(self, planes, rows, cols):
        self.planes, self.rows, self.cols = planes, rows, cols
        self.tiles = planes + 1
        self.width = cols // planes
        self.group = 2 * HALO
        self.pack = self.width // self.group
        self.sub = lax.broadcasted_iota(jnp.int32, (rows, cols), 0)
        self.lane = lax.broadcasted_iota(jnp.int32, (rows, cols), 1)

    def roll_rows(self, v, dx):
        return pltpu.roll(v, (-dx) % self.rows, 0)

    def roll_cols(self, v, dy):
        return pltpu.roll(v, (-dy) % self.cols, 1)

    def at_row(self, v, rim, dx):
        edge = self.rows - 1 if dx > 0 else 0
        return jnp.where(self.sub == edge, rim, self.roll_rows(v, dx))

    def in_row(self, v, dx):
        edge = self.rows - 1 if dx > 0 else 0
        return jnp.where(self.sub == edge, 0.0, self.roll_rows(v, dx))

    def sides(self, low, high):
        return jnp.where(self.sub == 0, low, high)

    def over(self, body):
        def step(p, carry):
            body(Tile(self, p, False))
            return carry

        lax.fori_loop(0, self.planes, step, 0)
        body(Tile(self, self.planes, True))


class Tile:
    def __init__(self, grid, index, edge):
        self.grid, self.index, self.edge = grid, index, edge

    def of(self, dz):
        if dz == 0 or self.edge:
            return self.index
        return lax.rem(self.index + (dz + self.grid.planes), self.grid.planes)

    def get(self, ref, c, dz=0):
        v = ref[c, self.of(dz)]
        if self.edge and dz != 0:
            v = self.grid.roll_cols(v, dz * self.grid.width)
        return v

    def split(self, main, edge, c, dz=0):
        if not self.edge:
            return main[c, self.of(dz)]
        v = edge[c]
        return v if dz == 0 else self.grid.roll_cols(v, dz * self.grid.width)


def plus(a, b):
    return b if a is None else a + b


def mixed(coefficients, values):
    total = None
    for k, v in zip(coefficients, values):
        if k == 0:
            continue
        term = v if k == 1 else (-v if k == -1 else k * v)
        total = plus(total, term)
    return total


def axis_pairs():
    for q in (0, 2, 17, 4, 6, 8, 10, 12, 14):
        c = VELOCITY[q]
        yield c, (W1 if sum(abs(i) for i in c) == 1 else W2)


def first_and_second(diff, total):
    first = [None] * 3
    second = {}
    for c, w in axis_pairs():
        for d in range(3):
            if c[d] == 0:
                continue
            if diff is not None:
                first[d] = plus(first[d], (w * c[d]) * diff[c])
            if total is not None:
                for e in range(d, 3):
                    if c[e] != 0:
                        second[d, e] = plus(second.get((d, e)), (w * c[d] * c[e]) * total[c])
    return first, second


def turned(second, v):
    return [sum(second[min(d, e), max(d, e)] * v[e] for e in range(3)) for d in range(3)]


def dot(a, b):
    return a[0] * b[0] + a[1] * b[1] + a[2] * b[2]


def field_forces(grid, tile, fields, rim, rim_psi, rim_dip, dipole):
    memo = {}

    def source(name, dz, edge):
        key = (name, dz, edge)
        if key in memo:
            return memo[key]
        if edge:
            load = lambda c: tile.get(rim, (rim_psi + c) if c < 3 else (rim_dip + c - 3), dz)
        else:
            load = lambda c: tile.get(fields, (9 + c) if c < 3 else (6 + c - 3), dz)
        if isinstance(name, int):
            v = load(name)
        elif name == "chi":
            v = source(0, dz, edge) - source(1, dz, edge)
        elif name[0] == "V":
            v = source(2, dz, edge) * source(3 + name[1], dz, edge)
        else:
            v = mixed(name[1], [source(("V", d), dz, edge) if name[1][d] else None for d in range(3)])
        memo[key] = v
        return v

    def shifted(name, c):
        key = (name, c, "shift")
        if key in memo:
            return memo[key]
        if c[1] != 0:
            v = grid.roll_cols(shifted(name, (c[0], 0, c[2])), c[1])
        elif c[0] != 0:
            v = grid.at_row(source(name, c[2], False), source(name, c[2], True), c[0])
        else:
            v = source(name, c[2], False)
        memo[key] = v
        return v

    def parts(name):
        diff, total = {}, {}
        for c, w in axis_pairs():
            back = tuple(-i for i in c)
            a, b = shifted(name, c), shifted(name, back)
            diff[c], total[c] = a - b, a + b
        return diff, total

    diff, unused = parts(0)
    s0, unused = first_and_second(diff, None)
    diff, unused = parts(2)
    s2, unused = first_and_second(diff, None)
    diff, total = parts("chi")
    schi, second = first_and_second(diff, total)
    s1 = [a - b for a, b in zip(s0, schi)]
    pull = [None] * 3
    for c, w in axis_pairs():
        back = tuple(-i for i in c)
        if sum(abs(i) for i in c) == 1:
            name = ("V", [i for i in range(3) if c[i]][0])
        else:
            name = ("L", c)
        total_c = shifted(name, c) + shifted(name, back)
        for d in range(3):
            if c[d] != 0:
                pull[d] = plus(pull[d], (w * c[d]) * total_c)
    md = turned(second, dipole)
    k0 = [-1.2 * s1[d] + 0.6 * s2[d] - pull[d] for d in range(3)]
    k1 = [-1.2 * s0[d] + 0.6 * s2[d] + pull[d] for d in range(3)]
    k2 = [0.6 * (s0[d] + s1[d]) + 0.3 * s2[d] + md[d] for d in range(3)]
    return k0, k1, k2


def collision_adjoint(grid, tile, load, rim, fields, forces, hold, ab, kept):
    u = [tile.get(fields, 3 + d) for d in range(3)]
    rho = [tile.get(fields, s) for s in range(3)]
    inverse_sum = 1.0 / (rho[0] + rho[1] + rho[2])
    grad_u = [None] * 3
    alphas = []
    t = tile.index
    for s in range(3):
        streamed = []
        for q in range(19):
            c = VELOCITY[q]
            v = load(s * 19 + q, c[2])
            if c[0] != 0:
                j = (AHEAD if c[0] > 0 else BEHIND).index(q)
                v = grid.at_row(v, tile.get(rim, s * 5 + j, c[2]), c[0])
            if c[1] != 0:
                v = grid.roll_cols(v, c[1])
            streamed.append(v)
            if s == 2:
                kept[q, t] = v
        diff, total = {}, {}
        for c, w in axis_pairs():
            a, b = streamed[INDEX[c]], streamed[INDEX[tuple(-i for i in c)]]
            diff[c], total[c] = a - b, a + b
        m1, m2 = first_and_second(diff, total)
        m0 = W0 * streamed[16]
        for c, w in axis_pairs():
            m0 = m0 + w * total[c]
        psi = tile.get(fields, 9 + s)
        inverse = 1.0 / rho[s]
        ratio = psi * inverse
        tau = RELAXATION[s]
        k = forces[s]
        v = [u[d] + (tau * ratio) * k[d] for d in range(3)]
        mv = turned(m2, v)
        g = [3.0 * (m1[d] + 3.0 * mv[d] - m0 * v[d]) for d in range(3)]
        feq = m0 + 3.0 * dot(m1, v) + 4.5 * dot(mv, v) - 1.5 * m0 * dot(v, v)
        alphas.append(feq * (1.0 / tau) + dot(g, k) * (1.0 - psi - ratio))
        scaled = rho[s] * (1.0 / tau)
        for d in range(3):
            grad_u[d] = plus(grad_u[d], scaled * g[d])
            hold[3 * s + d, t] = psi * g[d]
    beta = [grad_u[d] * inverse_sum for d in range(3)]
    along = dot(beta, u)
    for s in range(3):
        ab[s, t] = alphas[s] - along
        ab[3 + s, t] = beta[s]


def spread_plane(grid, get_h, get_d, sign, pairs):
    memo = {}

    def source(dz):
        if dz in memo:
            return memo[dz]
        h = [[get_h(3 * s + d, dz) for d in range(3)] for s in range(3)]
        dip = [get_d(d, dz) for d in range(3)]
        if not isinstance(sign, int):
            for vec in h + [dip]:
                vec[0] = vec[0] * sign
        memo[dz] = (h, dip)
        return memo[dz]

    cx = sign if isinstance(sign, int) else 1
    r = [None] * 3
    w_vec = [None] * 3
    lanes = {}
    for cy, cz in pairs:
        w = W1 if abs(cx) + abs(cy) + abs(cz) == 1 else W2
        h, dip = source(cz)
        c = (cx, cy, cz)
        e = [mixed(c, h[s]) for s in range(3)]
        f = e[2] * mixed(c, dip)
        half = 0.6 * e[2]
        r0 = 1.2 * e[1] - half + f
        r1 = 1.2 * e[0] - half - f
        r2 = -0.6 * (e[0] + e[1]) - 0.3 * e[2]
        qv = e[0] - e[1]
        vals = [w * r0, w * r1, w * r2]
        wq = w * qv
        vals += [wq if cx != 0 else None, wq if cy != 0 else None, wq if cz != 0 else None]
        vals = [vals[0], vals[1], vals[2]] + [
            None if x is None else (x if k == 1 else -x) for x, k in zip(vals[3:], (cx, cy, cz))
        ]
        acc = lanes.setdefault(cy, [None] * 6)
        for i, x in enumerate(vals):
            if x is not None:
                acc[i] = plus(acc[i], x)
    total = [None] * 6
    for cy, acc in lanes.items():
        for i, x in enumerate(acc):
            if x is not None:
                total[i] = plus(total[i], x if cy == 0 else grid.roll_cols(x, cy))
    if not isinstance(sign, int):
        total[3] = total[3] * sign
    return total


def met(total, dipole):
    meet = None
    for d in range(3):
        if total[3 + d] is not None:
            meet = plus(meet, total[3 + d] * dipole[d])
    return [total[0], total[1], total[2] - meet]


def spread_inside(grid, tile, hold, fields):
    get_h = lambda k, dz: tile.get(hold, k, dz)
    get_d = lambda k, dz: tile.get(fields, 6 + k, dz)
    total = spread_plane(grid, get_h, get_d, 0, SIDE)
    for dx in (1, -1):
        part = spread_plane(grid, get_h, get_d, dx, CROSS)
        for i, x in enumerate(part):
            total[i] = plus(total[i], grid.in_row(x, dx))
    return met(total, [tile.get(fields, 6 + d) for d in range(3)])


def rim_sign(grid):
    return jnp.where(
        grid.sub == 0, -1.0, jnp.where(grid.sub == grid.rows - 1, 1.0, 0.0)
    ).astype(F32)


def spread_rim(grid, get_h, get_d, target, sign):
    total = spread_plane(grid, get_h, get_d, sign, CROSS)
    return [x * (sign * sign) for x in met(total, target)]


def unpack_rims(grid, first, second, parity, lines, rims, pairs):
    lines[1 - parity] = first[...]
    lines[parity] = second[...]
    for at, c in enumerate(pairs):
        for t in range(grid.tiles):
            k = c * grid.tiles + t
            rims[at, t] = grid.sides(lines[0, k : k + 1, :], lines[1, k : k + 1, :])


def send_rows(grid, parity, lines, first, second):
    first[...] = lines[0]
    second[...] = lines[1]


def line_count(components, grid):
    lines = components * grid.tiles
    return -(-lines // 8) * 8


def parity_of(axis):
    return lax.rem(lax.axis_index(axis), 2)


def pack_columns_kernel(adj, late, early, dip_late, dip_early, send_c, send_d, own_left, own_right, fl, fe):
    planes, rows, cols = adj.shape[1:]
    grid = Grid(planes, rows, cols)
    for saved, dip, out in ((late, dip_late, fl), (early, dip_early, fe)):
        def step(p, carry):
            flows = [None] * 19
            rho = []
            for s in range(3):
                total = None
                for q in range(19):
                    v = saved[s * 19 + q, p].astype(F32)
                    flows[q] = plus(flows[q], v)
                    total = plus(total, v)
                rho.append(total)
                out[s, p] = total
            inverse = 1.0 / (rho[0] + rho[1] + rho[2])
            for d in range(3):
                momentum = None
                for q in range(19):
                    if VELOCITY[q][d] != 0:
                        momentum = plus(momentum, flows[q] if VELOCITY[q][d] > 0 else -flows[q])
                out[3 + d, p] = momentum * inverse
                out[6 + d, p] = dip[d, p].astype(F32)
            return carry

        lax.fori_loop(0, planes, step, 0)
    pops = adj.shape[0]
    components = pops + 18
    slot = grid.lane // grid.group
    for g in range(own_left.shape[0]):
        left = right = jnp.zeros((rows, cols), F32)
        for j in range(grid.pack):
            c = g * grid.pack + j
            if c >= components:
                continue
            for p in range(planes):
                if c < pops:
                    v = adj[c, p]
                elif c < pops + 9:
                    v = fl[c - pops, p]
                else:
                    v = fe[c - pops - 9, p]
                at = p * grid.pack + j
                rolled = pltpu.roll(v, at * grid.group, 1) if at else v
                left = jnp.where(slot == at, rolled, left)
                right = jnp.where(slot == (at - 1) % (cols // grid.group), rolled, right)
        own_left[g] = left
        own_right[g] = right
    low = lax.rem(grid.lane, grid.group) < HALO
    even = parity_of("gy") == 0
    for h in range(send_c.shape[0]):
        left = jnp.where(low, own_left[2 * h], pltpu.roll(own_left[2 * h + 1], HALO, 1))
        right = jnp.where(low, pltpu.roll(own_right[2 * h + 1], cols - HALO, 1), own_right[2 * h])
        send_c[h] = jnp.where(even, right, left)
        send_d[h] = jnp.where(even, left, right)


def pack_rows_kernel(
    adj, own_left, own_right, recv_c, recv_d, fl_main, fe_main, send_a, send_b, edge, fl, fe, lines
):
    pops, planes, rows, cols = adj.shape
    grid = Grid(planes, rows, cols)
    even = parity_of("gy") == 0
    slot = lax.rem(grid.lane // grid.group, grid.pack)
    left_half = lax.rem(grid.lane, grid.width) < grid.width // 2
    components = pops + 18
    for g in range(own_left.shape[0]):
        first, second = recv_c[g // 2], recv_d[g // 2]
        from_next = jnp.where(even, first, second)
        from_prior = jnp.where(even, second, first)
        if g % 2:
            from_next = pltpu.roll(from_next, cols - HALO, 1)
            from_prior = pltpu.roll(from_prior, HALO, 1)
        for j in range(grid.pack):
            c = g * grid.pack + j
            if c >= components:
                continue
            before = slot == (j - 1) % grid.pack
            low = jnp.where(before, from_prior, own_left[g])
            high = jnp.where(before, own_right[g], from_next)
            v = jnp.where(
                left_half,
                pltpu.roll(low, ((1 - j) * grid.group) % cols, 1),
                pltpu.roll(high, ((3 - j) * grid.group) % cols, 1),
            )
            if c < pops:
                edge[c] = v
            elif c < pops + 9:
                fl[c - pops, planes] = v
            else:
                fe[c - pops - 9, planes] = v
    for main, out in ((fl_main, fl), (fe_main, fe)):
        for c in range(9):
            for p in range(planes):
                out[c, p] = main[c, p]
        for s in range(3):
            for t in range(grid.tiles):
                out[9 + s, t] = 1.0 - jnp.exp(-out[s, t])
    up, down = parity_of("gx"), 1 - parity_of("gx")
    fill = 0

    def put(slot_at, v, row):
        lines[slot_at, fill : fill + 1, :] = v[row : row + 1, :]

    for s in range(3):
        for j in range(5):
            for t in range(grid.tiles):
                ahead, behind = s * 19 + AHEAD[j], s * 19 + BEHIND[j]
                put(up, adj[behind, t] if t < planes else edge[behind], rows - 1)
                put(down, adj[ahead, t] if t < planes else edge[ahead], 0)
                fill += 1
    for out in (fl, fe):
        for c in (9, 10, 11, 6, 7, 8):
            for t in range(grid.tiles):
                put(up, out[c, t], rows - 1)
                put(down, out[c, t], 0)
                fill += 1
    send_rows(grid, up, lines, send_a, send_b)


def late_kernel(
    adj, edge, fl, recv_a, recv_b, send_a, send_b, hold, ab, kept, lines, lines_out, rims
):
    pops, planes, rows, cols = adj.shape
    grid = Grid(planes, rows, cols)
    parity = parity_of("gx")
    unpack_rims(grid, recv_a, recv_b, parity, lines, rims, range(21))

    def collide(tile):
        dipole = [tile.get(fl, 6 + d) for d in range(3)]
        forces = field_forces(grid, tile, fl, rims, 15, 18, dipole)
        load = lambda c, dz: tile.split(adj, edge, c, dz)
        collision_adjoint(grid, tile, load, rims, fl, forces, hold, ab, kept)

    grid.over(collide)

    def finish(tile):
        back = spread_inside(grid, tile, hold, fl)
        for s in range(3):
            ab[s, tile.index] = ab[s, tile.index] + (1.0 - tile.get(fl, 9 + s)) * back[s]

    grid.over(finish)
    up, down = parity, 1 - parity
    fill = 0

    def put(v):
        lines_out[up, fill : fill + 1, :] = v[rows - 1 : rows, :]
        lines_out[down, fill : fill + 1, :] = v[0:1, :]

    for c in range(9):
        for t in range(grid.tiles):
            put(hold[c, t])
            fill += 1
    sign = -rim_sign(grid)
    for kind in range(9):
        for t in range(grid.tiles):
            if kind < 2:
                put(ab[kind, t] + sign * ab[3, t])
            elif kind < 4:
                put(ab[2 + kind, t])
            else:
                cy, cz = CROSS[kind - 4]
                part = ab[2, t] + sign * ab[3, t]
                if cy or cz:
                    part = part + mixed((cy, cz), (ab[4, t], ab[5, t]))
                put((1.0 - 1.0 / RELAXATION[2]) * grid.sides(kept[AHEAD[kind - 4], t], kept[BEHIND[kind - 4], t]) + part)
            fill += 1
    send_rows(grid, up, lines_out, send_a, send_b)


def early_kernel(
    fl, fe, hold1, ab1, kept1, first_a, first_b, recv_a, recv_b, send_a, send_b, hold, ab, kept,
    lines, lines2, lines_out, rims, near, mid, rim_mid,
):
    planes, rows, cols = fl.shape[1] - 1, fl.shape[2], fl.shape[3]
    grid = Grid(planes, rows, cols)
    parity = parity_of("gx")
    unpack_rims(grid, first_a, first_b, parity, lines, rims, range(15, 27))
    unpack_rims(grid, recv_a, recv_b, parity, lines2, near, range(18))
    sign = rim_sign(grid)
    rest = 1.0 - 1.0 / RELAXATION[2]

    def complete(tile):
        t = tile.index
        own_d = lambda k, dz: tile.get(fl, 6 + k, dz)
        rim_d = lambda k, dz: tile.get(rims, 3 + k, dz)
        inward = spread_rim(
            grid, lambda k, dz: tile.get(near, k, dz), rim_d, [own_d(d, 0) for d in range(3)], sign
        )
        outward = spread_rim(
            grid, lambda k, dz: tile.get(hold1, k, dz), own_d, [rim_d(d, 0) for d in range(3)], -sign
        )
        alpha = [tile.get(ab1, s) + (1.0 - tile.get(fl, 9 + s)) * inward[s] for s in range(3)]
        beta = [tile.get(ab1, 3 + d) for d in range(3)]
        for q in range(19):
            c = VELOCITY[q]
            along = mixed(c, beta) if q != 16 else None
            for s in range(3):
                v = alpha[s] if along is None else alpha[s] + along
                if s == 2:
                    v = v + rest * kept1[q, t]
                mid[s * 19 + q, t] = v
        fixes = [(1.0 - tile.get(rims, s)) * outward[s] for s in range(3)]
        sides = [tile.get(near, 11 + d) for d in range(2)]
        for s in range(2):
            base = tile.get(near, 9 + s) + fixes[s]
            for j, (cy, cz) in enumerate(CROSS):
                rim_mid[s * 5 + j, t] = base if j == 0 else base + mixed((cy, cz), sides)
        for j in range(5):
            rim_mid[10 + j, t] = tile.get(near, 13 + j) + fixes[2]

    grid.over(complete)

    def collide(tile):
        dipole = [tile.get(fe, 6 + d) for d in range(3)]
        forces = field_forces(grid, tile, fe, rims, 6, 9, dipole)
        load = lambda c, dz: tile.get(mid, c, dz)
        collision_adjoint(grid, tile, load, rim_mid, fe, forces, hold, ab, kept)

    grid.over(collide)
    up, down = parity, 1 - parity
    fill = 0
    for c in range(9):
        for t in range(grid.tiles):
            v = hold[c, t]
            lines_out[up, fill : fill + 1, :] = v[rows - 1 : rows, :]
            lines_out[down, fill : fill + 1, :] = v[0:1, :]
            fill += 1
    send_rows(grid, up, lines_out, send_a, send_b)


def out_kernel(fe, hold, ab, kept, first_a, first_b, recv_a, recv_b, out, lines, lines2, rims, near, total):
    planes, rows, cols = fe.shape[1] - 1, fe.shape[2], fe.shape[3]
    grid = Grid(planes, rows, cols)
    parity = parity_of("gx")
    unpack_rims(grid, first_a, first_b, parity, lines, rims, range(24, 27))
    unpack_rims(grid, recv_a, recv_b, parity, lines2, near, range(9))
    sign = rim_sign(grid)

    def finish(tile):
        back = spread_inside(grid, tile, hold, fe)
        inward = spread_rim(
            grid,
            lambda k, dz: tile.get(near, k, dz),
            lambda k, dz: tile.get(rims, k, dz),
            [tile.get(fe, 6 + d) for d in range(3)],
            sign,
        )
        for s in range(3):
            total[s, tile.index] = tile.get(ab, s) + (1.0 - tile.get(fe, 9 + s)) * (back[s] + inward[s])

    grid.over(finish)
    is_low, is_high = grid.lane < HALO, grid.lane >= cols - HALO

    def emit(p, carry):
        base = p * grid.width

        def patched(main, edge):
            low = pltpu.roll(edge, lax.rem(2 * cols - base - grid.group, cols), 1)
            high = pltpu.roll(edge, lax.rem(2 * cols - base - 3 * grid.group, cols), 1)
            return jnp.where(is_low, low, jnp.where(is_high, high, main))

        alpha = [patched(total[s, p], total[s, planes]) for s in range(3)]
        beta = [patched(ab[3 + d, p], ab[3 + d, planes]) for d in range(3)]
        for q in range(19):
            along = mixed(VELOCITY[q], beta) if q != 16 else None
            for s in range(3):
                v = alpha[s] if along is None else alpha[s] + along
                if s == 2:
                    v = v + (1.0 - 1.0 / RELAXATION[2]) * patched(kept[q, p], kept[q, planes])
                out[s * 19 + q, p] = v
        return carry

    lax.fori_loop(0, planes, emit, 0)


def call(kernel, outs, scratch, args):
    whole = pl.BlockSpec(memory_space=pltpu.VMEM)
    return pl.pallas_call(
        kernel,
        out_shape=[jax.ShapeDtypeStruct(s, F32) for s in outs],
        in_specs=[whole] * len(args),
        out_specs=[whole] * len(outs),
        scratch_shapes=[pltpu.VMEM(s, F32) for s in scratch],
        compiler_params=pltpu.CompilerParams(vmem_limit_bytes=VMEM_BYTES),
    )(*args)


def swap(block, axis, offset):
    size = lax.axis_size(axis)
    route = []
    for i in range(offset, size + offset, 2):
        a, b = i % size, (i + 1) % size
        route += [(a, b), (b, a)]
    return lax.ppermute(block, axis, route)


def shards(adjoint_in, populations_early, populations_late, dipoles_early, dipoles_late):
    pops, planes, rows, cols = adjoint_in.shape
    tiles = planes + 1
    tile = (rows, cols)
    pack = cols // planes // (2 * HALO)
    groups = -(-(pops + 18) // pack)
    groups += groups % 2

    def lines(n):
        return (-(-n * tiles // 8) * 8, cols)

    def both(n):
        return (2,) + lines(n)

    send_c, send_d, own_left, own_right, fl_main, fe_main = call(
        pack_columns_kernel,
        [(groups // 2,) + tile] * 2 + [(groups,) + tile] * 2 + [(9, planes) + tile] * 2,
        [],
        [adjoint_in, populations_late, populations_early, dipoles_late, dipoles_early],
    )
    recv_c, recv_d = swap(send_c, "gy", 0), swap(send_d, "gy", 1)
    send_a, send_b, edge, fl, fe = call(
        pack_rows_kernel,
        [lines(27)] * 2 + [(pops,) + tile] + [(12, tiles) + tile] * 2,
        [both(27)],
        [adjoint_in, own_left, own_right, recv_c, recv_d, fl_main, fe_main],
    )
    first_a, first_b = swap(send_a, "gx", 0), swap(send_b, "gx", 1)
    saved = [(9, tiles) + tile, (6, tiles) + tile, (19, tiles) + tile]
    send_a, send_b, hold1, ab1, kept1 = call(
        late_kernel,
        [lines(18)] * 2 + saved,
        [both(27), both(18), (21, tiles) + tile],
        [adjoint_in, edge, fl, first_a, first_b],
    )
    recv_a, recv_b = swap(send_a, "gx", 0), swap(send_b, "gx", 1)
    send_a, send_b, hold, ab, kept = call(
        early_kernel,
        [lines(9)] * 2 + saved,
        [
            both(27),
            both(18),
            both(9),
            (12, tiles) + tile,
            (18, tiles) + tile,
            (pops, tiles) + tile,
            (15, tiles) + tile,
        ],
        [fl, fe, hold1, ab1, kept1, first_a, first_b, recv_a, recv_b],
    )
    recv_a, recv_b = swap(send_a, "gx", 0), swap(send_b, "gx", 1)
    (out,) = call(
        out_kernel,
        [(pops, planes) + tile],
        [both(27), both(9), (3, tiles) + tile, (9, tiles) + tile, (3, tiles) + tile],
        [fe, hold, ab, kept, first_a, first_b, recv_a, recv_b],
    )
    return out


def solution(mesh):
    placed = P(None, None, "gx", "gy")
    return jax.shard_map(
        shards, mesh=mesh, in_specs=(placed,) * 5, out_specs=placed, check_vma=False
    )
```

```python
import jax
import jax.numpy as jnp
from jax import lax
from jax.experimental import pallas as pl
from jax.experimental.pallas import tpu as pltpu
from jax.sharding import PartitionSpec as P

VELOCITY = (
    (1, 0, 0),
    (-1, 0, 0),
    (0, 1, 0),
    (0, -1, 0),
    (1, 1, 0),
    (-1, -1, 0),
    (1, -1, 0),
    (-1, 1, 0),
    (1, 0, 1),
    (-1, 0, -1),
    (1, 0, -1),
    (-1, 0, 1),
    (0, 1, 1),
    (0, -1, -1),
    (0, 1, -1),
    (0, -1, 1),
    (0, 0, 0),
    (0, 0, 1),
    (0, 0, -1),
)
INDEX = {c: q for q, c in enumerate(VELOCITY)}
W1, W2, W0 = 1.0 / 18.0, 1.0 / 36.0, 1.0 / 3.0
RELAXATION = (1.0, 1.0, 1.25)
COUPLING = ((0.0, 1.2, -0.6), (1.2, 0.0, -0.6), (-0.6, -0.6, -0.3))
CROSS = ((0, 0), (1, 0), (-1, 0), (0, 1), (0, -1))
AHEAD = tuple(INDEX[(1,) + yz] for yz in CROSS)
BEHIND = tuple(INDEX[(-1,) + yz] for yz in CROSS)
SIDE = ((1, 0), (-1, 0), (0, 1), (0, -1), (1, 1), (-1, -1), (1, -1), (-1, 1))
F32 = jnp.float32
VMEM_BYTES = 40 * 1024 * 1024
HALO = 4


class Grid:
    def __init__(self, planes, rows, cols):
        self.planes, self.rows, self.cols = planes, rows, cols
        self.tiles = planes + 1
        self.width = cols // planes
        self.group = 2 * HALO
        self.pack = self.width // self.group
        self.sub = lax.broadcasted_iota(jnp.int32, (rows, cols), 0)
        self.lane = lax.broadcasted_iota(jnp.int32, (rows, cols), 1)

    def roll_rows(self, v, dx):
        return pltpu.roll(v, (-dx) % self.rows, 0)

    def roll_cols(self, v, dy):
        return pltpu.roll(v, (-dy) % self.cols, 1)

    def at_row(self, v, rim, dx):
        edge = self.rows - 1 if dx > 0 else 0
        return jnp.where(self.sub == edge, rim, self.roll_rows(v, dx))

    def in_row(self, v, dx):
        edge = self.rows - 1 if dx > 0 else 0
        return jnp.where(self.sub == edge, 0.0, self.roll_rows(v, dx))

    def sides(self, low, high):
        return jnp.where(self.sub == 0, low, high)

    def over(self, body):
        def step(p, carry):
            body(Tile(self, p, False))
            return carry

        lax.fori_loop(0, self.planes, step, 0)
        body(Tile(self, self.planes, True))


class Tile:
    def __init__(self, grid, index, edge):
        self.grid, self.index, self.edge = grid, index, edge

    def of(self, dz):
        if dz == 0 or self.edge:
            return self.index
        return lax.rem(self.index + (dz + self.grid.planes), self.grid.planes)

    def get(self, ref, c, dz=0):
        v = ref[c, self.of(dz)]
        if self.edge and dz != 0:
            v = self.grid.roll_cols(v, dz * self.grid.width)
        return v

    def split(self, main, edge, c, dz=0):
        if not self.edge:
            return main[c, self.of(dz)]
        v = edge[c]
        return v if dz == 0 else self.grid.roll_cols(v, dz * self.grid.width)


def plus(a, b):
    return b if a is None else a + b


def mixed(coefficients, values):
    total = None
    for k, v in zip(coefficients, values):
        if k == 0:
            continue
        term = v if k == 1 else (-v if k == -1 else k * v)
        total = plus(total, term)
    return total


def axis_pairs():
    for q in (0, 2, 17, 4, 6, 8, 10, 12, 14):
        c = VELOCITY[q]
        yield c, (W1 if sum(abs(i) for i in c) == 1 else W2)


def first_and_second(diff, total):
    first = [None] * 3
    second = {}
    for c, w in axis_pairs():
        for d in range(3):
            if c[d] == 0:
                continue
            if diff is not None:
                first[d] = plus(first[d], (w * c[d]) * diff[c])
            if total is not None:
                for e in range(d, 3):
                    if c[e] != 0:
                        second[d, e] = plus(second.get((d, e)), (w * c[d] * c[e]) * total[c])
    return first, second


def turned(second, v):
    return [sum(second[min(d, e), max(d, e)] * v[e] for e in range(3)) for d in range(3)]


def dot(a, b):
    return a[0] * b[0] + a[1] * b[1] + a[2] * b[2]


def field_forces(grid, tile, fields, rim, rim_psi, rim_dip, dipole):
    memo = {}

    def source(name, dz, edge):
        key = (name, dz, edge)
        if key in memo:
            return memo[key]
        if edge:
            load = lambda c: tile.get(rim, (rim_psi + c) if c < 3 else (rim_dip + c - 3), dz)
        else:
            load = lambda c: tile.get(fields, (9 + c) if c < 3 else (6 + c - 3), dz)
        if isinstance(name, int):
            v = load(name)
        elif name == "chi":
            v = source(0, dz, edge) - source(1, dz, edge)
        elif name[0] == "V":
            v = source(2, dz, edge) * source(3 + name[1], dz, edge)
        else:
            v = mixed(name[1], [source(("V", d), dz, edge) if name[1][d] else None for d in range(3)])
        memo[key] = v
        return v

    def shifted(name, c):
        key = (name, c, "shift")
        if key in memo:
            return memo[key]
        if c[1] != 0:
            v = grid.roll_cols(shifted(name, (c[0], 0, c[2])), c[1])
        elif c[0] != 0:
            v = grid.at_row(source(name, c[2], False), source(name, c[2], True), c[0])
        else:
            v = source(name, c[2], False)
        memo[key] = v
        return v

    def parts(name):
        diff, total = {}, {}
        for c, w in axis_pairs():
            back = tuple(-i for i in c)
            a, b = shifted(name, c), shifted(name, back)
            diff[c], total[c] = a - b, a + b
        return diff, total

    diff, unused = parts(0)
    s0, unused = first_and_second(diff, None)
    diff, unused = parts(2)
    s2, unused = first_and_second(diff, None)
    diff, total = parts("chi")
    schi, second = first_and_second(diff, total)
    s1 = [a - b for a, b in zip(s0, schi)]
    pull = [None] * 3
    for c, w in axis_pairs():
        back = tuple(-i for i in c)
        if sum(abs(i) for i in c) == 1:
            name = ("V", [i for i in range(3) if c[i]][0])
        else:
            name = ("L", c)
        total_c = shifted(name, c) + shifted(name, back)
        for d in range(3):
            if c[d] != 0:
                pull[d] = plus(pull[d], (w * c[d]) * total_c)
    md = turned(second, dipole)
    k0 = [-1.2 * s1[d] + 0.6 * s2[d] - pull[d] for d in range(3)]
    k1 = [-1.2 * s0[d] + 0.6 * s2[d] + pull[d] for d in range(3)]
    k2 = [0.6 * (s0[d] + s1[d]) + 0.3 * s2[d] + md[d] for d in range(3)]
    return k0, k1, k2


def collision_adjoint(grid, tile, load, rim, fields, forces, hold, ab, kept):
    u = [tile.get(fields, 3 + d) for d in range(3)]
    rho = [tile.get(fields, s) for s in range(3)]
    inverse_sum = 1.0 / (rho[0] + rho[1] + rho[2])
    grad_u = [None] * 3
    alphas = []
    t = tile.index
    for s in range(3):
        streamed = []
        for q in range(19):
            c = VELOCITY[q]
            v = load(s * 19 + q, c[2])
            if c[0] != 0:
                j = (AHEAD if c[0] > 0 else BEHIND).index(q)
                v = grid.at_row(v, tile.get(rim, s * 5 + j, c[2]), c[0])
            if c[1] != 0:
                v = grid.roll_cols(v, c[1])
            streamed.append(v)
            if s == 2:
                kept[q, t] = v
        diff, total = {}, {}
        for c, w in axis_pairs():
            a, b = streamed[INDEX[c]], streamed[INDEX[tuple(-i for i in c)]]
            diff[c], total[c] = a - b, a + b
        m1, m2 = first_and_second(diff, total)
        m0 = W0 * streamed[16]
        for c, w in axis_pairs():
            m0 = m0 + w * total[c]
        psi = tile.get(fields, 9 + s)
        inverse = 1.0 / rho[s]
        ratio = psi * inverse
        tau = RELAXATION[s]
        k = forces[s]
        v = [u[d] + (tau * ratio) * k[d] for d in range(3)]
        mv = turned(m2, v)
        g = [3.0 * (m1[d] + 3.0 * mv[d] - m0 * v[d]) for d in range(3)]
        feq = m0 + 3.0 * dot(m1, v) + 4.5 * dot(mv, v) - 1.5 * m0 * dot(v, v)
        alphas.append(feq * (1.0 / tau) + dot(g, k) * (1.0 - psi - ratio))
        scaled = rho[s] * (1.0 / tau)
        for d in range(3):
            grad_u[d] = plus(grad_u[d], scaled * g[d])
            hold[3 * s + d, t] = psi * g[d]
    beta = [grad_u[d] * inverse_sum for d in range(3)]
    along = dot(beta, u)
    for s in range(3):
        ab[s, t] = alphas[s] - along
        ab[3 + s, t] = beta[s]


def spread_plane(grid, get_h, get_d, sign, pairs):
    memo = {}

    def source(dz):
        if dz in memo:
            return memo[dz]
        h = [[get_h(3 * s + d, dz) for d in range(3)] for s in range(3)]
        dip = [get_d(d, dz) for d in range(3)]
        if not isinstance(sign, int):
            for vec in h + [dip]:
                vec[0] = vec[0] * sign
        memo[dz] = (h, dip)
        return memo[dz]

    cx = sign if isinstance(sign, int) else 1
    r = [None] * 3
    w_vec = [None] * 3
    lanes = {}
    for cy, cz in pairs:
        w = W1 if abs(cx) + abs(cy) + abs(cz) == 1 else W2
        h, dip = source(cz)
        c = (cx, cy, cz)
        e = [mixed(c, h[s]) for s in range(3)]
        f = e[2] * mixed(c, dip)
        half = 0.6 * e[2]
        r0 = 1.2 * e[1] - half + f
        r1 = 1.2 * e[0] - half - f
        r2 = -0.6 * (e[0] + e[1]) - 0.3 * e[2]
        qv = e[0] - e[1]
        vals = [w * r0, w * r1, w * r2]
        wq = w * qv
        vals += [wq if cx != 0 else None, wq if cy != 0 else None, wq if cz != 0 else None]
        vals = [vals[0], vals[1], vals[2]] + [
            None if x is None else (x if k == 1 else -x) for x, k in zip(vals[3:], (cx, cy, cz))
        ]
        acc = lanes.setdefault(cy, [None] * 6)
        for i, x in enumerate(vals):
            if x is not None:
                acc[i] = plus(acc[i], x)
    total = [None] * 6
    for cy, acc in lanes.items():
        for i, x in enumerate(acc):
            if x is not None:
                total[i] = plus(total[i], x if cy == 0 else grid.roll_cols(x, cy))
    if not isinstance(sign, int):
        total[3] = total[3] * sign
    return total


def met(total, dipole):
    meet = None
    for d in range(3):
        if total[3 + d] is not None:
            meet = plus(meet, total[3 + d] * dipole[d])
    return [total[0], total[1], total[2] - meet]


def spread_inside(grid, tile, hold, fields):
    get_h = lambda k, dz: tile.get(hold, k, dz)
    get_d = lambda k, dz: tile.get(fields, 6 + k, dz)
    total = spread_plane(grid, get_h, get_d, 0, SIDE)
    for dx in (1, -1):
        part = spread_plane(grid, get_h, get_d, dx, CROSS)
        for i, x in enumerate(part):
            total[i] = plus(total[i], grid.in_row(x, dx))
    return met(total, [tile.get(fields, 6 + d) for d in range(3)])


def rim_sign(grid):
    return jnp.where(
        grid.sub == 0, -1.0, jnp.where(grid.sub == grid.rows - 1, 1.0, 0.0)
    ).astype(F32)


def hand_over(grid, tile, hold, fields, rim, rim_dip, given):
    total = spread_plane(
        grid,
        lambda k, dz: tile.get(hold, k, dz),
        lambda k, dz: tile.get(fields, 6 + k, dz),
        -rim_sign(grid),
        CROSS,
    )
    for s, x in enumerate(met(total, [tile.get(rim, rim_dip + d) for d in range(3)])):
        given[s, tile.index] = x


def unpack_rims(grid, first, second, parity, lines, rims, pairs):
    lines[1 - parity] = first[...]
    lines[parity] = second[...]
    for at, c in enumerate(pairs):
        for t in range(grid.tiles):
            k = c * grid.tiles + t
            rims[at, t] = grid.sides(lines[0, k : k + 1, :], lines[1, k : k + 1, :])


def send_rows(grid, parity, lines, first, second):
    first[...] = lines[0]
    second[...] = lines[1]


def parity_of(axis):
    return lax.rem(lax.axis_index(axis), 2)


def pack_columns_kernel(
    adj_in, late_in, early_in, dip_late_in, dip_early_in,
    send_c, send_d, own_left, own_right, fl, fe, adj,
    late, early, dip_late, dip_early, sems,
):
    planes, rows, cols = adj.shape[1:]
    grid = Grid(planes, rows, cols)
    copies = [
        pltpu.make_async_copy(a, b, sems.at[i])
        for i, (a, b) in enumerate(
            (
                (dip_late_in, dip_late),
                (late_in, late),
                (dip_early_in, dip_early),
                (early_in, early),
                (adj_in, adj),
            )
        )
    ]
    for copy in copies:
        copy.start()
    for which, (saved, dip, out) in enumerate(((late, dip_late, fl), (early, dip_early, fe))):
        copies[2 * which].wait()
        copies[2 * which + 1].wait()

        def step(p, carry):
            flows = [None] * 19
            rho = []
            for s in range(3):
                total = None
                for q in range(19):
                    v = saved[s * 19 + q, p].astype(F32)
                    flows[q] = plus(flows[q], v)
                    total = plus(total, v)
                rho.append(total)
                out[s, p] = total
            inverse = 1.0 / (rho[0] + rho[1] + rho[2])
            for d in range(3):
                momentum = None
                for q in range(19):
                    if VELOCITY[q][d] != 0:
                        momentum = plus(momentum, flows[q] if VELOCITY[q][d] > 0 else -flows[q])
                out[3 + d, p] = momentum * inverse
                out[6 + d, p] = dip[d, p].astype(F32)
            return carry

        lax.fori_loop(0, planes, step, 0)
    copies[4].wait()
    pops = adj.shape[0]
    components = pops + 18
    slot = grid.lane // grid.group
    for g in range(own_left.shape[0]):
        left = right = jnp.zeros((rows, cols), F32)
        for j in range(grid.pack):
            c = g * grid.pack + j
            if c >= components:
                continue
            for p in range(planes):
                if c < pops:
                    v = adj[c, p]
                elif c < pops + 9:
                    v = fl[c - pops, p]
                else:
                    v = fe[c - pops - 9, p]
                at = p * grid.pack + j
                rolled = pltpu.roll(v, at * grid.group, 1) if at else v
                left = jnp.where(slot == at, rolled, left)
                right = jnp.where(slot == (at - 1) % (cols // grid.group), rolled, right)
        own_left[g] = left
        own_right[g] = right
    low = lax.rem(grid.lane, grid.group) < HALO
    even = parity_of("gy") == 0
    for h in range(send_c.shape[0]):
        left = jnp.where(low, own_left[2 * h], pltpu.roll(own_left[2 * h + 1], HALO, 1))
        right = jnp.where(low, pltpu.roll(own_right[2 * h + 1], cols - HALO, 1), own_right[2 * h])
        send_c[h] = jnp.where(even, right, left)
        send_d[h] = jnp.where(even, left, right)


def pack_rows_kernel(
    adj, own_left, own_right, recv_c, recv_d, fl_main, fe_main, send_a, send_b, edge, fl, fe, lines
):
    pops, planes, rows, cols = adj.shape
    grid = Grid(planes, rows, cols)
    even = parity_of("gy") == 0
    slot = lax.rem(grid.lane // grid.group, grid.pack)
    left_half = lax.rem(grid.lane, grid.width) < grid.width // 2
    components = pops + 18
    for g in range(own_left.shape[0]):
        first, second = recv_c[g // 2], recv_d[g // 2]
        from_next = jnp.where(even, first, second)
        from_prior = jnp.where(even, second, first)
        if g % 2:
            from_next = pltpu.roll(from_next, cols - HALO, 1)
            from_prior = pltpu.roll(from_prior, HALO, 1)
        for j in range(grid.pack):
            c = g * grid.pack + j
            if c >= components:
                continue
            before = slot == (j - 1) % grid.pack
            low = jnp.where(before, from_prior, own_left[g])
            high = jnp.where(before, own_right[g], from_next)
            v = jnp.where(
                left_half,
                pltpu.roll(low, ((1 - j) * grid.group) % cols, 1),
                pltpu.roll(high, ((3 - j) * grid.group) % cols, 1),
            )
            if c < pops:
                edge[c] = v
            elif c < pops + 9:
                fl[c - pops, planes] = v
            else:
                fe[c - pops - 9, planes] = v
    for main, out in ((fl_main, fl), (fe_main, fe)):
        for c in range(9):
            for p in range(planes):
                out[c, p] = main[c, p]
        for s in range(3):
            for t in range(grid.tiles):
                out[9 + s, t] = 1.0 - jnp.exp(-out[s, t])
    up, down = parity_of("gx"), 1 - parity_of("gx")
    fill = 0

    def put(slot_at, v, row):
        lines[slot_at, fill : fill + 1, :] = v[row : row + 1, :]

    for s in range(3):
        for j in range(5):
            for t in range(grid.tiles):
                ahead, behind = s * 19 + AHEAD[j], s * 19 + BEHIND[j]
                put(up, adj[behind, t] if t < planes else edge[behind], rows - 1)
                put(down, adj[ahead, t] if t < planes else edge[ahead], 0)
                fill += 1
    for out in (fl, fe):
        for c in (9, 10, 11, 6, 7, 8):
            for t in range(grid.tiles):
                put(up, out[c, t], rows - 1)
                put(down, out[c, t], 0)
                fill += 1
    send_rows(grid, up, lines, send_a, send_b)


def late_kernel(
    adj, edge, fl, recv_a, recv_b, send_a, send_b, ab, kept, given, lines, lines_out, rims, hold
):
    pops, planes, rows, cols = adj.shape
    grid = Grid(planes, rows, cols)
    parity = parity_of("gx")
    unpack_rims(grid, recv_a, recv_b, parity, lines, rims, range(21))

    def collide(tile):
        dipole = [tile.get(fl, 6 + d) for d in range(3)]
        forces = field_forces(grid, tile, fl, rims, 15, 18, dipole)
        load = lambda c, dz: tile.split(adj, edge, c, dz)
        collision_adjoint(grid, tile, load, rims, fl, forces, hold, ab, kept)

    grid.over(collide)
    sign = -rim_sign(grid)

    def finish(tile):
        back = spread_inside(grid, tile, hold, fl)
        for s in range(3):
            ab[s, tile.index] = ab[s, tile.index] + (1.0 - tile.get(fl, 9 + s)) * back[s]
        hand_over(grid, tile, hold, fl, rims, 18, given)

    grid.over(finish)
    up, down = parity, 1 - parity
    fill = 0

    def put(v):
        lines_out[up, fill : fill + 1, :] = v[rows - 1 : rows, :]
        lines_out[down, fill : fill + 1, :] = v[0:1, :]

    for c in range(3):
        for t in range(grid.tiles):
            put(given[c, t])
            fill += 1
    for kind in range(9):
        for t in range(grid.tiles):
            if kind < 2:
                put(ab[kind, t] + sign * ab[3, t])
            elif kind < 4:
                put(ab[2 + kind, t])
            else:
                cy, cz = CROSS[kind - 4]
                part = ab[2, t] + sign * ab[3, t]
                if cy or cz:
                    part = part + mixed((cy, cz), (ab[4, t], ab[5, t]))
                put((1.0 - 1.0 / RELAXATION[2]) * grid.sides(kept[AHEAD[kind - 4], t], kept[BEHIND[kind - 4], t]) + part)
            fill += 1
    send_rows(grid, up, lines_out, send_a, send_b)


def early_kernel(
    fl, fe, ab1, kept1, given1, first_a, first_b, recv_a, recv_b, send_a, send_b, hold, ab, kept,
    lines, lines2, lines_out, rims, near, mid, rim_mid, given,
):
    planes, rows, cols = fl.shape[1] - 1, fl.shape[2], fl.shape[3]
    grid = Grid(planes, rows, cols)
    parity = parity_of("gx")
    unpack_rims(grid, first_a, first_b, parity, lines, rims, (15, 16, 17) + tuple(range(21, 27)))
    unpack_rims(grid, recv_a, recv_b, parity, lines2, near, range(12))
    rest = 1.0 - 1.0 / RELAXATION[2]
    at_rim = (grid.sub == 0) | (grid.sub == rows - 1)

    def complete(tile):
        t = tile.index
        inward = [jnp.where(at_rim, tile.get(near, s), 0.0) for s in range(3)]
        alpha = [tile.get(ab1, s) + (1.0 - tile.get(fl, 9 + s)) * inward[s] for s in range(3)]
        beta = [tile.get(ab1, 3 + d) for d in range(3)]
        for q in range(19):
            c = VELOCITY[q]
            along = mixed(c, beta) if q != 16 else None
            for s in range(3):
                v = alpha[s] if along is None else alpha[s] + along
                if s == 2:
                    v = v + rest * kept1[q, t]
                mid[s * 19 + q, t] = v
        fixes = [(1.0 - tile.get(rims, s)) * tile.get(given1, s) for s in range(3)]
        sides = [tile.get(near, 5 + d) for d in range(2)]
        for s in range(2):
            base = tile.get(near, 3 + s) + fixes[s]
            for j, (cy, cz) in enumerate(CROSS):
                rim_mid[s * 5 + j, t] = base if j == 0 else base + mixed((cy, cz), sides)
        for j in range(5):
            rim_mid[10 + j, t] = tile.get(near, 7 + j) + fixes[2]

    grid.over(complete)

    def collide(tile):
        dipole = [tile.get(fe, 6 + d) for d in range(3)]
        forces = field_forces(grid, tile, fe, rims, 3, 6, dipole)
        load = lambda c, dz: tile.get(mid, c, dz)
        collision_adjoint(grid, tile, load, rim_mid, fe, forces, hold, ab, kept)

    grid.over(collide)
    grid.over(lambda tile: hand_over(grid, tile, hold, fe, rims, 6, given))
    up, down = parity, 1 - parity
    fill = 0
    for c in range(3):
        for t in range(grid.tiles):
            v = given[c, t]
            lines_out[up, fill : fill + 1, :] = v[rows - 1 : rows, :]
            lines_out[down, fill : fill + 1, :] = v[0:1, :]
            fill += 1
    send_rows(grid, up, lines_out, send_a, send_b)


def out_kernel(fe, hold, ab, kept, recv_a, recv_b, out, lines, near, total, staged, sems):
    planes, rows, cols = fe.shape[1] - 1, fe.shape[2], fe.shape[3]
    grid = Grid(planes, rows, cols)
    unpack_rims(grid, recv_a, recv_b, parity_of("gx"), lines, near, range(3))
    at_rim = (grid.sub == 0) | (grid.sub == rows - 1)

    def finish(tile):
        back = spread_inside(grid, tile, hold, fe)
        for s in range(3):
            back[s] = back[s] + jnp.where(at_rim, tile.get(near, s), 0.0)
            total[s, tile.index] = tile.get(ab, s) + (1.0 - tile.get(fe, 9 + s)) * back[s]

    grid.over(finish)
    is_low, is_high = grid.lane < HALO, grid.lane >= cols - HALO

    def to_out(p):
        return pltpu.make_async_copy(staged.at[:, p], out.at[:, p], sems.at[p])

    def emit(p, carry):
        base = p * grid.width

        def patched(main, edge):
            low = pltpu.roll(edge, lax.rem(2 * cols - base - grid.group, cols), 1)
            high = pltpu.roll(edge, lax.rem(2 * cols - base - 3 * grid.group, cols), 1)
            return jnp.where(is_low, low, jnp.where(is_high, high, main))

        alpha = [patched(total[s, p], total[s, planes]) for s in range(3)]
        beta = [patched(ab[3 + d, p], ab[3 + d, planes]) for d in range(3)]
        for q in range(19):
            along = mixed(VELOCITY[q], beta) if q != 16 else None
            for s in range(3):
                v = alpha[s] if along is None else alpha[s] + along
                if s == 2:
                    v = v + (1.0 - 1.0 / RELAXATION[2]) * patched(kept[q, p], kept[q, planes])
                staged[s * 19 + q, p] = v
        to_out(p).start()
        return carry

    lax.fori_loop(0, planes, emit, 0)
    for p in range(planes):
        to_out(p).wait()


def call(kernel, outs, scratch, args, in_hbm=False, out_hbm=False):
    vmem = pl.BlockSpec(memory_space=pltpu.VMEM)
    hbm = pl.BlockSpec(memory_space=pltpu.HBM)
    return pl.pallas_call(
        kernel,
        out_shape=[jax.ShapeDtypeStruct(s, F32) for s in outs],
        in_specs=[hbm if in_hbm else vmem] * len(args),
        out_specs=[hbm if out_hbm else vmem] * len(outs),
        scratch_shapes=[pltpu.VMEM(s, F32) if isinstance(s, tuple) else s for s in scratch],
        compiler_params=pltpu.CompilerParams(vmem_limit_bytes=VMEM_BYTES),
    )(*args)


def swap(block, axis, offset):
    size = lax.axis_size(axis)
    route = []
    for i in range(offset, size + offset, 2):
        a, b = i % size, (i + 1) % size
        route += [(a, b), (b, a)]
    return lax.ppermute(block, axis, route)


def shards(adjoint_in, populations_early, populations_late, dipoles_early, dipoles_late):
    pops, planes, rows, cols = adjoint_in.shape
    tiles = planes + 1
    tile = (rows, cols)
    pack = cols // planes // (2 * HALO)
    groups = -(-(pops + 18) // pack)
    groups += groups % 2

    def lines(n):
        return (-(-n * tiles // 8) * 8, cols)

    def both(n):
        return (2,) + lines(n)

    send_c, send_d, own_left, own_right, fl_main, fe_main, adj = call(
        pack_columns_kernel,
        [(groups // 2,) + tile] * 2
        + [(groups,) + tile] * 2
        + [(9, planes) + tile] * 2
        + [(pops, planes) + tile],
        [pltpu.VMEM(x.shape, x.dtype) for x in (populations_late, populations_early)]
        + [pltpu.VMEM(x.shape, x.dtype) for x in (dipoles_late, dipoles_early)]
        + [pltpu.SemaphoreType.DMA((5,))],
        [adjoint_in, populations_late, populations_early, dipoles_late, dipoles_early],
        in_hbm=True,
    )
    recv_c, recv_d = swap(send_c, "gy", 0), swap(send_d, "gy", 1)
    send_a, send_b, edge, fl, fe = call(
        pack_rows_kernel,
        [lines(27)] * 2 + [(pops,) + tile] + [(12, tiles) + tile] * 2,
        [both(27)],
        [adj, own_left, own_right, recv_c, recv_d, fl_main, fe_main],
    )
    first_a, first_b = swap(send_a, "gx", 0), swap(send_b, "gx", 1)
    hold_shape, ab_shape, kept_shape = [(n, tiles) + tile for n in (9, 6, 19)]
    three = (3, tiles) + tile
    send_a, send_b, ab1, kept1, given1 = call(
        late_kernel,
        [lines(12)] * 2 + [ab_shape, kept_shape, three],
        [both(27), both(12), (21, tiles) + tile, hold_shape],
        [adj, edge, fl, first_a, first_b],
    )
    recv_a, recv_b = swap(send_a, "gx", 0), swap(send_b, "gx", 1)
    send_a, send_b, hold, ab, kept = call(
        early_kernel,
        [lines(3)] * 2 + [hold_shape, ab_shape, kept_shape],
        [
            both(27),
            both(12),
            both(3),
            (9, tiles) + tile,
            (12, tiles) + tile,
            (pops, tiles) + tile,
            (15, tiles) + tile,
            three,
        ],
        [fl, fe, ab1, kept1, given1, first_a, first_b, recv_a, recv_b],
    )
    recv_a, recv_b = swap(send_a, "gx", 0), swap(send_b, "gx", 1)
    (out,) = call(
        out_kernel,
        [(pops, planes) + tile],
        [both(3), three, three, (pops, planes) + tile, pltpu.SemaphoreType.DMA((planes,))],
        [fe, hold, ab, kept, recv_a, recv_b],
        out_hbm=True,
    )
    return out


def solution(mesh):
    placed = P(None, None, "gx", "gy")
    return jax.shard_map(
        shards, mesh=mesh, in_specs=(placed,) * 5, out_specs=placed, check_vma=False
    )
```

```python
import jax
import jax.numpy as jnp
from jax import lax
from jax.experimental import pallas as pl
from jax.experimental.pallas import tpu as pltpu
from jax.sharding import PartitionSpec as P

VELOCITY = (
    (1, 0, 0),
    (-1, 0, 0),
    (0, 1, 0),
    (0, -1, 0),
    (1, 1, 0),
    (-1, -1, 0),
    (1, -1, 0),
    (-1, 1, 0),
    (1, 0, 1),
    (-1, 0, -1),
    (1, 0, -1),
    (-1, 0, 1),
    (0, 1, 1),
    (0, -1, -1),
    (0, 1, -1),
    (0, -1, 1),
    (0, 0, 0),
    (0, 0, 1),
    (0, 0, -1),
)
INDEX = {c: q for q, c in enumerate(VELOCITY)}
W1, W2, W0 = 1.0 / 18.0, 1.0 / 36.0, 1.0 / 3.0
RELAXATION = (1.0, 1.0, 1.25)
COUPLING = ((0.0, 1.2, -0.6), (1.2, 0.0, -0.6), (-0.6, -0.6, -0.3))
CROSS = ((0, 0), (1, 0), (-1, 0), (0, 1), (0, -1))
AHEAD = tuple(INDEX[(1,) + yz] for yz in CROSS)
BEHIND = tuple(INDEX[(-1,) + yz] for yz in CROSS)
SIDE = ((1, 0), (-1, 0), (0, 1), (0, -1), (1, 1), (-1, -1), (1, -1), (-1, 1))
F32 = jnp.float32
VMEM_BYTES = 40 * 1024 * 1024
HALO = 4


class Grid:
    def __init__(self, planes, rows, cols):
        self.planes, self.rows, self.cols = planes, rows, cols
        self.tiles = planes + 1
        self.width = cols // planes
        self.group = 2 * HALO
        self.pack = self.width // self.group
        self.sub = lax.broadcasted_iota(jnp.int32, (rows, cols), 0)
        self.lane = lax.broadcasted_iota(jnp.int32, (rows, cols), 1)

    def roll_rows(self, v, dx):
        return pltpu.roll(v, (-dx) % self.rows, 0)

    def roll_cols(self, v, dy):
        return pltpu.roll(v, (-dy) % self.cols, 1)

    def at_row(self, v, rim, dx):
        edge = self.rows - 1 if dx > 0 else 0
        return jnp.where(self.sub == edge, rim, self.roll_rows(v, dx))

    def in_row(self, v, dx):
        edge = self.rows - 1 if dx > 0 else 0
        return jnp.where(self.sub == edge, 0.0, self.roll_rows(v, dx))

    def sides(self, low, high):
        return jnp.where(self.sub == 0, low, high)

    def over(self, body):
        def step(p, carry):
            body(Tile(self, p, False))
            return carry

        lax.fori_loop(0, self.planes, step, 0)
        body(Tile(self, self.planes, True))


class Tile:
    def __init__(self, grid, index, edge):
        self.grid, self.index, self.edge = grid, index, edge

    def of(self, dz):
        if dz == 0 or self.edge:
            return self.index
        return lax.rem(self.index + (dz + self.grid.planes), self.grid.planes)

    def get(self, ref, c, dz=0):
        v = ref[c, self.of(dz)]
        if self.edge and dz != 0:
            v = self.grid.roll_cols(v, dz * self.grid.width)
        return v

    def split(self, main, edge, c, dz=0):
        if not self.edge:
            return main[c, self.of(dz)]
        v = edge[c]
        return v if dz == 0 else self.grid.roll_cols(v, dz * self.grid.width)


def plus(a, b):
    return b if a is None else a + b


def mixed(coefficients, values):
    total = None
    for k, v in zip(coefficients, values):
        if k == 0:
            continue
        term = v if k == 1 else (-v if k == -1 else k * v)
        total = plus(total, term)
    return total


def axis_pairs():
    for q in (0, 2, 17, 4, 6, 8, 10, 12, 14):
        c = VELOCITY[q]
        yield c, (W1 if sum(abs(i) for i in c) == 1 else W2)


def first_and_second(diff, total):
    first = [None] * 3
    second = {}
    for c, w in axis_pairs():
        for d in range(3):
            if c[d] == 0:
                continue
            if diff is not None:
                first[d] = plus(first[d], (w * c[d]) * diff[c])
            if total is not None:
                for e in range(d, 3):
                    if c[e] != 0:
                        second[d, e] = plus(second.get((d, e)), (w * c[d] * c[e]) * total[c])
    return first, second


def turned(second, v):
    return [sum(second[min(d, e), max(d, e)] * v[e] for e in range(3)) for d in range(3)]


def dot(a, b):
    return a[0] * b[0] + a[1] * b[1] + a[2] * b[2]


def field_forces(grid, tile, fields, rim, rim_psi, rim_dip, dipole):
    memo = {}

    def source(name, dz, edge):
        key = (name, dz, edge)
        if key in memo:
            return memo[key]
        if edge:
            load = lambda c: tile.get(rim, (rim_psi + c) if c < 3 else (rim_dip + c - 3), dz)
        else:
            load = lambda c: tile.get(fields, (9 + c) if c < 3 else (6 + c - 3), dz)
        if isinstance(name, int):
            v = load(name)
        elif name == "chi":
            v = source(0, dz, edge) - source(1, dz, edge)
        elif name[0] == "V":
            v = source(2, dz, edge) * source(3 + name[1], dz, edge)
        else:
            v = mixed(name[1], [source(("V", d), dz, edge) if name[1][d] else None for d in range(3)])
        memo[key] = v
        return v

    def shifted(name, c):
        key = (name, c, "shift")
        if key in memo:
            return memo[key]
        if c[1] != 0:
            v = grid.roll_cols(shifted(name, (c[0], 0, c[2])), c[1])
        elif c[0] != 0:
            v = grid.at_row(source(name, c[2], False), source(name, c[2], True), c[0])
        else:
            v = source(name, c[2], False)
        memo[key] = v
        return v

    def parts(name):
        diff, total = {}, {}
        for c, w in axis_pairs():
            back = tuple(-i for i in c)
            a, b = shifted(name, c), shifted(name, back)
            diff[c], total[c] = a - b, a + b
        return diff, total

    diff, unused = parts(0)
    s0, unused = first_and_second(diff, None)
    diff, unused = parts(2)
    s2, unused = first_and_second(diff, None)
    diff, total = parts("chi")
    schi, second = first_and_second(diff, total)
    s1 = [a - b for a, b in zip(s0, schi)]
    pull = [None] * 3
    for c, w in axis_pairs():
        back = tuple(-i for i in c)
        if sum(abs(i) for i in c) == 1:
            name = ("V", [i for i in range(3) if c[i]][0])
        else:
            name = ("L", c)
        total_c = shifted(name, c) + shifted(name, back)
        for d in range(3):
            if c[d] != 0:
                pull[d] = plus(pull[d], (w * c[d]) * total_c)
    md = turned(second, dipole)
    k0 = [-1.2 * s1[d] + 0.6 * s2[d] - pull[d] for d in range(3)]
    k1 = [-1.2 * s0[d] + 0.6 * s2[d] + pull[d] for d in range(3)]
    k2 = [0.6 * (s0[d] + s1[d]) + 0.3 * s2[d] + md[d] for d in range(3)]
    return k0, k1, k2


def collision_adjoint(grid, tile, load, rim, fields, forces, hold, ab, kept):
    u = [tile.get(fields, 3 + d) for d in range(3)]
    rho = [tile.get(fields, s) for s in range(3)]
    inverse_sum = 1.0 / (rho[0] + rho[1] + rho[2])
    grad_u = [None] * 3
    alphas = []
    t = tile.index
    for s in range(3):
        streamed = []
        for q in range(19):
            c = VELOCITY[q]
            v = load(s * 19 + q, c[2])
            if c[0] != 0:
                j = (AHEAD if c[0] > 0 else BEHIND).index(q)
                v = grid.at_row(v, tile.get(rim, s * 5 + j, c[2]), c[0])
            if c[1] != 0:
                v = grid.roll_cols(v, c[1])
            streamed.append(v)
            if s == 2:
                kept[q, t] = v
        diff, total = {}, {}
        for c, w in axis_pairs():
            a, b = streamed[INDEX[c]], streamed[INDEX[tuple(-i for i in c)]]
            diff[c], total[c] = a - b, a + b
        m1, m2 = first_and_second(diff, total)
        m0 = W0 * streamed[16]
        for c, w in axis_pairs():
            m0 = m0 + w * total[c]
        psi = tile.get(fields, 9 + s)
        inverse = 1.0 / rho[s]
        ratio = psi * inverse
        tau = RELAXATION[s]
        k = forces[s]
        v = [u[d] + (tau * ratio) * k[d] for d in range(3)]
        mv = turned(m2, v)
        g = [3.0 * (m1[d] + 3.0 * mv[d] - m0 * v[d]) for d in range(3)]
        feq = m0 + 3.0 * dot(m1, v) + 4.5 * dot(mv, v) - 1.5 * m0 * dot(v, v)
        alphas.append(feq * (1.0 / tau) + dot(g, k) * (1.0 - psi - ratio))
        scaled = rho[s] * (1.0 / tau)
        for d in range(3):
            grad_u[d] = plus(grad_u[d], scaled * g[d])
            hold[3 * s + d, t] = psi * g[d]
    beta = [grad_u[d] * inverse_sum for d in range(3)]
    along = dot(beta, u)
    for s in range(3):
        ab[s, t] = alphas[s] - along
        ab[3 + s, t] = beta[s]


def spread_plane(grid, get_h, get_d, sign, pairs):
    memo = {}

    def source(dz):
        if dz in memo:
            return memo[dz]
        h = [[get_h(3 * s + d, dz) for d in range(3)] for s in range(3)]
        dip = [get_d(d, dz) for d in range(3)]
        if not isinstance(sign, int):
            for vec in h + [dip]:
                vec[0] = vec[0] * sign
        memo[dz] = (h, dip)
        return memo[dz]

    cx = sign if isinstance(sign, int) else 1
    r = [None] * 3
    w_vec = [None] * 3
    lanes = {}
    for cy, cz in pairs:
        w = W1 if abs(cx) + abs(cy) + abs(cz) == 1 else W2
        h, dip = source(cz)
        c = (cx, cy, cz)
        e = [mixed(c, h[s]) for s in range(3)]
        f = e[2] * mixed(c, dip)
        half = 0.6 * e[2]
        r0 = 1.2 * e[1] - half + f
        r1 = 1.2 * e[0] - half - f
        r2 = -0.6 * (e[0] + e[1]) - 0.3 * e[2]
        qv = e[0] - e[1]
        vals = [w * r0, w * r1, w * r2]
        wq = w * qv
        vals += [wq if cx != 0 else None, wq if cy != 0 else None, wq if cz != 0 else None]
        vals = [vals[0], vals[1], vals[2]] + [
            None if x is None else (x if k == 1 else -x) for x, k in zip(vals[3:], (cx, cy, cz))
        ]
        acc = lanes.setdefault(cy, [None] * 6)
        for i, x in enumerate(vals):
            if x is not None:
                acc[i] = plus(acc[i], x)
    total = [None] * 6
    for cy, acc in lanes.items():
        for i, x in enumerate(acc):
            if x is not None:
                total[i] = plus(total[i], x if cy == 0 else grid.roll_cols(x, cy))
    if not isinstance(sign, int):
        total[3] = total[3] * sign
    return total


def met(total, dipole):
    meet = None
    for d in range(3):
        if total[3 + d] is not None:
            meet = plus(meet, total[3 + d] * dipole[d])
    return [total[0], total[1], total[2] - meet]


def spread_inside(grid, tile, hold, fields):
    get_h = lambda k, dz: tile.get(hold, k, dz)
    get_d = lambda k, dz: tile.get(fields, 6 + k, dz)
    total = spread_plane(grid, get_h, get_d, 0, SIDE)
    for dx in (1, -1):
        part = spread_plane(grid, get_h, get_d, dx, CROSS)
        for i, x in enumerate(part):
            total[i] = plus(total[i], grid.in_row(x, dx))
    return met(total, [tile.get(fields, 6 + d) for d in range(3)])


def rim_sign(grid):
    return jnp.where(
        grid.sub == 0, -1.0, jnp.where(grid.sub == grid.rows - 1, 1.0, 0.0)
    ).astype(F32)


def hand_over(grid, tile, hold, fields, rim, rim_dip, given):
    total = spread_plane(
        grid,
        lambda k, dz: tile.get(hold, k, dz),
        lambda k, dz: tile.get(fields, 6 + k, dz),
        -rim_sign(grid),
        CROSS,
    )
    for s, x in enumerate(met(total, [tile.get(rim, rim_dip + d) for d in range(3)])):
        given[s, tile.index] = x


def unpack_rims(grid, first, second, parity, lines, rims, pairs):
    lines[1 - parity] = first[...]
    lines[parity] = second[...]
    for at, c in enumerate(pairs):
        for t in range(grid.tiles):
            k = c * grid.tiles + t
            rims[at, t] = grid.sides(lines[0, k : k + 1, :], lines[1, k : k + 1, :])


def send_rows(grid, parity, lines, first, second):
    first[...] = lines[0]
    second[...] = lines[1]


def parity_of(axis):
    return lax.rem(lax.axis_index(axis), 2)


def pack_columns_kernel(
    adj_in, late_in, early_in, dip_late_in, dip_early_in,
    send_c, send_d, own_left, own_right, fl, fe, adj,
    late, early, dip_late, dip_early, sems,
):
    planes, rows, cols = adj.shape[1:]
    grid = Grid(planes, rows, cols)
    copies = [
        pltpu.make_async_copy(a, b, sems.at[i])
        for i, (a, b) in enumerate(
            (
                (dip_late_in, dip_late),
                (late_in, late),
                (dip_early_in, dip_early),
                (early_in, early),
                (adj_in, adj),
            )
        )
    ]
    for copy in copies:
        copy.start()
    for which, (saved, dip, out) in enumerate(((late, dip_late, fl), (early, dip_early, fe))):
        copies[2 * which].wait()
        copies[2 * which + 1].wait()

        def step(p, carry):
            flows = [None] * 19
            rho = []
            for s in range(3):
                total = None
                for q in range(19):
                    v = saved[s * 19 + q, p].astype(F32)
                    flows[q] = plus(flows[q], v)
                    total = plus(total, v)
                rho.append(total)
                out[s, p] = total
            inverse = 1.0 / (rho[0] + rho[1] + rho[2])
            for d in range(3):
                momentum = None
                for q in range(19):
                    if VELOCITY[q][d] != 0:
                        momentum = plus(momentum, flows[q] if VELOCITY[q][d] > 0 else -flows[q])
                out[3 + d, p] = momentum * inverse
                out[6 + d, p] = dip[d, p].astype(F32)
            return carry

        lax.fori_loop(0, planes, step, 0)
    copies[4].wait()
    pops = adj.shape[0]
    components = pops + 18
    slot = grid.lane // grid.group
    for g in range(own_left.shape[0]):
        left = right = jnp.zeros((rows, cols), F32)
        for j in range(grid.pack):
            c = g * grid.pack + j
            if c >= components:
                continue
            for p in range(planes):
                if c < pops:
                    v = adj[c, p]
                elif c < pops + 9:
                    v = fl[c - pops, p]
                else:
                    v = fe[c - pops - 9, p]
                at = p * grid.pack + j
                rolled = pltpu.roll(v, at * grid.group, 1) if at else v
                left = jnp.where(slot == at, rolled, left)
                right = jnp.where(slot == (at - 1) % (cols // grid.group), rolled, right)
        own_left[g] = left
        own_right[g] = right
    low = lax.rem(grid.lane, grid.group) < HALO
    even = parity_of("gy") == 0
    for h in range(send_c.shape[0]):
        left = jnp.where(low, own_left[2 * h], pltpu.roll(own_left[2 * h + 1], HALO, 1))
        right = jnp.where(low, pltpu.roll(own_right[2 * h + 1], cols - HALO, 1), own_right[2 * h])
        send_c[h] = jnp.where(even, right, left)
        send_d[h] = jnp.where(even, left, right)


def pack_rows_kernel(
    adj, own_left, own_right, recv_c, recv_d, fl_main, fe_main, send_a, send_b, edge, fl, fe, lines
):
    pops, planes, rows, cols = adj.shape
    grid = Grid(planes, rows, cols)
    even = parity_of("gy") == 0
    slot = lax.rem(grid.lane // grid.group, grid.pack)
    left_half = lax.rem(grid.lane, grid.width) < grid.width // 2
    components = pops + 18
    for g in range(own_left.shape[0]):
        first, second = recv_c[g // 2], recv_d[g // 2]
        from_next = jnp.where(even, first, second)
        from_prior = jnp.where(even, second, first)
        if g % 2:
            from_next = pltpu.roll(from_next, cols - HALO, 1)
            from_prior = pltpu.roll(from_prior, HALO, 1)
        for j in range(grid.pack):
            c = g * grid.pack + j
            if c >= components:
                continue
            before = slot == (j - 1) % grid.pack
            low = jnp.where(before, from_prior, own_left[g])
            high = jnp.where(before, own_right[g], from_next)
            v = jnp.where(
                left_half,
                pltpu.roll(low, ((1 - j) * grid.group) % cols, 1),
                pltpu.roll(high, ((3 - j) * grid.group) % cols, 1),
            )
            if c < pops:
                edge[c] = v
            elif c < pops + 9:
                fl[c - pops, planes] = v
            else:
                fe[c - pops - 9, planes] = v
    for main, out in ((fl_main, fl), (fe_main, fe)):
        for c in range(9):
            for p in range(planes):
                out[c, p] = main[c, p]
        for s in range(3):
            for t in range(grid.tiles):
                out[9 + s, t] = 1.0 - jnp.exp(-out[s, t])
    up, down = parity_of("gx"), 1 - parity_of("gx")
    fill = 0

    def put(slot_at, v, row):
        lines[slot_at, fill : fill + 1, :] = v[row : row + 1, :]

    for s in range(3):
        for j in range(5):
            for t in range(grid.tiles):
                ahead, behind = s * 19 + AHEAD[j], s * 19 + BEHIND[j]
                put(up, adj[behind, t] if t < planes else edge[behind], rows - 1)
                put(down, adj[ahead, t] if t < planes else edge[ahead], 0)
                fill += 1
    for out in (fl, fe):
        for c in (9, 10, 11, 6, 7, 8):
            for t in range(grid.tiles):
                put(up, out[c, t], rows - 1)
                put(down, out[c, t], 0)
                fill += 1
    send_rows(grid, up, lines, send_a, send_b)


def late_kernel(
    adj, edge, fl, recv_a, recv_b, send_a, send_b, ab, kept, given, lines, lines_out, rims, hold
):
    pops, planes, rows, cols = adj.shape
    grid = Grid(planes, rows, cols)
    parity = parity_of("gx")
    unpack_rims(grid, recv_a, recv_b, parity, lines, rims, range(21))

    def collide(tile):
        dipole = [tile.get(fl, 6 + d) for d in range(3)]
        forces = field_forces(grid, tile, fl, rims, 15, 18, dipole)
        load = lambda c, dz: tile.split(adj, edge, c, dz)
        collision_adjoint(grid, tile, load, rims, fl, forces, hold, ab, kept)

    grid.over(collide)
    sign = -rim_sign(grid)

    def finish(tile):
        back = spread_inside(grid, tile, hold, fl)
        for s in range(3):
            ab[s, tile.index] = ab[s, tile.index] + (1.0 - tile.get(fl, 9 + s)) * back[s]
        hand_over(grid, tile, hold, fl, rims, 18, given)

    grid.over(finish)
    up, down = parity, 1 - parity
    fill = 0

    def put(v):
        lines_out[up, fill : fill + 1, :] = v[rows - 1 : rows, :]
        lines_out[down, fill : fill + 1, :] = v[0:1, :]

    for c in range(3):
        for t in range(grid.tiles):
            put(given[c, t])
            fill += 1
    for kind in range(9):
        for t in range(grid.tiles):
            if kind < 2:
                put(ab[kind, t] + sign * ab[3, t])
            elif kind < 4:
                put(ab[2 + kind, t])
            else:
                cy, cz = CROSS[kind - 4]
                part = ab[2, t] + sign * ab[3, t]
                if cy or cz:
                    part = part + mixed((cy, cz), (ab[4, t], ab[5, t]))
                put((1.0 - 1.0 / RELAXATION[2]) * grid.sides(kept[AHEAD[kind - 4], t], kept[BEHIND[kind - 4], t]) + part)
            fill += 1
    send_rows(grid, up, lines_out, send_a, send_b)


def early_kernel(
    fl, fe, ab1, kept1, given1, first_a, first_b, recv_a, recv_b, send_a, send_b, hold, ab, kept,
    lines, lines2, lines_out, rims, near, mid, rim_mid, given,
):
    planes, rows, cols = fl.shape[1] - 1, fl.shape[2], fl.shape[3]
    grid = Grid(planes, rows, cols)
    parity = parity_of("gx")
    unpack_rims(grid, first_a, first_b, parity, lines, rims, (15, 16, 17) + tuple(range(21, 27)))
    unpack_rims(grid, recv_a, recv_b, parity, lines2, near, range(12))
    rest = 1.0 - 1.0 / RELAXATION[2]
    at_rim = (grid.sub == 0) | (grid.sub == rows - 1)

    def complete(tile):
        t = tile.index
        inward = [jnp.where(at_rim, tile.get(near, s), 0.0) for s in range(3)]
        alpha = [tile.get(ab1, s) + (1.0 - tile.get(fl, 9 + s)) * inward[s] for s in range(3)]
        beta = [tile.get(ab1, 3 + d) for d in range(3)]
        for q in range(19):
            c = VELOCITY[q]
            along = mixed(c, beta) if q != 16 else None
            for s in range(3):
                v = alpha[s] if along is None else alpha[s] + along
                if s == 2:
                    v = v + rest * kept1[q, t]
                mid[s * 19 + q, t] = v
        fixes = [(1.0 - tile.get(rims, s)) * tile.get(given1, s) for s in range(3)]
        sides = [tile.get(near, 5 + d) for d in range(2)]
        for s in range(2):
            base = tile.get(near, 3 + s) + fixes[s]
            for j, (cy, cz) in enumerate(CROSS):
                rim_mid[s * 5 + j, t] = base if j == 0 else base + mixed((cy, cz), sides)
        for j in range(5):
            rim_mid[10 + j, t] = tile.get(near, 7 + j) + fixes[2]

    grid.over(complete)

    def collide(tile):
        dipole = [tile.get(fe, 6 + d) for d in range(3)]
        forces = field_forces(grid, tile, fe, rims, 3, 6, dipole)
        load = lambda c, dz: tile.get(mid, c, dz)
        collision_adjoint(grid, tile, load, rim_mid, fe, forces, hold, ab, kept)

    grid.over(collide)
    grid.over(lambda tile: hand_over(grid, tile, hold, fe, rims, 6, given))
    up, down = parity, 1 - parity
    fill = 0
    for c in range(3):
        for t in range(grid.tiles):
            v = given[c, t]
            lines_out[up, fill : fill + 1, :] = v[rows - 1 : rows, :]
            lines_out[down, fill : fill + 1, :] = v[0:1, :]
            fill += 1
    send_rows(grid, up, lines_out, send_a, send_b)


def out_kernel(fe, hold, ab, kept, recv_a, recv_b, out, lines, near, total, staged, sems):
    planes, rows, cols = fe.shape[1] - 1, fe.shape[2], fe.shape[3]
    grid = Grid(planes, rows, cols)
    unpack_rims(grid, recv_a, recv_b, parity_of("gx"), lines, near, range(3))
    at_rim = (grid.sub == 0) | (grid.sub == rows - 1)

    def finish(tile):
        back = spread_inside(grid, tile, hold, fe)
        for s in range(3):
            back[s] = back[s] + jnp.where(at_rim, tile.get(near, s), 0.0)
            total[s, tile.index] = tile.get(ab, s) + (1.0 - tile.get(fe, 9 + s)) * back[s]

    grid.over(finish)
    is_low, is_high = grid.lane < HALO, grid.lane >= cols - HALO

    def to_out(p):
        return pltpu.make_async_copy(staged.at[:, p], out.at[:, p], sems.at[p])

    def emit(p, carry):
        base = p * grid.width

        def patched(main, edge):
            low = pltpu.roll(edge, lax.rem(2 * cols - base - grid.group, cols), 1)
            high = pltpu.roll(edge, lax.rem(2 * cols - base - 3 * grid.group, cols), 1)
            return jnp.where(is_low, low, jnp.where(is_high, high, main))

        alpha = [patched(total[s, p], total[s, planes]) for s in range(3)]
        beta = [patched(ab[3 + d, p], ab[3 + d, planes]) for d in range(3)]
        for q in range(19):
            along = mixed(VELOCITY[q], beta) if q != 16 else None
            for s in range(3):
                v = alpha[s] if along is None else alpha[s] + along
                if s == 2:
                    v = v + (1.0 - 1.0 / RELAXATION[2]) * patched(kept[q, p], kept[q, planes])
                staged[s * 19 + q, p] = v
        to_out(p).start()
        return carry

    lax.fori_loop(0, planes, emit, 0)
    for p in range(planes):
        to_out(p).wait()


def call(kernel, outs, scratch, args, in_hbm=False, out_hbm=False):
    vmem = pl.BlockSpec(memory_space=pltpu.VMEM)
    hbm = pl.BlockSpec(memory_space=pltpu.HBM)
    return pl.pallas_call(
        kernel,
        out_shape=[jax.ShapeDtypeStruct(s, F32) for s in outs],
        in_specs=[hbm if in_hbm else vmem] * len(args),
        out_specs=[hbm if out_hbm else vmem] * len(outs),
        scratch_shapes=[pltpu.VMEM(s, F32) if isinstance(s, tuple) else s for s in scratch],
        compiler_params=pltpu.CompilerParams(vmem_limit_bytes=VMEM_BYTES),
    )(*[pltpu.with_memory_space_constraint(x, pltpu.HBM) if in_hbm else x for x in args])


def swap(block, axis, offset):
    size = lax.axis_size(axis)
    route = []
    for i in range(offset, size + offset, 2):
        a, b = i % size, (i + 1) % size
        route += [(a, b), (b, a)]
    return lax.ppermute(block, axis, route)


def shards(adjoint_in, populations_early, populations_late, dipoles_early, dipoles_late):
    pops, planes, rows, cols = adjoint_in.shape
    tiles = planes + 1
    tile = (rows, cols)
    pack = cols // planes // (2 * HALO)
    groups = -(-(pops + 18) // pack)
    groups += groups % 2

    def lines(n):
        return (-(-n * tiles // 8) * 8, cols)

    def both(n):
        return (2,) + lines(n)

    send_c, send_d, own_left, own_right, fl_main, fe_main, adj = call(
        pack_columns_kernel,
        [(groups // 2,) + tile] * 2
        + [(groups,) + tile] * 2
        + [(9, planes) + tile] * 2
        + [(pops, planes) + tile],
        [pltpu.VMEM(x.shape, x.dtype) for x in (populations_late, populations_early)]
        + [pltpu.VMEM(x.shape, x.dtype) for x in (dipoles_late, dipoles_early)]
        + [pltpu.SemaphoreType.DMA((5,))],
        [adjoint_in, populations_late, populations_early, dipoles_late, dipoles_early],
        in_hbm=True,
    )
    recv_c, recv_d = swap(send_c, "gy", 0), swap(send_d, "gy", 1)
    send_a, send_b, edge, fl, fe = call(
        pack_rows_kernel,
        [lines(27)] * 2 + [(pops,) + tile] + [(12, tiles) + tile] * 2,
        [both(27)],
        [adj, own_left, own_right, recv_c, recv_d, fl_main, fe_main],
    )
    first_a, first_b = swap(send_a, "gx", 0), swap(send_b, "gx", 1)
    hold_shape, ab_shape, kept_shape = [(n, tiles) + tile for n in (9, 6, 19)]
    three = (3, tiles) + tile
    send_a, send_b, ab1, kept1, given1 = call(
        late_kernel,
        [lines(12)] * 2 + [ab_shape, kept_shape, three],
        [both(27), both(12), (21, tiles) + tile, hold_shape],
        [adj, edge, fl, first_a, first_b],
    )
    recv_a, recv_b = swap(send_a, "gx", 0), swap(send_b, "gx", 1)
    send_a, send_b, hold, ab, kept = call(
        early_kernel,
        [lines(3)] * 2 + [hold_shape, ab_shape, kept_shape],
        [
            both(27),
            both(12),
            both(3),
            (9, tiles) + tile,
            (12, tiles) + tile,
            (pops, tiles) + tile,
            (15, tiles) + tile,
            three,
        ],
        [fl, fe, ab1, kept1, given1, first_a, first_b, recv_a, recv_b],
    )
    recv_a, recv_b = swap(send_a, "gx", 0), swap(send_b, "gx", 1)
    (out,) = call(
        out_kernel,
        [(pops, planes) + tile],
        [both(3), three, three, (pops, planes) + tile, pltpu.SemaphoreType.DMA((planes,))],
        [fe, hold, ab, kept, recv_a, recv_b],
        out_hbm=True,
    )
    return out


def solution(mesh):
    placed = P(None, None, "gx", "gy")
    return jax.shard_map(
        shards, mesh=mesh, in_specs=(placed,) * 5, out_specs=placed, check_vma=False
    )
```

```python
import jax
import jax.numpy as jnp
from jax import lax
from jax.experimental import pallas as pl
from jax.experimental.pallas import tpu as pltpu
from jax.sharding import PartitionSpec as P

VELOCITY = (
    (1, 0, 0),
    (-1, 0, 0),
    (0, 1, 0),
    (0, -1, 0),
    (1, 1, 0),
    (-1, -1, 0),
    (1, -1, 0),
    (-1, 1, 0),
    (1, 0, 1),
    (-1, 0, -1),
    (1, 0, -1),
    (-1, 0, 1),
    (0, 1, 1),
    (0, -1, -1),
    (0, 1, -1),
    (0, -1, 1),
    (0, 0, 0),
    (0, 0, 1),
    (0, 0, -1),
)
INDEX = {c: q for q, c in enumerate(VELOCITY)}
W1, W2, W0 = 1.0 / 18.0, 1.0 / 36.0, 1.0 / 3.0
RELAXATION = (1.0, 1.0, 1.25)
COUPLING = ((0.0, 1.2, -0.6), (1.2, 0.0, -0.6), (-0.6, -0.6, -0.3))
CROSS = ((0, 0), (1, 0), (-1, 0), (0, 1), (0, -1))
AHEAD = tuple(INDEX[(1,) + yz] for yz in CROSS)
BEHIND = tuple(INDEX[(-1,) + yz] for yz in CROSS)
SIDE = ((1, 0), (-1, 0), (0, 1), (0, -1), (1, 1), (-1, -1), (1, -1), (-1, 1))
PSI_DIP = (9, 10, 11, 6, 7, 8)
FIRST_LINES = 15 + 6 + 12 + 6
KEPT_LINES = tuple(range(15, 18)) + tuple(range(21, 39))
RIM_EARLY, RIM_FAR = 3, 15
LEVEL = tuple(q for q in range(19) if VELOCITY[q][0] == 0)
SECOND_LINES = 3 + 5 + 4 + 5 + 5 + 9
F32 = jnp.float32
VMEM_BYTES = 40 * 1024 * 1024
HALO = 4


class Grid:
    def __init__(self, planes, rows, cols):
        self.planes, self.rows, self.cols = planes, rows, cols
        self.tiles = planes + 1
        self.width = cols // planes
        self.group = 2 * HALO
        self.pack = self.width // self.group
        self.sub = lax.broadcasted_iota(jnp.int32, (rows, cols), 0)
        self.lane = lax.broadcasted_iota(jnp.int32, (rows, cols), 1)

    def roll_rows(self, v, dx):
        return pltpu.roll(v, (-dx) % self.rows, 0)

    def roll_cols(self, v, dy):
        return pltpu.roll(v, (-dy) % self.cols, 1)

    def at_row(self, v, rim, dx):
        edge = self.rows - 1 if dx > 0 else 0
        return jnp.where(self.sub == edge, rim, self.roll_rows(v, dx))

    def in_row(self, v, dx):
        edge = self.rows - 1 if dx > 0 else 0
        return jnp.where(self.sub == edge, 0.0, self.roll_rows(v, dx))

    def sides(self, low, high):
        return jnp.where(self.sub == 0, low, high)

    def over(self, body):
        def step(p, carry):
            body(Tile(self, p, False))
            return carry

        lax.fori_loop(0, self.planes, step, 0)
        body(Tile(self, self.planes, True))


class Tile:
    def __init__(self, grid, index, edge):
        self.grid, self.index, self.edge = grid, index, edge

    def of(self, dz):
        if dz == 0 or self.edge:
            return self.index
        return lax.rem(self.index + (dz + self.grid.planes), self.grid.planes)

    def get(self, ref, c, dz=0):
        v = ref[c, self.of(dz)]
        if self.edge and dz != 0:
            v = self.grid.roll_cols(v, dz * self.grid.width)
        return v

    def split(self, main, edge, c, dz=0):
        if not self.edge:
            return main[c, self.of(dz)]
        v = edge[c]
        return v if dz == 0 else self.grid.roll_cols(v, dz * self.grid.width)


def plus(a, b):
    return b if a is None else a + b


def mixed(coefficients, values):
    total = None
    for k, v in zip(coefficients, values):
        if k == 0:
            continue
        term = v if k == 1 else (-v if k == -1 else k * v)
        total = plus(total, term)
    return total


def axis_pairs():
    for q in (0, 2, 17, 4, 6, 8, 10, 12, 14):
        c = VELOCITY[q]
        yield c, (W1 if sum(abs(i) for i in c) == 1 else W2)


def first_and_second(diff, total):
    first = [None] * 3
    second = {}
    for c, w in axis_pairs():
        for d in range(3):
            if c[d] == 0:
                continue
            if diff is not None:
                first[d] = plus(first[d], (w * c[d]) * diff[c])
            if total is not None:
                for e in range(d, 3):
                    if c[e] != 0:
                        second[d, e] = plus(second.get((d, e)), (w * c[d] * c[e]) * total[c])
    return first, second


def turned(second, v):
    return [sum(second[min(d, e), max(d, e)] * v[e] for e in range(3)) for d in range(3)]


def dot(a, b):
    return a[0] * b[0] + a[1] * b[1] + a[2] * b[2]


def field_forces(grid, loads, across, dipole):
    memo = {}

    def source(name, dz, place):
        key = (name, dz, place)
        if key in memo:
            return memo[key]
        if isinstance(name, int):
            v = loads[place](name, dz)
        elif name == "chi":
            v = source(0, dz, place) - source(1, dz, place)
        elif name[0] == "V":
            v = source(2, dz, place) * source(3 + name[1], dz, place)
        else:
            c = name[1]
            v = mixed(c, [source(("V", d), dz, place) if c[d] else None for d in range(3)])
        memo[key] = v
        return v

    def shifted(name, c):
        key = (name, c, "shift")
        if key in memo:
            return memo[key]
        if c[1] != 0:
            v = grid.roll_cols(shifted(name, (c[0], 0, c[2])), c[1])
        elif c[0] != 0:
            v = across(lambda place, dz: source(name, dz, place), c[0], c[2])
        else:
            v = source(name, c[2], 0)
        memo[key] = v
        return v

    def parts(name):
        diff, total = {}, {}
        for c, w in axis_pairs():
            back = tuple(-i for i in c)
            a, b = shifted(name, c), shifted(name, back)
            diff[c], total[c] = a - b, a + b
        return diff, total

    diff, unused = parts(0)
    s0, unused = first_and_second(diff, None)
    diff, unused = parts(2)
    s2, unused = first_and_second(diff, None)
    diff, total = parts("chi")
    schi, second = first_and_second(diff, total)
    s1 = [a - b for a, b in zip(s0, schi)]
    pull = [None] * 3
    for c, w in axis_pairs():
        back = tuple(-i for i in c)
        if sum(abs(i) for i in c) == 1:
            name = ("V", [i for i in range(3) if c[i]][0])
        else:
            name = ("L", c)
        total_c = shifted(name, c) + shifted(name, back)
        for d in range(3):
            if c[d] != 0:
                pull[d] = plus(pull[d], (w * c[d]) * total_c)
    md = turned(second, dipole)
    k0 = [-1.2 * s1[d] + 0.6 * s2[d] - pull[d] for d in range(3)]
    k1 = [-1.2 * s0[d] + 0.6 * s2[d] + pull[d] for d in range(3)]
    k2 = [0.6 * (s0[d] + s1[d]) + 0.3 * s2[d] + md[d] for d in range(3)]
    return k0, k1, k2


def brick_forces(grid, tile, fields, rim, rim_psi, rim_dip):
    def own(c, dz):
        return tile.get(fields, (9 + c) if c < 3 else (3 + c), dz)

    def beyond(c, dz):
        return tile.get(rim, (rim_psi + c) if c < 3 else (rim_dip + c - 3), dz)

    def across(get, cx, dz):
        return grid.at_row(get(0, dz), get(1, dz), cx)

    return field_forces(grid, (own, beyond), across, [own(3 + d, 0) for d in range(3)])


def rim_forces(grid, tile, fields, rim, psi1, dip1, psi2, dip2):
    outward = jnp.where(grid.sub < grid.rows // 2, -1.0, 1.0).astype(F32)

    def loader(ref, psi, dip):
        def load(c, dz):
            v = tile.get(ref, (psi + c) if c < 3 else (dip + c - 3), dz)
            return v * outward if c == 3 else v

        return load

    loads = {0: loader(rim, psi1, dip1), 1: loader(rim, psi2, dip2), -1: loader(fields, 9, 6)}
    dipole = [loads[0](3 + d, 0) for d in range(3)]
    return field_forces(grid, loads, lambda get, cx, dz: get(cx, dz), dipole)


def collision_adjoint(streamed_of, rho, u, psi, forces):
    inverse_sum = 1.0 / (rho[0] + rho[1] + rho[2])
    grad_u = [None] * 3
    alphas, held = [], []
    for s in range(3):
        streamed = streamed_of(s)
        diff, total = {}, {}
        for c, w in axis_pairs():
            a, b = streamed[INDEX[c]], streamed[INDEX[tuple(-i for i in c)]]
            diff[c], total[c] = a - b, a + b
        m1, m2 = first_and_second(diff, total)
        m0 = W0 * streamed[16]
        for c, w in axis_pairs():
            m0 = m0 + w * total[c]
        inverse = 1.0 / rho[s]
        ratio = psi[s] * inverse
        tau = RELAXATION[s]
        k = forces[s]
        v = [u[d] + (tau * ratio) * k[d] for d in range(3)]
        mv = turned(m2, v)
        g = [3.0 * (m1[d] + 3.0 * mv[d] - m0 * v[d]) for d in range(3)]
        feq = m0 + 3.0 * dot(m1, v) + 4.5 * dot(mv, v) - 1.5 * m0 * dot(v, v)
        alphas.append(feq * (1.0 / tau) + dot(g, k) * (1.0 - psi[s] - ratio))
        scaled = rho[s] * (1.0 / tau)
        for d in range(3):
            grad_u[d] = plus(grad_u[d], scaled * g[d])
            held.append(psi[s] * g[d])
    beta = [grad_u[d] * inverse_sum for d in range(3)]
    along = dot(beta, u)
    return held, [a - along for a in alphas], beta


def brick_collision(grid, tile, load, rim, fields, forces, hold, ab, kept):
    t = tile.index

    def streamed_of(s):
        streamed = []
        for q in range(19):
            c = VELOCITY[q]
            v = load(s * 19 + q, c[2])
            if c[0] != 0:
                j = (AHEAD if c[0] > 0 else BEHIND).index(q)
                v = grid.at_row(v, tile.get(rim, s * 5 + j, c[2]), c[0])
            if c[1] != 0:
                v = grid.roll_cols(v, c[1])
            streamed.append(v)
            if s == 2:
                kept[q, t] = v
        return streamed

    rho, u, psi = [[tile.get(fields, at + d) for d in range(3)] for at in (0, 3, 9)]
    held, alpha, beta = collision_adjoint(streamed_of, rho, u, psi, forces)
    for k in range(9):
        hold[k, t] = held[k]
    for s in range(3):
        ab[s, t] = alpha[s]
        ab[3 + s, t] = beta[s]


def spread_plane(grid, get_h, get_d, sign, pairs):
    memo = {}

    def source(dz):
        if dz in memo:
            return memo[dz]
        h = [[get_h(3 * s + d, dz) for d in range(3)] for s in range(3)]
        dip = [get_d(d, dz) for d in range(3)]
        if not isinstance(sign, int):
            for vec in h + [dip]:
                vec[0] = vec[0] * sign
        memo[dz] = (h, dip)
        return memo[dz]

    cx = sign if isinstance(sign, int) else 1
    r = [None] * 3
    w_vec = [None] * 3
    lanes = {}
    for cy, cz in pairs:
        w = W1 if abs(cx) + abs(cy) + abs(cz) == 1 else W2
        h, dip = source(cz)
        c = (cx, cy, cz)
        e = [mixed(c, h[s]) for s in range(3)]
        f = e[2] * mixed(c, dip)
        half = 0.6 * e[2]
        r0 = 1.2 * e[1] - half + f
        r1 = 1.2 * e[0] - half - f
        r2 = -0.6 * (e[0] + e[1]) - 0.3 * e[2]
        qv = e[0] - e[1]
        vals = [w * r0, w * r1, w * r2]
        wq = w * qv
        vals += [wq if cx != 0 else None, wq if cy != 0 else None, wq if cz != 0 else None]
        vals = [vals[0], vals[1], vals[2]] + [
            None if x is None else (x if k == 1 else -x) for x, k in zip(vals[3:], (cx, cy, cz))
        ]
        acc = lanes.setdefault(cy, [None] * 6)
        for i, x in enumerate(vals):
            if x is not None:
                acc[i] = plus(acc[i], x)
    total = [None] * 6
    for cy, acc in lanes.items():
        for i, x in enumerate(acc):
            if x is not None:
                total[i] = plus(total[i], x if cy == 0 else grid.roll_cols(x, cy))
    if not isinstance(sign, int):
        total[3] = total[3] * sign
    return total


def met(total, dipole):
    meet = None
    for d in range(3):
        if total[3 + d] is not None:
            meet = plus(meet, total[3 + d] * dipole[d])
    return [total[0], total[1], total[2] - meet]


def spread_inside(grid, tile, hold, fields):
    get_h = lambda k, dz: tile.get(hold, k, dz)
    get_d = lambda k, dz: tile.get(fields, 6 + k, dz)
    total = spread_plane(grid, get_h, get_d, 0, SIDE)
    for dx in (1, -1):
        part = spread_plane(grid, get_h, get_d, dx, CROSS)
        for i, x in enumerate(part):
            total[i] = plus(total[i], grid.in_row(x, dx))
    return met(total, [tile.get(fields, 6 + d) for d in range(3)])


def rim_sign(grid):
    return jnp.where(
        grid.sub == 0, -1.0, jnp.where(grid.sub == grid.rows - 1, 1.0, 0.0)
    ).astype(F32)


def hand_over(grid, tile, hold, fields, rim, rim_dip, given):
    total = spread_plane(
        grid,
        lambda k, dz: tile.get(hold, k, dz),
        lambda k, dz: tile.get(fields, 6 + k, dz),
        -rim_sign(grid),
        CROSS,
    )
    for s, x in enumerate(met(total, [tile.get(rim, rim_dip + d) for d in range(3)])):
        given[s, tile.index] = x


def unpack_rims(grid, first, second, parity, lines, rims, pairs):
    lines[1 - parity] = first[...]
    lines[parity] = second[...]
    for at, c in enumerate(pairs):
        for t in range(grid.tiles):
            k = c * grid.tiles + t
            rims[at, t] = grid.sides(lines[0, k : k + 1, :], lines[1, k : k + 1, :])


def send_rows(grid, parity, lines, first, second):
    first[...] = lines[0]
    second[...] = lines[1]


def parity_of(axis):
    return lax.rem(lax.axis_index(axis), 2)


def pack_columns_kernel(
    adj_in, late_in, early_in, dip_late_in, dip_early_in,
    send_c, send_d, own_left, own_right, fl, fe, adj,
    late, early, dip_late, dip_early, sems,
):
    planes, rows, cols = adj.shape[1:]
    grid = Grid(planes, rows, cols)
    copies = [
        pltpu.make_async_copy(a, b, sems.at[i])
        for i, (a, b) in enumerate(
            (
                (dip_late_in, dip_late),
                (late_in, late),
                (dip_early_in, dip_early),
                (early_in, early),
                (adj_in, adj),
            )
        )
    ]
    for copy in copies:
        copy.start()
    for which, (saved, dip, out) in enumerate(((late, dip_late, fl), (early, dip_early, fe))):
        copies[2 * which].wait()
        copies[2 * which + 1].wait()

        def step(p, carry):
            flows = [None] * 19
            rho = []
            for s in range(3):
                total = None
                for q in range(19):
                    v = saved[s * 19 + q, p].astype(F32)
                    flows[q] = plus(flows[q], v)
                    total = plus(total, v)
                rho.append(total)
                out[s, p] = total
            inverse = 1.0 / (rho[0] + rho[1] + rho[2])
            for d in range(3):
                momentum = None
                for q in range(19):
                    if VELOCITY[q][d] != 0:
                        momentum = plus(momentum, flows[q] if VELOCITY[q][d] > 0 else -flows[q])
                out[3 + d, p] = momentum * inverse
                out[6 + d, p] = dip[d, p].astype(F32)
            return carry

        lax.fori_loop(0, planes, step, 0)
    copies[4].wait()
    pops = adj.shape[0]
    components = pops + 18
    slot = grid.lane // grid.group
    for g in range(own_left.shape[0]):
        left = right = jnp.zeros((rows, cols), F32)
        for j in range(grid.pack):
            c = g * grid.pack + j
            if c >= components:
                continue
            for p in range(planes):
                if c < pops:
                    v = adj[c, p]
                elif c < pops + 9:
                    v = fl[c - pops, p]
                else:
                    v = fe[c - pops - 9, p]
                at = p * grid.pack + j
                rolled = pltpu.roll(v, at * grid.group, 1) if at else v
                left = jnp.where(slot == at, rolled, left)
                right = jnp.where(slot == (at - 1) % (cols // grid.group), rolled, right)
        own_left[g] = left
        own_right[g] = right
    low = lax.rem(grid.lane, grid.group) < HALO
    even = parity_of("gy") == 0
    for h in range(send_c.shape[0]):
        left = jnp.where(low, own_left[2 * h], pltpu.roll(own_left[2 * h + 1], HALO, 1))
        right = jnp.where(low, pltpu.roll(own_right[2 * h + 1], cols - HALO, 1), own_right[2 * h])
        send_c[h] = jnp.where(even, right, left)
        send_d[h] = jnp.where(even, left, right)


def pack_rows_kernel(
    adj, own_left, own_right, recv_c, recv_d, fl_main, fe_main, send_a, send_b, edge, fl, fe, lines
):
    pops, planes, rows, cols = adj.shape
    grid = Grid(planes, rows, cols)
    even = parity_of("gy") == 0
    slot = lax.rem(grid.lane // grid.group, grid.pack)
    left_half = lax.rem(grid.lane, grid.width) < grid.width // 2
    components = pops + 18
    for g in range(own_left.shape[0]):
        first, second = recv_c[g // 2], recv_d[g // 2]
        from_next = jnp.where(even, first, second)
        from_prior = jnp.where(even, second, first)
        if g % 2:
            from_next = pltpu.roll(from_next, cols - HALO, 1)
            from_prior = pltpu.roll(from_prior, HALO, 1)
        for j in range(grid.pack):
            c = g * grid.pack + j
            if c >= components:
                continue
            before = slot == (j - 1) % grid.pack
            low = jnp.where(before, from_prior, own_left[g])
            high = jnp.where(before, own_right[g], from_next)
            v = jnp.where(
                left_half,
                pltpu.roll(low, ((1 - j) * grid.group) % cols, 1),
                pltpu.roll(high, ((3 - j) * grid.group) % cols, 1),
            )
            if c < pops:
                edge[c] = v
            elif c < pops + 9:
                fl[c - pops, planes] = v
            else:
                fe[c - pops - 9, planes] = v
    for main, out in ((fl_main, fl), (fe_main, fe)):
        for c in range(9):
            for p in range(planes):
                out[c, p] = main[c, p]
        for s in range(3):
            for t in range(grid.tiles):
                out[9 + s, t] = 1.0 - jnp.exp(-out[s, t])
    up, down = parity_of("gx"), 1 - parity_of("gx")
    fill = 0

    def put(slot_at, v, row):
        lines[slot_at, fill : fill + 1, :] = v[row : row + 1, :]

    def put_both(out, c, depth):
        nonlocal fill
        for t in range(grid.tiles):
            put(up, out[c, t], rows - 1 - depth)
            put(down, out[c, t], depth)
            fill += 1

    for s in range(3):
        for j in range(5):
            for t in range(grid.tiles):
                ahead, behind = s * 19 + AHEAD[j], s * 19 + BEHIND[j]
                put(up, adj[behind, t] if t < planes else edge[behind], rows - 1)
                put(down, adj[ahead, t] if t < planes else edge[ahead], 0)
                fill += 1
    for c in PSI_DIP:
        put_both(fl, c, 0)
    for c in range(12):
        put_both(fe, c, 0)
    for c in PSI_DIP:
        put_both(fe, c, 1)
    send_rows(grid, up, lines, send_a, send_b)


def late_kernel(
    adj, edge, fl, recv_a, recv_b, send_a, send_b, ab, kept, given, lines, lines_out, rims, hold
):
    pops, planes, rows, cols = adj.shape
    grid = Grid(planes, rows, cols)
    parity = parity_of("gx")
    unpack_rims(grid, recv_a, recv_b, parity, lines, rims, range(21))

    def collide(tile):
        forces = brick_forces(grid, tile, fl, rims, 15, 18)
        load = lambda c, dz: tile.split(adj, edge, c, dz)
        brick_collision(grid, tile, load, rims, fl, forces, hold, ab, kept)

    grid.over(collide)

    def finish(tile):
        back = spread_inside(grid, tile, hold, fl)
        for s in range(3):
            ab[s, tile.index] = ab[s, tile.index] + (1.0 - tile.get(fl, 9 + s)) * back[s]
        hand_over(grid, tile, hold, fl, rims, 18, given)

    grid.over(finish)
    up, down = parity, 1 - parity
    fill = 0

    def put(make, depth=0):
        nonlocal fill
        for t in range(grid.tiles):
            v = make(t)
            lines_out[up, fill : fill + 1, :] = v[rows - 1 - depth : rows - depth, :]
            lines_out[down, fill : fill + 1, :] = v[depth : depth + 1, :]
            fill += 1

    low = grid.sub < rows // 2
    inward = jnp.where(low, 1.0, -1.0).astype(F32)
    rest = 1.0 - 1.0 / RELAXATION[2]

    def crossing(j):
        cy, cz = CROSS[j]

        def make(t):
            v = rest * jnp.where(low, kept[AHEAD[j], t], kept[BEHIND[j], t])
            v = v + (ab[2, t] + inward * ab[3, t])
            return v + mixed((cy, cz), (ab[4, t], ab[5, t])) if j else v

        return make

    def level(q):
        def make(t):
            v = rest * kept[q, t] + ab[2, t]
            return v + mixed(VELOCITY[q], [ab[3 + d, t] for d in range(3)]) if q != 16 else v

        return make

    for c in range(3):
        put(lambda t: given[c, t])
    for c in (0, 1, 3, 4, 5):
        put(lambda t: ab[c, t])
    for c in range(2):
        put(lambda t: ab[c, t] + inward * ab[3, t], 1)
    for c in (4, 5):
        put(lambda t: ab[c, t], 1)
    for depth in range(2):
        for j in range(5):
            put(crossing(j), depth)
    for q in LEVEL:
        put(level(q))
    send_rows(grid, up, lines_out, send_a, send_b)


def forces_kernel(fe, recv_a, recv_b, after, forces, forces_rim, rims, lines):
    planes, rows, cols = fe.shape[1] - 1, fe.shape[2], fe.shape[3]
    grid = Grid(planes, rows, cols)
    unpack_rims(grid, recv_a, recv_b, parity_of("gx"), lines, rims, KEPT_LINES)
    psi, dip = RIM_EARLY + 9, RIM_EARLY + 6

    def both(tile):
        brick = brick_forces(grid, tile, fe, rims, psi, dip)
        beyond = rim_forces(grid, tile, fe, rims, psi, dip, RIM_FAR, RIM_FAR + 3)
        for s in range(3):
            for d in range(3):
                forces[3 * s + d, tile.index] = brick[s][d]
                forces_rim[3 * s + d, tile.index] = beyond[s][d]

    grid.over(both)


def early_kernel(
    fl, fe, ab1, kept1, given1, forces, forces_rim, rims, recv_a, recv_b, out,
    lines, near, mid, rim_mid, rim_level, rim_far, hold, hold_rim, ab, kept, total, staged, sems,
):
    planes, rows, cols = fl.shape[1] - 1, fl.shape[2], fl.shape[3]
    grid = Grid(planes, rows, cols)
    unpack_rims(grid, recv_a, recv_b, parity_of("gx"), lines, near, range(SECOND_LINES))
    rest = 1.0 - 1.0 / RELAXATION[2]
    at_rim = (grid.sub == 0) | (grid.sub == rows - 1)
    outward = jnp.where(grid.sub < rows // 2, -1.0, 1.0).astype(F32)

    def complete(tile):
        t = tile.index
        inward = [jnp.where(at_rim, tile.get(near, s), 0.0) for s in range(3)]
        alpha = [tile.get(ab1, s) + (1.0 - tile.get(fl, 9 + s)) * inward[s] for s in range(3)]
        beta = [tile.get(ab1, 3 + d) for d in range(3)]
        for q in range(19):
            along = mixed(VELOCITY[q], beta) if q != 16 else None
            for s in range(3):
                v = alpha[s] if along is None else alpha[s] + along
                if s == 2:
                    v = v + rest * kept1[q, t]
                mid[s * 19 + q, t] = v
        fixes = [(1.0 - tile.get(rims, s)) * tile.get(given1, s) for s in range(3)]
        alpha = [tile.get(near, 3 + s) + fixes[s] for s in range(2)]
        beta = [tile.get(near, 5 + d) for d in range(3)]
        far = [tile.get(near, 8 + s) for s in range(4)]
        ahead = outward * beta[0]
        for j, yz in enumerate(CROSS):
            side = mixed(yz, beta[1:]) if j else None
            side_far = mixed(yz, far[2:]) if j else None
            for s in range(2):
                rim_mid[s * 5 + j, t] = plus(side, alpha[s] + ahead)
                rim_far[s * 5 + j, t] = plus(side_far, far[s])
            rim_mid[10 + j, t] = tile.get(near, 12 + j) + fixes[2]
            rim_far[10 + j, t] = tile.get(near, 17 + j)
        for i, q in enumerate(LEVEL):
            side = mixed(VELOCITY[q][1:], beta[1:]) if q != 16 else None
            for s in range(2):
                rim_level[s * 9 + i, t] = plus(side, alpha[s])
            rim_level[18 + i, t] = tile.get(near, 22 + i) + fixes[2]

    grid.over(complete)

    def collide(tile):
        t = tile.index
        load = lambda c, dz: tile.get(mid, c, dz)
        known = [[forces[3 * s + d, t] for d in range(3)] for s in range(3)]
        brick_collision(grid, tile, load, rim_mid, fe, known, hold, ab, kept)

    grid.over(collide)
    low = grid.sub < rows // 2

    def collide_rim(tile):
        t = tile.index

        def streamed_of(s):
            streamed = []
            for q in range(19):
                c = VELOCITY[q]
                if c[0] == 0:
                    v = tile.get(rim_level, s * 9 + LEVEL.index(q), c[2])
                elif c[0] > 0:
                    v = tile.get(rim_far, s * 5 + AHEAD.index(q), c[2])
                else:
                    j = BEHIND.index(q)
                    v = jnp.where(
                        low,
                        tile.get(mid, s * 19 + AHEAD[j], c[2]),
                        tile.get(mid, s * 19 + BEHIND[j], c[2]),
                    )
                if c[1] != 0:
                    v = grid.roll_cols(v, c[1])
                streamed.append(v)
            return streamed

        known = [[forces_rim[3 * s + d, t] for d in range(3)] for s in range(3)]
        rho, u, psi = [[rims[RIM_EARLY + at + d, t] for d in range(3)] for at in (0, 3, 9)]
        u[0] = u[0] * outward
        held, unused, unused = collision_adjoint(streamed_of, rho, u, psi, known)
        for k in range(9):
            hold_rim[k, t] = held[k] * outward if k % 3 == 0 else held[k]

    grid.over(collide_rim)

    def finish(tile):
        back = spread_inside(grid, tile, hold, fe)
        dipole = [tile.get(fe, 6 + d) for d in range(3)]
        part = spread_plane(
            grid,
            lambda k, dz: tile.get(hold_rim, k, dz),
            lambda k, dz: tile.get(rims, RIM_EARLY + 6 + k, dz),
            rim_sign(grid),
            CROSS,
        )
        for s, x in enumerate(met(part, dipole)):
            x = back[s] + jnp.where(at_rim, x, 0.0)
            total[s, tile.index] = tile.get(ab, s) + (1.0 - tile.get(fe, 9 + s)) * x

    grid.over(finish)
    is_low, is_high = grid.lane < HALO, grid.lane >= cols - HALO

    def to_out(p):
        return pltpu.make_async_copy(staged.at[:, p], out.at[:, p], sems.at[p])

    def emit(p, carry):
        base = p * grid.width

        def patched(main, edge):
            low = pltpu.roll(edge, lax.rem(2 * cols - base - grid.group, cols), 1)
            high = pltpu.roll(edge, lax.rem(2 * cols - base - 3 * grid.group, cols), 1)
            return jnp.where(is_low, low, jnp.where(is_high, high, main))

        alpha = [patched(total[s, p], total[s, planes]) for s in range(3)]
        beta = [patched(ab[3 + d, p], ab[3 + d, planes]) for d in range(3)]
        for q in range(19):
            along = mixed(VELOCITY[q], beta) if q != 16 else None
            for s in range(3):
                v = alpha[s] if along is None else alpha[s] + along
                if s == 2:
                    v = v + rest * patched(kept[q, p], kept[q, planes])
                staged[s * 19 + q, p] = v
        to_out(p).start()
        return carry

    lax.fori_loop(0, planes, emit, 0)
    for p in range(planes):
        to_out(p).wait()


def call(kernel, outs, scratch, args, in_hbm=False, out_hbm=False):
    vmem = pl.BlockSpec(memory_space=pltpu.VMEM)
    hbm = pl.BlockSpec(memory_space=pltpu.HBM)
    return pl.pallas_call(
        kernel,
        out_shape=[jax.ShapeDtypeStruct(s, F32) for s in outs],
        in_specs=[hbm if in_hbm else vmem] * len(args),
        out_specs=[hbm if out_hbm else vmem] * len(outs),
        scratch_shapes=[pltpu.VMEM(s, F32) if isinstance(s, tuple) else s for s in scratch],
        compiler_params=pltpu.CompilerParams(vmem_limit_bytes=VMEM_BYTES),
    )(*[pltpu.with_memory_space_constraint(x, pltpu.HBM) if in_hbm else x for x in args])


def swap(block, axis, offset):
    size = lax.axis_size(axis)
    route = []
    for i in range(offset, size + offset, 2):
        a, b = i % size, (i + 1) % size
        route += [(a, b), (b, a)]
    return lax.ppermute(block, axis, route)


def shards(adjoint_in, populations_early, populations_late, dipoles_early, dipoles_late):
    pops, planes, rows, cols = adjoint_in.shape
    tiles = planes + 1
    tile = (rows, cols)
    pack = cols // planes // (2 * HALO)
    groups = -(-(pops + 18) // pack)
    groups += groups % 2

    def lines(n):
        return (-(-n * tiles // 8) * 8, cols)

    def both(n):
        return (2,) + lines(n)

    send_c, send_d, own_left, own_right, fl_main, fe_main, adj = call(
        pack_columns_kernel,
        [(groups // 2,) + tile] * 2
        + [(groups,) + tile] * 2
        + [(9, planes) + tile] * 2
        + [(pops, planes) + tile],
        [pltpu.VMEM(x.shape, x.dtype) for x in (populations_late, populations_early)]
        + [pltpu.VMEM(x.shape, x.dtype) for x in (dipoles_late, dipoles_early)]
        + [pltpu.SemaphoreType.DMA((5,))],
        [adjoint_in, populations_late, populations_early, dipoles_late, dipoles_early],
        in_hbm=True,
    )
    recv_c, recv_d = swap(send_c, "gy", 0), swap(send_d, "gy", 1)
    send_a, send_b, edge, fl, fe = call(
        pack_rows_kernel,
        [lines(FIRST_LINES)] * 2 + [(pops,) + tile] + [(12, tiles) + tile] * 2,
        [both(FIRST_LINES)],
        [adj, own_left, own_right, recv_c, recv_d, fl_main, fe_main],
    )
    first_a, first_b = swap(send_a, "gx", 0), swap(send_b, "gx", 1)

    def tiled(*counts):
        return [(n, tiles) + tile for n in counts]

    send_a, send_b, ab1, kept1, given1 = call(
        late_kernel,
        [lines(SECOND_LINES)] * 2 + tiled(6, 19, 3),
        [both(FIRST_LINES), both(SECOND_LINES)] + tiled(21, 9),
        [adj, edge, fl, first_a, first_b],
    )
    recv_a, recv_b = swap(send_a, "gx", 0), swap(send_b, "gx", 1)
    forces, forces_rim, rims = call(
        forces_kernel,
        tiled(9, 9, len(KEPT_LINES)),
        [both(FIRST_LINES)],
        [fe, first_a, first_b, given1],
    )
    (out,) = call(
        early_kernel,
        [(pops, planes) + tile],
        [both(SECOND_LINES)]
        + tiled(SECOND_LINES, pops, 15, 27, 15, 9, 9, 6, 19, 3)
        + [(pops, planes) + tile, pltpu.SemaphoreType.DMA((planes,))],
        [fl, fe, ab1, kept1, given1, forces, forces_rim, rims, recv_a, recv_b],
        out_hbm=True,
    )
    return out


def solution(mesh):
    placed = P(None, None, "gx", "gy")
    return jax.shard_map(
        shards, mesh=mesh, in_specs=(placed,) * 5, out_specs=placed, check_vma=False
    )
```

```python
import jax
import jax.numpy as jnp
from jax import lax
from jax.experimental import pallas as pl
from jax.experimental.pallas import tpu as pltpu
from jax.sharding import PartitionSpec as P

VELOCITY = (
    (1, 0, 0),
    (-1, 0, 0),
    (0, 1, 0),
    (0, -1, 0),
    (1, 1, 0),
    (-1, -1, 0),
    (1, -1, 0),
    (-1, 1, 0),
    (1, 0, 1),
    (-1, 0, -1),
    (1, 0, -1),
    (-1, 0, 1),
    (0, 1, 1),
    (0, -1, -1),
    (0, 1, -1),
    (0, -1, 1),
    (0, 0, 0),
    (0, 0, 1),
    (0, 0, -1),
)
INDEX = {c: q for q, c in enumerate(VELOCITY)}
W1, W2, W0 = 1.0 / 18.0, 1.0 / 36.0, 1.0 / 3.0
RELAXATION = (1.0, 1.0, 1.25)
COUPLING = ((0.0, 1.2, -0.6), (1.2, 0.0, -0.6), (-0.6, -0.6, -0.3))
CROSS = ((0, 0), (1, 0), (-1, 0), (0, 1), (0, -1))
AHEAD = tuple(INDEX[(1,) + yz] for yz in CROSS)
BEHIND = tuple(INDEX[(-1,) + yz] for yz in CROSS)
SIDE = ((1, 0), (-1, 0), (0, 1), (0, -1), (1, 1), (-1, -1), (1, -1), (-1, 1))
LEVEL = tuple(q for q in range(19) if VELOCITY[q][0] == 0)
ALONG, AFTER, LATE, EARLY = 15, 42, 57, 72
STATIC = 87
FAR = 9
LATE_PSI, EARLY_PSI = STATIC, STATIC + 3
RIMS = STATIC + 6
DYNAMIC = 12
F32 = jnp.float32
CHUNKS = 4
VMEM_BYTES = 40 * 1024 * 1024
HALO = 4


class Grid:
    def __init__(self, planes, rows, cols):
        self.planes, self.rows, self.cols = planes, rows, cols
        self.tiles = planes + 1
        self.width = cols // planes
        self.group = 2 * HALO
        self.pack = self.width // self.group
        self.sub = lax.broadcasted_iota(jnp.int32, (rows, cols), 0)
        self.lane = lax.broadcasted_iota(jnp.int32, (rows, cols), 1)

    def roll_rows(self, v, dx):
        return pltpu.roll(v, (-dx) % self.rows, 0)

    def roll_cols(self, v, dy):
        return pltpu.roll(v, (-dy) % self.cols, 1)

    def at_row(self, v, rim, dx):
        edge = self.rows - 1 if dx > 0 else 0
        return jnp.where(self.sub == edge, rim, self.roll_rows(v, dx))

    def in_row(self, v, dx):
        edge = self.rows - 1 if dx > 0 else 0
        return jnp.where(self.sub == edge, 0.0, self.roll_rows(v, dx))

    def sides(self, low, high):
        return jnp.where(self.sub == 0, low, high)

    def over_main(self, body):
        def step(p, carry):
            body(Tile(self, p, False))
            return carry

        lax.fori_loop(0, self.planes, step, 0)

    def over_edge(self, body):
        body(Tile(self, self.planes, True))

    def over(self, body):
        self.over_main(body)
        self.over_edge(body)

    def at_rim(self):
        return (self.sub == 0) | (self.sub == self.rows - 1)

    def low(self):
        return self.sub < self.rows // 2

    def outward(self):
        return jnp.where(self.low(), -1.0, 1.0).astype(F32)


class Tile:
    def __init__(self, grid, index, edge):
        self.grid, self.index, self.edge = grid, index, edge

    def of(self, dz):
        if dz == 0 or self.edge:
            return self.index
        return lax.rem(self.index + (dz + self.grid.planes), self.grid.planes)

    def get(self, ref, c, dz=0):
        if isinstance(ref, Pair):
            v = ref.edge[c] if self.edge else ref.main[c, self.of(dz)]
        else:
            v = ref[c, self.of(dz)]
        if self.edge and dz != 0:
            v = self.grid.roll_cols(v, dz * self.grid.width)
        return v

    def put(self, ref, c, v):
        if not isinstance(ref, Pair):
            ref[c, self.index] = v
        elif self.edge:
            ref.edge[c] = v
        else:
            ref.main[c, self.index] = v


class Pair:
    def __init__(self, main, edge):
        self.main, self.edge = main, edge

    def at(self, c, t):
        return self.edge[c] if t == self.main.shape[1] else self.main[c, t]


def plus(a, b):
    return b if a is None else a + b


def mixed(coefficients, values):
    total = None
    for k, v in zip(coefficients, values):
        if k == 0:
            continue
        term = v if k == 1 else (-v if k == -1 else k * v)
        total = plus(total, term)
    return total


def axis_pairs():
    for q in (0, 2, 17, 4, 6, 8, 10, 12, 14):
        c = VELOCITY[q]
        yield c, (W1 if sum(abs(i) for i in c) == 1 else W2)


def first_and_second(diff, total):
    first = [None] * 3
    second = {}
    for c, w in axis_pairs():
        for d in range(3):
            if c[d] == 0:
                continue
            if diff is not None:
                first[d] = plus(first[d], (w * c[d]) * diff[c])
            if total is not None:
                for e in range(d, 3):
                    if c[e] != 0:
                        second[d, e] = plus(second.get((d, e)), (w * c[d] * c[e]) * total[c])
    return first, second


def turned(second, v):
    return [sum(second[min(d, e), max(d, e)] * v[e] for e in range(3)) for d in range(3)]


def dot(a, b):
    return a[0] * b[0] + a[1] * b[1] + a[2] * b[2]


def field_forces(grid, loads, across, dipole):
    memo = {}

    def source(name, dz, place):
        key = (name, dz, place)
        if key in memo:
            return memo[key]
        if isinstance(name, int):
            v = loads[place](name, dz)
        elif name == "chi":
            v = source(0, dz, place) - source(1, dz, place)
        elif name[0] == "V":
            v = source(2, dz, place) * source(3 + name[1], dz, place)
        else:
            c = name[1]
            v = mixed(c, [source(("V", d), dz, place) if c[d] else None for d in range(3)])
        memo[key] = v
        return v

    def shifted(name, c):
        key = (name, c, "shift")
        if key in memo:
            return memo[key]
        if c[1] != 0:
            v = grid.roll_cols(shifted(name, (c[0], 0, c[2])), c[1])
        elif c[0] != 0:
            v = across(lambda place, dz: source(name, dz, place), c[0], c[2])
        else:
            v = source(name, c[2], 0)
        memo[key] = v
        return v

    def parts(name):
        diff, total = {}, {}
        for c, w in axis_pairs():
            back = tuple(-i for i in c)
            a, b = shifted(name, c), shifted(name, back)
            diff[c], total[c] = a - b, a + b
        return diff, total

    diff, unused = parts(0)
    s0, unused = first_and_second(diff, None)
    diff, unused = parts(2)
    s2, unused = first_and_second(diff, None)
    diff, total = parts("chi")
    schi, second = first_and_second(diff, total)
    s1 = [a - b for a, b in zip(s0, schi)]
    pull = [None] * 3
    for c, w in axis_pairs():
        back = tuple(-i for i in c)
        if sum(abs(i) for i in c) == 1:
            name = ("V", [i for i in range(3) if c[i]][0])
        else:
            name = ("L", c)
        total_c = shifted(name, c) + shifted(name, back)
        for d in range(3):
            if c[d] != 0:
                pull[d] = plus(pull[d], (w * c[d]) * total_c)
    md = turned(second, dipole)
    k0 = [-1.2 * s1[d] + 0.6 * s2[d] - pull[d] for d in range(3)]
    k1 = [-1.2 * s0[d] + 0.6 * s2[d] + pull[d] for d in range(3)]
    k2 = [0.6 * (s0[d] + s1[d]) + 0.3 * s2[d] + md[d] for d in range(3)]
    return k0, k1, k2


def brick_forces(grid, tile, fields, rim, rim_psi, rim_dip):
    def own(c, dz):
        return tile.get(fields, (9 + c) if c < 3 else (3 + c), dz)

    def beyond(c, dz):
        return tile.get(rim, (rim_psi + c) if c < 3 else (rim_dip + c - 3), dz)

    def across(get, cx, dz):
        if rim is None:
            return grid.in_row(get(0, dz), cx)
        return grid.at_row(get(0, dz), get(1, dz), cx)

    return field_forces(grid, (own, beyond), across, [own(3 + d, 0) for d in range(3)])


def rim_forces(grid, tile, fields, rims, psi, base):
    outward = grid.outward()

    def loader(ref, psi_at, dip_at):
        def load(c, dz):
            v = tile.get(ref, (psi_at + c) if c < 3 else (dip_at + c - 3), dz)
            return v * outward if c == 3 else v

        return load

    loads = {
        0: loader(rims, psi, base + 6),
        1: loader(rims, base + FAR, base + FAR + 3),
        -1: loader(fields, 9, 6),
    }
    dipole = [loads[0](3 + d, 0) for d in range(3)]
    return field_forces(grid, loads, lambda get, cx, dz: get(cx, dz), dipole)


def collision_adjoint(streamed_of, rho, u, psi, forces):
    inverse_sum = 1.0 / (rho[0] + rho[1] + rho[2])
    grad_u = [None] * 3
    alphas, held = [], []
    for s in range(3):
        streamed = streamed_of(s)
        diff, total = {}, {}
        for c, w in axis_pairs():
            a, b = streamed[INDEX[c]], streamed[INDEX[tuple(-i for i in c)]]
            diff[c], total[c] = a - b, a + b
        m1, m2 = first_and_second(diff, total)
        m0 = W0 * streamed[16]
        for c, w in axis_pairs():
            m0 = m0 + w * total[c]
        inverse = 1.0 / rho[s]
        ratio = psi[s] * inverse
        tau = RELAXATION[s]
        k = forces[s]
        v = [u[d] + (tau * ratio) * k[d] for d in range(3)]
        mv = turned(m2, v)
        g = [3.0 * (m1[d] + 3.0 * mv[d] - m0 * v[d]) for d in range(3)]
        feq = m0 + 3.0 * dot(m1, v) + 4.5 * dot(mv, v) - 1.5 * m0 * dot(v, v)
        alphas.append(feq * (1.0 / tau) + dot(g, k) * (1.0 - psi[s] - ratio))
        scaled = rho[s] * (1.0 / tau)
        for d in range(3):
            grad_u[d] = plus(grad_u[d], scaled * g[d])
            held.append(psi[s] * g[d])
    beta = [grad_u[d] * inverse_sum for d in range(3)]
    along = dot(beta, u)
    return held, [a - along for a in alphas], beta


def brick_collision(grid, tile, load, rim, fields, forces, hold, ab, kept):
    def streamed_of(s):
        streamed = []
        for q in range(19):
            c = VELOCITY[q]
            v = load(s * 19 + q, c[2])
            if c[0] != 0:
                j = (AHEAD if c[0] > 0 else BEHIND).index(q)
                if rim is None:
                    v = grid.in_row(v, c[0])
                else:
                    v = grid.at_row(v, tile.get(rim, s * 5 + j, c[2]), c[0])
            if c[1] != 0:
                v = grid.roll_cols(v, c[1])
            streamed.append(v)
            if s == 2:
                tile.put(kept, q, v)
        return streamed

    rho, u, psi = [[tile.get(fields, at + d) for d in range(3)] for at in (0, 3, 9)]
    held, alpha, beta = collision_adjoint(streamed_of, rho, u, psi, forces)
    for k in range(9):
        tile.put(hold, k, held[k])
    for s in range(3):
        tile.put(ab, s, alpha[s])
        tile.put(ab, 3 + s, beta[s])


def rim_collision(grid, tile, level, after, inner, rho, u, psi, forces, hold, ab, kept):
    outward, low = grid.outward(), grid.low()

    def streamed_of(s):
        streamed = []
        for q in range(19):
            c = VELOCITY[q]
            if c[0] == 0:
                v = level(s, LEVEL.index(q), c[2])
            elif c[0] > 0:
                v = after(s, AHEAD.index(q), c[2])
            else:
                j = BEHIND.index(q)
                v = jnp.where(low, inner(s * 19 + AHEAD[j], c[2]), inner(s * 19 + BEHIND[j], c[2]))
            if c[1] != 0:
                v = grid.roll_cols(v, c[1])
            streamed.append(v)
            if s == 2 and kept is not None and c[0] >= 0:
                tile.put(kept, LEVEL.index(q) if c[0] == 0 else 9 + AHEAD.index(q), v)
        return streamed

    u = [u[0] * outward, u[1], u[2]]
    held, alpha, beta = collision_adjoint(streamed_of, rho, u, psi, forces)
    for k in range(9):
        tile.put(hold, k, held[k] * outward if k % 3 == 0 else held[k])
    if ab is not None:
        for s in range(3):
            tile.put(ab, s, alpha[s])
            tile.put(ab, 3 + s, beta[s] * outward if s == 0 else beta[s])


def spread_plane(grid, get_h, get_d, sign, pairs):
    memo = {}

    def source(dz):
        if dz in memo:
            return memo[dz]
        h = [[get_h(3 * s + d, dz) for d in range(3)] for s in range(3)]
        dip = [get_d(d, dz) for d in range(3)]
        if not isinstance(sign, int):
            for vec in h + [dip]:
                vec[0] = vec[0] * sign
        memo[dz] = (h, dip)
        return memo[dz]

    cx = sign if isinstance(sign, int) else 1
    r = [None] * 3
    w_vec = [None] * 3
    lanes = {}
    for cy, cz in pairs:
        w = W1 if abs(cx) + abs(cy) + abs(cz) == 1 else W2
        h, dip = source(cz)
        c = (cx, cy, cz)
        e = [mixed(c, h[s]) for s in range(3)]
        f = e[2] * mixed(c, dip)
        half = 0.6 * e[2]
        r0 = 1.2 * e[1] - half + f
        r1 = 1.2 * e[0] - half - f
        r2 = -0.6 * (e[0] + e[1]) - 0.3 * e[2]
        qv = e[0] - e[1]
        vals = [w * r0, w * r1, w * r2]
        wq = w * qv
        vals += [wq if cx != 0 else None, wq if cy != 0 else None, wq if cz != 0 else None]
        vals = [vals[0], vals[1], vals[2]] + [
            None if x is None else (x if k == 1 else -x) for x, k in zip(vals[3:], (cx, cy, cz))
        ]
        acc = lanes.setdefault(cy, [None] * 6)
        for i, x in enumerate(vals):
            if x is not None:
                acc[i] = plus(acc[i], x)
    total = [None] * 6
    for cy, acc in lanes.items():
        for i, x in enumerate(acc):
            if x is not None:
                total[i] = plus(total[i], x if cy == 0 else grid.roll_cols(x, cy))
    if not isinstance(sign, int):
        total[3] = total[3] * sign
    return total


def met(total, dipole):
    meet = None
    for d in range(3):
        if total[3 + d] is not None:
            meet = plus(meet, total[3 + d] * dipole[d])
    return [total[0], total[1], total[2] - meet]


def spread_inside(grid, tile, hold, fields):
    get_h = lambda k, dz: tile.get(hold, k, dz)
    get_d = lambda k, dz: tile.get(fields, 6 + k, dz)
    total = spread_plane(grid, get_h, get_d, 0, SIDE)
    for dx in (1, -1):
        part = spread_plane(grid, get_h, get_d, dx, CROSS)
        for i, x in enumerate(part):
            total[i] = plus(total[i], grid.in_row(x, dx))
    return met(total, [tile.get(fields, 6 + d) for d in range(3)])


def rim_sign(grid):
    return jnp.where(
        grid.sub == 0, -1.0, jnp.where(grid.sub == grid.rows - 1, 1.0, 0.0)
    ).astype(F32)


def hand_over(grid, tile, hold, hold_dip, target, sign):
    dip, at = hold_dip
    total = spread_plane(
        grid,
        lambda k, dz: tile.get(hold, k, dz),
        lambda k, dz: tile.get(dip, at + k, dz),
        sign,
        CROSS,
    )
    return met(total, target)


def spread_level(grid, tile, hold, dip, at):
    total = spread_plane(
        grid,
        lambda k, dz: tile.get(hold, k, dz),
        lambda k, dz: tile.get(dip, at + k, dz),
        0,
        SIDE,
    )
    return met(total, [tile.get(dip, at + d) for d in range(3)])


def parity_of(axis):
    return lax.rem(lax.axis_index(axis), 2)


def lines_from(first, second, parity, lines):
    lines[1 - parity] = first[...]
    lines[parity] = second[...]


def lines_to(first, second, lines):
    first[...] = lines[0]
    second[...] = lines[1]


def psi_of(rho):
    return 1.0 - jnp.exp(-rho)


def pack_static(get, tiles, rows, lines, parity):
    up, down = parity, 1 - parity
    fill = 0

    def put(kind, above, below, depth):
        nonlocal fill
        for t in tiles:
            v = get(kind, above, t)
            lines[up, fill : fill + 1, :] = v[rows - 1 - depth : rows - depth, :]
            v = get(kind, below, t)
            lines[down, fill : fill + 1, :] = v[depth : depth + 1, :]
            fill += 1

    for s in range(3):
        for j in range(5):
            put(0, s * 19 + BEHIND[j], s * 19 + AHEAD[j], 0)
    for s in range(3):
        for q in LEVEL:
            put(0, s * 19 + q, s * 19 + q, 0)
    for s in range(3):
        for j in range(5):
            put(0, s * 19 + BEHIND[j], s * 19 + AHEAD[j], 1)
    for kind in (1, 2):
        for c in range(9):
            put(kind, c, c, 0)
        for c in (9, 10, 11, 6, 7, 8):
            put(kind, c, c, 1)
    return fill


def pack_columns_kernel(
    adj_in, late_in, early_in, dip_late_in, dip_early_in,
    send_c, send_d, own_left, own_right, fl, fe, adj,
    late, early, dip_late, dip_early, sems,
):
    planes, rows, cols = adj.shape[1:]
    grid = Grid(planes, rows, cols)
    copies = [
        pltpu.make_async_copy(a, b, sems.at[i])
        for i, (a, b) in enumerate(
            (
                (dip_late_in, dip_late),
                (late_in, late),
                (dip_early_in, dip_early),
                (early_in, early),
            )
        )
    ]
    per_chunk = -(-adj.shape[0] // (CHUNKS * grid.pack)) * grid.pack
    for i in range(CHUNKS):
        part = pl.ds(i * per_chunk, min(per_chunk, adj.shape[0] - i * per_chunk))
        copies.append(pltpu.make_async_copy(adj_in.at[part], adj.at[part], sems.at[4 + i]))
    for copy in copies:
        copy.start()
    for which, (saved, dip, out) in enumerate(((late, dip_late, fl), (early, dip_early, fe))):
        copies[2 * which].wait()
        copies[2 * which + 1].wait()

        def step(p, carry):
            flows = [None] * 19
            rho = []
            for s in range(3):
                total = None
                for q in range(19):
                    v = saved[s * 19 + q, p].astype(F32)
                    flows[q] = plus(flows[q], v)
                    total = plus(total, v)
                rho.append(total)
                out[s, p] = total
                out[9 + s, p] = psi_of(total)
            inverse = 1.0 / (rho[0] + rho[1] + rho[2])
            for d in range(3):
                momentum = None
                for q in range(19):
                    if VELOCITY[q][d] != 0:
                        momentum = plus(momentum, flows[q] if VELOCITY[q][d] > 0 else -flows[q])
                out[3 + d, p] = momentum * inverse
                out[6 + d, p] = dip[d, p].astype(F32)
            return carry

        lax.fori_loop(0, planes, step, 0)
    pops = adj.shape[0]
    components = pops + 18
    slot = grid.lane // grid.group
    for g in range(own_left.shape[0]):
        if g * grid.pack % per_chunk == 0 and g * grid.pack < pops:
            copies[4 + g * grid.pack // per_chunk].wait()
        left = right = jnp.zeros((rows, cols), F32)
        for j in range(grid.pack):
            c = g * grid.pack + j
            if c >= components:
                continue
            for p in range(planes):
                if c < pops:
                    v = adj[c, p]
                elif c < pops + 9:
                    v = fl[c - pops, p]
                else:
                    v = fe[c - pops - 9, p]
                at = p * grid.pack + j
                rolled = pltpu.roll(v, at * grid.group, 1) if at else v
                left = jnp.where(slot == at, rolled, left)
                right = jnp.where(slot == (at - 1) % (cols // grid.group), rolled, right)
        own_left[g] = left
        own_right[g] = right
    low = lax.rem(grid.lane, grid.group) < HALO
    even = parity_of("gy") == 0
    for h in range(send_c.shape[0]):
        left = jnp.where(low, own_left[2 * h], pltpu.roll(own_left[2 * h + 1], HALO, 1))
        right = jnp.where(low, pltpu.roll(own_right[2 * h + 1], cols - HALO, 1), own_right[2 * h])
        send_c[h] = jnp.where(even, right, left)
        send_d[h] = jnp.where(even, left, right)


def static_kernel(adj, fl, fe, send_a, send_b, lines):
    planes, rows, cols = adj.shape[1:]
    kinds = (adj, fl, fe)
    pack_static(lambda kind, c, t: kinds[kind][c, t], range(planes), rows, lines, parity_of("gx"))
    lines_to(send_a, send_b, lines)


def inside_collision(grid, tile, load, fields, hold, ab, kept):
    forces = brick_forces(grid, tile, fields, None, 0, 0)
    brick_collision(grid, tile, load, None, fields, forces, hold, ab, kept)
    at_rim = grid.at_rim()
    for k in range(9):
        tile.put(hold, k, jnp.where(at_rim, 0.0, tile.get(hold, k)))


def inside_kernel(adj, fl, hold, ab, kept):
    grid = Grid(*adj.shape[1:])
    grid.over_main(
        lambda tile: inside_collision(
            grid, tile, lambda c, dz: tile.get(adj, c, dz), fl, hold, ab, kept
        )
    )


def edge_kernel(
    own_left, own_right, recv_c, recv_d, fl_main, hold_main, ab_main, kept_main,
    send_a, send_b, edge, fl, fe, lines, hold, ab, kept, sides,
):
    planes, rows, cols = fl_main.shape[1:]
    pops = edge.shape[0]
    grid = Grid(planes, rows, cols)
    even = parity_of("gy") == 0
    slot = lax.rem(grid.lane // grid.group, grid.pack)
    left_half = lax.rem(grid.lane, grid.width) < grid.width // 2
    components = pops + 18
    for g in range(own_left.shape[0]):
        first, second = recv_c[g // 2], recv_d[g // 2]
        from_next = jnp.where(even, first, second)
        from_prior = jnp.where(even, second, first)
        if g % 2:
            from_next = pltpu.roll(from_next, cols - HALO, 1)
            from_prior = pltpu.roll(from_prior, HALO, 1)
        for j in range(grid.pack):
            c = g * grid.pack + j
            if c >= components:
                continue
            before = slot == (j - 1) % grid.pack
            low = jnp.where(before, from_prior, own_left[g])
            high = jnp.where(before, own_right[g], from_next)
            v = jnp.where(
                left_half,
                pltpu.roll(low, ((1 - j) * grid.group) % cols, 1),
                pltpu.roll(high, ((3 - j) * grid.group) % cols, 1),
            )
            if c < pops:
                edge[c] = v
            else:
                field, k = (fl, c - pops) if c < pops + 9 else (fe, c - pops - 9)
                field[k] = v
                if k < 3:
                    field[9 + k] = psi_of(v)
    fields = Pair(fl_main, fl)
    hold, ab, kept = Pair(hold_main, hold), Pair(ab_main, ab), Pair(kept_main, kept)
    adj = Pair(None, edge)
    grid.over_edge(
        lambda tile: inside_collision(
            grid, tile, lambda c, dz: tile.get(adj, c, dz), fields, hold, ab, kept
        )
    )
    low = grid.low()
    inward = -grid.outward()
    rest = 1.0 - 1.0 / RELAXATION[2]

    def second_row(tile):
        back = spread_inside(grid, tile, hold, fields)
        alpha = [tile.get(ab, s) + (1.0 - tile.get(fields, 9 + s)) * back[s] for s in range(3)]
        beta = [tile.get(ab, 3 + d) for d in range(3)]
        ahead = inward * beta[0]
        for s in range(3):
            tile.put(sides, s, back[s])
        for s in range(2):
            tile.put(sides, 3 + s, alpha[s] + ahead)
            tile.put(sides, 5 + s, beta[1 + s])
        for j, yz in enumerate(CROSS):
            v = rest * jnp.where(low, tile.get(kept, AHEAD[j]), tile.get(kept, BEHIND[j]))
            v = v + (alpha[2] + ahead)
            tile.put(sides, 7 + j, v + mixed(yz, beta[1:]) if j else v)

    grid.over(second_row)
    parity = parity_of("gx")
    kinds = (edge, fl, fe)
    fill = pack_static(lambda kind, c, t: kinds[kind][c], (0,), rows, lines, parity)
    for c in range(DYNAMIC):
        depth = 0 if c < 3 else 1
        for t in range(grid.tiles):
            lines[parity, fill : fill + 1, :] = sides[c, t, rows - 1 - depth : rows - depth, :]
            lines[1 - parity, fill : fill + 1, :] = sides[c, t, depth : depth + 1, :]
            fill += 1
    lines_to(send_a, send_b, lines)


def first_step(grid, tile, adj, fl, rims, hold, ab, kept, hold_rim, ab_rim, kept_rim):
    forces = brick_forces(grid, tile, fl, rims, LATE_PSI, LATE + 6)
    load = lambda c, dz: tile.get(adj, c, dz)
    brick_collision(grid, tile, load, rims, fl, forces, hold, ab, kept)
    forces = rim_forces(grid, tile, fl, rims, LATE_PSI, LATE)
    rho, u = [[tile.get(rims, LATE + at + d) for d in range(3)] for at in (0, 3)]
    psi = [tile.get(rims, LATE_PSI + s) for s in range(3)]
    rim_collision(
        grid,
        tile,
        lambda s, i, dz: tile.get(rims, ALONG + s * 9 + i, dz),
        lambda s, j, dz: tile.get(rims, AFTER + s * 5 + j, dz),
        load,
        rho,
        u,
        psi,
        forces,
        hold_rim,
        ab_rim,
        kept_rim,
    )


def early_forces(grid, tile, fe, rims, forces, forces_rim):
    brick = brick_forces(grid, tile, fe, rims, EARLY_PSI, EARLY + 6)
    beyond = rim_forces(grid, tile, fe, rims, EARLY_PSI, EARLY)
    for s in range(3):
        for d in range(3):
            tile.put(forces, 3 * s + d, brick[s][d])
            tile.put(forces_rim, 3 * s + d, beyond[s][d])


def rim_psis(grid, tile, rims):
    for s in range(3):
        tile.put(rims, LATE_PSI + s, psi_of(tile.get(rims, LATE + s)))
        tile.put(rims, EARLY_PSI + s, psi_of(tile.get(rims, EARLY + s)))


def main_kernel(
    adj, fl, fe, recv_a, recv_b, after,
    rims, hold, ab, kept, hold_rim, ab_rim, kept_rim, forces, forces_rim, lines,
):
    planes, rows, cols = adj.shape[1:]
    grid = Grid(planes, rows, cols)
    lines_from(recv_a, recv_b, parity_of("gx"), lines)
    for c in range(STATIC):
        for p in range(planes):
            k = c * planes + p
            rims[c, p] = grid.sides(lines[0, k : k + 1, :], lines[1, k : k + 1, :])
    grid.over_main(lambda tile: rim_psis(grid, tile, rims))

    def step(tile):
        first_step(grid, tile, adj, fl, rims, hold, ab, kept, hold_rim, ab_rim, kept_rim)
        early_forces(grid, tile, fe, rims, forces, forces_rim)

    grid.over_main(step)


def last_kernel(
    fl_m, fe_m, edge, fl_e, fe_e, rims_m, hold_m, ab_m, kept_m, hold_rim_m, ab_rim_m, kept_rim_m,
    forces_m, forces_rim_m, recv_a, recv_b, out,
    rims_e, hold_e, ab_e, kept_e, hold_rim_e, ab_rim_e, kept_rim_e, forces_e, forces_rim_e,
    lines, near, mid, rim_mid, rim_level, rim_far, hold2, hold_rim2, ab2, kept2, total, staged,
    sems,
):
    planes, rows, cols = fl_m.shape[1:]
    grid = Grid(planes, rows, cols)
    lines_from(recv_a, recv_b, parity_of("gx"), lines)
    for c in range(STATIC):
        rims_e[c] = grid.sides(lines[0, c : c + 1, :], lines[1, c : c + 1, :])
    for c in range(DYNAMIC):
        for t in range(grid.tiles):
            k = STATIC + c * grid.tiles + t
            near[c, t] = grid.sides(lines[0, k : k + 1, :], lines[1, k : k + 1, :])
    fl, fe, rims = Pair(fl_m, fl_e), Pair(fe_m, fe_e), Pair(rims_m, rims_e)
    hold, ab, kept = Pair(hold_m, hold_e), Pair(ab_m, ab_e), Pair(kept_m, kept_e)
    hold_rim, ab_rim = Pair(hold_rim_m, hold_rim_e), Pair(ab_rim_m, ab_rim_e)
    kept_rim = Pair(kept_rim_m, kept_rim_e)
    forces, forces_rim = Pair(forces_m, forces_e), Pair(forces_rim_m, forces_rim_e)
    rest = 1.0 - 1.0 / RELAXATION[2]
    at_rim = grid.at_rim()
    sign = rim_sign(grid)
    outward = grid.outward()

    def edge_steps(tile):
        rim_psis(grid, tile, rims)
        first_step(
            grid, tile, Pair(None, edge), fl, rims, hold, ab, kept, hold_rim, ab_rim, kept_rim
        )
        early_forces(grid, tile, fe, rims, forces, forces_rim)

    grid.over_edge(edge_steps)

    def complete(tile):
        t = tile.index
        own_dip, rim_dip = (fl, 6), (rims, LATE + 6)
        dip = [tile.get(fl, 6 + d) for d in range(3)]
        dip_rim = [tile.get(rims, LATE + 6 + d) for d in range(3)]
        dip_far = [tile.get(rims, LATE + FAR + 3 + d) for d in range(3)]
        back = spread_inside(grid, tile, hold, fl)
        inward = hand_over(grid, tile, hold_rim, rim_dip, dip, sign)
        alpha = [
            tile.get(ab, s)
            + (1.0 - tile.get(fl, 9 + s)) * (back[s] + jnp.where(at_rim, inward[s], 0.0))
            for s in range(3)
        ]
        beta = [tile.get(ab, 3 + d) for d in range(3)]
        for q in range(19):
            along = mixed(VELOCITY[q], beta) if q != 16 else None
            for s in range(3):
                v = alpha[s] if along is None else alpha[s] + along
                if s == 2:
                    v = v + rest * tile.get(kept, q)
                mid[s * 19 + q, t] = v
        given = hand_over(grid, tile, hold, own_dip, dip_rim, -sign)
        level = spread_level(grid, tile, hold_rim, *rim_dip)
        alpha = [
            tile.get(ab_rim, s)
            + (1.0 - tile.get(rims, LATE_PSI + s)) * (given[s] + level[s] + near[s, t])
            for s in range(3)
        ]
        beta = [tile.get(ab_rim, 3 + d) for d in range(3)]
        given = hand_over(grid, tile, hold_rim, rim_dip, dip_far, -sign)
        fixes = [(1.0 - tile.get(rims, LATE + FAR + s)) * given[s] for s in range(3)]
        far = [near[3 + s, t] + fixes[s] for s in range(2)]
        far_beta = [near[5 + d, t] for d in range(2)]
        ahead = outward * beta[0]
        for j, yz in enumerate(CROSS):
            side = mixed(yz, beta[1:]) if j else None
            side_far = mixed(yz, far_beta) if j else None
            for s in range(3):
                v = plus(side, alpha[s] + ahead)
                if s == 2:
                    v = v + rest * tile.get(kept_rim, 9 + j)
                    rim_far[10 + j, t] = near[7 + j, t] + fixes[2]
                else:
                    rim_far[s * 5 + j, t] = plus(side_far, far[s])
                rim_mid[s * 5 + j, t] = v
        for i, q in enumerate(LEVEL):
            side = mixed(VELOCITY[q][1:], beta[1:]) if q != 16 else None
            for s in range(3):
                v = plus(side, alpha[s])
                if s == 2:
                    v = v + rest * tile.get(kept_rim, i)
                rim_level[s * 9 + i, t] = v

    grid.over(complete)

    def collide(tile):
        load = lambda c, dz: tile.get(mid, c, dz)
        known = [[tile.get(forces, 3 * s + d) for d in range(3)] for s in range(3)]
        brick_collision(grid, tile, load, rim_mid, fe, known, hold2, ab2, kept2)
        known = [[tile.get(forces_rim, 3 * s + d) for d in range(3)] for s in range(3)]
        rho, u = [[tile.get(rims, EARLY + at + d) for d in range(3)] for at in (0, 3)]
        psi = [tile.get(rims, EARLY_PSI + s) for s in range(3)]
        rim_collision(
            grid,
            tile,
            lambda s, i, dz: tile.get(rim_level, s * 9 + i, dz),
            lambda s, j, dz: tile.get(rim_far, s * 5 + j, dz),
            load,
            rho,
            u,
            psi,
            known,
            hold_rim2,
            None,
            None,
        )

    grid.over(collide)

    def finish(tile):
        back = spread_inside(grid, tile, hold2, fe)
        dip = [tile.get(fe, 6 + d) for d in range(3)]
        inward = hand_over(grid, tile, hold_rim2, (rims, EARLY + 6), dip, sign)
        for s in range(3):
            x = back[s] + jnp.where(at_rim, inward[s], 0.0)
            total[s, tile.index] = tile.get(ab2, s) + (1.0 - tile.get(fe, 9 + s)) * x

    grid.over(finish)
    is_low, is_high = grid.lane < HALO, grid.lane >= cols - HALO

    def to_out(p):
        return pltpu.make_async_copy(staged.at[:, p], out.at[:, p], sems.at[p])

    def emit(p, carry):
        base = p * grid.width

        def patched(main, edge):
            low = pltpu.roll(edge, lax.rem(2 * cols - base - grid.group, cols), 1)
            high = pltpu.roll(edge, lax.rem(2 * cols - base - 3 * grid.group, cols), 1)
            return jnp.where(is_low, low, jnp.where(is_high, high, main))

        alpha = [patched(total[s, p], total[s, planes]) for s in range(3)]
        beta = [patched(ab2[3 + d, p], ab2[3 + d, planes]) for d in range(3)]
        for q in range(19):
            along = mixed(VELOCITY[q], beta) if q != 16 else None
            for s in range(3):
                v = alpha[s] if along is None else alpha[s] + along
                if s == 2:
                    v = v + rest * patched(kept2[q, p], kept2[q, planes])
                staged[s * 19 + q, p] = v
        to_out(p).start()
        return carry

    lax.fori_loop(0, planes, emit, 0)
    for p in range(planes):
        to_out(p).wait()


def call(kernel, outs, scratch, args, in_hbm=False, out_hbm=False):
    vmem = pl.BlockSpec(memory_space=pltpu.VMEM)
    hbm = pl.BlockSpec(memory_space=pltpu.HBM)
    return pl.pallas_call(
        kernel,
        out_shape=[jax.ShapeDtypeStruct(s, F32) for s in outs],
        in_specs=[hbm if in_hbm else vmem] * len(args),
        out_specs=[hbm if out_hbm else vmem] * len(outs),
        scratch_shapes=[pltpu.VMEM(s, F32) if isinstance(s, tuple) else s for s in scratch],
        compiler_params=pltpu.CompilerParams(vmem_limit_bytes=VMEM_BYTES),
    )(*[pltpu.with_memory_space_constraint(x, pltpu.HBM) if in_hbm else x for x in args])


def swap(block, axis, offset):
    size = lax.axis_size(axis)
    route = []
    for i in range(offset, size + offset, 2):
        a, b = i % size, (i + 1) % size
        route += [(a, b), (b, a)]
    return lax.ppermute(block, axis, route)


def shards(adjoint_in, populations_early, populations_late, dipoles_early, dipoles_late):
    pops, planes, rows, cols = adjoint_in.shape
    tile = (rows, cols)
    pack = cols // planes // (2 * HALO)
    groups = -(-(pops + 18) // pack)
    groups += groups % 2

    def lines(n):
        return (-(-n // 8) * 8, cols)

    def main(*counts):
        return [(n, planes) + tile for n in counts]

    def edges(*counts):
        return [(n,) + tile for n in counts]

    def tiled(*counts):
        return [(n, planes + 1) + tile for n in counts]

    static = lines(STATIC * planes)
    second = lines(STATIC + DYNAMIC * (planes + 1))
    send_c, send_d, own_left, own_right, fl_m, fe_m, adj = call(
        pack_columns_kernel,
        edges(groups // 2, groups // 2, groups, groups) + main(12, 12, pops),
        [
            pltpu.VMEM(x.shape, x.dtype)
            for x in (populations_late, populations_early, dipoles_late, dipoles_early)
        ]
        + [pltpu.SemaphoreType.DMA((4 + CHUNKS,))],
        [adjoint_in, populations_late, populations_early, dipoles_late, dipoles_early],
        in_hbm=True,
    )
    recv_c, recv_d = swap(send_c, "gy", 0), swap(send_d, "gy", 1)
    send_a, send_b = call(static_kernel, [static] * 2, [(2,) + static], [adj, fl_m, fe_m])
    static_a, static_b = swap(send_a, "gx", 0), swap(send_b, "gx", 1)
    pre = list(call(inside_kernel, main(9, 6, 19), [], [adj, fl_m]))
    send_a, send_b, edge, fl_e, fe_e = call(
        edge_kernel,
        [second] * 2 + edges(pops, 12, 12),
        [(2,) + second] + edges(9, 6, 19) + tiled(DYNAMIC),
        [own_left, own_right, recv_c, recv_d, fl_m] + pre,
    )
    recv_a, recv_b = swap(send_a, "gx", 0), swap(send_b, "gx", 1)
    step = (RIMS, 9, 6, 19, 9, 6, 14, 9, 9)
    mains = call(
        main_kernel,
        main(*step),
        [(2,) + static],
        [adj, fl_m, fe_m, static_a, static_b, fl_e],
    )
    (out,) = call(
        last_kernel,
        [(pops, planes) + tile],
        edges(*step)
        + [(2,) + second]
        + tiled(DYNAMIC, pops, 15, 27, 15, 9, 9, 6, 19, 3)
        + main(pops)
        + [pltpu.SemaphoreType.DMA((planes,))],
        [fl_m, fe_m, edge, fl_e, fe_e, *mains] + [recv_a, recv_b],
        out_hbm=True,
    )
    return out


def solution(mesh):
    placed = P(None, None, "gx", "gy")
    return jax.shard_map(
        shards, mesh=mesh, in_specs=(placed,) * 5, out_specs=placed, check_vma=False
    )
```

```python
import jax
import jax.numpy as jnp
from jax import lax
from jax.experimental import pallas as pl
from jax.experimental.pallas import tpu as pltpu
from jax.sharding import PartitionSpec as P

VELOCITY = (
    (1, 0, 0),
    (-1, 0, 0),
    (0, 1, 0),
    (0, -1, 0),
    (1, 1, 0),
    (-1, -1, 0),
    (1, -1, 0),
    (-1, 1, 0),
    (1, 0, 1),
    (-1, 0, -1),
    (1, 0, -1),
    (-1, 0, 1),
    (0, 1, 1),
    (0, -1, -1),
    (0, 1, -1),
    (0, -1, 1),
    (0, 0, 0),
    (0, 0, 1),
    (0, 0, -1),
)
INDEX = {c: q for q, c in enumerate(VELOCITY)}
W1, W2, W0 = 1.0 / 18.0, 1.0 / 36.0, 1.0 / 3.0
RELAXATION = (1.0, 1.0, 1.25)
COUPLING = ((0.0, 1.2, -0.6), (1.2, 0.0, -0.6), (-0.6, -0.6, -0.3))
CROSS = ((0, 0), (1, 0), (-1, 0), (0, 1), (0, -1))
AHEAD = tuple(INDEX[(1,) + yz] for yz in CROSS)
BEHIND = tuple(INDEX[(-1,) + yz] for yz in CROSS)
SIDE = ((1, 0), (-1, 0), (0, 1), (0, -1), (1, 1), (-1, -1), (1, -1), (-1, 1))
LEVEL = tuple(q for q in range(19) if VELOCITY[q][0] == 0)
ALONG, AFTER, LATE, EARLY = 15, 42, 57, 72
STATIC = 87
FAR = 9
LATE_PSI, EARLY_PSI = STATIC, STATIC + 3
RIMS = STATIC + 6
DYNAMIC = 12
F32 = jnp.float32
CHUNKS = 4
INSIDE_COST, EDGE_COST, MAIN_COST = 10**7, 10**8, 10**8
VMEM_BYTES = 40 * 1024 * 1024
HALO = 4


class Grid:
    def __init__(self, planes, rows, cols):
        self.planes, self.rows, self.cols = planes, rows, cols
        self.tiles = planes + 1
        self.width = cols // planes
        self.group = 2 * HALO
        self.pack = self.width // self.group
        self.sub = lax.broadcasted_iota(jnp.int32, (rows, cols), 0)
        self.lane = lax.broadcasted_iota(jnp.int32, (rows, cols), 1)

    def roll_rows(self, v, dx):
        return pltpu.roll(v, (-dx) % self.rows, 0)

    def roll_cols(self, v, dy):
        return pltpu.roll(v, (-dy) % self.cols, 1)

    def at_row(self, v, rim, dx):
        edge = self.rows - 1 if dx > 0 else 0
        return jnp.where(self.sub == edge, rim, self.roll_rows(v, dx))

    def in_row(self, v, dx):
        edge = self.rows - 1 if dx > 0 else 0
        return jnp.where(self.sub == edge, 0.0, self.roll_rows(v, dx))

    def sides(self, low, high):
        return jnp.where(self.sub == 0, low, high)

    def over_main(self, body):
        def step(p, carry):
            body(Tile(self, p, False))
            return carry

        lax.fori_loop(0, self.planes, step, 0)

    def over_edge(self, body):
        body(Tile(self, self.planes, True))

    def over(self, body):
        self.over_main(body)
        self.over_edge(body)

    def at_rim(self):
        return (self.sub == 0) | (self.sub == self.rows - 1)

    def low(self):
        return self.sub < self.rows // 2

    def outward(self):
        return jnp.where(self.low(), -1.0, 1.0).astype(F32)


class Tile:
    def __init__(self, grid, index, edge):
        self.grid, self.index, self.edge = grid, index, edge

    def of(self, dz):
        if dz == 0 or self.edge:
            return self.index
        return lax.rem(self.index + (dz + self.grid.planes), self.grid.planes)

    def get(self, ref, c, dz=0):
        if isinstance(ref, Pair):
            v = ref.edge[c] if self.edge else ref.main[c, self.of(dz)]
        else:
            v = ref[c, self.of(dz)]
        if self.edge and dz != 0:
            v = self.grid.roll_cols(v, dz * self.grid.width)
        return v

    def put(self, ref, c, v):
        if not isinstance(ref, Pair):
            ref[c, self.index] = v
        elif self.edge:
            ref.edge[c] = v
        else:
            ref.main[c, self.index] = v


class Pair:
    def __init__(self, main, edge):
        self.main, self.edge = main, edge

    def at(self, c, t):
        return self.edge[c] if t == self.main.shape[1] else self.main[c, t]


def plus(a, b):
    return b if a is None else a + b


def mixed(coefficients, values):
    total = None
    for k, v in zip(coefficients, values):
        if k == 0:
            continue
        term = v if k == 1 else (-v if k == -1 else k * v)
        total = plus(total, term)
    return total


def axis_pairs():
    for q in (0, 2, 17, 4, 6, 8, 10, 12, 14):
        c = VELOCITY[q]
        yield c, (W1 if sum(abs(i) for i in c) == 1 else W2)


def first_and_second(diff, total):
    first = [None] * 3
    second = {}
    for c, w in axis_pairs():
        for d in range(3):
            if c[d] == 0:
                continue
            if diff is not None:
                first[d] = plus(first[d], (w * c[d]) * diff[c])
            if total is not None:
                for e in range(d, 3):
                    if c[e] != 0:
                        second[d, e] = plus(second.get((d, e)), (w * c[d] * c[e]) * total[c])
    return first, second


def turned(second, v):
    return [sum(second[min(d, e), max(d, e)] * v[e] for e in range(3)) for d in range(3)]


def dot(a, b):
    return a[0] * b[0] + a[1] * b[1] + a[2] * b[2]


def field_forces(grid, loads, across, dipole):
    memo = {}

    def source(name, dz, place):
        key = (name, dz, place)
        if key in memo:
            return memo[key]
        if isinstance(name, int):
            v = loads[place](name, dz)
        elif name == "chi":
            v = source(0, dz, place) - source(1, dz, place)
        elif name[0] == "V":
            v = source(2, dz, place) * source(3 + name[1], dz, place)
        else:
            c = name[1]
            v = mixed(c, [source(("V", d), dz, place) if c[d] else None for d in range(3)])
        memo[key] = v
        return v

    def shifted(name, c):
        key = (name, c, "shift")
        if key in memo:
            return memo[key]
        if c[1] != 0:
            v = grid.roll_cols(shifted(name, (c[0], 0, c[2])), c[1])
        elif c[0] != 0:
            v = across(lambda place, dz: source(name, dz, place), c[0], c[2])
        else:
            v = source(name, c[2], 0)
        memo[key] = v
        return v

    def parts(name):
        diff, total = {}, {}
        for c, w in axis_pairs():
            back = tuple(-i for i in c)
            a, b = shifted(name, c), shifted(name, back)
            diff[c], total[c] = a - b, a + b
        return diff, total

    diff, unused = parts(0)
    s0, unused = first_and_second(diff, None)
    diff, unused = parts(2)
    s2, unused = first_and_second(diff, None)
    diff, total = parts("chi")
    schi, second = first_and_second(diff, total)
    s1 = [a - b for a, b in zip(s0, schi)]
    pull = [None] * 3
    for c, w in axis_pairs():
        back = tuple(-i for i in c)
        if sum(abs(i) for i in c) == 1:
            name = ("V", [i for i in range(3) if c[i]][0])
        else:
            name = ("L", c)
        total_c = shifted(name, c) + shifted(name, back)
        for d in range(3):
            if c[d] != 0:
                pull[d] = plus(pull[d], (w * c[d]) * total_c)
    md = turned(second, dipole)
    k0 = [-1.2 * s1[d] + 0.6 * s2[d] - pull[d] for d in range(3)]
    k1 = [-1.2 * s0[d] + 0.6 * s2[d] + pull[d] for d in range(3)]
    k2 = [0.6 * (s0[d] + s1[d]) + 0.3 * s2[d] + md[d] for d in range(3)]
    return k0, k1, k2


def brick_forces(grid, tile, fields, rim, rim_psi, rim_dip):
    def own(c, dz):
        return tile.get(fields, (9 + c) if c < 3 else (3 + c), dz)

    def beyond(c, dz):
        return tile.get(rim, (rim_psi + c) if c < 3 else (rim_dip + c - 3), dz)

    def across(get, cx, dz):
        if rim is None:
            return grid.in_row(get(0, dz), cx)
        return grid.at_row(get(0, dz), get(1, dz), cx)

    return field_forces(grid, (own, beyond), across, [own(3 + d, 0) for d in range(3)])


def rim_forces(grid, tile, fields, rims, psi, base):
    outward = grid.outward()

    def loader(ref, psi_at, dip_at):
        def load(c, dz):
            v = tile.get(ref, (psi_at + c) if c < 3 else (dip_at + c - 3), dz)
            return v * outward if c == 3 else v

        return load

    loads = {
        0: loader(rims, psi, base + 6),
        1: loader(rims, base + FAR, base + FAR + 3),
        -1: loader(fields, 9, 6),
    }
    dipole = [loads[0](3 + d, 0) for d in range(3)]
    return field_forces(grid, loads, lambda get, cx, dz: get(cx, dz), dipole)


def collision_adjoint(streamed_of, rho, u, psi, forces):
    inverse_sum = 1.0 / (rho[0] + rho[1] + rho[2])
    grad_u = [None] * 3
    alphas, held = [], []
    for s in range(3):
        streamed = streamed_of(s)
        diff, total = {}, {}
        for c, w in axis_pairs():
            a, b = streamed[INDEX[c]], streamed[INDEX[tuple(-i for i in c)]]
            diff[c], total[c] = a - b, a + b
        m1, m2 = first_and_second(diff, total)
        m0 = W0 * streamed[16]
        for c, w in axis_pairs():
            m0 = m0 + w * total[c]
        inverse = 1.0 / rho[s]
        ratio = psi[s] * inverse
        tau = RELAXATION[s]
        k = forces[s]
        v = [u[d] + (tau * ratio) * k[d] for d in range(3)]
        mv = turned(m2, v)
        g = [3.0 * (m1[d] + 3.0 * mv[d] - m0 * v[d]) for d in range(3)]
        feq = m0 + 3.0 * dot(m1, v) + 4.5 * dot(mv, v) - 1.5 * m0 * dot(v, v)
        alphas.append(feq * (1.0 / tau) + dot(g, k) * (1.0 - psi[s] - ratio))
        scaled = rho[s] * (1.0 / tau)
        for d in range(3):
            grad_u[d] = plus(grad_u[d], scaled * g[d])
            held.append(psi[s] * g[d])
    beta = [grad_u[d] * inverse_sum for d in range(3)]
    along = dot(beta, u)
    return held, [a - along for a in alphas], beta


def brick_collision(grid, tile, load, rim, fields, forces, hold, ab, kept):
    def streamed_of(s):
        streamed = []
        for q in range(19):
            c = VELOCITY[q]
            v = load(s * 19 + q, c[2])
            if c[0] != 0:
                j = (AHEAD if c[0] > 0 else BEHIND).index(q)
                if rim is None:
                    v = grid.in_row(v, c[0])
                else:
                    v = grid.at_row(v, tile.get(rim, s * 5 + j, c[2]), c[0])
            if c[1] != 0:
                v = grid.roll_cols(v, c[1])
            streamed.append(v)
            if s == 2:
                tile.put(kept, q, v)
        return streamed

    rho, u, psi = [[tile.get(fields, at + d) for d in range(3)] for at in (0, 3, 9)]
    held, alpha, beta = collision_adjoint(streamed_of, rho, u, psi, forces)
    for k in range(9):
        tile.put(hold, k, held[k])
    for s in range(3):
        tile.put(ab, s, alpha[s])
        tile.put(ab, 3 + s, beta[s])


def rim_collision(grid, tile, level, after, inner, rho, u, psi, forces, hold, ab, kept):
    outward, low = grid.outward(), grid.low()

    def streamed_of(s):
        streamed = []
        for q in range(19):
            c = VELOCITY[q]
            if c[0] == 0:
                v = level(s, LEVEL.index(q), c[2])
            elif c[0] > 0:
                v = after(s, AHEAD.index(q), c[2])
            else:
                j = BEHIND.index(q)
                v = jnp.where(low, inner(s * 19 + AHEAD[j], c[2]), inner(s * 19 + BEHIND[j], c[2]))
            if c[1] != 0:
                v = grid.roll_cols(v, c[1])
            streamed.append(v)
            if s == 2 and kept is not None and c[0] >= 0:
                tile.put(kept, LEVEL.index(q) if c[0] == 0 else 9 + AHEAD.index(q), v)
        return streamed

    u = [u[0] * outward, u[1], u[2]]
    held, alpha, beta = collision_adjoint(streamed_of, rho, u, psi, forces)
    for k in range(9):
        tile.put(hold, k, held[k] * outward if k % 3 == 0 else held[k])
    if ab is not None:
        for s in range(3):
            tile.put(ab, s, alpha[s])
            tile.put(ab, 3 + s, beta[s] * outward if s == 0 else beta[s])


def spread_plane(grid, get_h, get_d, sign, pairs):
    memo = {}

    def source(dz):
        if dz in memo:
            return memo[dz]
        h = [[get_h(3 * s + d, dz) for d in range(3)] for s in range(3)]
        dip = [get_d(d, dz) for d in range(3)]
        if not isinstance(sign, int):
            for vec in h + [dip]:
                vec[0] = vec[0] * sign
        memo[dz] = (h, dip)
        return memo[dz]

    cx = sign if isinstance(sign, int) else 1
    r = [None] * 3
    w_vec = [None] * 3
    lanes = {}
    for cy, cz in pairs:
        w = W1 if abs(cx) + abs(cy) + abs(cz) == 1 else W2
        h, dip = source(cz)
        c = (cx, cy, cz)
        e = [mixed(c, h[s]) for s in range(3)]
        f = e[2] * mixed(c, dip)
        half = 0.6 * e[2]
        r0 = 1.2 * e[1] - half + f
        r1 = 1.2 * e[0] - half - f
        r2 = -0.6 * (e[0] + e[1]) - 0.3 * e[2]
        qv = e[0] - e[1]
        vals = [w * r0, w * r1, w * r2]
        wq = w * qv
        vals += [wq if cx != 0 else None, wq if cy != 0 else None, wq if cz != 0 else None]
        vals = [vals[0], vals[1], vals[2]] + [
            None if x is None else (x if k == 1 else -x) for x, k in zip(vals[3:], (cx, cy, cz))
        ]
        acc = lanes.setdefault(cy, [None] * 6)
        for i, x in enumerate(vals):
            if x is not None:
                acc[i] = plus(acc[i], x)
    total = [None] * 6
    for cy, acc in lanes.items():
        for i, x in enumerate(acc):
            if x is not None:
                total[i] = plus(total[i], x if cy == 0 else grid.roll_cols(x, cy))
    if not isinstance(sign, int):
        total[3] = total[3] * sign
    return total


def met(total, dipole):
    meet = None
    for d in range(3):
        if total[3 + d] is not None:
            meet = plus(meet, total[3 + d] * dipole[d])
    return [total[0], total[1], total[2] - meet]


def spread_inside(grid, tile, hold, fields):
    get_h = lambda k, dz: tile.get(hold, k, dz)
    get_d = lambda k, dz: tile.get(fields, 6 + k, dz)
    total = spread_plane(grid, get_h, get_d, 0, SIDE)
    for dx in (1, -1):
        part = spread_plane(grid, get_h, get_d, dx, CROSS)
        for i, x in enumerate(part):
            total[i] = plus(total[i], grid.in_row(x, dx))
    return met(total, [tile.get(fields, 6 + d) for d in range(3)])


def rim_sign(grid):
    return jnp.where(
        grid.sub == 0, -1.0, jnp.where(grid.sub == grid.rows - 1, 1.0, 0.0)
    ).astype(F32)


def hand_over(grid, tile, hold, hold_dip, target, sign):
    dip, at = hold_dip
    total = spread_plane(
        grid,
        lambda k, dz: tile.get(hold, k, dz),
        lambda k, dz: tile.get(dip, at + k, dz),
        sign,
        CROSS,
    )
    return met(total, target)


def spread_level(grid, tile, hold, dip, at):
    total = spread_plane(
        grid,
        lambda k, dz: tile.get(hold, k, dz),
        lambda k, dz: tile.get(dip, at + k, dz),
        0,
        SIDE,
    )
    return met(total, [tile.get(dip, at + d) for d in range(3)])


def parity_of(axis):
    return lax.rem(lax.axis_index(axis) + 1, 2)


def lines_from(first, second, parity, lines):
    lines[1 - parity] = first[...]
    lines[parity] = second[...]


def lines_to(first, second, lines):
    first[...] = lines[0]
    second[...] = lines[1]


def psi_of(rho):
    return 1.0 - jnp.exp(-rho)


def pack_static(get, tiles, rows, lines, parity):
    up, down = parity, 1 - parity
    fill = 0

    def put(kind, above, below, depth):
        nonlocal fill
        for t in tiles:
            v = get(kind, above, t)
            lines[up, fill : fill + 1, :] = v[rows - 1 - depth : rows - depth, :]
            v = get(kind, below, t)
            lines[down, fill : fill + 1, :] = v[depth : depth + 1, :]
            fill += 1

    for s in range(3):
        for j in range(5):
            put(0, s * 19 + BEHIND[j], s * 19 + AHEAD[j], 0)
    for s in range(3):
        for q in LEVEL:
            put(0, s * 19 + q, s * 19 + q, 0)
    for s in range(3):
        for j in range(5):
            put(0, s * 19 + BEHIND[j], s * 19 + AHEAD[j], 1)
    for kind in (1, 2):
        for c in range(9):
            put(kind, c, c, 0)
        for c in (9, 10, 11, 6, 7, 8):
            put(kind, c, c, 1)
    return fill


def pack_columns_kernel(
    adj_in, late_in, early_in, dip_late_in, dip_early_in,
    send_c, send_d, own_left, own_right, fl, fe, adj,
    late, early, dip_late, dip_early, sems,
):
    planes, rows, cols = adj.shape[1:]
    grid = Grid(planes, rows, cols)
    copies = [
        pltpu.make_async_copy(a, b, sems.at[i])
        for i, (a, b) in enumerate(
            (
                (dip_late_in, dip_late),
                (late_in, late),
                (dip_early_in, dip_early),
                (early_in, early),
            )
        )
    ]
    per_chunk = -(-adj.shape[0] // (CHUNKS * grid.pack)) * grid.pack
    for i in range(CHUNKS):
        part = pl.ds(i * per_chunk, min(per_chunk, adj.shape[0] - i * per_chunk))
        copies.append(pltpu.make_async_copy(adj_in.at[part], adj.at[part], sems.at[4 + i]))
    for copy in copies:
        copy.start()
    for which, (saved, dip, out) in enumerate(((late, dip_late, fl), (early, dip_early, fe))):
        copies[2 * which].wait()
        copies[2 * which + 1].wait()

        def step(p, carry):
            flows = [None] * 19
            rho = []
            for s in range(3):
                total = None
                for q in range(19):
                    v = saved[s * 19 + q, p].astype(F32)
                    flows[q] = plus(flows[q], v)
                    total = plus(total, v)
                rho.append(total)
                out[s, p] = total
                out[9 + s, p] = psi_of(total)
            inverse = 1.0 / (rho[0] + rho[1] + rho[2])
            for d in range(3):
                momentum = None
                for q in range(19):
                    if VELOCITY[q][d] != 0:
                        momentum = plus(momentum, flows[q] if VELOCITY[q][d] > 0 else -flows[q])
                out[3 + d, p] = momentum * inverse
                out[6 + d, p] = dip[d, p].astype(F32)
            return carry

        lax.fori_loop(0, planes, step, 0)
    pops = adj.shape[0]
    components = pops + 18
    slot = grid.lane // grid.group
    for g in range(own_left.shape[0]):
        if g * grid.pack % per_chunk == 0 and g * grid.pack < pops:
            copies[4 + g * grid.pack // per_chunk].wait()
        left = right = jnp.zeros((rows, cols), F32)
        for j in range(grid.pack):
            c = g * grid.pack + j
            if c >= components:
                continue
            for p in range(planes):
                if c < pops:
                    v = adj[c, p]
                elif c < pops + 9:
                    v = fl[c - pops, p]
                else:
                    v = fe[c - pops - 9, p]
                at = p * grid.pack + j
                rolled = pltpu.roll(v, at * grid.group, 1) if at else v
                left = jnp.where(slot == at, rolled, left)
                right = jnp.where(slot == (at - 1) % (cols // grid.group), rolled, right)
        own_left[g] = left
        own_right[g] = right
    low = lax.rem(grid.lane, grid.group) < HALO
    even = parity_of("gy") == 0
    for h in range(send_c.shape[0]):
        left = jnp.where(low, own_left[2 * h], pltpu.roll(own_left[2 * h + 1], HALO, 1))
        right = jnp.where(low, pltpu.roll(own_right[2 * h + 1], cols - HALO, 1), own_right[2 * h])
        send_c[h] = jnp.where(even, right, left)
        send_d[h] = jnp.where(even, left, right)


def inside_collision(grid, tile, load, fields, hold, ab, kept):
    forces = brick_forces(grid, tile, fields, None, 0, 0)
    brick_collision(grid, tile, load, None, fields, forces, hold, ab, kept)
    at_rim = grid.at_rim()
    for k in range(9):
        tile.put(hold, k, jnp.where(at_rim, 0.0, tile.get(hold, k)))


def second_row(grid, tile, fields, hold, ab, kept, sides):
    low = grid.low()
    rest = 1.0 - 1.0 / RELAXATION[2]
    back = spread_inside(grid, tile, hold, fields)
    alpha = [tile.get(ab, s) + (1.0 - tile.get(fields, 9 + s)) * back[s] for s in range(3)]
    beta = [tile.get(ab, 3 + d) for d in range(3)]
    ahead = -grid.outward() * beta[0]
    for s in range(3):
        tile.put(sides, s, back[s])
    for s in range(2):
        tile.put(sides, 3 + s, alpha[s] + ahead)
        tile.put(sides, 5 + s, beta[1 + s])
    for j, yz in enumerate(CROSS):
        v = rest * jnp.where(low, tile.get(kept, AHEAD[j]), tile.get(kept, BEHIND[j]))
        v = v + (alpha[2] + ahead)
        tile.put(sides, 7 + j, v + mixed(yz, beta[1:]) if j else v)


def static_kernel(adj, fl, fe, send_a, send_b, lines):
    planes, rows, cols = adj.shape[1:]
    kinds = (adj, fl, fe)
    pack_static(lambda kind, c, t: kinds[kind][c, t], range(planes), rows, lines, parity_of("gx"))
    lines_to(send_a, send_b, lines)


def inside_kernel(adj, fl, sides, hold, ab, kept):
    planes, rows, cols = adj.shape[1:]
    grid = Grid(planes, rows, cols)
    load = lambda tile: lambda c, dz: tile.get(adj, c, dz)
    grid.over_main(lambda tile: inside_collision(grid, tile, load(tile), fl, hold, ab, kept))
    grid.over_main(lambda tile: second_row(grid, tile, fl, hold, ab, kept, sides))


def edge_kernel(
    own_left, own_right, recv_c, recv_d, sides_main,
    send_a, send_b, edge, fl, fe, lines, hold, ab, kept, sides,
):
    planes, rows, cols = sides_main.shape[1:]
    pops = edge.shape[0]
    grid = Grid(planes, rows, cols)
    even = parity_of("gy") == 0
    slot = lax.rem(grid.lane // grid.group, grid.pack)
    left_half = lax.rem(grid.lane, grid.width) < grid.width // 2
    components = pops + 18
    for g in range(own_left.shape[0]):
        first, second = recv_c[g // 2], recv_d[g // 2]
        from_next = jnp.where(even, first, second)
        from_prior = jnp.where(even, second, first)
        if g % 2:
            from_next = pltpu.roll(from_next, cols - HALO, 1)
            from_prior = pltpu.roll(from_prior, HALO, 1)
        for j in range(grid.pack):
            c = g * grid.pack + j
            if c >= components:
                continue
            before = slot == (j - 1) % grid.pack
            low = jnp.where(before, from_prior, own_left[g])
            high = jnp.where(before, own_right[g], from_next)
            v = jnp.where(
                left_half,
                pltpu.roll(low, ((1 - j) * grid.group) % cols, 1),
                pltpu.roll(high, ((3 - j) * grid.group) % cols, 1),
            )
            if c < pops:
                edge[c] = v
            else:
                field, k = (fl, c - pops) if c < pops + 9 else (fe, c - pops - 9)
                field[k] = v
                if k < 3:
                    field[9 + k] = psi_of(v)
    adj, fields, both = Pair(None, edge), Pair(None, fl), Pair(sides_main, sides)
    hold, ab, kept = Pair(None, hold), Pair(None, ab), Pair(None, kept)

    def inside(tile):
        load = lambda c, dz: tile.get(adj, c, dz)
        inside_collision(grid, tile, load, fields, hold, ab, kept)
        second_row(grid, tile, fields, hold, ab, kept, both)

    grid.over_edge(inside)
    parity = parity_of("gx")
    kinds = (edge, fl, fe)
    fill = pack_static(lambda kind, c, t: kinds[kind][c], (0,), rows, lines, parity)
    for c in range(DYNAMIC):
        depth = 0 if c < 3 else 1
        for t in range(grid.tiles):
            v = both.at(c, t)
            lines[parity, fill : fill + 1, :] = v[rows - 1 - depth : rows - depth, :]
            lines[1 - parity, fill : fill + 1, :] = v[depth : depth + 1, :]
            fill += 1
    lines_to(send_a, send_b, lines)


def first_step(grid, tile, adj, fl, rims, hold, ab, kept, hold_rim, ab_rim, kept_rim):
    forces = brick_forces(grid, tile, fl, rims, LATE_PSI, LATE + 6)
    load = lambda c, dz: tile.get(adj, c, dz)
    brick_collision(grid, tile, load, rims, fl, forces, hold, ab, kept)
    forces = rim_forces(grid, tile, fl, rims, LATE_PSI, LATE)
    rho, u = [[tile.get(rims, LATE + at + d) for d in range(3)] for at in (0, 3)]
    psi = [tile.get(rims, LATE_PSI + s) for s in range(3)]
    rim_collision(
        grid,
        tile,
        lambda s, i, dz: tile.get(rims, ALONG + s * 9 + i, dz),
        lambda s, j, dz: tile.get(rims, AFTER + s * 5 + j, dz),
        load,
        rho,
        u,
        psi,
        forces,
        hold_rim,
        ab_rim,
        kept_rim,
    )


def early_forces(grid, tile, fe, rims, forces, forces_rim):
    brick = brick_forces(grid, tile, fe, rims, EARLY_PSI, EARLY + 6)
    beyond = rim_forces(grid, tile, fe, rims, EARLY_PSI, EARLY)
    for s in range(3):
        for d in range(3):
            tile.put(forces, 3 * s + d, brick[s][d])
            tile.put(forces_rim, 3 * s + d, beyond[s][d])


def rim_psis(grid, tile, rims):
    for s in range(3):
        tile.put(rims, LATE_PSI + s, psi_of(tile.get(rims, LATE + s)))
        tile.put(rims, EARLY_PSI + s, psi_of(tile.get(rims, EARLY + s)))


def finish_first(grid, tile, fl, rims, hold, ab, kept, hold_rim, ab_rim, mid, part):
    rest = 1.0 - 1.0 / RELAXATION[2]
    sign, at_rim = rim_sign(grid), grid.at_rim()
    own_dip, rim_dip = (fl, 6), (rims, LATE + 6)
    dip = [tile.get(fl, 6 + d) for d in range(3)]
    dip_rim = [tile.get(rims, LATE + 6 + d) for d in range(3)]
    dip_far = [tile.get(rims, LATE + FAR + 3 + d) for d in range(3)]
    back = spread_inside(grid, tile, hold, fl)
    inward = hand_over(grid, tile, hold_rim, rim_dip, dip, sign)
    alpha = [
        tile.get(ab, s)
        + (1.0 - tile.get(fl, 9 + s)) * (back[s] + jnp.where(at_rim, inward[s], 0.0))
        for s in range(3)
    ]
    beta = [tile.get(ab, 3 + d) for d in range(3)]
    for q in range(19):
        along = mixed(VELOCITY[q], beta) if q != 16 else None
        for s in range(3):
            v = alpha[s] if along is None else alpha[s] + along
            if s == 2:
                v = v + rest * tile.get(kept, q)
            tile.put(mid, s * 19 + q, v)
    given = hand_over(grid, tile, hold, own_dip, dip_rim, -sign)
    level = spread_level(grid, tile, hold_rim, *rim_dip)
    after = hand_over(grid, tile, hold_rim, rim_dip, dip_far, -sign)
    for s in range(3):
        open_share = 1.0 - tile.get(rims, LATE_PSI + s)
        tile.put(part, s, tile.get(ab_rim, s) + open_share * (given[s] + level[s]))
        tile.put(part, 3 + s, tile.get(ab_rim, 3 + s))
        tile.put(part, 6 + s, (1.0 - tile.get(rims, LATE + FAR + s)) * after[s])


def main_kernel(
    adj, fl, fe, recv_a, recv_b, after,
    rims, mid, part, kept_rim, forces, forces_rim, lines, hold, ab, kept, hold_rim, ab_rim,
):
    planes, rows, cols = adj.shape[1:]
    grid = Grid(planes, rows, cols)
    lines_from(recv_a, recv_b, parity_of("gx"), lines)
    for c in range(STATIC):
        for p in range(planes):
            k = c * planes + p
            rims[c, p] = grid.sides(lines[0, k : k + 1, :], lines[1, k : k + 1, :])
    grid.over_main(lambda tile: rim_psis(grid, tile, rims))

    def step(tile):
        first_step(grid, tile, adj, fl, rims, hold, ab, kept, hold_rim, ab_rim, kept_rim)
        early_forces(grid, tile, fe, rims, forces, forces_rim)

    grid.over_main(step)
    grid.over_main(
        lambda tile: finish_first(
            grid, tile, fl, rims, hold, ab, kept, hold_rim, ab_rim, mid, part
        )
    )


def last_kernel(
    fe_m, rims_m, mid_m, part_m, kept_rim_m, forces_m, forces_rim_m, edge, fl_e, fe_e,
    recv_a, recv_b, out,
    rims_e, mid_e, part_e, kept_rim_e, forces_e, forces_rim_e, hold_e, ab_e, kept_e, hold_rim_e,
    ab_rim_e, patches, lines, near, rim_mid, rim_level, rim_far, hold2, hold_rim2, ab2, kept2,
    total, staged, sems,
):
    planes, rows, cols = fe_m.shape[1:]
    grid = Grid(planes, rows, cols)
    lines_from(recv_a, recv_b, parity_of("gx"), lines)
    for c in range(STATIC):
        rims_e[c] = grid.sides(lines[0, c : c + 1, :], lines[1, c : c + 1, :])
    for c in range(DYNAMIC):
        for t in range(grid.tiles):
            k = STATIC + c * grid.tiles + t
            near[c, t] = grid.sides(lines[0, k : k + 1, :], lines[1, k : k + 1, :])
    fe, rims, mid = Pair(fe_m, fe_e), Pair(rims_m, rims_e), Pair(mid_m, mid_e)
    part, kept_rim = Pair(part_m, part_e), Pair(kept_rim_m, kept_rim_e)
    forces, forces_rim = Pair(forces_m, forces_e), Pair(forces_rim_m, forces_rim_e)
    rest = 1.0 - 1.0 / RELAXATION[2]
    at_rim = grid.at_rim()
    sign = rim_sign(grid)
    outward = grid.outward()

    def edge_steps(tile):
        adj, fl = Pair(None, edge), Pair(None, fl_e)
        hold, ab, kept = Pair(None, hold_e), Pair(None, ab_e), Pair(None, kept_e)
        hold_rim, ab_rim = Pair(None, hold_rim_e), Pair(None, ab_rim_e)
        rim_psis(grid, tile, rims)
        first_step(grid, tile, adj, fl, rims, hold, ab, kept, hold_rim, ab_rim, kept_rim)
        early_forces(grid, tile, fe, rims, forces, forces_rim)
        finish_first(grid, tile, fl, rims, hold, ab, kept, hold_rim, ab_rim, mid, part)

    grid.over_edge(edge_steps)

    def complete(tile):
        t = tile.index
        alpha = [
            tile.get(part, s) + (1.0 - tile.get(rims, LATE_PSI + s)) * near[s, t]
            for s in range(3)
        ]
        beta = [tile.get(part, 3 + d) for d in range(3)]
        far = [near[3 + s, t] + tile.get(part, 6 + s) for s in range(2)]
        far_beta = [near[5 + d, t] for d in range(2)]
        ahead = outward * beta[0]
        for j, yz in enumerate(CROSS):
            side = mixed(yz, beta[1:]) if j else None
            side_far = mixed(yz, far_beta) if j else None
            for s in range(3):
                v = plus(side, alpha[s] + ahead)
                if s == 2:
                    v = v + rest * tile.get(kept_rim, 9 + j)
                    rim_far[10 + j, t] = near[7 + j, t] + tile.get(part, 8)
                else:
                    rim_far[s * 5 + j, t] = plus(side_far, far[s])
                rim_mid[s * 5 + j, t] = v
        for i, q in enumerate(LEVEL):
            side = mixed(VELOCITY[q][1:], beta[1:]) if q != 16 else None
            for s in range(3):
                v = plus(side, alpha[s])
                if s == 2:
                    v = v + rest * tile.get(kept_rim, i)
                rim_level[s * 9 + i, t] = v

    grid.over(complete)

    def collide(tile):
        load = lambda c, dz: tile.get(mid, c, dz)
        known = [[tile.get(forces, 3 * s + d) for d in range(3)] for s in range(3)]
        brick_collision(grid, tile, load, rim_mid, fe, known, hold2, ab2, kept2)
        known = [[tile.get(forces_rim, 3 * s + d) for d in range(3)] for s in range(3)]
        rho, u = [[tile.get(rims, EARLY + at + d) for d in range(3)] for at in (0, 3)]
        psi = [tile.get(rims, EARLY_PSI + s) for s in range(3)]
        rim_collision(
            grid,
            tile,
            lambda s, i, dz: tile.get(rim_level, s * 9 + i, dz),
            lambda s, j, dz: tile.get(rim_far, s * 5 + j, dz),
            load,
            rho,
            u,
            psi,
            known,
            hold_rim2,
            None,
            None,
        )

    grid.over(collide)

    def finish(tile):
        back = spread_inside(grid, tile, hold2, fe)
        dip = [tile.get(fe, 6 + d) for d in range(3)]
        inward = hand_over(grid, tile, hold_rim2, (rims, EARLY + 6), dip, sign)
        for s in range(3):
            x = back[s] + jnp.where(at_rim, inward[s], 0.0)
            total[s, tile.index] = tile.get(ab2, s) + (1.0 - tile.get(fe, 9 + s)) * x

    grid.over(finish)
    at_side = (grid.lane < HALO) | (grid.lane >= cols - HALO)
    first_group = lax.rem(grid.lane, grid.width) < grid.group
    sources = [total.at[s] for s in range(3)] + [ab2.at[3 + d] for d in range(3)]
    sources += [kept2.at[q] for q in range(19)]
    for i, ref in enumerate(sources):
        v = ref[planes]
        patches[i] = jnp.where(first_group, pltpu.roll(v, cols - 2 * grid.group, 1), v)
    copies = []
    for p in range(planes):
        turn = (cols - p * grid.width - grid.group) % cols

        def patched(i):
            return jnp.where(at_side, pltpu.roll(patches[i], turn, 1), sources[i][p])

        alpha = [patched(s) for s in range(3)]
        beta = [patched(3 + d) for d in range(3)]
        for q in range(19):
            along = mixed(VELOCITY[q], beta) if q != 16 else None
            for s in range(3):
                v = alpha[s] if along is None else alpha[s] + along
                if s == 2:
                    v = v + rest * patched(6 + q)
                staged[s * 19 + q, p] = v
        copies.append(pltpu.make_async_copy(staged.at[:, p], out.at[:, p], sems.at[p]))
        copies[p].start()
    for copy in copies:
        copy.wait()


def call(kernel, outs, scratch, args, in_hbm=False, out_hbm=False, cost=0):
    vmem = pl.BlockSpec(memory_space=pltpu.VMEM)
    hbm = pl.BlockSpec(memory_space=pltpu.HBM)
    return pl.pallas_call(
        kernel,
        out_shape=[jax.ShapeDtypeStruct(s, F32) for s in outs],
        in_specs=[hbm if in_hbm else vmem] * len(args),
        out_specs=[hbm if out_hbm else vmem] * len(outs),
        scratch_shapes=[pltpu.VMEM(s, F32) if isinstance(s, tuple) else s for s in scratch],
        compiler_params=pltpu.CompilerParams(vmem_limit_bytes=VMEM_BYTES),
        cost_estimate=pl.CostEstimate(flops=cost, bytes_accessed=cost, transcendentals=0),
    )(*[pltpu.with_memory_space_constraint(x, pltpu.HBM) if in_hbm else x for x in args])


def swap(block, axis, offset):
    size = lax.axis_size(axis)
    route = []
    for i in range(offset, size + offset, 2):
        a, b = i % size, (i + 1) % size
        route += [(a, b), (b, a)]
    return lax.ppermute(block, axis, route)


def shards(adjoint_in, populations_early, populations_late, dipoles_early, dipoles_late):
    pops, planes, rows, cols = adjoint_in.shape
    tile = (rows, cols)
    pack = cols // planes // (2 * HALO)
    groups = -(-(pops + 18) // pack)
    groups += groups % 2

    def lines(n):
        return (-(-n // 8) * 8, cols)

    def main(*counts):
        return [(n, planes) + tile for n in counts]

    def edges(*counts):
        return [(n,) + tile for n in counts]

    def tiled(*counts):
        return [(n, planes + 1) + tile for n in counts]

    static = lines(STATIC * planes)
    second = lines(STATIC + DYNAMIC * (planes + 1))
    send_c, send_d, own_left, own_right, fl_m, fe_m, adj = call(
        pack_columns_kernel,
        edges(groups // 2, groups // 2, groups, groups) + main(12, 12, pops),
        [
            pltpu.VMEM(x.shape, x.dtype)
            for x in (populations_late, populations_early, dipoles_late, dipoles_early)
        ]
        + [pltpu.SemaphoreType.DMA((4 + CHUNKS,))],
        [adjoint_in, populations_late, populations_early, dipoles_late, dipoles_early],
        in_hbm=True,
    )
    recv_c, recv_d = swap(send_c, "gy", 1), swap(send_d, "gy", 0)
    send_a, send_b = call(
        static_kernel, [static] * 2, [(2,) + static], [adj, fl_m, fe_m]
    )
    (sides,) = call(
        inside_kernel, main(DYNAMIC), main(9, 6, 19), [adj, fl_m], cost=INSIDE_COST
    )
    static_a, static_b = swap(send_a, "gx", 1), swap(send_b, "gx", 0)
    send_a, send_b, edge, fl_e, fe_e = call(
        edge_kernel,
        [second] * 2 + edges(pops, 12, 12),
        [(2,) + second] + edges(9, 6, 19, DYNAMIC),
        [own_left, own_right, recv_c, recv_d, sides],
        cost=EDGE_COST,
    )
    recv_a, recv_b = swap(send_a, "gx", 1), swap(send_b, "gx", 0)
    known = (RIMS, pops, 9, 14, 9, 9)
    mains = call(
        main_kernel,
        main(*known),
        [(2,) + static] + main(9, 6, 19, 9, 6),
        [adj, fl_m, fe_m, static_a, static_b, fl_e],
        cost=MAIN_COST,
    )
    (out,) = call(
        last_kernel,
        [(pops, planes) + tile],
        edges(*known, 9, 6, 19, 9, 6, 25)
        + [(2,) + second]
        + tiled(DYNAMIC, 15, 27, 15, 9, 9, 6, 19, 3)
        + main(pops)
        + [pltpu.SemaphoreType.DMA((planes,))],
        [fe_m, *mains, edge, fl_e, fe_e, recv_a, recv_b],
        out_hbm=True,
    )
    return out


def solution(mesh):
    placed = P(None, None, "gx", "gy")
    return jax.shard_map(
        shards, mesh=mesh, in_specs=(placed,) * 5, out_specs=placed, check_vma=False
    )
```

```python
import jax
import jax.numpy as jnp
from jax import lax
from jax.experimental import pallas as pl
from jax.experimental.pallas import tpu as pltpu
from jax.sharding import PartitionSpec as P

VELOCITY = (
    (1, 0, 0),
    (-1, 0, 0),
    (0, 1, 0),
    (0, -1, 0),
    (1, 1, 0),
    (-1, -1, 0),
    (1, -1, 0),
    (-1, 1, 0),
    (1, 0, 1),
    (-1, 0, -1),
    (1, 0, -1),
    (-1, 0, 1),
    (0, 1, 1),
    (0, -1, -1),
    (0, 1, -1),
    (0, -1, 1),
    (0, 0, 0),
    (0, 0, 1),
    (0, 0, -1),
)
INDEX = {c: q for q, c in enumerate(VELOCITY)}
W1, W2, W0 = 1.0 / 18.0, 1.0 / 36.0, 1.0 / 3.0
RELAXATION = (1.0, 1.0, 1.25)
COUPLING = ((0.0, 1.2, -0.6), (1.2, 0.0, -0.6), (-0.6, -0.6, -0.3))
CROSS = ((0, 0), (1, 0), (-1, 0), (0, 1), (0, -1))
AHEAD = tuple(INDEX[(1,) + yz] for yz in CROSS)
BEHIND = tuple(INDEX[(-1,) + yz] for yz in CROSS)
SIDE = ((1, 0), (-1, 0), (0, 1), (0, -1), (1, 1), (-1, -1), (1, -1), (-1, 1))
LEVEL = tuple(q for q in range(19) if VELOCITY[q][0] == 0)
ALONG, AFTER, LATE, EARLY = 15, 42, 57, 72
STATIC = 87
FAR = 9
LATE_PSI, EARLY_PSI = STATIC, STATIC + 3
RIMS = STATIC + 6
DYNAMIC = 12
F32 = jnp.float32
CHUNKS = 4
INSIDE_COST, EDGE_COST, MAIN_COST = 10**7, 10**8, 10**8
VMEM_BYTES = 40 * 1024 * 1024
HALO = 4


class Grid:
    def __init__(self, planes, rows, cols):
        self.planes, self.rows, self.cols = planes, rows, cols
        self.tiles = planes + 1
        self.width = cols // planes
        self.group = 2 * HALO
        self.pack = self.width // self.group
        self.sub = lax.broadcasted_iota(jnp.int32, (rows, cols), 0)
        self.lane = lax.broadcasted_iota(jnp.int32, (rows, cols), 1)

    def roll_rows(self, v, dx):
        return pltpu.roll(v, (-dx) % self.rows, 0)

    def roll_cols(self, v, dy):
        return pltpu.roll(v, (-dy) % self.cols, 1)

    def at_row(self, v, rim, dx):
        edge = self.rows - 1 if dx > 0 else 0
        return jnp.where(self.sub == edge, rim, self.roll_rows(v, dx))

    def in_row(self, v, dx):
        edge = self.rows - 1 if dx > 0 else 0
        return jnp.where(self.sub == edge, 0.0, self.roll_rows(v, dx))

    def sides(self, low, high):
        return jnp.where(self.sub == 0, low, high)

    def over_main(self, body):
        for p in range(self.planes):
            body(Tile(self, p, False))

    def over_edge(self, body):
        body(Tile(self, self.planes, True))

    def over(self, body):
        self.over_main(body)
        self.over_edge(body)

    def at_rim(self):
        return (self.sub == 0) | (self.sub == self.rows - 1)

    def low(self):
        return self.sub < self.rows // 2

    def outward(self):
        return jnp.where(self.low(), -1.0, 1.0).astype(F32)


class Tile:
    def __init__(self, grid, index, edge):
        self.grid, self.index, self.edge = grid, index, edge

    def of(self, dz):
        if dz == 0 or self.edge:
            return self.index
        return (self.index + dz) % self.grid.planes

    def get(self, ref, c, dz=0):
        if isinstance(ref, Pair):
            v = ref.edge[c] if self.edge else ref.main[c, self.of(dz)]
        else:
            v = ref[c, self.of(dz)]
        if self.edge and dz != 0:
            v = self.grid.roll_cols(v, dz * self.grid.width)
        return v

    def put(self, ref, c, v):
        if not isinstance(ref, Pair):
            ref[c, self.index] = v
        elif self.edge:
            ref.edge[c] = v
        else:
            ref.main[c, self.index] = v


class Pair:
    def __init__(self, main, edge):
        self.main, self.edge = main, edge

    def at(self, c, t):
        return self.edge[c] if t == self.main.shape[1] else self.main[c, t]


def plus(a, b):
    return b if a is None else a + b


def mixed(coefficients, values):
    total = None
    for k, v in zip(coefficients, values):
        if k == 0:
            continue
        term = v if k == 1 else (-v if k == -1 else k * v)
        total = plus(total, term)
    return total


def axis_pairs():
    for q in (0, 2, 17, 4, 6, 8, 10, 12, 14):
        c = VELOCITY[q]
        yield c, (W1 if sum(abs(i) for i in c) == 1 else W2)


def first_and_second(diff, total):
    first = [None] * 3
    second = {}
    for c, w in axis_pairs():
        for d in range(3):
            if c[d] == 0:
                continue
            if diff is not None:
                first[d] = plus(first[d], (w * c[d]) * diff[c])
            if total is not None:
                for e in range(d, 3):
                    if c[e] != 0:
                        second[d, e] = plus(second.get((d, e)), (w * c[d] * c[e]) * total[c])
    return first, second


def turned(second, v):
    return [sum(second[min(d, e), max(d, e)] * v[e] for e in range(3)) for d in range(3)]


def dot(a, b):
    return a[0] * b[0] + a[1] * b[1] + a[2] * b[2]


def field_forces(grid, loads, across, dipole):
    memo = {}

    def source(name, dz, place):
        key = (name, dz, place)
        if key in memo:
            return memo[key]
        if isinstance(name, int):
            v = loads[place](name, dz)
        elif name == "chi":
            v = source(0, dz, place) - source(1, dz, place)
        elif name[0] == "V":
            v = source(2, dz, place) * source(3 + name[1], dz, place)
        else:
            c = name[1]
            v = mixed(c, [source(("V", d), dz, place) if c[d] else None for d in range(3)])
        memo[key] = v
        return v

    def shifted(name, c):
        key = (name, c, "shift")
        if key in memo:
            return memo[key]
        if c[1] != 0:
            v = grid.roll_cols(shifted(name, (c[0], 0, c[2])), c[1])
        elif c[0] != 0:
            v = across(lambda place, dz: source(name, dz, place), c[0], c[2])
        else:
            v = source(name, c[2], 0)
        memo[key] = v
        return v

    def parts(name):
        diff, total = {}, {}
        for c, w in axis_pairs():
            back = tuple(-i for i in c)
            a, b = shifted(name, c), shifted(name, back)
            diff[c], total[c] = a - b, a + b
        return diff, total

    diff, unused = parts(0)
    s0, unused = first_and_second(diff, None)
    diff, unused = parts(2)
    s2, unused = first_and_second(diff, None)
    diff, total = parts("chi")
    schi, second = first_and_second(diff, total)
    s1 = [a - b for a, b in zip(s0, schi)]
    pull = [None] * 3
    for c, w in axis_pairs():
        back = tuple(-i for i in c)
        if sum(abs(i) for i in c) == 1:
            name = ("V", [i for i in range(3) if c[i]][0])
        else:
            name = ("L", c)
        total_c = shifted(name, c) + shifted(name, back)
        for d in range(3):
            if c[d] != 0:
                pull[d] = plus(pull[d], (w * c[d]) * total_c)
    md = turned(second, dipole)
    k0 = [-1.2 * s1[d] + 0.6 * s2[d] - pull[d] for d in range(3)]
    k1 = [-1.2 * s0[d] + 0.6 * s2[d] + pull[d] for d in range(3)]
    k2 = [0.6 * (s0[d] + s1[d]) + 0.3 * s2[d] + md[d] for d in range(3)]
    return k0, k1, k2


def brick_forces(grid, tile, fields, rim, rim_psi, rim_dip):
    def own(c, dz):
        return tile.get(fields, (9 + c) if c < 3 else (3 + c), dz)

    def beyond(c, dz):
        return tile.get(rim, (rim_psi + c) if c < 3 else (rim_dip + c - 3), dz)

    def across(get, cx, dz):
        if rim is None:
            return grid.in_row(get(0, dz), cx)
        return grid.at_row(get(0, dz), get(1, dz), cx)

    return field_forces(grid, (own, beyond), across, [own(3 + d, 0) for d in range(3)])


def rim_forces(grid, tile, fields, rims, psi, base):
    outward = grid.outward()

    def loader(ref, psi_at, dip_at):
        def load(c, dz):
            v = tile.get(ref, (psi_at + c) if c < 3 else (dip_at + c - 3), dz)
            return v * outward if c == 3 else v

        return load

    loads = {
        0: loader(rims, psi, base + 6),
        1: loader(rims, base + FAR, base + FAR + 3),
        -1: loader(fields, 9, 6),
    }
    dipole = [loads[0](3 + d, 0) for d in range(3)]
    return field_forces(grid, loads, lambda get, cx, dz: get(cx, dz), dipole)


def collision_adjoint(streamed_of, rho, u, psi, forces):
    inverse_sum = 1.0 / (rho[0] + rho[1] + rho[2])
    grad_u = [None] * 3
    alphas, held = [], []
    for s in range(3):
        streamed = streamed_of(s)
        diff, total = {}, {}
        for c, w in axis_pairs():
            a, b = streamed[INDEX[c]], streamed[INDEX[tuple(-i for i in c)]]
            diff[c], total[c] = a - b, a + b
        m1, m2 = first_and_second(diff, total)
        m0 = W0 * streamed[16]
        for c, w in axis_pairs():
            m0 = m0 + w * total[c]
        inverse = 1.0 / rho[s]
        ratio = psi[s] * inverse
        tau = RELAXATION[s]
        k = forces[s]
        v = [u[d] + (tau * ratio) * k[d] for d in range(3)]
        mv = turned(m2, v)
        g = [3.0 * (m1[d] + 3.0 * mv[d] - m0 * v[d]) for d in range(3)]
        feq = m0 + 3.0 * dot(m1, v) + 4.5 * dot(mv, v) - 1.5 * m0 * dot(v, v)
        alphas.append(feq * (1.0 / tau) + dot(g, k) * (1.0 - psi[s] - ratio))
        scaled = rho[s] * (1.0 / tau)
        for d in range(3):
            grad_u[d] = plus(grad_u[d], scaled * g[d])
            held.append(psi[s] * g[d])
    beta = [grad_u[d] * inverse_sum for d in range(3)]
    along = dot(beta, u)
    return held, [a - along for a in alphas], beta


def brick_collision(grid, tile, load, rim, fields, forces, hold, ab, kept):
    def streamed_of(s):
        streamed = []
        for q in range(19):
            c = VELOCITY[q]
            v = load(s * 19 + q, c[2])
            if c[0] != 0:
                j = (AHEAD if c[0] > 0 else BEHIND).index(q)
                if rim is None:
                    v = grid.in_row(v, c[0])
                else:
                    v = grid.at_row(v, tile.get(rim, s * 5 + j, c[2]), c[0])
            if c[1] != 0:
                v = grid.roll_cols(v, c[1])
            streamed.append(v)
            if s == 2:
                tile.put(kept, q, v)
        return streamed

    rho, u, psi = [[tile.get(fields, at + d) for d in range(3)] for at in (0, 3, 9)]
    held, alpha, beta = collision_adjoint(streamed_of, rho, u, psi, forces)
    for k in range(9):
        tile.put(hold, k, held[k])
    for s in range(3):
        tile.put(ab, s, alpha[s])
        tile.put(ab, 3 + s, beta[s])


def rim_collision(grid, tile, level, after, inner, rho, u, psi, forces, hold, ab, kept):
    outward, low = grid.outward(), grid.low()

    def streamed_of(s):
        streamed = []
        for q in range(19):
            c = VELOCITY[q]
            if c[0] == 0:
                v = level(s, LEVEL.index(q), c[2])
            elif c[0] > 0:
                v = after(s, AHEAD.index(q), c[2])
            else:
                j = BEHIND.index(q)
                v = jnp.where(low, inner(s * 19 + AHEAD[j], c[2]), inner(s * 19 + BEHIND[j], c[2]))
            if c[1] != 0:
                v = grid.roll_cols(v, c[1])
            streamed.append(v)
            if s == 2 and kept is not None and c[0] >= 0:
                tile.put(kept, LEVEL.index(q) if c[0] == 0 else 9 + AHEAD.index(q), v)
        return streamed

    u = [u[0] * outward, u[1], u[2]]
    held, alpha, beta = collision_adjoint(streamed_of, rho, u, psi, forces)
    for k in range(9):
        tile.put(hold, k, held[k] * outward if k % 3 == 0 else held[k])
    if ab is not None:
        for s in range(3):
            tile.put(ab, s, alpha[s])
            tile.put(ab, 3 + s, beta[s] * outward if s == 0 else beta[s])


def spread_plane(grid, get_h, get_d, sign, pairs):
    memo = {}

    def source(dz):
        if dz in memo:
            return memo[dz]
        h = [[get_h(3 * s + d, dz) for d in range(3)] for s in range(3)]
        dip = [get_d(d, dz) for d in range(3)]
        if not isinstance(sign, int):
            for vec in h + [dip]:
                vec[0] = vec[0] * sign
        memo[dz] = (h, dip)
        return memo[dz]

    cx = sign if isinstance(sign, int) else 1
    r = [None] * 3
    w_vec = [None] * 3
    lanes = {}
    for cy, cz in pairs:
        w = W1 if abs(cx) + abs(cy) + abs(cz) == 1 else W2
        h, dip = source(cz)
        c = (cx, cy, cz)
        e = [mixed(c, h[s]) for s in range(3)]
        f = e[2] * mixed(c, dip)
        half = 0.6 * e[2]
        r0 = 1.2 * e[1] - half + f
        r1 = 1.2 * e[0] - half - f
        r2 = -0.6 * (e[0] + e[1]) - 0.3 * e[2]
        qv = e[0] - e[1]
        vals = [w * r0, w * r1, w * r2]
        wq = w * qv
        vals += [wq if cx != 0 else None, wq if cy != 0 else None, wq if cz != 0 else None]
        vals = [vals[0], vals[1], vals[2]] + [
            None if x is None else (x if k == 1 else -x) for x, k in zip(vals[3:], (cx, cy, cz))
        ]
        acc = lanes.setdefault(cy, [None] * 6)
        for i, x in enumerate(vals):
            if x is not None:
                acc[i] = plus(acc[i], x)
    total = [None] * 6
    for cy, acc in lanes.items():
        for i, x in enumerate(acc):
            if x is not None:
                total[i] = plus(total[i], x if cy == 0 else grid.roll_cols(x, cy))
    if not isinstance(sign, int):
        total[3] = total[3] * sign
    return total


def met(total, dipole):
    meet = None
    for d in range(3):
        if total[3 + d] is not None:
            meet = plus(meet, total[3 + d] * dipole[d])
    return [total[0], total[1], total[2] - meet]


def spread_inside(grid, tile, hold, fields):
    get_h = lambda k, dz: tile.get(hold, k, dz)
    get_d = lambda k, dz: tile.get(fields, 6 + k, dz)
    total = spread_plane(grid, get_h, get_d, 0, SIDE)
    for dx in (1, -1):
        part = spread_plane(grid, get_h, get_d, dx, CROSS)
        for i, x in enumerate(part):
            total[i] = plus(total[i], grid.in_row(x, dx))
    return met(total, [tile.get(fields, 6 + d) for d in range(3)])


def rim_sign(grid):
    return jnp.where(
        grid.sub == 0, -1.0, jnp.where(grid.sub == grid.rows - 1, 1.0, 0.0)
    ).astype(F32)


def hand_over(grid, tile, hold, hold_dip, target, sign):
    dip, at = hold_dip
    total = spread_plane(
        grid,
        lambda k, dz: tile.get(hold, k, dz),
        lambda k, dz: tile.get(dip, at + k, dz),
        sign,
        CROSS,
    )
    return met(total, target)


def spread_level(grid, tile, hold, dip, at):
    total = spread_plane(
        grid,
        lambda k, dz: tile.get(hold, k, dz),
        lambda k, dz: tile.get(dip, at + k, dz),
        0,
        SIDE,
    )
    return met(total, [tile.get(dip, at + d) for d in range(3)])


def parity_of(axis):
    return lax.rem(lax.axis_index(axis) + 1, 2)


def lines_from(first, second, parity, lines):
    lines[1 - parity] = first[...]
    lines[parity] = second[...]


def lines_to(first, second, lines):
    first[...] = lines[0]
    second[...] = lines[1]


def psi_of(rho):
    return 1.0 - jnp.exp(-rho)


def pack_static(get, tiles, rows, lines, parity):
    up, down = parity, 1 - parity
    fill = 0

    def put(kind, above, below, depth):
        nonlocal fill
        for t in tiles:
            v = get(kind, above, t)
            lines[up, fill : fill + 1, :] = v[rows - 1 - depth : rows - depth, :]
            v = get(kind, below, t)
            lines[down, fill : fill + 1, :] = v[depth : depth + 1, :]
            fill += 1

    for s in range(3):
        for j in range(5):
            put(0, s * 19 + BEHIND[j], s * 19 + AHEAD[j], 0)
    for s in range(3):
        for q in LEVEL:
            put(0, s * 19 + q, s * 19 + q, 0)
    for s in range(3):
        for j in range(5):
            put(0, s * 19 + BEHIND[j], s * 19 + AHEAD[j], 1)
    for kind in (1, 2):
        for c in range(9):
            put(kind, c, c, 0)
        for c in (9, 10, 11, 6, 7, 8):
            put(kind, c, c, 1)
    return fill


def pack_columns_kernel(
    adj_in, late_in, early_in, dip_late_in, dip_early_in,
    send_c, send_d, own_left, own_right, fl, fe, adj,
    late, early, dip_late, dip_early, sems,
):
    planes, rows, cols = adj.shape[1:]
    grid = Grid(planes, rows, cols)
    copies = [
        pltpu.make_async_copy(a, b, sems.at[i])
        for i, (a, b) in enumerate(
            (
                (dip_late_in, dip_late),
                (late_in, late),
                (dip_early_in, dip_early),
                (early_in, early),
            )
        )
    ]
    per_chunk = -(-adj.shape[0] // (CHUNKS * grid.pack)) * grid.pack
    for i in range(CHUNKS):
        part = pl.ds(i * per_chunk, min(per_chunk, adj.shape[0] - i * per_chunk))
        copies.append(pltpu.make_async_copy(adj_in.at[part], adj.at[part], sems.at[4 + i]))
    for copy in copies:
        copy.start()
    for which, (saved, dip, out) in enumerate(((late, dip_late, fl), (early, dip_early, fe))):
        copies[2 * which].wait()
        copies[2 * which + 1].wait()

        for p in range(planes):
            flows = [None] * 19
            rho = []
            for s in range(3):
                total = None
                for q in range(19):
                    v = saved[s * 19 + q, p].astype(F32)
                    flows[q] = plus(flows[q], v)
                    total = plus(total, v)
                rho.append(total)
                out[s, p] = total
                out[9 + s, p] = psi_of(total)
            inverse = 1.0 / (rho[0] + rho[1] + rho[2])
            for d in range(3):
                momentum = None
                for q in range(19):
                    if VELOCITY[q][d] != 0:
                        momentum = plus(momentum, flows[q] if VELOCITY[q][d] > 0 else -flows[q])
                out[3 + d, p] = momentum * inverse
                out[6 + d, p] = dip[d, p].astype(F32)
    pops = adj.shape[0]
    components = pops + 18
    slot = grid.lane // grid.group
    for g in range(own_left.shape[0]):
        if g * grid.pack % per_chunk == 0 and g * grid.pack < pops:
            copies[4 + g * grid.pack // per_chunk].wait()
        left = right = jnp.zeros((rows, cols), F32)
        for j in range(grid.pack):
            c = g * grid.pack + j
            if c >= components:
                continue
            for p in range(planes):
                if c < pops:
                    v = adj[c, p]
                elif c < pops + 9:
                    v = fl[c - pops, p]
                else:
                    v = fe[c - pops - 9, p]
                at = p * grid.pack + j
                rolled = pltpu.roll(v, at * grid.group, 1) if at else v
                left = jnp.where(slot == at, rolled, left)
                right = jnp.where(slot == (at - 1) % (cols // grid.group), rolled, right)
        own_left[g] = left
        own_right[g] = right
    low = lax.rem(grid.lane, grid.group) < HALO
    even = parity_of("gy") == 0
    for h in range(send_c.shape[0]):
        left = jnp.where(low, own_left[2 * h], pltpu.roll(own_left[2 * h + 1], HALO, 1))
        right = jnp.where(low, pltpu.roll(own_right[2 * h + 1], cols - HALO, 1), own_right[2 * h])
        send_c[h] = jnp.where(even, right, left)
        send_d[h] = jnp.where(even, left, right)


def inside_collision(grid, tile, load, fields, hold, ab, kept):
    forces = brick_forces(grid, tile, fields, None, 0, 0)
    brick_collision(grid, tile, load, None, fields, forces, hold, ab, kept)
    at_rim = grid.at_rim()
    for k in range(9):
        tile.put(hold, k, jnp.where(at_rim, 0.0, tile.get(hold, k)))


def second_row(grid, tile, fields, hold, ab, kept, sides):
    low = grid.low()
    rest = 1.0 - 1.0 / RELAXATION[2]
    back = spread_inside(grid, tile, hold, fields)
    alpha = [tile.get(ab, s) + (1.0 - tile.get(fields, 9 + s)) * back[s] for s in range(3)]
    beta = [tile.get(ab, 3 + d) for d in range(3)]
    ahead = -grid.outward() * beta[0]
    for s in range(3):
        tile.put(sides, s, back[s])
    for s in range(2):
        tile.put(sides, 3 + s, alpha[s] + ahead)
        tile.put(sides, 5 + s, beta[1 + s])
    for j, yz in enumerate(CROSS):
        v = rest * jnp.where(low, tile.get(kept, AHEAD[j]), tile.get(kept, BEHIND[j]))
        v = v + (alpha[2] + ahead)
        tile.put(sides, 7 + j, v + mixed(yz, beta[1:]) if j else v)


def static_kernel(adj, fl, fe, send_a, send_b, lines):
    planes, rows, cols = adj.shape[1:]
    kinds = (adj, fl, fe)
    pack_static(lambda kind, c, t: kinds[kind][c, t], range(planes), rows, lines, parity_of("gx"))
    lines_to(send_a, send_b, lines)


def inside_kernel(adj, fl, sides, hold, ab, kept):
    planes, rows, cols = adj.shape[1:]
    grid = Grid(planes, rows, cols)
    load = lambda tile: lambda c, dz: tile.get(adj, c, dz)
    grid.over_main(lambda tile: inside_collision(grid, tile, load(tile), fl, hold, ab, kept))
    grid.over_main(lambda tile: second_row(grid, tile, fl, hold, ab, kept, sides))


def edge_kernel(
    own_left, own_right, recv_c, recv_d, sides_main,
    send_a, send_b, edge, fl, fe, lines, hold, ab, kept, sides,
):
    planes, rows, cols = sides_main.shape[1:]
    pops = edge.shape[0]
    grid = Grid(planes, rows, cols)
    even = parity_of("gy") == 0
    slot = lax.rem(grid.lane // grid.group, grid.pack)
    left_half = lax.rem(grid.lane, grid.width) < grid.width // 2
    components = pops + 18
    for g in range(own_left.shape[0]):
        first, second = recv_c[g // 2], recv_d[g // 2]
        from_next = jnp.where(even, first, second)
        from_prior = jnp.where(even, second, first)
        if g % 2:
            from_next = pltpu.roll(from_next, cols - HALO, 1)
            from_prior = pltpu.roll(from_prior, HALO, 1)
        for j in range(grid.pack):
            c = g * grid.pack + j
            if c >= components:
                continue
            before = slot == (j - 1) % grid.pack
            low = jnp.where(before, from_prior, own_left[g])
            high = jnp.where(before, own_right[g], from_next)
            v = jnp.where(
                left_half,
                pltpu.roll(low, ((1 - j) * grid.group) % cols, 1),
                pltpu.roll(high, ((3 - j) * grid.group) % cols, 1),
            )
            if c < pops:
                edge[c] = v
            else:
                field, k = (fl, c - pops) if c < pops + 9 else (fe, c - pops - 9)
                field[k] = v
                if k < 3:
                    field[9 + k] = psi_of(v)
    adj, fields, both = Pair(None, edge), Pair(None, fl), Pair(sides_main, sides)
    hold, ab, kept = Pair(None, hold), Pair(None, ab), Pair(None, kept)

    def inside(tile):
        load = lambda c, dz: tile.get(adj, c, dz)
        inside_collision(grid, tile, load, fields, hold, ab, kept)
        second_row(grid, tile, fields, hold, ab, kept, both)

    grid.over_edge(inside)
    parity = parity_of("gx")
    kinds = (edge, fl, fe)
    fill = pack_static(lambda kind, c, t: kinds[kind][c], (0,), rows, lines, parity)
    for c in range(DYNAMIC):
        depth = 0 if c < 3 else 1
        for t in range(grid.tiles):
            v = both.at(c, t)
            lines[parity, fill : fill + 1, :] = v[rows - 1 - depth : rows - depth, :]
            lines[1 - parity, fill : fill + 1, :] = v[depth : depth + 1, :]
            fill += 1
    lines_to(send_a, send_b, lines)


def first_step(grid, tile, adj, fl, rims, hold, ab, kept, hold_rim, ab_rim, kept_rim):
    forces = brick_forces(grid, tile, fl, rims, LATE_PSI, LATE + 6)
    load = lambda c, dz: tile.get(adj, c, dz)
    brick_collision(grid, tile, load, rims, fl, forces, hold, ab, kept)
    forces = rim_forces(grid, tile, fl, rims, LATE_PSI, LATE)
    rho, u = [[tile.get(rims, LATE + at + d) for d in range(3)] for at in (0, 3)]
    psi = [tile.get(rims, LATE_PSI + s) for s in range(3)]
    rim_collision(
        grid,
        tile,
        lambda s, i, dz: tile.get(rims, ALONG + s * 9 + i, dz),
        lambda s, j, dz: tile.get(rims, AFTER + s * 5 + j, dz),
        load,
        rho,
        u,
        psi,
        forces,
        hold_rim,
        ab_rim,
        kept_rim,
    )


def early_forces(grid, tile, fe, rims, forces, forces_rim):
    brick = brick_forces(grid, tile, fe, rims, EARLY_PSI, EARLY + 6)
    beyond = rim_forces(grid, tile, fe, rims, EARLY_PSI, EARLY)
    for s in range(3):
        for d in range(3):
            tile.put(forces, 3 * s + d, brick[s][d])
            tile.put(forces_rim, 3 * s + d, beyond[s][d])


def rim_psis(grid, tile, rims):
    for s in range(3):
        tile.put(rims, LATE_PSI + s, psi_of(tile.get(rims, LATE + s)))
        tile.put(rims, EARLY_PSI + s, psi_of(tile.get(rims, EARLY + s)))


def finish_first(grid, tile, fl, rims, hold, ab, kept, hold_rim, ab_rim, mid, part):
    rest = 1.0 - 1.0 / RELAXATION[2]
    sign, at_rim = rim_sign(grid), grid.at_rim()
    own_dip, rim_dip = (fl, 6), (rims, LATE + 6)
    dip = [tile.get(fl, 6 + d) for d in range(3)]
    dip_rim = [tile.get(rims, LATE + 6 + d) for d in range(3)]
    dip_far = [tile.get(rims, LATE + FAR + 3 + d) for d in range(3)]
    back = spread_inside(grid, tile, hold, fl)
    inward = hand_over(grid, tile, hold_rim, rim_dip, dip, sign)
    alpha = [
        tile.get(ab, s)
        + (1.0 - tile.get(fl, 9 + s)) * (back[s] + jnp.where(at_rim, inward[s], 0.0))
        for s in range(3)
    ]
    beta = [tile.get(ab, 3 + d) for d in range(3)]
    for q in range(19):
        along = mixed(VELOCITY[q], beta) if q != 16 else None
        for s in range(3):
            v = alpha[s] if along is None else alpha[s] + along
            if s == 2:
                v = v + rest * tile.get(kept, q)
            tile.put(mid, s * 19 + q, v)
    given = hand_over(grid, tile, hold, own_dip, dip_rim, -sign)
    level = spread_level(grid, tile, hold_rim, *rim_dip)
    after = hand_over(grid, tile, hold_rim, rim_dip, dip_far, -sign)
    for s in range(3):
        open_share = 1.0 - tile.get(rims, LATE_PSI + s)
        tile.put(part, s, tile.get(ab_rim, s) + open_share * (given[s] + level[s]))
        tile.put(part, 3 + s, tile.get(ab_rim, 3 + s))
        tile.put(part, 6 + s, (1.0 - tile.get(rims, LATE + FAR + s)) * after[s])


def main_kernel(
    adj, fl, fe, recv_a, recv_b, after,
    rims, mid, part, kept_rim, forces, forces_rim, lines, hold, ab, kept, hold_rim, ab_rim,
):
    planes, rows, cols = adj.shape[1:]
    grid = Grid(planes, rows, cols)
    lines_from(recv_a, recv_b, parity_of("gx"), lines)
    for c in range(STATIC):
        for p in range(planes):
            k = c * planes + p
            rims[c, p] = grid.sides(lines[0, k : k + 1, :], lines[1, k : k + 1, :])
    grid.over_main(lambda tile: rim_psis(grid, tile, rims))

    def step(tile):
        first_step(grid, tile, adj, fl, rims, hold, ab, kept, hold_rim, ab_rim, kept_rim)
        early_forces(grid, tile, fe, rims, forces, forces_rim)

    grid.over_main(step)
    grid.over_main(
        lambda tile: finish_first(
            grid, tile, fl, rims, hold, ab, kept, hold_rim, ab_rim, mid, part
        )
    )


def last_kernel(
    fe_m, rims_m, mid_m, part_m, kept_rim_m, forces_m, forces_rim_m, edge, fl_e, fe_e,
    recv_a, recv_b, out,
    rims_e, mid_e, part_e, kept_rim_e, forces_e, forces_rim_e, hold_e, ab_e, kept_e, hold_rim_e,
    ab_rim_e, patches, lines, near, rim_mid, rim_level, rim_far, hold2, hold_rim2, ab2, kept2,
    total, staged, sems,
):
    planes, rows, cols = fe_m.shape[1:]
    grid = Grid(planes, rows, cols)
    lines_from(recv_a, recv_b, parity_of("gx"), lines)
    for c in range(STATIC):
        rims_e[c] = grid.sides(lines[0, c : c + 1, :], lines[1, c : c + 1, :])
    for c in range(DYNAMIC):
        for t in range(grid.tiles):
            k = STATIC + c * grid.tiles + t
            near[c, t] = grid.sides(lines[0, k : k + 1, :], lines[1, k : k + 1, :])
    fe, rims, mid = Pair(fe_m, fe_e), Pair(rims_m, rims_e), Pair(mid_m, mid_e)
    part, kept_rim = Pair(part_m, part_e), Pair(kept_rim_m, kept_rim_e)
    forces, forces_rim = Pair(forces_m, forces_e), Pair(forces_rim_m, forces_rim_e)
    rest = 1.0 - 1.0 / RELAXATION[2]
    at_rim = grid.at_rim()
    sign = rim_sign(grid)
    outward = grid.outward()

    def edge_steps(tile):
        adj, fl = Pair(None, edge), Pair(None, fl_e)
        hold, ab, kept = Pair(None, hold_e), Pair(None, ab_e), Pair(None, kept_e)
        hold_rim, ab_rim = Pair(None, hold_rim_e), Pair(None, ab_rim_e)
        rim_psis(grid, tile, rims)
        first_step(grid, tile, adj, fl, rims, hold, ab, kept, hold_rim, ab_rim, kept_rim)
        early_forces(grid, tile, fe, rims, forces, forces_rim)
        finish_first(grid, tile, fl, rims, hold, ab, kept, hold_rim, ab_rim, mid, part)

    grid.over_edge(edge_steps)

    def complete(tile):
        t = tile.index
        alpha = [
            tile.get(part, s) + (1.0 - tile.get(rims, LATE_PSI + s)) * near[s, t]
            for s in range(3)
        ]
        beta = [tile.get(part, 3 + d) for d in range(3)]
        far = [near[3 + s, t] + tile.get(part, 6 + s) for s in range(2)]
        far_beta = [near[5 + d, t] for d in range(2)]
        ahead = outward * beta[0]
        for j, yz in enumerate(CROSS):
            side = mixed(yz, beta[1:]) if j else None
            side_far = mixed(yz, far_beta) if j else None
            for s in range(3):
                v = plus(side, alpha[s] + ahead)
                if s == 2:
                    v = v + rest * tile.get(kept_rim, 9 + j)
                    rim_far[10 + j, t] = near[7 + j, t] + tile.get(part, 8)
                else:
                    rim_far[s * 5 + j, t] = plus(side_far, far[s])
                rim_mid[s * 5 + j, t] = v
        for i, q in enumerate(LEVEL):
            side = mixed(VELOCITY[q][1:], beta[1:]) if q != 16 else None
            for s in range(3):
                v = plus(side, alpha[s])
                if s == 2:
                    v = v + rest * tile.get(kept_rim, i)
                rim_level[s * 9 + i, t] = v

    grid.over(complete)

    def collide(tile):
        load = lambda c, dz: tile.get(mid, c, dz)
        known = [[tile.get(forces, 3 * s + d) for d in range(3)] for s in range(3)]
        brick_collision(grid, tile, load, rim_mid, fe, known, hold2, ab2, kept2)
        known = [[tile.get(forces_rim, 3 * s + d) for d in range(3)] for s in range(3)]
        rho, u = [[tile.get(rims, EARLY + at + d) for d in range(3)] for at in (0, 3)]
        psi = [tile.get(rims, EARLY_PSI + s) for s in range(3)]
        rim_collision(
            grid,
            tile,
            lambda s, i, dz: tile.get(rim_level, s * 9 + i, dz),
            lambda s, j, dz: tile.get(rim_far, s * 5 + j, dz),
            load,
            rho,
            u,
            psi,
            known,
            hold_rim2,
            None,
            None,
        )

    grid.over(collide)

    def finish(tile):
        back = spread_inside(grid, tile, hold2, fe)
        dip = [tile.get(fe, 6 + d) for d in range(3)]
        inward = hand_over(grid, tile, hold_rim2, (rims, EARLY + 6), dip, sign)
        for s in range(3):
            x = back[s] + jnp.where(at_rim, inward[s], 0.0)
            total[s, tile.index] = tile.get(ab2, s) + (1.0 - tile.get(fe, 9 + s)) * x

    grid.over(finish)
    at_side = (grid.lane < HALO) | (grid.lane >= cols - HALO)
    first_group = lax.rem(grid.lane, grid.width) < grid.group
    sources = [total.at[s] for s in range(3)] + [ab2.at[3 + d] for d in range(3)]
    sources += [kept2.at[q] for q in range(19)]
    for i, ref in enumerate(sources):
        v = ref[planes]
        patches[i] = jnp.where(first_group, pltpu.roll(v, cols - 2 * grid.group, 1), v)
    copies = []
    for p in range(planes):
        turn = (cols - p * grid.width - grid.group) % cols

        def patched(i):
            return jnp.where(at_side, pltpu.roll(patches[i], turn, 1), sources[i][p])

        alpha = [patched(s) for s in range(3)]
        beta = [patched(3 + d) for d in range(3)]
        for q in range(19):
            along = mixed(VELOCITY[q], beta) if q != 16 else None
            for s in range(3):
                v = alpha[s] if along is None else alpha[s] + along
                if s == 2:
                    v = v + rest * patched(6 + q)
                staged[s * 19 + q, p] = v
        copies.append(pltpu.make_async_copy(staged.at[:, p], out.at[:, p], sems.at[p]))
        copies[p].start()
    for copy in copies:
        copy.wait()


def call(kernel, outs, scratch, args, in_hbm=False, out_hbm=False, cost=0):
    vmem = pl.BlockSpec(memory_space=pltpu.VMEM)
    hbm = pl.BlockSpec(memory_space=pltpu.HBM)
    return pl.pallas_call(
        kernel,
        out_shape=[jax.ShapeDtypeStruct(s, F32) for s in outs],
        in_specs=[hbm if in_hbm else vmem] * len(args),
        out_specs=[hbm if out_hbm else vmem] * len(outs),
        scratch_shapes=[pltpu.VMEM(s, F32) if isinstance(s, tuple) else s for s in scratch],
        compiler_params=pltpu.CompilerParams(vmem_limit_bytes=VMEM_BYTES),
        cost_estimate=pl.CostEstimate(flops=cost, bytes_accessed=cost, transcendentals=0),
    )(*[pltpu.with_memory_space_constraint(x, pltpu.HBM) if in_hbm else x for x in args])


def swap(block, axis, offset):
    size = lax.axis_size(axis)
    route = []
    for i in range(offset, size + offset, 2):
        a, b = i % size, (i + 1) % size
        route += [(a, b), (b, a)]
    return lax.ppermute(block, axis, route)


def shards(adjoint_in, populations_early, populations_late, dipoles_early, dipoles_late):
    pops, planes, rows, cols = adjoint_in.shape
    tile = (rows, cols)
    pack = cols // planes // (2 * HALO)
    groups = -(-(pops + 18) // pack)
    groups += groups % 2

    def lines(n):
        return (-(-n // 8) * 8, cols)

    def main(*counts):
        return [(n, planes) + tile for n in counts]

    def edges(*counts):
        return [(n,) + tile for n in counts]

    def tiled(*counts):
        return [(n, planes + 1) + tile for n in counts]

    static = lines(STATIC * planes)
    second = lines(STATIC + DYNAMIC * (planes + 1))
    send_c, send_d, own_left, own_right, fl_m, fe_m, adj = call(
        pack_columns_kernel,
        edges(groups // 2, groups // 2, groups, groups) + main(12, 12, pops),
        [
            pltpu.VMEM(x.shape, x.dtype)
            for x in (populations_late, populations_early, dipoles_late, dipoles_early)
        ]
        + [pltpu.SemaphoreType.DMA((4 + CHUNKS,))],
        [adjoint_in, populations_late, populations_early, dipoles_late, dipoles_early],
        in_hbm=True,
    )
    recv_c, recv_d = swap(send_c, "gy", 1), swap(send_d, "gy", 0)
    send_a, send_b = call(
        static_kernel, [static] * 2, [(2,) + static], [adj, fl_m, fe_m]
    )
    (sides,) = call(
        inside_kernel, main(DYNAMIC), main(9, 6, 19), [adj, fl_m], cost=INSIDE_COST
    )
    static_a, static_b = swap(send_a, "gx", 1), swap(send_b, "gx", 0)
    send_a, send_b, edge, fl_e, fe_e = call(
        edge_kernel,
        [second] * 2 + edges(pops, 12, 12),
        [(2,) + second] + edges(9, 6, 19, DYNAMIC),
        [own_left, own_right, recv_c, recv_d, sides],
        cost=EDGE_COST,
    )
    recv_a, recv_b = swap(send_a, "gx", 1), swap(send_b, "gx", 0)
    known = (RIMS, pops, 9, 14, 9, 9)
    mains = call(
        main_kernel,
        main(*known),
        [(2,) + static] + main(9, 6, 19, 9, 6),
        [adj, fl_m, fe_m, static_a, static_b, fl_e],
        cost=MAIN_COST,
    )
    (out,) = call(
        last_kernel,
        [(pops, planes) + tile],
        edges(*known, 9, 6, 19, 9, 6, 25)
        + [(2,) + second]
        + tiled(DYNAMIC, 15, 27, 15, 9, 9, 6, 19, 3)
        + main(pops)
        + [pltpu.SemaphoreType.DMA((planes,))],
        [fe_m, *mains, edge, fl_e, fe_e, recv_a, recv_b],
        out_hbm=True,
    )
    return out


def solution(mesh):
    placed = P(None, None, "gx", "gy")
    return jax.shard_map(
        shards, mesh=mesh, in_specs=(placed,) * 5, out_specs=placed, check_vma=False
    )
```

```python
import jax
import jax.numpy as jnp
from jax import lax
from jax.experimental import pallas as pl
from jax.experimental.pallas import tpu as pltpu
from jax.sharding import PartitionSpec as P

VELOCITY = (
    (1, 0, 0),
    (-1, 0, 0),
    (0, 1, 0),
    (0, -1, 0),
    (1, 1, 0),
    (-1, -1, 0),
    (1, -1, 0),
    (-1, 1, 0),
    (1, 0, 1),
    (-1, 0, -1),
    (1, 0, -1),
    (-1, 0, 1),
    (0, 1, 1),
    (0, -1, -1),
    (0, 1, -1),
    (0, -1, 1),
    (0, 0, 0),
    (0, 0, 1),
    (0, 0, -1),
)
INDEX = {c: q for q, c in enumerate(VELOCITY)}
W1, W2, W0 = 1.0 / 18.0, 1.0 / 36.0, 1.0 / 3.0
RELAXATION = (1.0, 1.0, 1.25)
COUPLING = ((0.0, 1.2, -0.6), (1.2, 0.0, -0.6), (-0.6, -0.6, -0.3))
CROSS = ((0, 0), (1, 0), (-1, 0), (0, 1), (0, -1))
AHEAD = tuple(INDEX[(1,) + yz] for yz in CROSS)
BEHIND = tuple(INDEX[(-1,) + yz] for yz in CROSS)
SIDE = ((1, 0), (-1, 0), (0, 1), (0, -1), (1, 1), (-1, -1), (1, -1), (-1, 1))
LEVEL = tuple(q for q in range(19) if VELOCITY[q][0] == 0)
ALONG, AFTER, LATE, EARLY = 15, 42, 57, 72
STATIC = 87
FAR = 9
LATE_PSI, EARLY_PSI = STATIC, STATIC + 3
RIMS = STATIC + 6
DYNAMIC = 12
F32 = jnp.float32
CHUNKS = 4
INSIDE_COST, EDGE_COST, MAIN_COST = 10**7, 10**8, 10**8
VMEM_BYTES = 40 * 1024 * 1024
HALO = 4


class Grid:
    def __init__(self, planes, rows, cols):
        self.planes, self.rows, self.cols = planes, rows, cols
        self.tiles = planes + 1
        self.width = cols // planes
        self.group = 2 * HALO
        self.pack = self.width // self.group
        self.sub = lax.broadcasted_iota(jnp.int32, (rows, cols), 0)
        self.lane = lax.broadcasted_iota(jnp.int32, (rows, cols), 1)

    def roll_rows(self, v, dx):
        return pltpu.roll(v, (-dx) % self.rows, 0)

    def roll_cols(self, v, dy):
        return pltpu.roll(v, (-dy) % self.cols, 1)

    def at_row(self, v, rim, dx):
        edge = self.rows - 1 if dx > 0 else 0
        return jnp.where(self.sub == edge, rim, self.roll_rows(v, dx))

    def in_row(self, v, dx):
        edge = self.rows - 1 if dx > 0 else 0
        return jnp.where(self.sub == edge, 0.0, self.roll_rows(v, dx))

    def sides(self, low, high):
        return jnp.where(self.sub == 0, low, high)

    def over_main(self, body):
        for p in range(self.planes):
            body(Tile(self, p, False))

    def over_edge(self, body):
        body(Tile(self, self.planes, True))

    def over(self, body):
        self.over_main(body)
        self.over_edge(body)

    def at_rim(self):
        return (self.sub == 0) | (self.sub == self.rows - 1)

    def low(self):
        return self.sub < self.rows // 2

    def corners(self, j):
        at = lax.rem(self.lane + (self.cols - j * self.group), self.width)
        high = 3 * self.group
        return ((at >= HALO) & (at < 2 * HALO)) | ((at >= high) & (at < high + HALO))

    def turn(self, v, lanes):
        return pltpu.roll(v, lanes % self.cols, 1) if lanes % self.cols else v

    def outward(self):
        return jnp.where(self.low(), -1.0, 1.0).astype(F32)


class Tile:
    def __init__(self, grid, index, edge):
        self.grid, self.index, self.edge = grid, index, edge

    def of(self, dz):
        if dz == 0 or self.edge:
            return self.index
        return (self.index + dz) % self.grid.planes

    def get(self, ref, c, dz=0):
        if isinstance(ref, Pair):
            v = ref.edge[c] if self.edge else ref.main[c, self.of(dz)]
        else:
            v = ref[c, self.of(dz)]
        if self.edge and dz != 0:
            v = self.grid.roll_cols(v, dz * self.grid.width)
        return v

    def put(self, ref, c, v):
        if not isinstance(ref, Pair):
            ref[c, self.index] = v
        elif self.edge:
            ref.edge[c] = v
        else:
            ref.main[c, self.index] = v


class Pair:
    def __init__(self, main, edge):
        self.main, self.edge = main, edge

    def at(self, c, t):
        return self.edge[c] if t == self.main.shape[1] else self.main[c, t]


def plus(a, b):
    return b if a is None else a + b


def mixed(coefficients, values):
    total = None
    for k, v in zip(coefficients, values):
        if k == 0:
            continue
        term = v if k == 1 else (-v if k == -1 else k * v)
        total = plus(total, term)
    return total


def axis_pairs():
    for q in (0, 2, 17, 4, 6, 8, 10, 12, 14):
        c = VELOCITY[q]
        yield c, (W1 if sum(abs(i) for i in c) == 1 else W2)


def first_and_second(diff, total):
    first = [None] * 3
    second = {}
    for c, w in axis_pairs():
        for d in range(3):
            if c[d] == 0:
                continue
            if diff is not None:
                first[d] = plus(first[d], (w * c[d]) * diff[c])
            if total is not None:
                for e in range(d, 3):
                    if c[e] != 0:
                        second[d, e] = plus(second.get((d, e)), (w * c[d] * c[e]) * total[c])
    return first, second


def turned(second, v):
    return [sum(second[min(d, e), max(d, e)] * v[e] for e in range(3)) for d in range(3)]


def dot(a, b):
    return a[0] * b[0] + a[1] * b[1] + a[2] * b[2]


def field_forces(grid, loads, across, dipole):
    memo = {}

    def source(name, dz, place):
        key = (name, dz, place)
        if key in memo:
            return memo[key]
        if isinstance(name, int):
            v = loads[place](name, dz)
        elif name == "chi":
            v = source(0, dz, place) - source(1, dz, place)
        elif name[0] == "V":
            v = source(2, dz, place) * source(3 + name[1], dz, place)
        else:
            c = name[1]
            v = mixed(c, [source(("V", d), dz, place) if c[d] else None for d in range(3)])
        memo[key] = v
        return v

    def shifted(name, c):
        key = (name, c, "shift")
        if key in memo:
            return memo[key]
        if c[1] != 0:
            v = grid.roll_cols(shifted(name, (c[0], 0, c[2])), c[1])
        elif c[0] != 0:
            v = across(lambda place, dz: source(name, dz, place), c[0], c[2])
        else:
            v = source(name, c[2], 0)
        memo[key] = v
        return v

    def parts(name):
        diff, total = {}, {}
        for c, w in axis_pairs():
            back = tuple(-i for i in c)
            a, b = shifted(name, c), shifted(name, back)
            diff[c], total[c] = a - b, a + b
        return diff, total

    diff, unused = parts(0)
    s0, unused = first_and_second(diff, None)
    diff, unused = parts(2)
    s2, unused = first_and_second(diff, None)
    diff, total = parts("chi")
    schi, second = first_and_second(diff, total)
    s1 = [a - b for a, b in zip(s0, schi)]
    pull = [None] * 3
    for c, w in axis_pairs():
        back = tuple(-i for i in c)
        if sum(abs(i) for i in c) == 1:
            name = ("V", [i for i in range(3) if c[i]][0])
        else:
            name = ("L", c)
        total_c = shifted(name, c) + shifted(name, back)
        for d in range(3):
            if c[d] != 0:
                pull[d] = plus(pull[d], (w * c[d]) * total_c)
    md = turned(second, dipole)
    k0 = [-1.2 * s1[d] + 0.6 * s2[d] - pull[d] for d in range(3)]
    k1 = [-1.2 * s0[d] + 0.6 * s2[d] + pull[d] for d in range(3)]
    k2 = [0.6 * (s0[d] + s1[d]) + 0.3 * s2[d] + md[d] for d in range(3)]
    return k0, k1, k2


def brick_forces(grid, tile, fields, rim, rim_psi, rim_dip):
    def own(c, dz):
        return tile.get(fields, (9 + c) if c < 3 else (3 + c), dz)

    def beyond(c, dz):
        return tile.get(rim, (rim_psi + c) if c < 3 else (rim_dip + c - 3), dz)

    def across(get, cx, dz):
        if rim is None:
            return grid.in_row(get(0, dz), cx)
        return grid.at_row(get(0, dz), get(1, dz), cx)

    return field_forces(grid, (own, beyond), across, [own(3 + d, 0) for d in range(3)])


def rim_forces(grid, tile, fields, rims, psi, base):
    outward = grid.outward()

    def loader(ref, psi_at, dip_at):
        def load(c, dz):
            v = tile.get(ref, (psi_at + c) if c < 3 else (dip_at + c - 3), dz)
            return v * outward if c == 3 else v

        return load

    loads = {
        0: loader(rims, psi, base + 6),
        1: loader(rims, base + FAR, base + FAR + 3),
        -1: loader(fields, 9, 6),
    }
    dipole = [loads[0](3 + d, 0) for d in range(3)]
    return field_forces(grid, loads, lambda get, cx, dz: get(cx, dz), dipole)


def collision_adjoint(streamed_of, rho, u, psi, forces):
    inverse_sum = 1.0 / (rho[0] + rho[1] + rho[2])
    grad_u = [None] * 3
    alphas, held = [], []
    for s in range(3):
        streamed = streamed_of(s)
        diff, total = {}, {}
        for c, w in axis_pairs():
            a, b = streamed[INDEX[c]], streamed[INDEX[tuple(-i for i in c)]]
            diff[c], total[c] = a - b, a + b
        m1, m2 = first_and_second(diff, total)
        m0 = W0 * streamed[16]
        for c, w in axis_pairs():
            m0 = m0 + w * total[c]
        inverse = 1.0 / rho[s]
        ratio = psi[s] * inverse
        tau = RELAXATION[s]
        k = forces[s]
        v = [u[d] + (tau * ratio) * k[d] for d in range(3)]
        mv = turned(m2, v)
        g = [3.0 * (m1[d] + 3.0 * mv[d] - m0 * v[d]) for d in range(3)]
        feq = m0 + 3.0 * dot(m1, v) + 4.5 * dot(mv, v) - 1.5 * m0 * dot(v, v)
        alphas.append(feq * (1.0 / tau) + dot(g, k) * (1.0 - psi[s] - ratio))
        scaled = rho[s] * (1.0 / tau)
        for d in range(3):
            grad_u[d] = plus(grad_u[d], scaled * g[d])
            held.append(psi[s] * g[d])
    beta = [grad_u[d] * inverse_sum for d in range(3)]
    along = dot(beta, u)
    return held, [a - along for a in alphas], beta


def brick_collision(grid, tile, load, rim, fields, forces, hold, ab, kept):
    def streamed_of(s):
        streamed = []
        for q in range(19):
            c = VELOCITY[q]
            v = load(s * 19 + q, c[2])
            if c[0] != 0:
                j = (AHEAD if c[0] > 0 else BEHIND).index(q)
                if rim is None:
                    v = grid.in_row(v, c[0])
                else:
                    v = grid.at_row(v, tile.get(rim, s * 5 + j, c[2]), c[0])
            if c[1] != 0:
                v = grid.roll_cols(v, c[1])
            streamed.append(v)
            if s == 2:
                tile.put(kept, q, v)
        return streamed

    rho, u, psi = [[tile.get(fields, at + d) for d in range(3)] for at in (0, 3, 9)]
    held, alpha, beta = collision_adjoint(streamed_of, rho, u, psi, forces)
    for k in range(9):
        tile.put(hold, k, held[k])
    for s in range(3):
        tile.put(ab, s, alpha[s])
        tile.put(ab, 3 + s, beta[s])


def rim_collision(grid, tile, level, after, inner, rho, u, psi, forces, hold, ab, kept):
    outward, low = grid.outward(), grid.low()

    def streamed_of(s):
        streamed = []
        for q in range(19):
            c = VELOCITY[q]
            if c[0] == 0:
                v = level(s, LEVEL.index(q), c[2])
            elif c[0] > 0:
                v = after(s, AHEAD.index(q), c[2])
            else:
                j = BEHIND.index(q)
                v = jnp.where(low, inner(s * 19 + AHEAD[j], c[2]), inner(s * 19 + BEHIND[j], c[2]))
            if c[1] != 0:
                v = grid.roll_cols(v, c[1])
            streamed.append(v)
            if s == 2 and kept is not None and c[0] >= 0:
                tile.put(kept, LEVEL.index(q) if c[0] == 0 else 9 + AHEAD.index(q), v)
        return streamed

    u = [u[0] * outward, u[1], u[2]]
    held, alpha, beta = collision_adjoint(streamed_of, rho, u, psi, forces)
    for k in range(9):
        tile.put(hold, k, held[k] * outward if k % 3 == 0 else held[k])
    if ab is not None:
        for s in range(3):
            tile.put(ab, s, alpha[s])
            tile.put(ab, 3 + s, beta[s] * outward if s == 0 else beta[s])


def spread_plane(grid, get_h, get_d, sign, pairs):
    memo = {}

    def source(dz):
        if dz in memo:
            return memo[dz]
        h = [[get_h(3 * s + d, dz) for d in range(3)] for s in range(3)]
        dip = [get_d(d, dz) for d in range(3)]
        if not isinstance(sign, int):
            for vec in h + [dip]:
                vec[0] = vec[0] * sign
        memo[dz] = (h, dip)
        return memo[dz]

    cx = sign if isinstance(sign, int) else 1
    r = [None] * 3
    w_vec = [None] * 3
    lanes = {}
    for cy, cz in pairs:
        w = W1 if abs(cx) + abs(cy) + abs(cz) == 1 else W2
        h, dip = source(cz)
        c = (cx, cy, cz)
        e = [mixed(c, h[s]) for s in range(3)]
        f = e[2] * mixed(c, dip)
        half = 0.6 * e[2]
        r0 = 1.2 * e[1] - half + f
        r1 = 1.2 * e[0] - half - f
        r2 = -0.6 * (e[0] + e[1]) - 0.3 * e[2]
        qv = e[0] - e[1]
        vals = [w * r0, w * r1, w * r2]
        wq = w * qv
        vals += [wq if cx != 0 else None, wq if cy != 0 else None, wq if cz != 0 else None]
        vals = [vals[0], vals[1], vals[2]] + [
            None if x is None else (x if k == 1 else -x) for x, k in zip(vals[3:], (cx, cy, cz))
        ]
        acc = lanes.setdefault(cy, [None] * 6)
        for i, x in enumerate(vals):
            if x is not None:
                acc[i] = plus(acc[i], x)
    total = [None] * 6
    for cy, acc in lanes.items():
        for i, x in enumerate(acc):
            if x is not None:
                total[i] = plus(total[i], x if cy == 0 else grid.roll_cols(x, cy))
    if not isinstance(sign, int):
        total[3] = total[3] * sign
    return total


def met(total, dipole):
    meet = None
    for d in range(3):
        if total[3 + d] is not None:
            meet = plus(meet, total[3 + d] * dipole[d])
    return [total[0], total[1], total[2] - meet]


def spread_inside(grid, tile, hold, fields):
    get_h = lambda k, dz: tile.get(hold, k, dz)
    get_d = lambda k, dz: tile.get(fields, 6 + k, dz)
    total = spread_plane(grid, get_h, get_d, 0, SIDE)
    for dx in (1, -1):
        part = spread_plane(grid, get_h, get_d, dx, CROSS)
        for i, x in enumerate(part):
            total[i] = plus(total[i], grid.in_row(x, dx))
    return met(total, [tile.get(fields, 6 + d) for d in range(3)])


def rim_sign(grid):
    return jnp.where(
        grid.sub == 0, -1.0, jnp.where(grid.sub == grid.rows - 1, 1.0, 0.0)
    ).astype(F32)


def hand_over(grid, tile, hold, hold_dip, target, sign):
    dip, at = hold_dip
    total = spread_plane(
        grid,
        lambda k, dz: tile.get(hold, k, dz),
        lambda k, dz: tile.get(dip, at + k, dz),
        sign,
        CROSS,
    )
    return met(total, target)


def spread_level(grid, tile, hold, dip, at):
    total = spread_plane(
        grid,
        lambda k, dz: tile.get(hold, k, dz),
        lambda k, dz: tile.get(dip, at + k, dz),
        0,
        SIDE,
    )
    return met(total, [tile.get(dip, at + d) for d in range(3)])


def parity_of(axis):
    return lax.rem(lax.axis_index(axis) + 1, 2)


def lines_from(first, second, parity, lines):
    lines[1 - parity] = first[...]
    lines[parity] = second[...]


def lines_to(first, second, lines):
    first[...] = lines[0]
    second[...] = lines[1]


def psi_of(rho):
    return 1.0 - jnp.exp(-rho)


def static_rows():
    for s in range(3):
        for j in range(5):
            yield 0, s * 19 + BEHIND[j], s * 19 + AHEAD[j], 0
    for s in range(3):
        for q in LEVEL:
            yield 0, s * 19 + q, s * 19 + q, 0
    for s in range(3):
        for j in range(5):
            yield 0, s * 19 + BEHIND[j], s * 19 + AHEAD[j], 1
    for kind in (1, 2):
        for c in range(9):
            yield kind, c, c, 0
        for c in (9, 10, 11, 6, 7, 8):
            yield kind, c, c, 1


def corner_groups(pack):
    for depth in range(2):
        found = [c for c, row in enumerate(static_rows()) if row[3] == depth]
        for at in range(0, len(found), pack):
            yield depth, found[at : at + pack]


def pack_static(kinds, planes, rows, lines, parity):
    up, down = parity, 1 - parity
    fill = 0
    for kind, above, below, depth in static_rows():
        for p in range(planes):
            v = kinds[kind][above, p]
            lines[up, fill : fill + 1, :] = v[rows - 1 - depth : rows - depth, :]
            v = kinds[kind][below, p]
            lines[down, fill : fill + 1, :] = v[depth : depth + 1, :]
            fill += 1


def pack_columns_kernel(
    adj_in, late_in, early_in, dip_late_in, dip_early_in,
    send_c, send_d, own_left, own_right, fl, fe, adj, send_a, send_b,
    late, early, dip_late, dip_early, lines, sems,
):
    planes, rows, cols = adj.shape[1:]
    grid = Grid(planes, rows, cols)
    copies = [
        pltpu.make_async_copy(a, b, sems.at[i])
        for i, (a, b) in enumerate(
            (
                (dip_late_in, dip_late),
                (late_in, late),
                (dip_early_in, dip_early),
                (early_in, early),
            )
        )
    ]
    per_chunk = -(-adj.shape[0] // (CHUNKS * grid.pack)) * grid.pack
    for i in range(CHUNKS):
        part = pl.ds(i * per_chunk, min(per_chunk, adj.shape[0] - i * per_chunk))
        copies.append(pltpu.make_async_copy(adj_in.at[part], adj.at[part], sems.at[4 + i]))
    for copy in copies:
        copy.start()
    for which, (saved, dip, out) in enumerate(((late, dip_late, fl), (early, dip_early, fe))):
        copies[2 * which].wait()
        copies[2 * which + 1].wait()

        for p in range(planes):
            flows = [None] * 19
            rho = []
            for s in range(3):
                total = None
                for q in range(19):
                    v = saved[s * 19 + q, p].astype(F32)
                    flows[q] = plus(flows[q], v)
                    total = plus(total, v)
                rho.append(total)
                out[s, p] = total
                out[9 + s, p] = psi_of(total)
            inverse = 1.0 / (rho[0] + rho[1] + rho[2])
            for d in range(3):
                momentum = None
                for q in range(19):
                    if VELOCITY[q][d] != 0:
                        momentum = plus(momentum, flows[q] if VELOCITY[q][d] > 0 else -flows[q])
                out[3 + d, p] = momentum * inverse
                out[6 + d, p] = dip[d, p].astype(F32)
    pops = adj.shape[0]
    components = pops + 18
    slot = grid.lane // grid.group
    for g in range(own_left.shape[0]):
        if g * grid.pack % per_chunk == 0 and g * grid.pack < pops:
            copies[4 + g * grid.pack // per_chunk].wait()
        left = right = jnp.zeros((rows, cols), F32)
        for j in range(grid.pack):
            c = g * grid.pack + j
            if c >= components:
                continue
            for p in range(planes):
                if c < pops:
                    v = adj[c, p]
                elif c < pops + 9:
                    v = fl[c - pops, p]
                else:
                    v = fe[c - pops - 9, p]
                at = p * grid.pack + j
                rolled = pltpu.roll(v, at * grid.group, 1) if at else v
                left = jnp.where(slot == at, rolled, left)
                right = jnp.where(slot == (at - 1) % (cols // grid.group), rolled, right)
        own_left[g] = left
        own_right[g] = right
    low = lax.rem(grid.lane, grid.group) < HALO
    even = parity_of("gy") == 0
    for h in range(send_c.shape[0]):
        left = jnp.where(low, own_left[2 * h], pltpu.roll(own_left[2 * h + 1], HALO, 1))
        right = jnp.where(low, pltpu.roll(own_right[2 * h + 1], cols - HALO, 1), own_right[2 * h])
        send_c[h] = jnp.where(even, right, left)
        send_d[h] = jnp.where(even, left, right)
    pack_static((adj, fl, fe), planes, rows, lines, parity_of("gx"))
    lines_to(send_a, send_b, lines)


def inside_collision(grid, tile, load, fields, hold, ab, kept):
    forces = brick_forces(grid, tile, fields, None, 0, 0)
    brick_collision(grid, tile, load, None, fields, forces, hold, ab, kept)
    at_rim = grid.at_rim()
    for k in range(9):
        tile.put(hold, k, jnp.where(at_rim, 0.0, tile.get(hold, k)))


def second_row(grid, tile, fields, hold, ab, kept, sides):
    low = grid.low()
    rest = 1.0 - 1.0 / RELAXATION[2]
    back = spread_inside(grid, tile, hold, fields)
    alpha = [tile.get(ab, s) + (1.0 - tile.get(fields, 9 + s)) * back[s] for s in range(3)]
    beta = [tile.get(ab, 3 + d) for d in range(3)]
    ahead = -grid.outward() * beta[0]
    for s in range(3):
        tile.put(sides, s, back[s])
    for s in range(2):
        tile.put(sides, 3 + s, alpha[s] + ahead)
        tile.put(sides, 5 + s, beta[1 + s])
    for j, yz in enumerate(CROSS):
        v = rest * jnp.where(low, tile.get(kept, AHEAD[j]), tile.get(kept, BEHIND[j]))
        v = v + (alpha[2] + ahead)
        tile.put(sides, 7 + j, v + mixed(yz, beta[1:]) if j else v)


def inside_kernel(adj, fl, sides, hold, ab, kept):
    planes, rows, cols = adj.shape[1:]
    grid = Grid(planes, rows, cols)
    load = lambda tile: lambda c, dz: tile.get(adj, c, dz)
    grid.over_main(lambda tile: inside_collision(grid, tile, load(tile), fl, hold, ab, kept))
    grid.over_main(lambda tile: second_row(grid, tile, fl, hold, ab, kept, sides))


def edge_kernel(
    own_left, own_right, recv_c, recv_d, sides_main,
    send_a, send_b, edge, fl, fe, lines, hold, ab, kept, sides,
):
    planes, rows, cols = sides_main.shape[1:]
    pops = edge.shape[0]
    grid = Grid(planes, rows, cols)
    even = parity_of("gy") == 0
    slot = lax.rem(grid.lane // grid.group, grid.pack)
    left_half = lax.rem(grid.lane, grid.width) < grid.width // 2
    components = pops + 18
    for g in range(own_left.shape[0]):
        first, second = recv_c[g // 2], recv_d[g // 2]
        from_next = jnp.where(even, first, second)
        from_prior = jnp.where(even, second, first)
        if g % 2:
            from_next = pltpu.roll(from_next, cols - HALO, 1)
            from_prior = pltpu.roll(from_prior, HALO, 1)
        for j in range(grid.pack):
            c = g * grid.pack + j
            if c >= components:
                continue
            before = slot == (j - 1) % grid.pack
            low = jnp.where(before, from_prior, own_left[g])
            high = jnp.where(before, own_right[g], from_next)
            v = jnp.where(
                left_half,
                pltpu.roll(low, ((1 - j) * grid.group) % cols, 1),
                pltpu.roll(high, ((3 - j) * grid.group) % cols, 1),
            )
            if c < pops:
                edge[c] = v
            else:
                field, k = (fl, c - pops) if c < pops + 9 else (fe, c - pops - 9)
                field[k] = v
                if k < 3:
                    field[9 + k] = psi_of(v)
    adj, fields, both = Pair(None, edge), Pair(None, fl), Pair(sides_main, sides)
    hold, ab, kept = Pair(None, hold), Pair(None, ab), Pair(None, kept)

    def inside(tile):
        load = lambda c, dz: tile.get(adj, c, dz)
        inside_collision(grid, tile, load, fields, hold, ab, kept)
        second_row(grid, tile, fields, hold, ab, kept, both)

    grid.over_edge(inside)
    parity = parity_of("gx")
    kinds = (edge, fl, fe)
    rows_of = list(static_rows())
    low = grid.low()
    fill = 0
    for depth, members in corner_groups(grid.pack):
        v = None
        for j, c in enumerate(members):
            kind, above, below, unused = rows_of[c]
            one = kinds[kind][above]
            if above != below:
                one = jnp.where(low, kinds[kind][below], one)
            one = grid.turn(one, j * grid.group)
            v = one if j == 0 else jnp.where(grid.corners(j), one, v)
        lines[parity, fill : fill + 1, :] = v[rows - 1 - depth : rows - depth, :]
        lines[1 - parity, fill : fill + 1, :] = v[depth : depth + 1, :]
        fill += 1
    for c in range(DYNAMIC):
        depth = 0 if c < 3 else 1
        for t in range(grid.tiles):
            v = both.at(c, t)
            lines[parity, fill : fill + 1, :] = v[rows - 1 - depth : rows - depth, :]
            lines[1 - parity, fill : fill + 1, :] = v[depth : depth + 1, :]
            fill += 1
    lines_to(send_a, send_b, lines)


def first_step(grid, tile, adj, fl, rims, hold, ab, kept, hold_rim, ab_rim, kept_rim):
    forces = brick_forces(grid, tile, fl, rims, LATE_PSI, LATE + 6)
    load = lambda c, dz: tile.get(adj, c, dz)
    brick_collision(grid, tile, load, rims, fl, forces, hold, ab, kept)
    forces = rim_forces(grid, tile, fl, rims, LATE_PSI, LATE)
    rho, u = [[tile.get(rims, LATE + at + d) for d in range(3)] for at in (0, 3)]
    psi = [tile.get(rims, LATE_PSI + s) for s in range(3)]
    rim_collision(
        grid,
        tile,
        lambda s, i, dz: tile.get(rims, ALONG + s * 9 + i, dz),
        lambda s, j, dz: tile.get(rims, AFTER + s * 5 + j, dz),
        load,
        rho,
        u,
        psi,
        forces,
        hold_rim,
        ab_rim,
        kept_rim,
    )


def early_forces(grid, tile, fe, rims, forces, forces_rim):
    brick = brick_forces(grid, tile, fe, rims, EARLY_PSI, EARLY + 6)
    beyond = rim_forces(grid, tile, fe, rims, EARLY_PSI, EARLY)
    for s in range(3):
        for d in range(3):
            tile.put(forces, 3 * s + d, brick[s][d])
            tile.put(forces_rim, 3 * s + d, beyond[s][d])


def rim_psis(grid, tile, rims):
    for s in range(3):
        tile.put(rims, LATE_PSI + s, psi_of(tile.get(rims, LATE + s)))
        tile.put(rims, EARLY_PSI + s, psi_of(tile.get(rims, EARLY + s)))


def finish_first(grid, tile, fl, rims, hold, ab, kept, hold_rim, ab_rim, mid, part):
    rest = 1.0 - 1.0 / RELAXATION[2]
    sign, at_rim = rim_sign(grid), grid.at_rim()
    own_dip, rim_dip = (fl, 6), (rims, LATE + 6)
    dip = [tile.get(fl, 6 + d) for d in range(3)]
    dip_rim = [tile.get(rims, LATE + 6 + d) for d in range(3)]
    dip_far = [tile.get(rims, LATE + FAR + 3 + d) for d in range(3)]
    back = spread_inside(grid, tile, hold, fl)
    inward = hand_over(grid, tile, hold_rim, rim_dip, dip, sign)
    alpha = [
        tile.get(ab, s)
        + (1.0 - tile.get(fl, 9 + s)) * (back[s] + jnp.where(at_rim, inward[s], 0.0))
        for s in range(3)
    ]
    beta = [tile.get(ab, 3 + d) for d in range(3)]
    for q in range(19):
        along = mixed(VELOCITY[q], beta) if q != 16 else None
        for s in range(3):
            v = alpha[s] if along is None else alpha[s] + along
            if s == 2:
                v = v + rest * tile.get(kept, q)
            tile.put(mid, s * 19 + q, v)
    given = hand_over(grid, tile, hold, own_dip, dip_rim, -sign)
    level = spread_level(grid, tile, hold_rim, *rim_dip)
    after = hand_over(grid, tile, hold_rim, rim_dip, dip_far, -sign)
    for s in range(3):
        open_share = 1.0 - tile.get(rims, LATE_PSI + s)
        tile.put(part, s, tile.get(ab_rim, s) + open_share * (given[s] + level[s]))
        tile.put(part, 3 + s, tile.get(ab_rim, 3 + s))
        tile.put(part, 6 + s, (1.0 - tile.get(rims, LATE + FAR + s)) * after[s])


def main_kernel(
    adj, fl, fe, recv_a, recv_b, after,
    rims, mid, part, kept_rim, forces, forces_rim, known, lines, hold, ab, kept, hold_rim, ab_rim,
):
    planes, rows, cols = adj.shape[1:]
    grid = Grid(planes, rows, cols)
    lines_from(recv_a, recv_b, parity_of("gx"), lines)
    for c in range(STATIC):
        for p in range(planes):
            k = c * planes + p
            rims[c, p] = grid.sides(lines[0, k : k + 1, :], lines[1, k : k + 1, :])
    grid.over_main(lambda tile: rim_psis(grid, tile, rims))
    left_half = lax.rem(grid.lane, grid.width) < grid.width // 2
    for c in range(STATIC):
        v = None
        for p in range(planes):
            one = grid.turn(rims[c, p], p * grid.width + 2 * grid.group)
            v = one if p == 0 else jnp.where(grid.lane // grid.width == p, one, v)
        known[c] = jnp.where(left_half, grid.turn(v, -grid.group), grid.turn(v, grid.group))

    def step(tile):
        first_step(grid, tile, adj, fl, rims, hold, ab, kept, hold_rim, ab_rim, kept_rim)
        early_forces(grid, tile, fe, rims, forces, forces_rim)

    grid.over_main(step)
    grid.over_main(
        lambda tile: finish_first(
            grid, tile, fl, rims, hold, ab, kept, hold_rim, ab_rim, mid, part
        )
    )


def last_kernel(
    fe_m, rims_m, mid_m, part_m, kept_rim_m, forces_m, forces_rim_m, known, edge, fl_e, fe_e,
    recv_a, recv_b, out,
    rims_e, mid_e, part_e, kept_rim_e, forces_e, forces_rim_e, hold_e, ab_e, kept_e, hold_rim_e,
    ab_rim_e, patches, lines, near, rim_mid, rim_level, rim_far, hold2, hold_rim2, ab2, kept2,
    total, staged, sems,
):
    planes, rows, cols = fe_m.shape[1:]
    grid = Grid(planes, rows, cols)
    lines_from(recv_a, recv_b, parity_of("gx"), lines)
    is_corner = grid.corners(0)
    corner_lines = 0
    for k, (unused, members) in enumerate(corner_groups(grid.pack)):
        v = grid.sides(lines[0, k : k + 1, :], lines[1, k : k + 1, :])
        for j, c in enumerate(members):
            rims_e[c] = jnp.where(is_corner, grid.turn(v, -j * grid.group), known[c])
        corner_lines += 1
    for c in range(DYNAMIC):
        for t in range(grid.tiles):
            k = corner_lines + c * grid.tiles + t
            near[c, t] = grid.sides(lines[0, k : k + 1, :], lines[1, k : k + 1, :])
    fe, rims, mid = Pair(fe_m, fe_e), Pair(rims_m, rims_e), Pair(mid_m, mid_e)
    part, kept_rim = Pair(part_m, part_e), Pair(kept_rim_m, kept_rim_e)
    forces, forces_rim = Pair(forces_m, forces_e), Pair(forces_rim_m, forces_rim_e)
    rest = 1.0 - 1.0 / RELAXATION[2]
    at_rim = grid.at_rim()
    sign = rim_sign(grid)
    outward = grid.outward()

    def edge_steps(tile):
        adj, fl = Pair(None, edge), Pair(None, fl_e)
        hold, ab, kept = Pair(None, hold_e), Pair(None, ab_e), Pair(None, kept_e)
        hold_rim, ab_rim = Pair(None, hold_rim_e), Pair(None, ab_rim_e)
        rim_psis(grid, tile, rims)
        first_step(grid, tile, adj, fl, rims, hold, ab, kept, hold_rim, ab_rim, kept_rim)
        early_forces(grid, tile, fe, rims, forces, forces_rim)
        finish_first(grid, tile, fl, rims, hold, ab, kept, hold_rim, ab_rim, mid, part)

    grid.over_edge(edge_steps)

    def complete(tile):
        t = tile.index
        alpha = [
            tile.get(part, s) + (1.0 - tile.get(rims, LATE_PSI + s)) * near[s, t]
            for s in range(3)
        ]
        beta = [tile.get(part, 3 + d) for d in range(3)]
        far = [near[3 + s, t] + tile.get(part, 6 + s) for s in range(2)]
        far_beta = [near[5 + d, t] for d in range(2)]
        ahead = outward * beta[0]
        for j, yz in enumerate(CROSS):
            side = mixed(yz, beta[1:]) if j else None
            side_far = mixed(yz, far_beta) if j else None
            for s in range(3):
                v = plus(side, alpha[s] + ahead)
                if s == 2:
                    v = v + rest * tile.get(kept_rim, 9 + j)
                    rim_far[10 + j, t] = near[7 + j, t] + tile.get(part, 8)
                else:
                    rim_far[s * 5 + j, t] = plus(side_far, far[s])
                rim_mid[s * 5 + j, t] = v
        for i, q in enumerate(LEVEL):
            side = mixed(VELOCITY[q][1:], beta[1:]) if q != 16 else None
            for s in range(3):
                v = plus(side, alpha[s])
                if s == 2:
                    v = v + rest * tile.get(kept_rim, i)
                rim_level[s * 9 + i, t] = v

    grid.over(complete)

    def collide(tile):
        load = lambda c, dz: tile.get(mid, c, dz)
        known = [[tile.get(forces, 3 * s + d) for d in range(3)] for s in range(3)]
        brick_collision(grid, tile, load, rim_mid, fe, known, hold2, ab2, kept2)
        known = [[tile.get(forces_rim, 3 * s + d) for d in range(3)] for s in range(3)]
        rho, u = [[tile.get(rims, EARLY + at + d) for d in range(3)] for at in (0, 3)]
        psi = [tile.get(rims, EARLY_PSI + s) for s in range(3)]
        rim_collision(
            grid,
            tile,
            lambda s, i, dz: tile.get(rim_level, s * 9 + i, dz),
            lambda s, j, dz: tile.get(rim_far, s * 5 + j, dz),
            load,
            rho,
            u,
            psi,
            known,
            hold_rim2,
            None,
            None,
        )

    grid.over(collide)

    def finish(tile):
        back = spread_inside(grid, tile, hold2, fe)
        dip = [tile.get(fe, 6 + d) for d in range(3)]
        inward = hand_over(grid, tile, hold_rim2, (rims, EARLY + 6), dip, sign)
        for s in range(3):
            x = back[s] + jnp.where(at_rim, inward[s], 0.0)
            total[s, tile.index] = tile.get(ab2, s) + (1.0 - tile.get(fe, 9 + s)) * x

    grid.over(finish)
    at_side = (grid.lane < HALO) | (grid.lane >= cols - HALO)
    first_group = lax.rem(grid.lane, grid.width) < grid.group
    sources = [total.at[s] for s in range(3)] + [ab2.at[3 + d] for d in range(3)]
    sources += [kept2.at[q] for q in range(19)]
    for i, ref in enumerate(sources):
        v = ref[planes]
        patches[i] = jnp.where(first_group, pltpu.roll(v, cols - 2 * grid.group, 1), v)
    copies = []
    for p in range(planes):
        turn = (cols - p * grid.width - grid.group) % cols

        def patched(i):
            return jnp.where(at_side, pltpu.roll(patches[i], turn, 1), sources[i][p])

        alpha = [patched(s) for s in range(3)]
        beta = [patched(3 + d) for d in range(3)]
        for q in range(19):
            along = mixed(VELOCITY[q], beta) if q != 16 else None
            for s in range(3):
                v = alpha[s] if along is None else alpha[s] + along
                if s == 2:
                    v = v + rest * patched(6 + q)
                staged[s * 19 + q, p] = v
        copies.append(pltpu.make_async_copy(staged.at[:, p], out.at[:, p], sems.at[p]))
        copies[p].start()
    for copy in copies:
        copy.wait()


def call(kernel, outs, scratch, args, in_hbm=False, out_hbm=False, cost=0):
    vmem = pl.BlockSpec(memory_space=pltpu.VMEM)
    hbm = pl.BlockSpec(memory_space=pltpu.HBM)
    return pl.pallas_call(
        kernel,
        out_shape=[jax.ShapeDtypeStruct(s, F32) for s in outs],
        in_specs=[hbm if in_hbm else vmem] * len(args),
        out_specs=[hbm if out_hbm else vmem] * len(outs),
        scratch_shapes=[pltpu.VMEM(s, F32) if isinstance(s, tuple) else s for s in scratch],
        compiler_params=pltpu.CompilerParams(vmem_limit_bytes=VMEM_BYTES),
        cost_estimate=pl.CostEstimate(flops=cost, bytes_accessed=cost, transcendentals=0),
    )(*[pltpu.with_memory_space_constraint(x, pltpu.HBM) if in_hbm else x for x in args])


def swap(block, axis, offset):
    size = lax.axis_size(axis)
    route = []
    for i in range(offset, size + offset, 2):
        a, b = i % size, (i + 1) % size
        route += [(a, b), (b, a)]
    return lax.ppermute(block, axis, route)


def shards(adjoint_in, populations_early, populations_late, dipoles_early, dipoles_late):
    pops, planes, rows, cols = adjoint_in.shape
    tile = (rows, cols)
    pack = cols // planes // (2 * HALO)
    groups = -(-(pops + 18) // pack)
    groups += groups % 2

    def lines(n):
        return (-(-n // 8) * 8, cols)

    def main(*counts):
        return [(n, planes) + tile for n in counts]

    def edges(*counts):
        return [(n,) + tile for n in counts]

    def tiled(*counts):
        return [(n, planes + 1) + tile for n in counts]

    static = lines(STATIC * planes)
    second = lines(len(list(corner_groups(pack))) + DYNAMIC * (planes + 1))
    send_c, send_d, own_left, own_right, fl_m, fe_m, adj, send_a, send_b = call(
        pack_columns_kernel,
        edges(groups // 2, groups // 2, groups, groups) + main(12, 12, pops) + [static] * 2,
        [
            pltpu.VMEM(x.shape, x.dtype)
            for x in (populations_late, populations_early, dipoles_late, dipoles_early)
        ]
        + [(2,) + static, pltpu.SemaphoreType.DMA((4 + CHUNKS,))],
        [adjoint_in, populations_late, populations_early, dipoles_late, dipoles_early],
        in_hbm=True,
    )
    static_a, static_b = swap(send_a, "gx", 1), swap(send_b, "gx", 0)
    recv_c, recv_d = swap(send_c, "gy", 1), swap(send_d, "gy", 0)
    (sides,) = call(
        inside_kernel, main(DYNAMIC), main(9, 6, 19), [adj, fl_m], cost=INSIDE_COST
    )
    send_a, send_b, edge, fl_e, fe_e = call(
        edge_kernel,
        [second] * 2 + edges(pops, 12, 12),
        [(2,) + second] + edges(9, 6, 19, DYNAMIC),
        [own_left, own_right, recv_c, recv_d, sides],
        cost=EDGE_COST,
    )
    recv_a, recv_b = swap(send_a, "gx", 1), swap(send_b, "gx", 0)
    known = (RIMS, pops, 9, 14, 9, 9)
    mains = call(
        main_kernel,
        main(*known) + edges(STATIC),
        [(2,) + static] + main(9, 6, 19, 9, 6),
        [adj, fl_m, fe_m, static_a, static_b, fl_e],
        cost=MAIN_COST,
    )
    (out,) = call(
        last_kernel,
        [(pops, planes) + tile],
        edges(*known, 9, 6, 19, 9, 6, 25)
        + [(2,) + second]
        + tiled(DYNAMIC, 15, 27, 15, 9, 9, 6, 19, 3)
        + main(pops)
        + [pltpu.SemaphoreType.DMA((planes,))],
        [fe_m, *mains, edge, fl_e, fe_e, recv_a, recv_b],
        out_hbm=True,
    )
    return out


def solution(mesh):
    placed = P(None, None, "gx", "gy")
    return jax.shard_map(
        shards, mesh=mesh, in_specs=(placed,) * 5, out_specs=placed, check_vma=False
    )
```

```python
import jax
import jax.numpy as jnp
from jax import lax
from jax.experimental import pallas as pl
from jax.experimental.pallas import tpu as pltpu
from jax.sharding import PartitionSpec as P

VELOCITY = (
    (1, 0, 0),
    (-1, 0, 0),
    (0, 1, 0),
    (0, -1, 0),
    (1, 1, 0),
    (-1, -1, 0),
    (1, -1, 0),
    (-1, 1, 0),
    (1, 0, 1),
    (-1, 0, -1),
    (1, 0, -1),
    (-1, 0, 1),
    (0, 1, 1),
    (0, -1, -1),
    (0, 1, -1),
    (0, -1, 1),
    (0, 0, 0),
    (0, 0, 1),
    (0, 0, -1),
)
INDEX = {c: q for q, c in enumerate(VELOCITY)}
W1, W2, W0 = 1.0 / 18.0, 1.0 / 36.0, 1.0 / 3.0
RELAXATION = (1.0, 1.0, 1.25)
COUPLING = ((0.0, 1.2, -0.6), (1.2, 0.0, -0.6), (-0.6, -0.6, -0.3))
CROSS = ((0, 0), (1, 0), (-1, 0), (0, 1), (0, -1))
AHEAD = tuple(INDEX[(1,) + yz] for yz in CROSS)
BEHIND = tuple(INDEX[(-1,) + yz] for yz in CROSS)
SIDE = ((1, 0), (-1, 0), (0, 1), (0, -1), (1, 1), (-1, -1), (1, -1), (-1, 1))
LEVEL = tuple(q for q in range(19) if VELOCITY[q][0] == 0)
ALONG, AFTER, LATE, EARLY = 15, 42, 57, 72
STATIC = 87
FAR = 9
LATE_PSI, EARLY_PSI = STATIC, STATIC + 3
RIMS = STATIC + 6
DYNAMIC = 12
F32 = jnp.float32
CHUNKS = 4
INSIDE_COST, EDGE_COST, MAIN_COST = 10**7, 10**8, 10**8
VMEM_BYTES = 40 * 1024 * 1024
HALO = 4


class Grid:
    def __init__(self, planes, rows, cols):
        self.planes, self.rows, self.cols = planes, rows, cols
        self.tiles = planes + 1
        self.width = cols // planes
        self.group = 2 * HALO
        self.pack = self.width // self.group
        self.sub = lax.broadcasted_iota(jnp.int32, (rows, cols), 0)
        self.lane = lax.broadcasted_iota(jnp.int32, (rows, cols), 1)
        self.masks = {}

    def once(self, name, make):
        if name not in self.masks:
            self.masks[name] = make()
        return self.masks[name]

    def in_width(self):
        return self.once("width", lambda: lax.rem(self.lane, self.width))

    def plane_lanes(self, p):
        low, high = p * self.width, (p + 1) * self.width
        return self.once(("plane", p), lambda: (self.lane >= low) & (self.lane < high))

    def left_half(self):
        return self.once("left", lambda: self.in_width() < self.width // 2)

    def roll_rows(self, v, dx):
        return pltpu.roll(v, (-dx) % self.rows, 0)

    def roll_cols(self, v, dy):
        return pltpu.roll(v, (-dy) % self.cols, 1)

    def at_row(self, v, rim, dx):
        edge = self.rows - 1 if dx > 0 else 0
        return jnp.where(self.sub == edge, rim, self.roll_rows(v, dx))

    def in_row(self, v, dx):
        edge = self.rows - 1 if dx > 0 else 0
        return jnp.where(self.sub == edge, 0.0, self.roll_rows(v, dx))

    def sides(self, low, high):
        return jnp.where(self.sub == 0, low, high)

    def over_main(self, body):
        for p in range(self.planes):
            body(Tile(self, p, False))

    def over_edge(self, body):
        body(Tile(self, self.planes, True))

    def over(self, body):
        self.over_main(body)
        self.over_edge(body)

    def at_rim(self):
        return self.once("rim", lambda: (self.sub == 0) | (self.sub == self.rows - 1))

    def low(self):
        return self.once("low", lambda: self.sub < self.rows // 2)

    def corners(self, j):
        return self.once(("corner", j), lambda: self.make_corners(j))

    def make_corners(self, j):
        at, inside = self.in_width(), None
        for low in (HALO, 3 * self.group):
            low = (low + j * self.group) % self.width
            window = (at >= low) & (at < low + HALO)
            inside = window if inside is None else inside | window
        return inside

    def turn(self, v, lanes):
        return pltpu.roll(v, lanes % self.cols, 1) if lanes % self.cols else v

    def outward(self):
        return self.once("out", lambda: jnp.where(self.low(), -1.0, 1.0).astype(F32))


class Tile:
    def __init__(self, grid, index, edge):
        self.grid, self.index, self.edge = grid, index, edge

    def of(self, dz):
        if dz == 0 or self.edge:
            return self.index
        return (self.index + dz) % self.grid.planes

    def get(self, ref, c, dz=0):
        if isinstance(ref, Pair):
            v = ref.edge[c] if self.edge else ref.main[c, self.of(dz)]
        else:
            v = ref[c, self.of(dz)]
        if self.edge and dz != 0:
            v = self.grid.roll_cols(v, dz * self.grid.width)
        return v

    def put(self, ref, c, v):
        if not isinstance(ref, Pair):
            ref[c, self.index] = v
        elif self.edge:
            ref.edge[c] = v
        else:
            ref.main[c, self.index] = v


class Pair:
    def __init__(self, main, edge):
        self.main, self.edge = main, edge

    def at(self, c, t):
        return self.edge[c] if t == self.main.shape[1] else self.main[c, t]


def plus(a, b):
    return b if a is None else a + b


def mixed(coefficients, values):
    total = None
    for k, v in zip(coefficients, values):
        if k == 0:
            continue
        term = v if k == 1 else (-v if k == -1 else k * v)
        total = plus(total, term)
    return total


def axis_pairs():
    for q in (0, 2, 17, 4, 6, 8, 10, 12, 14):
        c = VELOCITY[q]
        yield c, (W1 if sum(abs(i) for i in c) == 1 else W2)


def first_and_second(diff, total):
    first = [None] * 3
    second = {}
    for c, w in axis_pairs():
        for d in range(3):
            if c[d] == 0:
                continue
            if diff is not None:
                first[d] = plus(first[d], (w * c[d]) * diff[c])
            if total is not None:
                for e in range(d, 3):
                    if c[e] != 0:
                        second[d, e] = plus(second.get((d, e)), (w * c[d] * c[e]) * total[c])
    return first, second


def turned(second, v):
    return [sum(second[min(d, e), max(d, e)] * v[e] for e in range(3)) for d in range(3)]


def dot(a, b):
    return a[0] * b[0] + a[1] * b[1] + a[2] * b[2]


def field_forces(grid, loads, across, dipole):
    memo = {}

    def source(name, dz, place):
        key = (name, dz, place)
        if key in memo:
            return memo[key]
        if isinstance(name, int):
            v = loads[place](name, dz)
        elif name == "chi":
            v = source(0, dz, place) - source(1, dz, place)
        elif name[0] == "V":
            v = source(2, dz, place) * source(3 + name[1], dz, place)
        else:
            c = name[1]
            v = mixed(c, [source(("V", d), dz, place) if c[d] else None for d in range(3)])
        memo[key] = v
        return v

    def shifted(name, c):
        key = (name, c, "shift")
        if key in memo:
            return memo[key]
        if c[1] != 0:
            v = grid.roll_cols(shifted(name, (c[0], 0, c[2])), c[1])
        elif c[0] != 0:
            v = across(lambda place, dz: source(name, dz, place), c[0], c[2])
        else:
            v = source(name, c[2], 0)
        memo[key] = v
        return v

    def parts(name):
        diff, total = {}, {}
        for c, w in axis_pairs():
            back = tuple(-i for i in c)
            a, b = shifted(name, c), shifted(name, back)
            diff[c], total[c] = a - b, a + b
        return diff, total

    diff, unused = parts(0)
    s0, unused = first_and_second(diff, None)
    diff, unused = parts(2)
    s2, unused = first_and_second(diff, None)
    diff, total = parts("chi")
    schi, second = first_and_second(diff, total)
    s1 = [a - b for a, b in zip(s0, schi)]
    pull = [None] * 3
    for c, w in axis_pairs():
        back = tuple(-i for i in c)
        if sum(abs(i) for i in c) == 1:
            name = ("V", [i for i in range(3) if c[i]][0])
        else:
            name = ("L", c)
        total_c = shifted(name, c) + shifted(name, back)
        for d in range(3):
            if c[d] != 0:
                pull[d] = plus(pull[d], (w * c[d]) * total_c)
    md = turned(second, dipole)
    k0 = [-1.2 * s1[d] + 0.6 * s2[d] - pull[d] for d in range(3)]
    k1 = [-1.2 * s0[d] + 0.6 * s2[d] + pull[d] for d in range(3)]
    k2 = [0.6 * (s0[d] + s1[d]) + 0.3 * s2[d] + md[d] for d in range(3)]
    return k0, k1, k2


def brick_forces(grid, tile, fields, rim, rim_psi, rim_dip):
    def own(c, dz):
        return tile.get(fields, (9 + c) if c < 3 else (3 + c), dz)

    def beyond(c, dz):
        return tile.get(rim, (rim_psi + c) if c < 3 else (rim_dip + c - 3), dz)

    def across(get, cx, dz):
        if rim is None:
            return grid.in_row(get(0, dz), cx)
        return grid.at_row(get(0, dz), get(1, dz), cx)

    return field_forces(grid, (own, beyond), across, [own(3 + d, 0) for d in range(3)])


def rim_forces(grid, tile, fields, rims, psi, base):
    outward = grid.outward()

    def loader(ref, psi_at, dip_at):
        def load(c, dz):
            v = tile.get(ref, (psi_at + c) if c < 3 else (dip_at + c - 3), dz)
            return v * outward if c == 3 else v

        return load

    loads = {
        0: loader(rims, psi, base + 6),
        1: loader(rims, base + FAR, base + FAR + 3),
        -1: loader(fields, 9, 6),
    }
    dipole = [loads[0](3 + d, 0) for d in range(3)]
    return field_forces(grid, loads, lambda get, cx, dz: get(cx, dz), dipole)


def collision_adjoint(streamed_of, rho, u, psi, forces):
    inverse_sum = 1.0 / (rho[0] + rho[1] + rho[2])
    grad_u = [None] * 3
    alphas, held = [], []
    for s in range(3):
        streamed = streamed_of(s)
        diff, total = {}, {}
        for c, w in axis_pairs():
            a, b = streamed[INDEX[c]], streamed[INDEX[tuple(-i for i in c)]]
            diff[c], total[c] = a - b, a + b
        m1, m2 = first_and_second(diff, total)
        m0 = W0 * streamed[16]
        for c, w in axis_pairs():
            m0 = m0 + w * total[c]
        inverse = 1.0 / rho[s]
        ratio = psi[s] * inverse
        tau = RELAXATION[s]
        k = forces[s]
        v = [u[d] + (tau * ratio) * k[d] for d in range(3)]
        mv = turned(m2, v)
        g = [3.0 * (m1[d] + 3.0 * mv[d] - m0 * v[d]) for d in range(3)]
        feq = m0 + 3.0 * dot(m1, v) + 4.5 * dot(mv, v) - 1.5 * m0 * dot(v, v)
        alphas.append(feq * (1.0 / tau) + dot(g, k) * (1.0 - psi[s] - ratio))
        scaled = rho[s] * (1.0 / tau)
        for d in range(3):
            grad_u[d] = plus(grad_u[d], scaled * g[d])
            held.append(psi[s] * g[d])
    beta = [grad_u[d] * inverse_sum for d in range(3)]
    along = dot(beta, u)
    return held, [a - along for a in alphas], beta


def brick_collision(grid, tile, load, rim, fields, forces, hold, ab, kept):
    def streamed_of(s):
        streamed = []
        for q in range(19):
            c = VELOCITY[q]
            v = load(s * 19 + q, c[2])
            if c[0] != 0:
                j = (AHEAD if c[0] > 0 else BEHIND).index(q)
                if rim is None:
                    v = grid.in_row(v, c[0])
                else:
                    v = grid.at_row(v, tile.get(rim, s * 5 + j, c[2]), c[0])
            if c[1] != 0:
                v = grid.roll_cols(v, c[1])
            streamed.append(v)
            if s == 2:
                tile.put(kept, q, v)
        return streamed

    rho, u, psi = [[tile.get(fields, at + d) for d in range(3)] for at in (0, 3, 9)]
    held, alpha, beta = collision_adjoint(streamed_of, rho, u, psi, forces)
    for k in range(9):
        tile.put(hold, k, held[k])
    for s in range(3):
        tile.put(ab, s, alpha[s])
        tile.put(ab, 3 + s, beta[s])


def rim_collision(grid, tile, level, after, inner, rho, u, psi, forces, hold, ab, kept):
    outward, low = grid.outward(), grid.low()

    def streamed_of(s):
        streamed = []
        for q in range(19):
            c = VELOCITY[q]
            if c[0] == 0:
                v = level(s, LEVEL.index(q), c[2])
            elif c[0] > 0:
                v = after(s, AHEAD.index(q), c[2])
            else:
                j = BEHIND.index(q)
                v = jnp.where(low, inner(s * 19 + AHEAD[j], c[2]), inner(s * 19 + BEHIND[j], c[2]))
            if c[1] != 0:
                v = grid.roll_cols(v, c[1])
            streamed.append(v)
            if s == 2 and kept is not None and c[0] >= 0:
                tile.put(kept, LEVEL.index(q) if c[0] == 0 else 9 + AHEAD.index(q), v)
        return streamed

    u = [u[0] * outward, u[1], u[2]]
    held, alpha, beta = collision_adjoint(streamed_of, rho, u, psi, forces)
    for k in range(9):
        tile.put(hold, k, held[k] * outward if k % 3 == 0 else held[k])
    if ab is not None:
        for s in range(3):
            tile.put(ab, s, alpha[s])
            tile.put(ab, 3 + s, beta[s] * outward if s == 0 else beta[s])


def spread_plane(grid, get_h, get_d, sign, pairs):
    memo = {}

    def source(dz):
        if dz in memo:
            return memo[dz]
        h = [[get_h(3 * s + d, dz) for d in range(3)] for s in range(3)]
        dip = [get_d(d, dz) for d in range(3)]
        if not isinstance(sign, int):
            for vec in h + [dip]:
                vec[0] = vec[0] * sign
        memo[dz] = (h, dip)
        return memo[dz]

    cx = sign if isinstance(sign, int) else 1
    r = [None] * 3
    w_vec = [None] * 3
    lanes = {}
    for cy, cz in pairs:
        w = W1 if abs(cx) + abs(cy) + abs(cz) == 1 else W2
        h, dip = source(cz)
        c = (cx, cy, cz)
        e = [mixed(c, h[s]) for s in range(3)]
        f = e[2] * mixed(c, dip)
        half = 0.6 * e[2]
        r0 = 1.2 * e[1] - half + f
        r1 = 1.2 * e[0] - half - f
        r2 = -0.6 * (e[0] + e[1]) - 0.3 * e[2]
        qv = e[0] - e[1]
        vals = [w * r0, w * r1, w * r2]
        wq = w * qv
        vals += [wq if cx != 0 else None, wq if cy != 0 else None, wq if cz != 0 else None]
        vals = [vals[0], vals[1], vals[2]] + [
            None if x is None else (x if k == 1 else -x) for x, k in zip(vals[3:], (cx, cy, cz))
        ]
        acc = lanes.setdefault(cy, [None] * 6)
        for i, x in enumerate(vals):
            if x is not None:
                acc[i] = plus(acc[i], x)
    total = [None] * 6
    for cy, acc in lanes.items():
        for i, x in enumerate(acc):
            if x is not None:
                total[i] = plus(total[i], x if cy == 0 else grid.roll_cols(x, cy))
    if not isinstance(sign, int):
        total[3] = total[3] * sign
    return total


def met(total, dipole):
    meet = None
    for d in range(3):
        if total[3 + d] is not None:
            meet = plus(meet, total[3 + d] * dipole[d])
    return [total[0], total[1], total[2] - meet]


def spread_inside(grid, tile, hold, fields):
    get_h = lambda k, dz: tile.get(hold, k, dz)
    get_d = lambda k, dz: tile.get(fields, 6 + k, dz)
    total = spread_plane(grid, get_h, get_d, 0, SIDE)
    for dx in (1, -1):
        part = spread_plane(grid, get_h, get_d, dx, CROSS)
        for i, x in enumerate(part):
            total[i] = plus(total[i], grid.in_row(x, dx))
    return met(total, [tile.get(fields, 6 + d) for d in range(3)])


def rim_sign(grid):
    return grid.once("sign", lambda: jnp.where(grid.at_rim(), grid.outward(), 0.0))


def hand_over(grid, tile, hold, hold_dip, target, sign):
    dip, at = hold_dip
    total = spread_plane(
        grid,
        lambda k, dz: tile.get(hold, k, dz),
        lambda k, dz: tile.get(dip, at + k, dz),
        sign,
        CROSS,
    )
    return met(total, target)


def spread_level(grid, tile, hold, dip, at):
    total = spread_plane(
        grid,
        lambda k, dz: tile.get(hold, k, dz),
        lambda k, dz: tile.get(dip, at + k, dz),
        0,
        SIDE,
    )
    return met(total, [tile.get(dip, at + d) for d in range(3)])


def parity_of(axis):
    return lax.rem(lax.axis_index(axis) + 1, 2)


def lines_from(first, second, parity, lines):
    lines[1 - parity] = first[...]
    lines[parity] = second[...]


def lines_to(first, second, lines):
    first[...] = lines[0]
    second[...] = lines[1]


def psi_of(rho):
    return 1.0 - jnp.exp(-rho)


def static_rows():
    for s in range(3):
        for j in range(5):
            yield 0, s * 19 + BEHIND[j], s * 19 + AHEAD[j], 0
    for s in range(3):
        for q in LEVEL:
            yield 0, s * 19 + q, s * 19 + q, 0
    for s in range(3):
        for j in range(5):
            yield 0, s * 19 + BEHIND[j], s * 19 + AHEAD[j], 1
    for kind in (1, 2):
        for c in range(9):
            yield kind, c, c, 0
        for c in (9, 10, 11, 6, 7, 8):
            yield kind, c, c, 1


def corner_groups(pack):
    for depth in range(2):
        found = [c for c, row in enumerate(static_rows()) if row[3] == depth]
        for at in range(0, len(found), pack):
            yield depth, found[at : at + pack]


def pack_static(kinds, planes, rows, lines, parity):
    up, down = parity, 1 - parity
    fill = 0
    for kind, above, below, depth in static_rows():
        for p in range(planes):
            v = kinds[kind][above, p]
            lines[up, fill : fill + 1, :] = v[rows - 1 - depth : rows - depth, :]
            v = kinds[kind][below, p]
            lines[down, fill : fill + 1, :] = v[depth : depth + 1, :]
            fill += 1


def pack_columns_kernel(
    adj_in, late_in, early_in, dip_late_in, dip_early_in,
    send_c, send_d, own_left, own_right, fl, fe, adj, send_a, send_b,
    late, early, dip_late, dip_early, lines, sems,
):
    planes, rows, cols = adj.shape[1:]
    grid = Grid(planes, rows, cols)
    copies = [
        pltpu.make_async_copy(a, b, sems.at[i])
        for i, (a, b) in enumerate(
            (
                (dip_late_in, dip_late),
                (late_in, late),
                (dip_early_in, dip_early),
                (early_in, early),
            )
        )
    ]
    per_chunk = -(-adj.shape[0] // (CHUNKS * grid.pack)) * grid.pack
    for i in range(CHUNKS):
        part = pl.ds(i * per_chunk, min(per_chunk, adj.shape[0] - i * per_chunk))
        copies.append(pltpu.make_async_copy(adj_in.at[part], adj.at[part], sems.at[4 + i]))
    for copy in copies:
        copy.start()
    for which, (saved, dip, out) in enumerate(((late, dip_late, fl), (early, dip_early, fe))):
        copies[2 * which].wait()
        copies[2 * which + 1].wait()

        for p in range(planes):
            flows = [None] * 19
            rho = []
            for s in range(3):
                total = None
                for q in range(19):
                    v = saved[s * 19 + q, p].astype(F32)
                    flows[q] = plus(flows[q], v)
                    total = plus(total, v)
                rho.append(total)
                out[s, p] = total
                out[9 + s, p] = psi_of(total)
            inverse = 1.0 / (rho[0] + rho[1] + rho[2])
            for d in range(3):
                momentum = None
                for q in range(19):
                    if VELOCITY[q][d] != 0:
                        momentum = plus(momentum, flows[q] if VELOCITY[q][d] > 0 else -flows[q])
                out[3 + d, p] = momentum * inverse
                out[6 + d, p] = dip[d, p].astype(F32)
    pops = adj.shape[0]
    components = pops + 18
    slot = grid.lane // grid.group
    for g in range(own_left.shape[0]):
        if g * grid.pack % per_chunk == 0 and g * grid.pack < pops:
            copies[4 + g * grid.pack // per_chunk].wait()
        left = right = jnp.zeros((rows, cols), F32)
        for j in range(grid.pack):
            c = g * grid.pack + j
            if c >= components:
                continue
            for p in range(planes):
                if c < pops:
                    v = adj[c, p]
                elif c < pops + 9:
                    v = fl[c - pops, p]
                else:
                    v = fe[c - pops - 9, p]
                at = p * grid.pack + j
                rolled = pltpu.roll(v, at * grid.group, 1) if at else v
                here, prior = [
                    grid.once(("slot", k), lambda: slot == k)
                    for k in (at, (at - 1) % (cols // grid.group))
                ]
                left = jnp.where(here, rolled, left)
                right = jnp.where(prior, rolled, right)
        own_left[g] = left
        own_right[g] = right
    low = lax.rem(grid.lane, grid.group) < HALO
    even = parity_of("gy") == 0
    for h in range(send_c.shape[0]):
        left = jnp.where(low, own_left[2 * h], pltpu.roll(own_left[2 * h + 1], HALO, 1))
        right = jnp.where(low, pltpu.roll(own_right[2 * h + 1], cols - HALO, 1), own_right[2 * h])
        send_c[h] = jnp.where(even, right, left)
        send_d[h] = jnp.where(even, left, right)
    pack_static((adj, fl, fe), planes, rows, lines, parity_of("gx"))
    lines_to(send_a, send_b, lines)


def inside_collision(grid, tile, load, fields, hold, ab, kept):
    forces = brick_forces(grid, tile, fields, None, 0, 0)
    brick_collision(grid, tile, load, None, fields, forces, hold, ab, kept)
    at_rim = grid.at_rim()
    for k in range(9):
        tile.put(hold, k, jnp.where(at_rim, 0.0, tile.get(hold, k)))


def second_row(grid, tile, fields, hold, ab, kept, sides):
    low = grid.low()
    rest = 1.0 - 1.0 / RELAXATION[2]
    back = spread_inside(grid, tile, hold, fields)
    alpha = [tile.get(ab, s) + (1.0 - tile.get(fields, 9 + s)) * back[s] for s in range(3)]
    beta = [tile.get(ab, 3 + d) for d in range(3)]
    ahead = -grid.outward() * beta[0]
    for s in range(3):
        tile.put(sides, s, back[s])
    for s in range(2):
        tile.put(sides, 3 + s, alpha[s] + ahead)
        tile.put(sides, 5 + s, beta[1 + s])
    for j, yz in enumerate(CROSS):
        v = rest * jnp.where(low, tile.get(kept, AHEAD[j]), tile.get(kept, BEHIND[j]))
        v = v + (alpha[2] + ahead)
        tile.put(sides, 7 + j, v + mixed(yz, beta[1:]) if j else v)


def inside_kernel(adj, fl, sides, hold, ab, kept):
    planes, rows, cols = adj.shape[1:]
    grid = Grid(planes, rows, cols)
    load = lambda tile: lambda c, dz: tile.get(adj, c, dz)
    grid.over_main(lambda tile: inside_collision(grid, tile, load(tile), fl, hold, ab, kept))
    grid.over_main(lambda tile: second_row(grid, tile, fl, hold, ab, kept, sides))


def edge_kernel(
    own_left, own_right, recv_c, recv_d, sides_main,
    send_a, send_b, edge, fl, fe, lines, hold, ab, kept, sides,
):
    planes, rows, cols = sides_main.shape[1:]
    pops = edge.shape[0]
    grid = Grid(planes, rows, cols)
    even = parity_of("gy") == 0
    slot = lax.rem(grid.lane // grid.group, grid.pack)
    left_half = grid.left_half()
    components = pops + 18
    for g in range(own_left.shape[0]):
        first, second = recv_c[g // 2], recv_d[g // 2]
        from_next = jnp.where(even, first, second)
        from_prior = jnp.where(even, second, first)
        if g % 2:
            from_next = pltpu.roll(from_next, cols - HALO, 1)
            from_prior = pltpu.roll(from_prior, HALO, 1)
        for j in range(grid.pack):
            c = g * grid.pack + j
            if c >= components:
                continue
            before = grid.once(("slot", j), lambda: slot == (j - 1) % grid.pack)
            low = jnp.where(before, from_prior, own_left[g])
            high = jnp.where(before, own_right[g], from_next)
            v = jnp.where(
                left_half,
                pltpu.roll(low, ((1 - j) * grid.group) % cols, 1),
                pltpu.roll(high, ((3 - j) * grid.group) % cols, 1),
            )
            if c < pops:
                edge[c] = v
            else:
                field, k = (fl, c - pops) if c < pops + 9 else (fe, c - pops - 9)
                field[k] = v
                if k < 3:
                    field[9 + k] = psi_of(v)
    adj, fields, both = Pair(None, edge), Pair(None, fl), Pair(sides_main, sides)
    hold, ab, kept = Pair(None, hold), Pair(None, ab), Pair(None, kept)

    def inside(tile):
        load = lambda c, dz: tile.get(adj, c, dz)
        inside_collision(grid, tile, load, fields, hold, ab, kept)
        second_row(grid, tile, fields, hold, ab, kept, both)

    grid.over_edge(inside)
    parity = parity_of("gx")
    kinds = (edge, fl, fe)
    rows_of = list(static_rows())
    low = grid.low()
    fill = 0
    for depth, members in corner_groups(grid.pack):
        v = None
        for j, c in enumerate(members):
            kind, above, below, unused = rows_of[c]
            one = kinds[kind][above]
            if above != below:
                one = jnp.where(low, kinds[kind][below], one)
            one = grid.turn(one, j * grid.group)
            v = one if j == 0 else jnp.where(grid.corners(j), one, v)
        lines[parity, fill : fill + 1, :] = v[rows - 1 - depth : rows - depth, :]
        lines[1 - parity, fill : fill + 1, :] = v[depth : depth + 1, :]
        fill += 1
    for c in range(DYNAMIC):
        depth = 0 if c < 3 else 1
        for t in range(grid.tiles):
            v = both.at(c, t)
            lines[parity, fill : fill + 1, :] = v[rows - 1 - depth : rows - depth, :]
            lines[1 - parity, fill : fill + 1, :] = v[depth : depth + 1, :]
            fill += 1
    lines_to(send_a, send_b, lines)


def first_step(grid, tile, adj, fl, rims, hold, ab, kept, hold_rim, ab_rim, kept_rim):
    forces = brick_forces(grid, tile, fl, rims, LATE_PSI, LATE + 6)
    load = lambda c, dz: tile.get(adj, c, dz)
    brick_collision(grid, tile, load, rims, fl, forces, hold, ab, kept)
    forces = rim_forces(grid, tile, fl, rims, LATE_PSI, LATE)
    rho, u = [[tile.get(rims, LATE + at + d) for d in range(3)] for at in (0, 3)]
    psi = [tile.get(rims, LATE_PSI + s) for s in range(3)]
    rim_collision(
        grid,
        tile,
        lambda s, i, dz: tile.get(rims, ALONG + s * 9 + i, dz),
        lambda s, j, dz: tile.get(rims, AFTER + s * 5 + j, dz),
        load,
        rho,
        u,
        psi,
        forces,
        hold_rim,
        ab_rim,
        kept_rim,
    )


def early_forces(grid, tile, fe, rims, forces, forces_rim):
    brick = brick_forces(grid, tile, fe, rims, EARLY_PSI, EARLY + 6)
    beyond = rim_forces(grid, tile, fe, rims, EARLY_PSI, EARLY)
    for s in range(3):
        for d in range(3):
            tile.put(forces, 3 * s + d, brick[s][d])
            tile.put(forces_rim, 3 * s + d, beyond[s][d])


def rim_psis(grid, tile, rims):
    for s in range(3):
        tile.put(rims, LATE_PSI + s, psi_of(tile.get(rims, LATE + s)))
        tile.put(rims, EARLY_PSI + s, psi_of(tile.get(rims, EARLY + s)))


def finish_first(grid, tile, fl, rims, hold, ab, kept, hold_rim, ab_rim, mid, part):
    rest = 1.0 - 1.0 / RELAXATION[2]
    sign, at_rim = rim_sign(grid), grid.at_rim()
    own_dip, rim_dip = (fl, 6), (rims, LATE + 6)
    dip = [tile.get(fl, 6 + d) for d in range(3)]
    dip_rim = [tile.get(rims, LATE + 6 + d) for d in range(3)]
    dip_far = [tile.get(rims, LATE + FAR + 3 + d) for d in range(3)]
    back = spread_inside(grid, tile, hold, fl)
    inward = hand_over(grid, tile, hold_rim, rim_dip, dip, sign)
    alpha = [
        tile.get(ab, s)
        + (1.0 - tile.get(fl, 9 + s)) * (back[s] + jnp.where(at_rim, inward[s], 0.0))
        for s in range(3)
    ]
    beta = [tile.get(ab, 3 + d) for d in range(3)]
    for q in range(19):
        along = mixed(VELOCITY[q], beta) if q != 16 else None
        for s in range(3):
            v = alpha[s] if along is None else alpha[s] + along
            if s == 2:
                v = v + rest * tile.get(kept, q)
            tile.put(mid, s * 19 + q, v)
    given = hand_over(grid, tile, hold, own_dip, dip_rim, -sign)
    level = spread_level(grid, tile, hold_rim, *rim_dip)
    after = hand_over(grid, tile, hold_rim, rim_dip, dip_far, -sign)
    for s in range(3):
        open_share = 1.0 - tile.get(rims, LATE_PSI + s)
        tile.put(part, s, tile.get(ab_rim, s) + open_share * (given[s] + level[s]))
        tile.put(part, 3 + s, tile.get(ab_rim, 3 + s))
        tile.put(part, 6 + s, (1.0 - tile.get(rims, LATE + FAR + s)) * after[s])


def main_kernel(
    adj, fl, fe, recv_a, recv_b, after,
    rims, mid, part, kept_rim, forces, forces_rim, known, lines, hold, ab, kept, hold_rim, ab_rim,
):
    planes, rows, cols = adj.shape[1:]
    grid = Grid(planes, rows, cols)
    lines_from(recv_a, recv_b, parity_of("gx"), lines)
    for c in range(STATIC):
        for p in range(planes):
            k = c * planes + p
            rims[c, p] = grid.sides(lines[0, k : k + 1, :], lines[1, k : k + 1, :])
    grid.over_main(lambda tile: rim_psis(grid, tile, rims))
    for c in range(STATIC):
        v = None
        for p in range(planes):
            one = grid.turn(rims[c, p], p * grid.width + 2 * grid.group)
            v = one if p == 0 else jnp.where(grid.plane_lanes(p), one, v)
        known[c] = jnp.where(grid.left_half(), grid.turn(v, -grid.group), grid.turn(v, grid.group))

    def step(tile):
        first_step(grid, tile, adj, fl, rims, hold, ab, kept, hold_rim, ab_rim, kept_rim)
        early_forces(grid, tile, fe, rims, forces, forces_rim)

    grid.over_main(step)
    grid.over_main(
        lambda tile: finish_first(
            grid, tile, fl, rims, hold, ab, kept, hold_rim, ab_rim, mid, part
        )
    )


def last_kernel(
    fe_m, rims_m, mid_m, part_m, kept_rim_m, forces_m, forces_rim_m, known, edge, fl_e, fe_e,
    recv_a, recv_b, out,
    rims_e, mid_e, part_e, kept_rim_e, forces_e, forces_rim_e, hold_e, ab_e, kept_e, hold_rim_e,
    ab_rim_e, patches, lines, near, rim_mid, rim_level, rim_far, hold2, hold_rim2, ab2, kept2,
    total, staged, sems,
):
    planes, rows, cols = fe_m.shape[1:]
    grid = Grid(planes, rows, cols)
    lines_from(recv_a, recv_b, parity_of("gx"), lines)
    is_corner = grid.corners(0)
    corner_lines = 0
    for k, (unused, members) in enumerate(corner_groups(grid.pack)):
        v = grid.sides(lines[0, k : k + 1, :], lines[1, k : k + 1, :])
        for j, c in enumerate(members):
            rims_e[c] = jnp.where(is_corner, grid.turn(v, -j * grid.group), known[c])
        corner_lines += 1
    for c in range(DYNAMIC):
        for t in range(grid.tiles):
            k = corner_lines + c * grid.tiles + t
            near[c, t] = grid.sides(lines[0, k : k + 1, :], lines[1, k : k + 1, :])
    fe, rims, mid = Pair(fe_m, fe_e), Pair(rims_m, rims_e), Pair(mid_m, mid_e)
    part, kept_rim = Pair(part_m, part_e), Pair(kept_rim_m, kept_rim_e)
    forces, forces_rim = Pair(forces_m, forces_e), Pair(forces_rim_m, forces_rim_e)
    rest = 1.0 - 1.0 / RELAXATION[2]
    at_rim = grid.at_rim()
    sign = rim_sign(grid)
    outward = grid.outward()

    def edge_steps(tile):
        adj, fl = Pair(None, edge), Pair(None, fl_e)
        hold, ab, kept = Pair(None, hold_e), Pair(None, ab_e), Pair(None, kept_e)
        hold_rim, ab_rim = Pair(None, hold_rim_e), Pair(None, ab_rim_e)
        rim_psis(grid, tile, rims)
        first_step(grid, tile, adj, fl, rims, hold, ab, kept, hold_rim, ab_rim, kept_rim)
        early_forces(grid, tile, fe, rims, forces, forces_rim)
        finish_first(grid, tile, fl, rims, hold, ab, kept, hold_rim, ab_rim, mid, part)

    grid.over_edge(edge_steps)

    def complete(tile):
        t = tile.index
        alpha = [
            tile.get(part, s) + (1.0 - tile.get(rims, LATE_PSI + s)) * near[s, t]
            for s in range(3)
        ]
        beta = [tile.get(part, 3 + d) for d in range(3)]
        far = [near[3 + s, t] + tile.get(part, 6 + s) for s in range(2)]
        far_beta = [near[5 + d, t] for d in range(2)]
        ahead = outward * beta[0]
        for j, yz in enumerate(CROSS):
            side = mixed(yz, beta[1:]) if j else None
            side_far = mixed(yz, far_beta) if j else None
            for s in range(3):
                v = plus(side, alpha[s] + ahead)
                if s == 2:
                    v = v + rest * tile.get(kept_rim, 9 + j)
                    rim_far[10 + j, t] = near[7 + j, t] + tile.get(part, 8)
                else:
                    rim_far[s * 5 + j, t] = plus(side_far, far[s])
                rim_mid[s * 5 + j, t] = v
        for i, q in enumerate(LEVEL):
            side = mixed(VELOCITY[q][1:], beta[1:]) if q != 16 else None
            for s in range(3):
                v = plus(side, alpha[s])
                if s == 2:
                    v = v + rest * tile.get(kept_rim, i)
                rim_level[s * 9 + i, t] = v

    grid.over(complete)

    def collide(tile):
        load = lambda c, dz: tile.get(mid, c, dz)
        known = [[tile.get(forces, 3 * s + d) for d in range(3)] for s in range(3)]
        brick_collision(grid, tile, load, rim_mid, fe, known, hold2, ab2, kept2)
        known = [[tile.get(forces_rim, 3 * s + d) for d in range(3)] for s in range(3)]
        rho, u = [[tile.get(rims, EARLY + at + d) for d in range(3)] for at in (0, 3)]
        psi = [tile.get(rims, EARLY_PSI + s) for s in range(3)]
        rim_collision(
            grid,
            tile,
            lambda s, i, dz: tile.get(rim_level, s * 9 + i, dz),
            lambda s, j, dz: tile.get(rim_far, s * 5 + j, dz),
            load,
            rho,
            u,
            psi,
            known,
            hold_rim2,
            None,
            None,
        )

    grid.over(collide)

    def finish(tile):
        back = spread_inside(grid, tile, hold2, fe)
        dip = [tile.get(fe, 6 + d) for d in range(3)]
        inward = hand_over(grid, tile, hold_rim2, (rims, EARLY + 6), dip, sign)
        for s in range(3):
            x = back[s] + jnp.where(at_rim, inward[s], 0.0)
            total[s, tile.index] = tile.get(ab2, s) + (1.0 - tile.get(fe, 9 + s)) * x

    grid.over(finish)
    at_side = (grid.lane < HALO) | (grid.lane >= cols - HALO)
    first_group = lax.rem(grid.lane, grid.width) < grid.group
    sources = [total.at[s] for s in range(3)] + [ab2.at[3 + d] for d in range(3)]
    sources += [kept2.at[q] for q in range(19)]
    for i, ref in enumerate(sources):
        v = ref[planes]
        patches[i] = jnp.where(first_group, pltpu.roll(v, cols - 2 * grid.group, 1), v)
    copies = []
    for p in range(planes):
        turn = (cols - p * grid.width - grid.group) % cols

        def patched(i):
            return jnp.where(at_side, pltpu.roll(patches[i], turn, 1), sources[i][p])

        alpha = [patched(s) for s in range(3)]
        beta = [patched(3 + d) for d in range(3)]
        for q in range(19):
            along = mixed(VELOCITY[q], beta) if q != 16 else None
            for s in range(3):
                v = alpha[s] if along is None else alpha[s] + along
                if s == 2:
                    v = v + rest * patched(6 + q)
                staged[s * 19 + q, p] = v
        copies.append(pltpu.make_async_copy(staged.at[:, p], out.at[:, p], sems.at[p]))
        copies[p].start()
    for copy in copies:
        copy.wait()


def call(kernel, outs, scratch, args, in_hbm=False, out_hbm=False, cost=0):
    vmem = pl.BlockSpec(memory_space=pltpu.VMEM)
    hbm = pl.BlockSpec(memory_space=pltpu.HBM)
    return pl.pallas_call(
        kernel,
        out_shape=[jax.ShapeDtypeStruct(s, F32) for s in outs],
        in_specs=[hbm if in_hbm else vmem] * len(args),
        out_specs=[hbm if out_hbm else vmem] * len(outs),
        scratch_shapes=[pltpu.VMEM(s, F32) if isinstance(s, tuple) else s for s in scratch],
        compiler_params=pltpu.CompilerParams(vmem_limit_bytes=VMEM_BYTES),
        cost_estimate=pl.CostEstimate(flops=cost, bytes_accessed=cost, transcendentals=0),
    )(*[pltpu.with_memory_space_constraint(x, pltpu.HBM) if in_hbm else x for x in args])


def swap(block, axis, offset):
    size = lax.axis_size(axis)
    route = []
    for i in range(offset, size + offset, 2):
        a, b = i % size, (i + 1) % size
        route += [(a, b), (b, a)]
    return lax.ppermute(block, axis, route)


def shards(adjoint_in, populations_early, populations_late, dipoles_early, dipoles_late):
    pops, planes, rows, cols = adjoint_in.shape
    tile = (rows, cols)
    pack = cols // planes // (2 * HALO)
    groups = -(-(pops + 18) // pack)
    groups += groups % 2

    def lines(n):
        return (-(-n // 8) * 8, cols)

    def main(*counts):
        return [(n, planes) + tile for n in counts]

    def edges(*counts):
        return [(n,) + tile for n in counts]

    def tiled(*counts):
        return [(n, planes + 1) + tile for n in counts]

    static = lines(STATIC * planes)
    second = lines(len(list(corner_groups(pack))) + DYNAMIC * (planes + 1))
    send_c, send_d, own_left, own_right, fl_m, fe_m, adj, send_a, send_b = call(
        pack_columns_kernel,
        edges(groups // 2, groups // 2, groups, groups) + main(12, 12, pops) + [static] * 2,
        [
            pltpu.VMEM(x.shape, x.dtype)
            for x in (populations_late, populations_early, dipoles_late, dipoles_early)
        ]
        + [(2,) + static, pltpu.SemaphoreType.DMA((4 + CHUNKS,))],
        [adjoint_in, populations_late, populations_early, dipoles_late, dipoles_early],
        in_hbm=True,
    )
    static_a, static_b = swap(send_a, "gx", 1), swap(send_b, "gx", 0)
    recv_c, recv_d = swap(send_c, "gy", 1), swap(send_d, "gy", 0)
    (sides,) = call(
        inside_kernel, main(DYNAMIC), main(9, 6, 19), [adj, fl_m], cost=INSIDE_COST
    )
    send_a, send_b, edge, fl_e, fe_e = call(
        edge_kernel,
        [second] * 2 + edges(pops, 12, 12),
        [(2,) + second] + edges(9, 6, 19, DYNAMIC),
        [own_left, own_right, recv_c, recv_d, sides],
        cost=EDGE_COST,
    )
    recv_a, recv_b = swap(send_a, "gx", 1), swap(send_b, "gx", 0)
    known = (RIMS, pops, 9, 14, 9, 9)
    mains = call(
        main_kernel,
        main(*known) + edges(STATIC),
        [(2,) + static] + main(9, 6, 19, 9, 6),
        [adj, fl_m, fe_m, static_a, static_b, fl_e],
        cost=MAIN_COST,
    )
    (out,) = call(
        last_kernel,
        [(pops, planes) + tile],
        edges(*known, 9, 6, 19, 9, 6, 25)
        + [(2,) + second]
        + tiled(DYNAMIC, 15, 27, 15, 9, 9, 6, 19, 3)
        + main(pops)
        + [pltpu.SemaphoreType.DMA((planes,))],
        [fe_m, *mains, edge, fl_e, fe_e, recv_a, recv_b],
        out_hbm=True,
    )
    return out


def solution(mesh):
    placed = P(None, None, "gx", "gy")
    return jax.shard_map(
        shards, mesh=mesh, in_specs=(placed,) * 5, out_specs=placed, check_vma=False
    )
```

```python
import jax
import jax.numpy as jnp
from jax import lax
from jax.experimental import pallas as pl
from jax.experimental.pallas import tpu as pltpu
from jax.sharding import PartitionSpec as P

VELOCITY = (
    (1, 0, 0),
    (-1, 0, 0),
    (0, 1, 0),
    (0, -1, 0),
    (1, 1, 0),
    (-1, -1, 0),
    (1, -1, 0),
    (-1, 1, 0),
    (1, 0, 1),
    (-1, 0, -1),
    (1, 0, -1),
    (-1, 0, 1),
    (0, 1, 1),
    (0, -1, -1),
    (0, 1, -1),
    (0, -1, 1),
    (0, 0, 0),
    (0, 0, 1),
    (0, 0, -1),
)
INDEX = {c: q for q, c in enumerate(VELOCITY)}
W1, W2, W0 = 1.0 / 18.0, 1.0 / 36.0, 1.0 / 3.0
RELAXATION = (1.0, 1.0, 1.25)
COUPLING = ((0.0, 1.2, -0.6), (1.2, 0.0, -0.6), (-0.6, -0.6, -0.3))
CROSS = ((0, 0), (1, 0), (-1, 0), (0, 1), (0, -1))
AHEAD = tuple(INDEX[(1,) + yz] for yz in CROSS)
BEHIND = tuple(INDEX[(-1,) + yz] for yz in CROSS)
SIDE = ((1, 0), (-1, 0), (0, 1), (0, -1), (1, 1), (-1, -1), (1, -1), (-1, 1))
LEVEL = tuple(q for q in range(19) if VELOCITY[q][0] == 0)
ALONG, AFTER, LATE, EARLY = 15, 42, 57, 72
STATIC = 87
FAR = 9
LATE_PSI, EARLY_PSI = STATIC, STATIC + 3
RIMS = STATIC + 6
DYNAMIC = 12
F32 = jnp.float32
CHUNKS = 4
INSIDE_COST, EDGE_COST, MAIN_COST = 10**7, 10**8, 10**8
VMEM_BYTES = 40 * 1024 * 1024
HALO = 4


class Grid:
    def __init__(self, planes, rows, cols):
        self.planes, self.rows, self.cols = planes, rows, cols
        self.tiles = planes + 1
        self.width = cols // planes
        self.group = 2 * HALO
        self.pack = self.width // self.group
        self.sub = lax.broadcasted_iota(jnp.int32, (rows, cols), 0)
        self.lane = lax.broadcasted_iota(jnp.int32, (rows, cols), 1)
        self.masks = {}

    def once(self, name, make):
        if name not in self.masks:
            self.masks[name] = make()
        return self.masks[name]

    def in_width(self):
        return self.once("width", lambda: lax.rem(self.lane, self.width))

    def left_half(self):
        return self.once("left", lambda: self.in_width() < self.width // 2)

    def roll_rows(self, v, dx):
        return pltpu.roll(v, (-dx) % self.rows, 0)

    def roll_cols(self, v, dy):
        return pltpu.roll(v, (-dy) % self.cols, 1)

    def at_row(self, v, rim, dx):
        edge = self.rows - 1 if dx > 0 else 0
        return jnp.where(self.sub == edge, rim, self.roll_rows(v, dx))

    def in_row(self, v, dx):
        edge = self.rows - 1 if dx > 0 else 0
        return jnp.where(self.sub == edge, 0.0, self.roll_rows(v, dx))

    def sides(self, low, high):
        return jnp.where(self.sub == 0, low, high)

    def over_main(self, body):
        for p in range(self.planes):
            body(Tile(self, p, False))

    def over_edge(self, body):
        body(Tile(self, self.planes, True))

    def over(self, body):
        self.over_main(body)
        self.over_edge(body)

    def at_rim(self):
        return self.once("rim", lambda: (self.sub == 0) | (self.sub == self.rows - 1))

    def low(self):
        return self.once("low", lambda: self.sub < self.rows // 2)

    def outward(self):
        return self.once("out", lambda: jnp.where(self.low(), -1.0, 1.0).astype(F32))


class Tile:
    def __init__(self, grid, index, edge):
        self.grid, self.index, self.edge = grid, index, edge

    def of(self, dz):
        if dz == 0 or self.edge:
            return self.index
        return (self.index + dz) % self.grid.planes

    def get(self, ref, c, dz=0):
        if isinstance(ref, Pair):
            v = ref.edge[c] if self.edge else ref.main[c, self.of(dz)]
        else:
            v = ref[c, self.of(dz)]
        if self.edge and dz != 0:
            v = self.grid.roll_cols(v, dz * self.grid.width)
        return v

    def put(self, ref, c, v):
        if not isinstance(ref, Pair):
            ref[c, self.index] = v
        elif self.edge:
            ref.edge[c] = v
        else:
            ref.main[c, self.index] = v


class Pair:
    def __init__(self, main, edge):
        self.main, self.edge = main, edge

    def at(self, c, t):
        return self.edge[c] if t == self.main.shape[1] else self.main[c, t]


def plus(a, b):
    return b if a is None else a + b


def mixed(coefficients, values):
    total = None
    for k, v in zip(coefficients, values):
        if k == 0:
            continue
        term = v if k == 1 else (-v if k == -1 else k * v)
        total = plus(total, term)
    return total


def axis_pairs():
    for q in (0, 2, 17, 4, 6, 8, 10, 12, 14):
        c = VELOCITY[q]
        yield c, (W1 if sum(abs(i) for i in c) == 1 else W2)


def first_and_second(diff, total):
    first = [None] * 3
    second = {}
    for c, w in axis_pairs():
        for d in range(3):
            if c[d] == 0:
                continue
            if diff is not None and diff[c] is not None:
                first[d] = plus(first[d], (w * c[d]) * diff[c])
            if total is not None and total[c] is not None:
                for e in range(d, 3):
                    if c[e] != 0:
                        second[d, e] = plus(second.get((d, e)), (w * c[d] * c[e]) * total[c])
    return first, second


PAIRS = tuple((d, e) for d in range(3) for e in range(d, 3))


def moments_of(streamed):
    diff, total = {}, {}
    for c, w in axis_pairs():
        a, b = streamed[INDEX[c]], streamed[INDEX[tuple(-i for i in c)]]
        if a is None or b is None:
            diff[c] = a if b is None else -b
            total[c] = b if a is None else a
        else:
            diff[c], total[c] = a - b, a + b
    first, second = first_and_second(diff, total)
    zeroth = None if streamed[16] is None else W0 * streamed[16]
    for c, w in axis_pairs():
        if total[c] is not None:
            zeroth = plus(zeroth, w * total[c])
    return [zeroth] + first + [second.get(k) for k in PAIRS]


def summed(known, change):
    return [k if x is None else k + x for k, x in zip(known, change)]


def turned(second, v):
    return [sum(second[min(d, e), max(d, e)] * v[e] for e in range(3)) for d in range(3)]


def dot(a, b):
    return a[0] * b[0] + a[1] * b[1] + a[2] * b[2]


def field_forces(grid, loads, across, dipole):
    memo = {}

    def source(name, dz, place):
        key = (name, dz, place)
        if key in memo:
            return memo[key]
        if isinstance(name, int):
            v = loads[place](name, dz)
        elif name == "chi":
            v = source(0, dz, place) - source(1, dz, place)
        elif name[0] == "V":
            v = source(2, dz, place) * source(3 + name[1], dz, place)
        else:
            c = name[1]
            v = mixed(c, [source(("V", d), dz, place) if c[d] else None for d in range(3)])
        memo[key] = v
        return v

    def shifted(name, c):
        key = (name, c, "shift")
        if key in memo:
            return memo[key]
        if c[1] != 0:
            v = grid.roll_cols(shifted(name, (c[0], 0, c[2])), c[1])
        elif c[0] != 0:
            v = across(lambda place, dz: source(name, dz, place), c[0], c[2])
        else:
            v = source(name, c[2], 0)
        memo[key] = v
        return v

    def parts(name):
        diff, total = {}, {}
        for c, w in axis_pairs():
            back = tuple(-i for i in c)
            a, b = shifted(name, c), shifted(name, back)
            diff[c], total[c] = a - b, a + b
        return diff, total

    diff, unused = parts(0)
    s0, unused = first_and_second(diff, None)
    diff, unused = parts(2)
    s2, unused = first_and_second(diff, None)
    diff, total = parts("chi")
    schi, second = first_and_second(diff, total)
    s1 = [a - b for a, b in zip(s0, schi)]
    pull = [None] * 3
    for c, w in axis_pairs():
        back = tuple(-i for i in c)
        if sum(abs(i) for i in c) == 1:
            name = ("V", [i for i in range(3) if c[i]][0])
        else:
            name = ("L", c)
        total_c = shifted(name, c) + shifted(name, back)
        for d in range(3):
            if c[d] != 0:
                pull[d] = plus(pull[d], (w * c[d]) * total_c)
    md = turned(second, dipole)
    k0 = [-1.2 * s1[d] + 0.6 * s2[d] - pull[d] for d in range(3)]
    k1 = [-1.2 * s0[d] + 0.6 * s2[d] + pull[d] for d in range(3)]
    k2 = [0.6 * (s0[d] + s1[d]) + 0.3 * s2[d] + md[d] for d in range(3)]
    return k0, k1, k2


def brick_forces(grid, tile, fields, rim, rim_psi, rim_dip):
    def own(c, dz):
        return tile.get(fields, (9 + c) if c < 3 else (3 + c), dz)

    def beyond(c, dz):
        return tile.get(rim, (rim_psi + c) if c < 3 else (rim_dip + c - 3), dz)

    def across(get, cx, dz):
        if rim is None:
            return grid.in_row(get(0, dz), cx)
        return grid.at_row(get(0, dz), get(1, dz), cx)

    return field_forces(grid, (own, beyond), across, [own(3 + d, 0) for d in range(3)])


def rim_forces(grid, tile, fields, rims, psi, base):
    outward = grid.outward()

    def loader(ref, psi_at, dip_at):
        def load(c, dz):
            v = tile.get(ref, (psi_at + c) if c < 3 else (dip_at + c - 3), dz)
            return v * outward if c == 3 else v

        return load

    loads = {
        0: loader(rims, psi, base + 6),
        1: loader(rims, base + FAR, base + FAR + 3),
        -1: loader(fields, 9, 6),
    }
    dipole = [loads[0](3 + d, 0) for d in range(3)]
    return field_forces(grid, loads, lambda get, cx, dz: get(cx, dz), dipole)


def collision_adjoint(moments, rho, u, psi, forces):
    inverse_sum = 1.0 / (rho[0] + rho[1] + rho[2])
    grad_u = [None] * 3
    alphas, held = [], []
    for s in range(3):
        m0, m1 = moments[s][0], moments[s][1:4]
        m2 = dict(zip(PAIRS, moments[s][4:]))
        inverse = 1.0 / rho[s]
        ratio = psi[s] * inverse
        tau = RELAXATION[s]
        k = forces[s]
        v = [u[d] + (tau * ratio) * k[d] for d in range(3)]
        mv = turned(m2, v)
        g = [3.0 * (m1[d] + 3.0 * mv[d] - m0 * v[d]) for d in range(3)]
        feq = m0 + 3.0 * dot(m1, v) + 4.5 * dot(mv, v) - 1.5 * m0 * dot(v, v)
        alphas.append(feq * (1.0 / tau) + dot(g, k) * (1.0 - psi[s] - ratio))
        scaled = rho[s] * (1.0 / tau)
        for d in range(3):
            grad_u[d] = plus(grad_u[d], scaled * g[d])
            held.append(psi[s] * g[d])
    beta = [grad_u[d] * inverse_sum for d in range(3)]
    along = dot(beta, u)
    return held, [a - along for a in alphas], beta


def brick_moments(grid, tile, load, rim, kept):
    def streamed_of(s):
        streamed = []
        for q in range(19):
            c = VELOCITY[q]
            v = load(s * 19 + q, c[2])
            if c[0] != 0:
                j = (AHEAD if c[0] > 0 else BEHIND).index(q)
                if rim is None:
                    v = grid.in_row(v, c[0])
                else:
                    v = grid.at_row(v, tile.get(rim, s * 5 + j, c[2]), c[0])
            if c[1] != 0:
                v = grid.roll_cols(v, c[1])
            streamed.append(v)
            if s == 2:
                tile.put(kept, q, v)
        return streamed

    return [moments_of(streamed_of(s)) for s in range(3)]


def crossing_moments(grid, tile, rim, kept):
    first, last = grid.sub == 0, grid.sub == grid.rows - 1

    def streamed_of(s):
        streamed = [None] * 19
        for j, (cy, cz) in enumerate(CROSS):
            v = tile.get(rim, s * 5 + j, cz)
            if cy != 0:
                v = grid.roll_cols(v, cy)
            streamed[AHEAD[j]] = jnp.where(last, v, 0.0)
            streamed[BEHIND[j]] = jnp.where(first, v, 0.0)
        if s == 2:
            for q in AHEAD + BEHIND:
                tile.put(kept, q, tile.get(kept, q) + streamed[q])
        return streamed

    return [moments_of(streamed_of(s)) for s in range(3)]


def brick_adjoint(tile, moments, fields, forces, hold, ab):
    rho, u, psi = [[tile.get(fields, at + d) for d in range(3)] for at in (0, 3, 9)]
    held, alpha, beta = collision_adjoint(moments, rho, u, psi, forces)
    for k in range(9):
        tile.put(hold, k, held[k])
    for s in range(3):
        tile.put(ab, s, alpha[s])
        tile.put(ab, 3 + s, beta[s])


def brick_collision(grid, tile, load, rim, fields, forces, hold, ab, kept):
    moments = brick_moments(grid, tile, load, rim, kept)
    brick_adjoint(tile, moments, fields, forces, hold, ab)


def rim_moments(grid, tile, level, after, inner, kept):
    low = grid.low()

    def streamed_of(s):
        streamed = []
        for q in range(19):
            c = VELOCITY[q]
            v = None
            if c[0] == 0 and level is not None:
                v = level(s, LEVEL.index(q), c[2])
            elif c[0] > 0 and after is not None:
                v = after(s, AHEAD.index(q), c[2])
            elif c[0] < 0 and inner is not None:
                j = BEHIND.index(q)
                v = jnp.where(low, inner(s * 19 + AHEAD[j], c[2]), inner(s * 19 + BEHIND[j], c[2]))
            if c[1] != 0 and v is not None:
                v = grid.roll_cols(v, c[1])
            streamed.append(v)
            if s == 2 and kept is not None and c[0] >= 0:
                tile.put(kept, LEVEL.index(q) if c[0] == 0 else 9 + AHEAD.index(q), v)
        return streamed

    return [moments_of(streamed_of(s)) for s in range(3)]


def rim_adjoint(grid, tile, moments, rho, u, psi, forces, hold, ab):
    outward = grid.outward()
    u = [u[0] * outward, u[1], u[2]]
    held, alpha, beta = collision_adjoint(moments, rho, u, psi, forces)
    for k in range(9):
        tile.put(hold, k, held[k] * outward if k % 3 == 0 else held[k])
    if ab is not None:
        for s in range(3):
            tile.put(ab, s, alpha[s])
            tile.put(ab, 3 + s, beta[s] * outward if s == 0 else beta[s])


def put_moments(tile, ref, moments):
    for s in range(3):
        for k in range(10):
            v = moments[s][k]
            tile.put(ref, s * 10 + k, jnp.zeros(ref.shape[-2:], F32) if v is None else v)


def get_moments(tile, ref):
    return [[tile.get(ref, s * 10 + k) for k in range(10)] for s in range(3)]


def spread_plane(grid, get_h, get_d, sign, pairs):
    memo = {}

    def source(dz):
        if dz in memo:
            return memo[dz]
        h = [[get_h(3 * s + d, dz) for d in range(3)] for s in range(3)]
        dip = [get_d(d, dz) for d in range(3)]
        if not isinstance(sign, int):
            for vec in h + [dip]:
                vec[0] = vec[0] * sign
        memo[dz] = (h, dip)
        return memo[dz]

    cx = sign if isinstance(sign, int) else 1
    r = [None] * 3
    w_vec = [None] * 3
    lanes = {}
    for cy, cz in pairs:
        w = W1 if abs(cx) + abs(cy) + abs(cz) == 1 else W2
        h, dip = source(cz)
        c = (cx, cy, cz)
        e = [mixed(c, h[s]) for s in range(3)]
        f = e[2] * mixed(c, dip)
        half = 0.6 * e[2]
        r0 = 1.2 * e[1] - half + f
        r1 = 1.2 * e[0] - half - f
        r2 = -0.6 * (e[0] + e[1]) - 0.3 * e[2]
        qv = e[0] - e[1]
        vals = [w * r0, w * r1, w * r2]
        wq = w * qv
        vals += [wq if cx != 0 else None, wq if cy != 0 else None, wq if cz != 0 else None]
        vals = [vals[0], vals[1], vals[2]] + [
            None if x is None else (x if k == 1 else -x) for x, k in zip(vals[3:], (cx, cy, cz))
        ]
        acc = lanes.setdefault(cy, [None] * 6)
        for i, x in enumerate(vals):
            if x is not None:
                acc[i] = plus(acc[i], x)
    total = [None] * 6
    for cy, acc in lanes.items():
        for i, x in enumerate(acc):
            if x is not None:
                total[i] = plus(total[i], x if cy == 0 else grid.roll_cols(x, cy))
    if not isinstance(sign, int):
        total[3] = total[3] * sign
    return total


def met(total, dipole):
    meet = None
    for d in range(3):
        if total[3 + d] is not None:
            meet = plus(meet, total[3 + d] * dipole[d])
    return [total[0], total[1], total[2] - meet]


def spread_inside(grid, tile, hold, fields):
    get_h = lambda k, dz: tile.get(hold, k, dz)
    get_d = lambda k, dz: tile.get(fields, 6 + k, dz)
    total = spread_plane(grid, get_h, get_d, 0, SIDE)
    for dx in (1, -1):
        part = spread_plane(grid, get_h, get_d, dx, CROSS)
        for i, x in enumerate(part):
            total[i] = plus(total[i], grid.in_row(x, dx))
    return met(total, [tile.get(fields, 6 + d) for d in range(3)])


def rim_sign(grid):
    return grid.once("sign", lambda: jnp.where(grid.at_rim(), grid.outward(), 0.0))


def hand_over(grid, tile, hold, hold_dip, target, sign):
    dip, at = hold_dip
    total = spread_plane(
        grid,
        lambda k, dz: tile.get(hold, k, dz),
        lambda k, dz: tile.get(dip, at + k, dz),
        sign,
        CROSS,
    )
    return met(total, target)


def spread_level(grid, tile, hold, dip, at):
    total = spread_plane(
        grid,
        lambda k, dz: tile.get(hold, k, dz),
        lambda k, dz: tile.get(dip, at + k, dz),
        0,
        SIDE,
    )
    return met(total, [tile.get(dip, at + d) for d in range(3)])


def parity_of(axis):
    return lax.rem(lax.axis_index(axis) + 1, 2)


def lines_from(first, second, parity, lines):
    lines[1 - parity] = first[...]
    lines[parity] = second[...]


def lines_to(first, second, lines):
    first[...] = lines[0]
    second[...] = lines[1]


def psi_of(rho):
    return 1.0 - jnp.exp(-rho)


def static_rows():
    for s in range(3):
        for j in range(5):
            yield 0, s * 19 + BEHIND[j], s * 19 + AHEAD[j], 0
    for s in range(3):
        for q in LEVEL:
            yield 0, s * 19 + q, s * 19 + q, 0
    for s in range(3):
        for j in range(5):
            yield 0, s * 19 + BEHIND[j], s * 19 + AHEAD[j], 1
    for kind in (1, 2):
        for c in range(9):
            yield kind, c, c, 0
        for c in (9, 10, 11, 6, 7, 8):
            yield kind, c, c, 1


def pack_static(get, tiles, rows, lines, parity):
    up, down = parity, 1 - parity
    fill = 0
    for kind, above, below, depth in static_rows():
        for t in tiles:
            v = get(kind, above, t)
            lines[up, fill : fill + 1, :] = v[rows - 1 - depth : rows - depth, :]
            v = get(kind, below, t)
            lines[down, fill : fill + 1, :] = v[depth : depth + 1, :]
            fill += 1
    return fill


def pack_columns_kernel(
    adj_in, late_in, early_in, dip_late_in, dip_early_in,
    send_c, send_d, own_left, own_right, fl, fe, adj, send_a, send_b,
    late, early, dip_late, dip_early, lines, sems,
):
    planes, rows, cols = adj.shape[1:]
    grid = Grid(planes, rows, cols)
    copies = [
        pltpu.make_async_copy(a, b, sems.at[i])
        for i, (a, b) in enumerate(
            (
                (dip_late_in, dip_late),
                (late_in, late),
                (dip_early_in, dip_early),
                (early_in, early),
            )
        )
    ]
    per_chunk = -(-adj.shape[0] // (CHUNKS * grid.pack)) * grid.pack
    for i in range(CHUNKS):
        part = pl.ds(i * per_chunk, min(per_chunk, adj.shape[0] - i * per_chunk))
        copies.append(pltpu.make_async_copy(adj_in.at[part], adj.at[part], sems.at[4 + i]))
    for copy in copies:
        copy.start()
    for which, (saved, dip, out) in enumerate(((late, dip_late, fl), (early, dip_early, fe))):
        copies[2 * which].wait()
        copies[2 * which + 1].wait()

        for p in range(planes):
            flows = [None] * 19
            rho = []
            for s in range(3):
                total = None
                for q in range(19):
                    v = saved[s * 19 + q, p].astype(F32)
                    flows[q] = plus(flows[q], v)
                    total = plus(total, v)
                rho.append(total)
                out[s, p] = total
                out[9 + s, p] = psi_of(total)
            inverse = 1.0 / (rho[0] + rho[1] + rho[2])
            for d in range(3):
                momentum = None
                for q in range(19):
                    if VELOCITY[q][d] != 0:
                        momentum = plus(momentum, flows[q] if VELOCITY[q][d] > 0 else -flows[q])
                out[3 + d, p] = momentum * inverse
                out[6 + d, p] = dip[d, p].astype(F32)
    pops = adj.shape[0]
    components = pops + 18
    slot = grid.lane // grid.group
    for g in range(own_left.shape[0]):
        if g * grid.pack % per_chunk == 0 and g * grid.pack < pops:
            copies[4 + g * grid.pack // per_chunk].wait()
        left = right = jnp.zeros((rows, cols), F32)
        for j in range(grid.pack):
            c = g * grid.pack + j
            if c >= components:
                continue
            for p in range(planes):
                if c < pops:
                    v = adj[c, p]
                elif c < pops + 9:
                    v = fl[c - pops, p]
                else:
                    v = fe[c - pops - 9, p]
                at = p * grid.pack + j
                rolled = pltpu.roll(v, at * grid.group, 1) if at else v
                here, prior = [
                    grid.once(("slot", k), lambda: slot == k)
                    for k in (at, (at - 1) % (cols // grid.group))
                ]
                left = jnp.where(here, rolled, left)
                right = jnp.where(prior, rolled, right)
        own_left[g] = left
        own_right[g] = right
    low = lax.rem(grid.lane, grid.group) < HALO
    even = parity_of("gy") == 0
    for h in range(send_c.shape[0]):
        left = jnp.where(low, own_left[2 * h], pltpu.roll(own_left[2 * h + 1], HALO, 1))
        right = jnp.where(low, pltpu.roll(own_right[2 * h + 1], cols - HALO, 1), own_right[2 * h])
        send_c[h] = jnp.where(even, right, left)
        send_d[h] = jnp.where(even, left, right)
    kinds = (adj, fl, fe)
    pack_static(lambda kind, c, t: kinds[kind][c, t], range(planes), rows, lines, parity_of("gx"))
    lines_to(send_a, send_b, lines)


def inside_collision(grid, tile, load, fields, hold, ab, kept):
    forces = brick_forces(grid, tile, fields, None, 0, 0)
    brick_collision(grid, tile, load, None, fields, forces, hold, ab, kept)
    at_rim = grid.at_rim()
    for k in range(9):
        tile.put(hold, k, jnp.where(at_rim, 0.0, tile.get(hold, k)))


def second_row(grid, tile, fields, hold, ab, kept, sides):
    low = grid.low()
    rest = 1.0 - 1.0 / RELAXATION[2]
    back = spread_inside(grid, tile, hold, fields)
    alpha = [tile.get(ab, s) + (1.0 - tile.get(fields, 9 + s)) * back[s] for s in range(3)]
    beta = [tile.get(ab, 3 + d) for d in range(3)]
    ahead = -grid.outward() * beta[0]
    for s in range(3):
        tile.put(sides, s, back[s])
    for s in range(2):
        tile.put(sides, 3 + s, alpha[s] + ahead)
        tile.put(sides, 5 + s, beta[1 + s])
    for j, yz in enumerate(CROSS):
        v = rest * jnp.where(low, tile.get(kept, AHEAD[j]), tile.get(kept, BEHIND[j]))
        v = v + (alpha[2] + ahead)
        tile.put(sides, 7 + j, v + mixed(yz, beta[1:]) if j else v)


def inside_kernel(adj, fl, sides, hold, ab, kept):
    planes, rows, cols = adj.shape[1:]
    grid = Grid(planes, rows, cols)
    load = lambda tile: lambda c, dz: tile.get(adj, c, dz)
    grid.over_main(lambda tile: inside_collision(grid, tile, load(tile), fl, hold, ab, kept))
    grid.over_main(lambda tile: second_row(grid, tile, fl, hold, ab, kept, sides))


def edge_kernel(
    own_left, own_right, recv_c, recv_d, sides_main,
    send_a, send_b, edge, fl, fe, lines, hold, ab, kept, sides,
):
    planes, rows, cols = sides_main.shape[1:]
    pops = edge.shape[0]
    grid = Grid(planes, rows, cols)
    even = parity_of("gy") == 0
    slot = lax.rem(grid.lane // grid.group, grid.pack)
    left_half = grid.left_half()
    components = pops + 18
    for g in range(own_left.shape[0]):
        first, second = recv_c[g // 2], recv_d[g // 2]
        from_next = jnp.where(even, first, second)
        from_prior = jnp.where(even, second, first)
        if g % 2:
            from_next = pltpu.roll(from_next, cols - HALO, 1)
            from_prior = pltpu.roll(from_prior, HALO, 1)
        for j in range(grid.pack):
            c = g * grid.pack + j
            if c >= components:
                continue
            before = grid.once(("slot", j), lambda: slot == (j - 1) % grid.pack)
            low = jnp.where(before, from_prior, own_left[g])
            high = jnp.where(before, own_right[g], from_next)
            v = jnp.where(
                left_half,
                pltpu.roll(low, ((1 - j) * grid.group) % cols, 1),
                pltpu.roll(high, ((3 - j) * grid.group) % cols, 1),
            )
            if c < pops:
                edge[c] = v
            else:
                field, k = (fl, c - pops) if c < pops + 9 else (fe, c - pops - 9)
                field[k] = v
                if k < 3:
                    field[9 + k] = psi_of(v)
    adj, fields, both = Pair(None, edge), Pair(None, fl), Pair(sides_main, sides)
    hold, ab, kept = Pair(None, hold), Pair(None, ab), Pair(None, kept)

    def inside(tile):
        load = lambda c, dz: tile.get(adj, c, dz)
        inside_collision(grid, tile, load, fields, hold, ab, kept)
        second_row(grid, tile, fields, hold, ab, kept, both)

    grid.over_edge(inside)
    kinds = (edge, fl, fe)
    parity = parity_of("gx")
    fill = pack_static(lambda kind, c, t: kinds[kind][c], (0,), rows, lines, parity)
    for c in range(DYNAMIC):
        depth = 0 if c < 3 else 1
        for t in range(grid.tiles):
            v = both.at(c, t)
            lines[parity, fill : fill + 1, :] = v[rows - 1 - depth : rows - depth, :]
            lines[1 - parity, fill : fill + 1, :] = v[depth : depth + 1, :]
            fill += 1
    lines_to(send_a, send_b, lines)


def first_step(grid, tile, adj, fl, rims, hold, ab, kept, hold_rim, ab_rim, kept_rim):
    forces = brick_forces(grid, tile, fl, rims, LATE_PSI, LATE + 6)
    load = lambda c, dz: tile.get(adj, c, dz)
    brick_collision(grid, tile, load, rims, fl, forces, hold, ab, kept)
    forces = rim_forces(grid, tile, fl, rims, LATE_PSI, LATE)
    rho, u = [[tile.get(rims, LATE + at + d) for d in range(3)] for at in (0, 3)]
    psi = [tile.get(rims, LATE_PSI + s) for s in range(3)]
    moments = rim_moments(
        grid,
        tile,
        lambda s, i, dz: tile.get(rims, ALONG + s * 9 + i, dz),
        lambda s, j, dz: tile.get(rims, AFTER + s * 5 + j, dz),
        load,
        kept_rim,
    )
    rim_adjoint(grid, tile, moments, rho, u, psi, forces, hold_rim, ab_rim)


def early_forces(grid, tile, fe, rims, forces, forces_rim):
    brick = brick_forces(grid, tile, fe, rims, EARLY_PSI, EARLY + 6)
    beyond = rim_forces(grid, tile, fe, rims, EARLY_PSI, EARLY)
    for s in range(3):
        for d in range(3):
            tile.put(forces, 3 * s + d, brick[s][d])
            tile.put(forces_rim, 3 * s + d, beyond[s][d])


def rim_psis(grid, tile, rims):
    for s in range(3):
        tile.put(rims, LATE_PSI + s, psi_of(tile.get(rims, LATE + s)))
        tile.put(rims, EARLY_PSI + s, psi_of(tile.get(rims, EARLY + s)))


def finish_first(grid, tile, fl, rims, hold, ab, kept, hold_rim, ab_rim, mid, part):
    rest = 1.0 - 1.0 / RELAXATION[2]
    sign, at_rim = rim_sign(grid), grid.at_rim()
    own_dip, rim_dip = (fl, 6), (rims, LATE + 6)
    dip = [tile.get(fl, 6 + d) for d in range(3)]
    dip_rim = [tile.get(rims, LATE + 6 + d) for d in range(3)]
    dip_far = [tile.get(rims, LATE + FAR + 3 + d) for d in range(3)]
    back = spread_inside(grid, tile, hold, fl)
    inward = hand_over(grid, tile, hold_rim, rim_dip, dip, sign)
    alpha = [
        tile.get(ab, s)
        + (1.0 - tile.get(fl, 9 + s)) * (back[s] + jnp.where(at_rim, inward[s], 0.0))
        for s in range(3)
    ]
    beta = [tile.get(ab, 3 + d) for d in range(3)]
    for q in range(19):
        along = mixed(VELOCITY[q], beta) if q != 16 else None
        for s in range(3):
            v = alpha[s] if along is None else alpha[s] + along
            if s == 2:
                v = v + rest * tile.get(kept, q)
            tile.put(mid, s * 19 + q, v)
    given = hand_over(grid, tile, hold, own_dip, dip_rim, -sign)
    level = spread_level(grid, tile, hold_rim, *rim_dip)
    after = hand_over(grid, tile, hold_rim, rim_dip, dip_far, -sign)
    for s in range(3):
        open_share = 1.0 - tile.get(rims, LATE_PSI + s)
        tile.put(part, s, tile.get(ab_rim, s) + open_share * (given[s] + level[s]))
        tile.put(part, 3 + s, tile.get(ab_rim, 3 + s))
        tile.put(part, 6 + s, (1.0 - tile.get(rims, LATE + FAR + s)) * after[s])


def level_row(tile, alpha, part, kept_rim, level):
    rest = 1.0 - 1.0 / RELAXATION[2]
    beta = [tile.get(part, 3 + d) for d in range(3)]
    for i, q in enumerate(LEVEL):
        side = mixed(VELOCITY[q][1:], beta[1:]) if q != 16 else None
        for s in range(3):
            v = plus(side, alpha[s])
            if s == 2:
                v = v + rest * tile.get(kept_rim, i)
            tile.put(level, s * 9 + i, v)


def main_kernel(
    adj, fl, fe, recv_a, recv_b, after,
    rims, mid, part, kept_rim, forces, forces_rim, brick2, rim2, kept2,
    lines, hold, ab, kept, hold_rim, ab_rim, level,
):
    planes, rows, cols = adj.shape[1:]
    grid = Grid(planes, rows, cols)
    lines_from(recv_a, recv_b, parity_of("gx"), lines)
    for c in range(STATIC):
        for p in range(planes):
            k = c * planes + p
            rims[c, p] = grid.sides(lines[0, k : k + 1, :], lines[1, k : k + 1, :])
    grid.over_main(lambda tile: rim_psis(grid, tile, rims))

    def step(tile):
        first_step(grid, tile, adj, fl, rims, hold, ab, kept, hold_rim, ab_rim, kept_rim)
        early_forces(grid, tile, fe, rims, forces, forces_rim)

    grid.over_main(step)
    grid.over_main(
        lambda tile: finish_first(
            grid, tile, fl, rims, hold, ab, kept, hold_rim, ab_rim, mid, part
        )
    )
    grid.over_main(lambda tile: level_row(tile, [tile.get(part, s) for s in range(3)], part, kept_rim, level))

    def known_moments(tile):
        load = lambda c, dz: tile.get(mid, c, dz)
        put_moments(tile, brick2, brick_moments(grid, tile, load, None, kept2))
        along = lambda s, i, dz: tile.get(level, s * 9 + i, dz)
        put_moments(tile, rim2, rim_moments(grid, tile, along, None, load, None))

    grid.over_main(known_moments)


def last_kernel(
    fe_m, rims_m, mid_m, part_m, kept_rim_m, forces_m, forces_rim_m, brick2_m, rim2_m, kept2_m,
    edge, fl_e, fe_e,
    recv_a, recv_b, out,
    rims_e, mid_e, part_e, kept_rim_e, forces_e, forces_rim_e, hold_e, ab_e, kept_e, hold_rim_e,
    ab_rim_e, patches, lines, near, change, rim_mid, rim_level, rim_far, hold2, hold_rim2, ab2, kept2,
    total, staged, sems,
):
    planes, rows, cols = fe_m.shape[1:]
    grid = Grid(planes, rows, cols)
    lines_from(recv_a, recv_b, parity_of("gx"), lines)
    for c in range(STATIC):
        rims_e[c] = grid.sides(lines[0, c : c + 1, :], lines[1, c : c + 1, :])
    for c in range(DYNAMIC):
        for t in range(grid.tiles):
            k = STATIC + c * grid.tiles + t
            near[c, t] = grid.sides(lines[0, k : k + 1, :], lines[1, k : k + 1, :])
    fe, rims, mid = Pair(fe_m, fe_e), Pair(rims_m, rims_e), Pair(mid_m, mid_e)
    part, kept_rim = Pair(part_m, part_e), Pair(kept_rim_m, kept_rim_e)
    forces, forces_rim = Pair(forces_m, forces_e), Pair(forces_rim_m, forces_rim_e)
    rest = 1.0 - 1.0 / RELAXATION[2]
    at_rim = grid.at_rim()
    sign = rim_sign(grid)
    outward = grid.outward()

    def edge_steps(tile):
        adj, fl = Pair(None, edge), Pair(None, fl_e)
        hold, ab, kept = Pair(None, hold_e), Pair(None, ab_e), Pair(None, kept_e)
        hold_rim, ab_rim = Pair(None, hold_rim_e), Pair(None, ab_rim_e)
        rim_psis(grid, tile, rims)
        first_step(grid, tile, adj, fl, rims, hold, ab, kept, hold_rim, ab_rim, kept_rim)
        early_forces(grid, tile, fe, rims, forces, forces_rim)
        finish_first(grid, tile, fl, rims, hold, ab, kept, hold_rim, ab_rim, mid, part)

    grid.over_edge(edge_steps)

    def complete(tile):
        t = tile.index
        added = [(1.0 - tile.get(rims, LATE_PSI + s)) * near[s, t] for s in range(3)]
        alpha = [tile.get(part, s) + added[s] for s in range(3)]
        beta = [tile.get(part, 3 + d) for d in range(3)]
        far = [near[3 + s, t] + tile.get(part, 6 + s) for s in range(2)]
        far_beta = [near[5 + d, t] for d in range(2)]
        ahead = outward * beta[0]
        for s in range(3):
            change[s, t] = added[s]
        for j, yz in enumerate(CROSS):
            side = mixed(yz, beta[1:]) if j else None
            side_far = mixed(yz, far_beta) if j else None
            for s in range(3):
                v = plus(side, alpha[s] + ahead)
                if s == 2:
                    v = v + rest * tile.get(kept_rim, 9 + j)
                    rim_far[10 + j, t] = near[7 + j, t] + tile.get(part, 8)
                else:
                    rim_far[s * 5 + j, t] = plus(side_far, far[s])
                rim_mid[s * 5 + j, t] = v
        if tile.edge:
            level_row(tile, alpha, part, kept_rim, rim_level)

    grid.over(complete)

    def collide(tile):
        load = lambda c, dz: tile.get(mid, c, dz)
        after = lambda s, j, dz: tile.get(rim_far, s * 5 + j, dz)
        if tile.edge:
            moments = brick_moments(grid, tile, load, rim_mid, kept2)
            along = lambda s, i, dz: tile.get(rim_level, s * 9 + i, dz)
            moments_rim = rim_moments(grid, tile, along, after, load, None)
        else:
            for q in range(19):
                kept2[q, tile.index] = kept2_m[q, tile.index]
            moments, moments_rim = get_moments(tile, brick2_m), get_moments(tile, rim2_m)
            along = lambda s, i, dz: tile.get(change, s, dz)
            more = crossing_moments(grid, tile, rim_mid, kept2)
            more_rim = rim_moments(grid, tile, along, after, None, None)
            for s in range(3):
                moments[s] = summed(moments[s], more[s])
                moments_rim[s] = summed(moments_rim[s], more_rim[s])
        known = [[tile.get(forces, 3 * s + d) for d in range(3)] for s in range(3)]
        brick_adjoint(tile, moments, fe, known, hold2, ab2)
        known = [[tile.get(forces_rim, 3 * s + d) for d in range(3)] for s in range(3)]
        rho, u = [[tile.get(rims, EARLY + at + d) for d in range(3)] for at in (0, 3)]
        psi = [tile.get(rims, EARLY_PSI + s) for s in range(3)]
        rim_adjoint(grid, tile, moments_rim, rho, u, psi, known, hold_rim2, None)

    grid.over(collide)

    def finish(tile):
        back = spread_inside(grid, tile, hold2, fe)
        dip = [tile.get(fe, 6 + d) for d in range(3)]
        inward = hand_over(grid, tile, hold_rim2, (rims, EARLY + 6), dip, sign)
        for s in range(3):
            x = back[s] + jnp.where(at_rim, inward[s], 0.0)
            total[s, tile.index] = tile.get(ab2, s) + (1.0 - tile.get(fe, 9 + s)) * x

    grid.over(finish)
    at_side = (grid.lane < HALO) | (grid.lane >= cols - HALO)
    first_group = lax.rem(grid.lane, grid.width) < grid.group
    sources = [total.at[s] for s in range(3)] + [ab2.at[3 + d] for d in range(3)]
    sources += [kept2.at[q] for q in range(19)]
    for i, ref in enumerate(sources):
        v = ref[planes]
        patches[i] = jnp.where(first_group, pltpu.roll(v, cols - 2 * grid.group, 1), v)
    copies = []
    for p in range(planes):
        turn = (cols - p * grid.width - grid.group) % cols

        def patched(i):
            return jnp.where(at_side, pltpu.roll(patches[i], turn, 1), sources[i][p])

        alpha = [patched(s) for s in range(3)]
        beta = [patched(3 + d) for d in range(3)]
        for q in range(19):
            along = mixed(VELOCITY[q], beta) if q != 16 else None
            for s in range(3):
                v = alpha[s] if along is None else alpha[s] + along
                if s == 2:
                    v = v + rest * patched(6 + q)
                staged[s * 19 + q, p] = v
        copies.append(pltpu.make_async_copy(staged.at[:, p], out.at[:, p], sems.at[p]))
        copies[p].start()
    for copy in copies:
        copy.wait()


def call(kernel, outs, scratch, args, in_hbm=False, out_hbm=False, cost=0):
    vmem = pl.BlockSpec(memory_space=pltpu.VMEM)
    hbm = pl.BlockSpec(memory_space=pltpu.HBM)
    return pl.pallas_call(
        kernel,
        out_shape=[jax.ShapeDtypeStruct(s, F32) for s in outs],
        in_specs=[hbm if in_hbm else vmem] * len(args),
        out_specs=[hbm if out_hbm else vmem] * len(outs),
        scratch_shapes=[pltpu.VMEM(s, F32) if isinstance(s, tuple) else s for s in scratch],
        compiler_params=pltpu.CompilerParams(vmem_limit_bytes=VMEM_BYTES),
        cost_estimate=pl.CostEstimate(flops=cost, bytes_accessed=cost, transcendentals=0),
    )(*[pltpu.with_memory_space_constraint(x, pltpu.HBM) if in_hbm else x for x in args])


def swap(block, axis, offset):
    size = lax.axis_size(axis)
    route = []
    for i in range(offset, size + offset, 2):
        a, b = i % size, (i + 1) % size
        route += [(a, b), (b, a)]
    return lax.ppermute(block, axis, route)


def shards(adjoint_in, populations_early, populations_late, dipoles_early, dipoles_late):
    pops, planes, rows, cols = adjoint_in.shape
    tile = (rows, cols)
    pack = cols // planes // (2 * HALO)
    groups = -(-(pops + 18) // pack)
    groups += groups % 2

    def lines(n):
        return (-(-n // 8) * 8, cols)

    def main(*counts):
        return [(n, planes) + tile for n in counts]

    def edges(*counts):
        return [(n,) + tile for n in counts]

    def tiled(*counts):
        return [(n, planes + 1) + tile for n in counts]

    static = lines(STATIC * planes)
    second = lines(STATIC + DYNAMIC * (planes + 1))
    send_c, send_d, own_left, own_right, fl_m, fe_m, adj, send_a, send_b = call(
        pack_columns_kernel,
        edges(groups // 2, groups // 2, groups, groups) + main(12, 12, pops) + [static] * 2,
        [
            pltpu.VMEM(x.shape, x.dtype)
            for x in (populations_late, populations_early, dipoles_late, dipoles_early)
        ]
        + [(2,) + static, pltpu.SemaphoreType.DMA((4 + CHUNKS,))],
        [adjoint_in, populations_late, populations_early, dipoles_late, dipoles_early],
        in_hbm=True,
    )
    static_a, static_b = swap(send_a, "gx", 1), swap(send_b, "gx", 0)
    recv_c, recv_d = swap(send_c, "gy", 1), swap(send_d, "gy", 0)
    (sides,) = call(
        inside_kernel, main(DYNAMIC), main(9, 6, 19), [adj, fl_m], cost=INSIDE_COST
    )
    send_a, send_b, edge, fl_e, fe_e = call(
        edge_kernel,
        [second] * 2 + edges(pops, 12, 12),
        [(2,) + second] + edges(9, 6, 19, DYNAMIC),
        [own_left, own_right, recv_c, recv_d, sides],
        cost=EDGE_COST,
    )
    recv_a, recv_b = swap(send_a, "gx", 1), swap(send_b, "gx", 0)
    known = (RIMS, pops, 9, 14, 9, 9)
    mains = call(
        main_kernel,
        main(*known, 30, 30, 19),
        [(2,) + static] + main(9, 6, 19, 9, 6, 27),
        [adj, fl_m, fe_m, static_a, static_b, fl_e],
        cost=MAIN_COST,
    )
    (out,) = call(
        last_kernel,
        [(pops, planes) + tile],
        edges(*known, 9, 6, 19, 9, 6, 25)
        + [(2,) + second]
        + tiled(DYNAMIC, 3, 15, 27, 15, 9, 9, 6, 19, 3)
        + main(pops)
        + [pltpu.SemaphoreType.DMA((planes,))],
        [fe_m, *mains, edge, fl_e, fe_e, recv_a, recv_b],
        out_hbm=True,
    )
    return out


def solution(mesh):
    placed = P(None, None, "gx", "gy")
    return jax.shard_map(
        shards, mesh=mesh, in_specs=(placed,) * 5, out_specs=placed, check_vma=False
    )
```

```python
import jax
import jax.numpy as jnp
from jax import lax
from jax.experimental import pallas as pl
from jax.experimental.pallas import tpu as pltpu
from jax.sharding import PartitionSpec as P

VELOCITY = (
    (1, 0, 0),
    (-1, 0, 0),
    (0, 1, 0),
    (0, -1, 0),
    (1, 1, 0),
    (-1, -1, 0),
    (1, -1, 0),
    (-1, 1, 0),
    (1, 0, 1),
    (-1, 0, -1),
    (1, 0, -1),
    (-1, 0, 1),
    (0, 1, 1),
    (0, -1, -1),
    (0, 1, -1),
    (0, -1, 1),
    (0, 0, 0),
    (0, 0, 1),
    (0, 0, -1),
)
INDEX = {c: q for q, c in enumerate(VELOCITY)}
W1, W2, W0 = 1.0 / 18.0, 1.0 / 36.0, 1.0 / 3.0
RELAXATION = (1.0, 1.0, 1.25)
COUPLING = ((0.0, 1.2, -0.6), (1.2, 0.0, -0.6), (-0.6, -0.6, -0.3))
CROSS = ((0, 0), (1, 0), (-1, 0), (0, 1), (0, -1))
AHEAD = tuple(INDEX[(1,) + yz] for yz in CROSS)
BEHIND = tuple(INDEX[(-1,) + yz] for yz in CROSS)
SIDE = ((1, 0), (-1, 0), (0, 1), (0, -1), (1, 1), (-1, -1), (1, -1), (-1, 1))
LEVEL = tuple(q for q in range(19) if VELOCITY[q][0] == 0)
ALONG, AFTER, LATE, EARLY = 15, 42, 57, 72
STATIC = 87
FAR = 9
LATE_PSI, EARLY_PSI = STATIC, STATIC + 3
RIMS = STATIC + 6
DYNAMIC = 12
F32 = jnp.float32
CHUNKS = 4
INSIDE_COST, EDGE_COST, MAIN_COST = 10**7, 10**8, 10**8
VMEM_BYTES = 40 * 1024 * 1024
HALO = 4


class Grid:
    def __init__(self, planes, rows, cols):
        self.planes, self.rows, self.cols = planes, rows, cols
        self.tiles = planes + 1
        self.width = cols // planes
        self.group = 2 * HALO
        self.pack = self.width // self.group
        self.sub = lax.broadcasted_iota(jnp.int32, (rows, cols), 0)
        self.lane = lax.broadcasted_iota(jnp.int32, (rows, cols), 1)
        self.masks = {}

    def once(self, name, make):
        if name not in self.masks:
            self.masks[name] = make()
        return self.masks[name]

    def in_width(self):
        return self.once("width", lambda: lax.rem(self.lane, self.width))

    def left_half(self):
        return self.once("left", lambda: self.in_width() < self.width // 2)

    def roll_rows(self, v, dx):
        return pltpu.roll(v, (-dx) % self.rows, 0)

    def roll_cols(self, v, dy):
        return pltpu.roll(v, (-dy) % self.cols, 1)

    def at_row(self, v, rim, dx):
        edge = self.rows - 1 if dx > 0 else 0
        return jnp.where(self.sub == edge, rim, self.roll_rows(v, dx))

    def in_row(self, v, dx):
        edge = self.rows - 1 if dx > 0 else 0
        return jnp.where(self.sub == edge, 0.0, self.roll_rows(v, dx))

    def sides(self, low, high):
        return jnp.where(self.sub == 0, low, high)

    def over_main(self, body):
        for p in range(self.planes):
            body(Tile(self, p, False))

    def over_edge(self, body):
        body(Tile(self, self.planes, True))

    def over(self, body):
        self.over_main(body)
        self.over_edge(body)

    def at_rim(self):
        return self.once("rim", lambda: (self.sub == 0) | (self.sub == self.rows - 1))

    def low(self):
        return self.once("low", lambda: self.sub < self.rows // 2)

    def outward(self):
        return self.once("out", lambda: jnp.where(self.low(), -1.0, 1.0).astype(F32))


class Tile:
    def __init__(self, grid, index, edge):
        self.grid, self.index, self.edge = grid, index, edge

    def of(self, dz):
        if dz == 0 or self.edge:
            return self.index
        return (self.index + dz) % self.grid.planes

    def get(self, ref, c, dz=0):
        if isinstance(ref, Pair):
            v = ref.edge[c] if self.edge else ref.main[c, self.of(dz)]
        else:
            v = ref[c, self.of(dz)]
        if self.edge and dz != 0:
            v = self.grid.roll_cols(v, dz * self.grid.width)
        return v

    def put(self, ref, c, v):
        if not isinstance(ref, Pair):
            ref[c, self.index] = v
        elif self.edge:
            ref.edge[c] = v
        else:
            ref.main[c, self.index] = v


class Pair:
    def __init__(self, main, edge):
        self.main, self.edge = main, edge

    def at(self, c, t):
        return self.edge[c] if t == self.main.shape[1] else self.main[c, t]


def plus(a, b):
    return b if a is None else a + b


def mixed(coefficients, values):
    total = None
    for k, v in zip(coefficients, values):
        if k == 0:
            continue
        term = v if k == 1 else (-v if k == -1 else k * v)
        total = plus(total, term)
    return total


def axis_pairs():
    for q in (0, 2, 17, 4, 6, 8, 10, 12, 14):
        c = VELOCITY[q]
        yield c, (W1 if sum(abs(i) for i in c) == 1 else W2)


def first_and_second(diff, total):
    first = [None] * 3
    second = {}
    for c, w in axis_pairs():
        for d in range(3):
            if c[d] == 0:
                continue
            if diff is not None and diff[c] is not None:
                first[d] = plus(first[d], (w * c[d]) * diff[c])
            if total is not None and total[c] is not None:
                for e in range(d, 3):
                    if c[e] != 0:
                        second[d, e] = plus(second.get((d, e)), (w * c[d] * c[e]) * total[c])
    return first, second


PAIRS = tuple((d, e) for d in range(3) for e in range(d, 3))


def moments_of(streamed):
    diff, total = {}, {}
    for c, w in axis_pairs():
        a, b = streamed[INDEX[c]], streamed[INDEX[tuple(-i for i in c)]]
        if a is None or b is None:
            diff[c] = a if b is None else -b
            total[c] = b if a is None else a
        else:
            diff[c], total[c] = a - b, a + b
    first, second = first_and_second(diff, total)
    zeroth = None if streamed[16] is None else W0 * streamed[16]
    for c, w in axis_pairs():
        if total[c] is not None:
            zeroth = plus(zeroth, w * total[c])
    return [zeroth] + first + [second.get(k) for k in PAIRS]


def summed(known, change):
    return [k if x is None else k + x for k, x in zip(known, change)]


def turned(second, v):
    return [sum(second[min(d, e), max(d, e)] * v[e] for e in range(3)) for d in range(3)]


def dot(a, b):
    return a[0] * b[0] + a[1] * b[1] + a[2] * b[2]


def field_forces(grid, loads, across, dipole):
    memo = {}

    def source(name, dz, place):
        key = (name, dz, place)
        if key in memo:
            return memo[key]
        if isinstance(name, int):
            v = loads[place](name, dz)
        elif name == "chi":
            v = source(0, dz, place) - source(1, dz, place)
        elif name[0] == "V":
            v = source(2, dz, place) * source(3 + name[1], dz, place)
        else:
            c = name[1]
            v = mixed(c, [source(("V", d), dz, place) if c[d] else None for d in range(3)])
        memo[key] = v
        return v

    def shifted(name, c):
        key = (name, c, "shift")
        if key in memo:
            return memo[key]
        if c[1] != 0:
            v = grid.roll_cols(shifted(name, (c[0], 0, c[2])), c[1])
        elif c[0] != 0:
            v = across(lambda place, dz: source(name, dz, place), c[0], c[2])
        else:
            v = source(name, c[2], 0)
        memo[key] = v
        return v

    def parts(name):
        diff, total = {}, {}
        for c, w in axis_pairs():
            back = tuple(-i for i in c)
            a, b = shifted(name, c), shifted(name, back)
            diff[c], total[c] = a - b, a + b
        return diff, total

    diff, unused = parts(0)
    s0, unused = first_and_second(diff, None)
    diff, unused = parts(2)
    s2, unused = first_and_second(diff, None)
    diff, total = parts("chi")
    schi, second = first_and_second(diff, total)
    s1 = [a - b for a, b in zip(s0, schi)]
    pull = [None] * 3
    for c, w in axis_pairs():
        back = tuple(-i for i in c)
        if sum(abs(i) for i in c) == 1:
            name = ("V", [i for i in range(3) if c[i]][0])
        else:
            name = ("L", c)
        total_c = shifted(name, c) + shifted(name, back)
        for d in range(3):
            if c[d] != 0:
                pull[d] = plus(pull[d], (w * c[d]) * total_c)
    md = turned(second, dipole)
    k0 = [-1.2 * s1[d] + 0.6 * s2[d] - pull[d] for d in range(3)]
    k1 = [-1.2 * s0[d] + 0.6 * s2[d] + pull[d] for d in range(3)]
    k2 = [0.6 * (s0[d] + s1[d]) + 0.3 * s2[d] + md[d] for d in range(3)]
    return k0, k1, k2


def brick_forces(grid, tile, fields, rim, rim_psi, rim_dip):
    def own(c, dz):
        return tile.get(fields, (9 + c) if c < 3 else (3 + c), dz)

    def beyond(c, dz):
        return tile.get(rim, (rim_psi + c) if c < 3 else (rim_dip + c - 3), dz)

    def across(get, cx, dz):
        if rim is None:
            return grid.in_row(get(0, dz), cx)
        return grid.at_row(get(0, dz), get(1, dz), cx)

    return field_forces(grid, (own, beyond), across, [own(3 + d, 0) for d in range(3)])


def rim_forces(grid, tile, fields, rims, psi, base):
    outward = grid.outward()

    def loader(ref, psi_at, dip_at):
        def load(c, dz):
            v = tile.get(ref, (psi_at + c) if c < 3 else (dip_at + c - 3), dz)
            return v * outward if c == 3 else v

        return load

    loads = {
        0: loader(rims, psi, base + 6),
        1: loader(rims, base + FAR, base + FAR + 3),
        -1: loader(fields, 9, 6),
    }
    dipole = [loads[0](3 + d, 0) for d in range(3)]
    return field_forces(grid, loads, lambda get, cx, dz: get(cx, dz), dipole)


def collision_adjoint(moments, rho, u, psi, forces):
    inverse_sum = 1.0 / (rho[0] + rho[1] + rho[2])
    grad_u = [None] * 3
    alphas, held = [], []
    for s in range(3):
        m0, m1 = moments[s][0], moments[s][1:4]
        m2 = dict(zip(PAIRS, moments[s][4:]))
        inverse = 1.0 / rho[s]
        ratio = psi[s] * inverse
        tau = RELAXATION[s]
        k = forces[s]
        v = [u[d] + (tau * ratio) * k[d] for d in range(3)]
        mv = turned(m2, v)
        g = [3.0 * (m1[d] + 3.0 * mv[d] - m0 * v[d]) for d in range(3)]
        feq = m0 + 3.0 * dot(m1, v) + 4.5 * dot(mv, v) - 1.5 * m0 * dot(v, v)
        alphas.append(feq * (1.0 / tau) + dot(g, k) * (1.0 - psi[s] - ratio))
        scaled = rho[s] * (1.0 / tau)
        for d in range(3):
            grad_u[d] = plus(grad_u[d], scaled * g[d])
            held.append(psi[s] * g[d])
    beta = [grad_u[d] * inverse_sum for d in range(3)]
    along = dot(beta, u)
    return held, [a - along for a in alphas], beta


def brick_moments(grid, tile, load, rim, kept):
    def streamed_of(s):
        streamed = []
        for q in range(19):
            c = VELOCITY[q]
            v = load(s * 19 + q, c[2])
            if c[0] != 0:
                j = (AHEAD if c[0] > 0 else BEHIND).index(q)
                if rim is None:
                    v = grid.in_row(v, c[0])
                else:
                    v = grid.at_row(v, tile.get(rim, s * 5 + j, c[2]), c[0])
            if c[1] != 0:
                v = grid.roll_cols(v, c[1])
            streamed.append(v)
            if s == 2:
                tile.put(kept, q, v)
        return streamed

    return [moments_of(streamed_of(s)) for s in range(3)]


def crossing_moments(grid, tile, rim, kept):
    first, last = grid.sub == 0, grid.sub == grid.rows - 1

    def streamed_of(s):
        streamed = [None] * 19
        for j, (cy, cz) in enumerate(CROSS):
            v = tile.get(rim, s * 5 + j, cz)
            if cy != 0:
                v = grid.roll_cols(v, cy)
            streamed[AHEAD[j]] = jnp.where(last, v, 0.0)
            streamed[BEHIND[j]] = jnp.where(first, v, 0.0)
        if s == 2:
            for q in AHEAD + BEHIND:
                tile.put(kept, q, tile.get(kept, q) + streamed[q])
        return streamed

    return [moments_of(streamed_of(s)) for s in range(3)]


def brick_adjoint(tile, moments, fields, forces, hold, ab):
    rho, u, psi = [[tile.get(fields, at + d) for d in range(3)] for at in (0, 3, 9)]
    held, alpha, beta = collision_adjoint(moments, rho, u, psi, forces)
    for k in range(9):
        tile.put(hold, k, held[k])
    for s in range(3):
        tile.put(ab, s, alpha[s])
        tile.put(ab, 3 + s, beta[s])


def brick_collision(grid, tile, load, rim, fields, forces, hold, ab, kept):
    moments = brick_moments(grid, tile, load, rim, kept)
    brick_adjoint(tile, moments, fields, forces, hold, ab)


def rim_moments(grid, tile, level, after, inner, kept):
    low = grid.low()

    def streamed_of(s):
        streamed = []
        for q in range(19):
            c = VELOCITY[q]
            v = None
            if c[0] == 0 and level is not None:
                v = level(s, LEVEL.index(q), c[2])
            elif c[0] > 0 and after is not None:
                v = after(s, AHEAD.index(q), c[2])
            elif c[0] < 0 and inner is not None:
                j = BEHIND.index(q)
                v = jnp.where(low, inner(s * 19 + AHEAD[j], c[2]), inner(s * 19 + BEHIND[j], c[2]))
            if c[1] != 0 and v is not None:
                v = grid.roll_cols(v, c[1])
            streamed.append(v)
            if s == 2 and kept is not None and c[0] >= 0:
                tile.put(kept, LEVEL.index(q) if c[0] == 0 else 9 + AHEAD.index(q), v)
        return streamed

    return [moments_of(streamed_of(s)) for s in range(3)]


def rim_adjoint(grid, tile, moments, rho, u, psi, forces, hold, ab):
    outward = grid.outward()
    u = [u[0] * outward, u[1], u[2]]
    held, alpha, beta = collision_adjoint(moments, rho, u, psi, forces)
    for k in range(9):
        tile.put(hold, k, held[k] * outward if k % 3 == 0 else held[k])
    if ab is not None:
        for s in range(3):
            tile.put(ab, s, alpha[s])
            tile.put(ab, 3 + s, beta[s] * outward if s == 0 else beta[s])


def put_moments(tile, ref, moments):
    for s in range(3):
        for k in range(10):
            v = moments[s][k]
            tile.put(ref, s * 10 + k, jnp.zeros(ref.shape[-2:], F32) if v is None else v)


def get_moments(tile, ref):
    return [[tile.get(ref, s * 10 + k) for k in range(10)] for s in range(3)]


def spread_plane(grid, get_h, get_d, sign, pairs):
    memo = {}

    def source(dz):
        if dz in memo:
            return memo[dz]
        h = [[get_h(3 * s + d, dz) for d in range(3)] for s in range(3)]
        dip = [get_d(d, dz) for d in range(3)]
        if not isinstance(sign, int):
            for vec in h + [dip]:
                vec[0] = vec[0] * sign
        memo[dz] = (h, dip)
        return memo[dz]

    cx = sign if isinstance(sign, int) else 1
    r = [None] * 3
    w_vec = [None] * 3
    lanes = {}
    for cy, cz in pairs:
        w = W1 if abs(cx) + abs(cy) + abs(cz) == 1 else W2
        h, dip = source(cz)
        c = (cx, cy, cz)
        e = [mixed(c, h[s]) for s in range(3)]
        f = e[2] * mixed(c, dip)
        half = 0.6 * e[2]
        r0 = 1.2 * e[1] - half + f
        r1 = 1.2 * e[0] - half - f
        r2 = -0.6 * (e[0] + e[1]) - 0.3 * e[2]
        qv = e[0] - e[1]
        vals = [w * r0, w * r1, w * r2]
        wq = w * qv
        vals += [wq if cx != 0 else None, wq if cy != 0 else None, wq if cz != 0 else None]
        vals = [vals[0], vals[1], vals[2]] + [
            None if x is None else (x if k == 1 else -x) for x, k in zip(vals[3:], (cx, cy, cz))
        ]
        acc = lanes.setdefault(cy, [None] * 6)
        for i, x in enumerate(vals):
            if x is not None:
                acc[i] = plus(acc[i], x)
    total = [None] * 6
    for cy, acc in lanes.items():
        for i, x in enumerate(acc):
            if x is not None:
                total[i] = plus(total[i], x if cy == 0 else grid.roll_cols(x, cy))
    if not isinstance(sign, int):
        total[3] = total[3] * sign
    return total


def met(total, dipole):
    meet = None
    for d in range(3):
        if total[3 + d] is not None:
            meet = plus(meet, total[3 + d] * dipole[d])
    return [total[0], total[1], total[2] - meet]


def spread_inside(grid, tile, hold, fields):
    get_h = lambda k, dz: tile.get(hold, k, dz)
    get_d = lambda k, dz: tile.get(fields, 6 + k, dz)
    total = spread_plane(grid, get_h, get_d, 0, SIDE)
    for dx in (1, -1):
        part = spread_plane(grid, get_h, get_d, dx, CROSS)
        for i, x in enumerate(part):
            total[i] = plus(total[i], grid.in_row(x, dx))
    return met(total, [tile.get(fields, 6 + d) for d in range(3)])


def rim_sign(grid):
    return grid.once("sign", lambda: jnp.where(grid.at_rim(), grid.outward(), 0.0))


def hand_over(grid, tile, hold, hold_dip, target, sign):
    dip, at = hold_dip
    total = spread_plane(
        grid,
        lambda k, dz: tile.get(hold, k, dz),
        lambda k, dz: tile.get(dip, at + k, dz),
        sign,
        CROSS,
    )
    return met(total, target)


def spread_level(grid, tile, hold, dip, at):
    total = spread_plane(
        grid,
        lambda k, dz: tile.get(hold, k, dz),
        lambda k, dz: tile.get(dip, at + k, dz),
        0,
        SIDE,
    )
    return met(total, [tile.get(dip, at + d) for d in range(3)])


def parity_of(axis):
    return lax.rem(lax.axis_index(axis) + 1, 2)


def lines_from(first, second, parity, lines):
    lines[1 - parity] = first[...]
    lines[parity] = second[...]


def lines_to(first, second, lines):
    first[...] = lines[0]
    second[...] = lines[1]


def psi_of(rho):
    return 1.0 - jnp.exp(-rho)


def static_rows():
    for s in range(3):
        for j in range(5):
            yield 0, s * 19 + BEHIND[j], s * 19 + AHEAD[j], 0
    for s in range(3):
        for q in LEVEL:
            yield 0, s * 19 + q, s * 19 + q, 0
    for s in range(3):
        for j in range(5):
            yield 0, s * 19 + BEHIND[j], s * 19 + AHEAD[j], 1
    for kind in (1, 2):
        for c in range(9):
            yield kind, c, c, 0
        for c in (9, 10, 11, 6, 7, 8):
            yield kind, c, c, 1


def pack_static(get, tiles, rows, lines, parity, wanted=None):
    up, down = parity, 1 - parity
    fill = 0
    for kind, above, below, depth in static_rows():
        if wanted is not None and not wanted(kind, max(above, below)):
            fill += len(tiles)
            continue
        for t in tiles:
            v = get(kind, above, t)
            lines[up, fill : fill + 1, :] = v[rows - 1 - depth : rows - depth, :]
            v = get(kind, below, t)
            lines[down, fill : fill + 1, :] = v[depth : depth + 1, :]
            fill += 1
    return fill


def pack_columns_kernel(
    adj_in, late_in, early_in, dip_late_in, dip_early_in,
    send_c, send_d, own_left, own_right, fl, fe, adj, send_a, send_b,
    late, early, dip_late, dip_early, lines, sems,
):
    planes, rows, cols = adj.shape[1:]
    grid = Grid(planes, rows, cols)
    copies = [
        pltpu.make_async_copy(a, b, sems.at[i])
        for i, (a, b) in enumerate(
            (
                (dip_late_in, dip_late),
                (late_in, late),
                (dip_early_in, dip_early),
                (early_in, early),
            )
        )
    ]
    per_chunk = -(-adj.shape[0] // (CHUNKS * grid.pack)) * grid.pack
    for i in range(CHUNKS):
        part = pl.ds(i * per_chunk, min(per_chunk, adj.shape[0] - i * per_chunk))
        copies.append(pltpu.make_async_copy(adj_in.at[part], adj.at[part], sems.at[4 + i]))
    for copy in copies:
        copy.start()
    for which, (saved, dip, out) in enumerate(((late, dip_late, fl), (early, dip_early, fe))):
        copies[2 * which].wait()
        copies[2 * which + 1].wait()

        for p in range(planes):
            flows = [None] * 19
            rho = []
            for s in range(3):
                total = None
                for q in range(19):
                    v = saved[s * 19 + q, p].astype(F32)
                    flows[q] = plus(flows[q], v)
                    total = plus(total, v)
                rho.append(total)
                out[s, p] = total
                out[9 + s, p] = psi_of(total)
            inverse = 1.0 / (rho[0] + rho[1] + rho[2])
            for d in range(3):
                momentum = None
                for q in range(19):
                    if VELOCITY[q][d] != 0:
                        momentum = plus(momentum, flows[q] if VELOCITY[q][d] > 0 else -flows[q])
                out[3 + d, p] = momentum * inverse
                out[6 + d, p] = dip[d, p].astype(F32)
    kinds = (adj, fl, fe)
    parity = parity_of("gx")

    def pack_rows(wanted):
        get = lambda kind, c, t: kinds[kind][c, t]
        pack_static(get, range(planes), rows, lines, parity, wanted)

    pack_rows(lambda kind, c: kind > 0)
    pops = adj.shape[0]
    components = pops + 18
    slot = grid.lane // grid.group
    for g in range(own_left.shape[0]):
        if g * grid.pack % per_chunk == 0 and g * grid.pack < pops:
            chunk = g * grid.pack // per_chunk
            copies[4 + chunk].wait()
            pack_rows(lambda kind, c: kind == 0 and c // per_chunk == chunk)
        left = right = jnp.zeros((rows, cols), F32)
        for j in range(grid.pack):
            c = g * grid.pack + j
            if c >= components:
                continue
            for p in range(planes):
                if c < pops:
                    v = adj[c, p]
                elif c < pops + 9:
                    v = fl[c - pops, p]
                else:
                    v = fe[c - pops - 9, p]
                at = p * grid.pack + j
                rolled = pltpu.roll(v, at * grid.group, 1) if at else v
                here, prior = [
                    grid.once(("slot", k), lambda: slot == k)
                    for k in (at, (at - 1) % (cols // grid.group))
                ]
                left = jnp.where(here, rolled, left)
                right = jnp.where(prior, rolled, right)
        own_left[g] = left
        own_right[g] = right
    low = lax.rem(grid.lane, grid.group) < HALO
    even = parity_of("gy") == 0
    for h in range(send_c.shape[0]):
        left = jnp.where(low, own_left[2 * h], pltpu.roll(own_left[2 * h + 1], HALO, 1))
        right = jnp.where(low, pltpu.roll(own_right[2 * h + 1], cols - HALO, 1), own_right[2 * h])
        send_c[h] = jnp.where(even, right, left)
        send_d[h] = jnp.where(even, left, right)
    lines_to(send_a, send_b, lines)


def inside_collision(grid, tile, load, fields, hold, ab, kept):
    forces = brick_forces(grid, tile, fields, None, 0, 0)
    brick_collision(grid, tile, load, None, fields, forces, hold, ab, kept)
    at_rim = grid.at_rim()
    for k in range(9):
        tile.put(hold, k, jnp.where(at_rim, 0.0, tile.get(hold, k)))


def second_row(grid, tile, fields, hold, ab, kept, sides):
    low = grid.low()
    rest = 1.0 - 1.0 / RELAXATION[2]
    back = spread_inside(grid, tile, hold, fields)
    alpha = [tile.get(ab, s) + (1.0 - tile.get(fields, 9 + s)) * back[s] for s in range(3)]
    beta = [tile.get(ab, 3 + d) for d in range(3)]
    ahead = -grid.outward() * beta[0]
    for s in range(3):
        tile.put(sides, s, back[s])
    for s in range(2):
        tile.put(sides, 3 + s, alpha[s] + ahead)
        tile.put(sides, 5 + s, beta[1 + s])
    for j, yz in enumerate(CROSS):
        v = rest * jnp.where(low, tile.get(kept, AHEAD[j]), tile.get(kept, BEHIND[j]))
        v = v + (alpha[2] + ahead)
        tile.put(sides, 7 + j, v + mixed(yz, beta[1:]) if j else v)


def inside_kernel(adj, fl, sides, hold, ab, kept):
    planes, rows, cols = adj.shape[1:]
    grid = Grid(planes, rows, cols)
    load = lambda tile: lambda c, dz: tile.get(adj, c, dz)
    grid.over_main(lambda tile: inside_collision(grid, tile, load(tile), fl, hold, ab, kept))
    grid.over_main(lambda tile: second_row(grid, tile, fl, hold, ab, kept, sides))


def edge_kernel(
    own_left, own_right, recv_c, recv_d, sides_main,
    send_a, send_b, edge, fl, fe, lines, hold, ab, kept, sides,
):
    planes, rows, cols = sides_main.shape[1:]
    pops = edge.shape[0]
    grid = Grid(planes, rows, cols)
    even = parity_of("gy") == 0
    slot = lax.rem(grid.lane // grid.group, grid.pack)
    left_half = grid.left_half()
    components = pops + 18
    for g in range(own_left.shape[0]):
        first, second = recv_c[g // 2], recv_d[g // 2]
        from_next = jnp.where(even, first, second)
        from_prior = jnp.where(even, second, first)
        if g % 2:
            from_next = pltpu.roll(from_next, cols - HALO, 1)
            from_prior = pltpu.roll(from_prior, HALO, 1)
        for j in range(grid.pack):
            c = g * grid.pack + j
            if c >= components:
                continue
            before = grid.once(("slot", j), lambda: slot == (j - 1) % grid.pack)
            low = jnp.where(before, from_prior, own_left[g])
            high = jnp.where(before, own_right[g], from_next)
            v = jnp.where(
                left_half,
                pltpu.roll(low, ((1 - j) * grid.group) % cols, 1),
                pltpu.roll(high, ((3 - j) * grid.group) % cols, 1),
            )
            if c < pops:
                edge[c] = v
            else:
                field, k = (fl, c - pops) if c < pops + 9 else (fe, c - pops - 9)
                field[k] = v
                if k < 3:
                    field[9 + k] = psi_of(v)
    adj, fields, both = Pair(None, edge), Pair(None, fl), Pair(sides_main, sides)
    hold, ab, kept = Pair(None, hold), Pair(None, ab), Pair(None, kept)

    def inside(tile):
        load = lambda c, dz: tile.get(adj, c, dz)
        inside_collision(grid, tile, load, fields, hold, ab, kept)
        second_row(grid, tile, fields, hold, ab, kept, both)

    grid.over_edge(inside)
    kinds = (edge, fl, fe)
    parity = parity_of("gx")
    fill = pack_static(lambda kind, c, t: kinds[kind][c], (0,), rows, lines, parity)
    for c in range(DYNAMIC):
        depth = 0 if c < 3 else 1
        for t in range(grid.tiles):
            v = both.at(c, t)
            lines[parity, fill : fill + 1, :] = v[rows - 1 - depth : rows - depth, :]
            lines[1 - parity, fill : fill + 1, :] = v[depth : depth + 1, :]
            fill += 1
    lines_to(send_a, send_b, lines)


def first_step(grid, tile, adj, fl, rims, hold, ab, kept, hold_rim, ab_rim, kept_rim):
    forces = brick_forces(grid, tile, fl, rims, LATE_PSI, LATE + 6)
    load = lambda c, dz: tile.get(adj, c, dz)
    brick_collision(grid, tile, load, rims, fl, forces, hold, ab, kept)
    forces = rim_forces(grid, tile, fl, rims, LATE_PSI, LATE)
    rho, u = [[tile.get(rims, LATE + at + d) for d in range(3)] for at in (0, 3)]
    psi = [tile.get(rims, LATE_PSI + s) for s in range(3)]
    moments = rim_moments(
        grid,
        tile,
        lambda s, i, dz: tile.get(rims, ALONG + s * 9 + i, dz),
        lambda s, j, dz: tile.get(rims, AFTER + s * 5 + j, dz),
        load,
        kept_rim,
    )
    rim_adjoint(grid, tile, moments, rho, u, psi, forces, hold_rim, ab_rim)


def early_forces(grid, tile, fe, rims, forces, forces_rim):
    brick = brick_forces(grid, tile, fe, rims, EARLY_PSI, EARLY + 6)
    beyond = rim_forces(grid, tile, fe, rims, EARLY_PSI, EARLY)
    for s in range(3):
        for d in range(3):
            tile.put(forces, 3 * s + d, brick[s][d])
            tile.put(forces_rim, 3 * s + d, beyond[s][d])


def rim_psis(grid, tile, rims):
    for s in range(3):
        tile.put(rims, LATE_PSI + s, psi_of(tile.get(rims, LATE + s)))
        tile.put(rims, EARLY_PSI + s, psi_of(tile.get(rims, EARLY + s)))


def finish_first(grid, tile, fl, rims, hold, ab, kept, hold_rim, ab_rim, mid, part):
    rest = 1.0 - 1.0 / RELAXATION[2]
    sign, at_rim = rim_sign(grid), grid.at_rim()
    own_dip, rim_dip = (fl, 6), (rims, LATE + 6)
    dip = [tile.get(fl, 6 + d) for d in range(3)]
    dip_rim = [tile.get(rims, LATE + 6 + d) for d in range(3)]
    dip_far = [tile.get(rims, LATE + FAR + 3 + d) for d in range(3)]
    back = spread_inside(grid, tile, hold, fl)
    inward = hand_over(grid, tile, hold_rim, rim_dip, dip, sign)
    alpha = [
        tile.get(ab, s)
        + (1.0 - tile.get(fl, 9 + s)) * (back[s] + jnp.where(at_rim, inward[s], 0.0))
        for s in range(3)
    ]
    beta = [tile.get(ab, 3 + d) for d in range(3)]
    for q in range(19):
        along = mixed(VELOCITY[q], beta) if q != 16 else None
        for s in range(3):
            v = alpha[s] if along is None else alpha[s] + along
            if s == 2:
                v = v + rest * tile.get(kept, q)
            tile.put(mid, s * 19 + q, v)
    given = hand_over(grid, tile, hold, own_dip, dip_rim, -sign)
    level = spread_level(grid, tile, hold_rim, *rim_dip)
    after = hand_over(grid, tile, hold_rim, rim_dip, dip_far, -sign)
    for s in range(3):
        open_share = 1.0 - tile.get(rims, LATE_PSI + s)
        tile.put(part, s, tile.get(ab_rim, s) + open_share * (given[s] + level[s]))
        tile.put(part, 3 + s, tile.get(ab_rim, 3 + s))
        tile.put(part, 6 + s, (1.0 - tile.get(rims, LATE + FAR + s)) * after[s])


def level_row(tile, alpha, part, kept_rim, level):
    rest = 1.0 - 1.0 / RELAXATION[2]
    beta = [tile.get(part, 3 + d) for d in range(3)]
    for i, q in enumerate(LEVEL):
        side = mixed(VELOCITY[q][1:], beta[1:]) if q != 16 else None
        for s in range(3):
            v = plus(side, alpha[s])
            if s == 2:
                v = v + rest * tile.get(kept_rim, i)
            tile.put(level, s * 9 + i, v)


def main_kernel(
    adj, fl, fe, recv_a, recv_b, after,
    rims, mid, part, kept_rim, forces, forces_rim, brick2, rim2, kept2,
    lines, hold, ab, kept, hold_rim, ab_rim, level,
):
    planes, rows, cols = adj.shape[1:]
    grid = Grid(planes, rows, cols)
    lines_from(recv_a, recv_b, parity_of("gx"), lines)
    for c in range(STATIC):
        for p in range(planes):
            k = c * planes + p
            rims[c, p] = grid.sides(lines[0, k : k + 1, :], lines[1, k : k + 1, :])
    grid.over_main(lambda tile: rim_psis(grid, tile, rims))

    def step(tile):
        first_step(grid, tile, adj, fl, rims, hold, ab, kept, hold_rim, ab_rim, kept_rim)
        early_forces(grid, tile, fe, rims, forces, forces_rim)

    grid.over_main(step)
    grid.over_main(
        lambda tile: finish_first(
            grid, tile, fl, rims, hold, ab, kept, hold_rim, ab_rim, mid, part
        )
    )
    grid.over_main(lambda tile: level_row(tile, [tile.get(part, s) for s in range(3)], part, kept_rim, level))

    def known_moments(tile):
        load = lambda c, dz: tile.get(mid, c, dz)
        put_moments(tile, brick2, brick_moments(grid, tile, load, None, kept2))
        along = lambda s, i, dz: tile.get(level, s * 9 + i, dz)
        put_moments(tile, rim2, rim_moments(grid, tile, along, None, load, None))

    grid.over_main(known_moments)


def last_kernel(
    fe_m, rims_m, mid_m, part_m, kept_rim_m, forces_m, forces_rim_m, brick2_m, rim2_m, kept2_m,
    edge, fl_e, fe_e,
    recv_a, recv_b, out,
    rims_e, mid_e, part_e, kept_rim_e, forces_e, forces_rim_e, hold_e, ab_e, kept_e, hold_rim_e,
    ab_rim_e, patches, lines, near, change, rim_mid, rim_level, rim_far, hold2, hold_rim2, ab2, kept2,
    total, staged, sems,
):
    planes, rows, cols = fe_m.shape[1:]
    grid = Grid(planes, rows, cols)
    lines_from(recv_a, recv_b, parity_of("gx"), lines)
    for c in range(STATIC):
        rims_e[c] = grid.sides(lines[0, c : c + 1, :], lines[1, c : c + 1, :])
    for c in range(DYNAMIC):
        for t in range(grid.tiles):
            k = STATIC + c * grid.tiles + t
            near[c, t] = grid.sides(lines[0, k : k + 1, :], lines[1, k : k + 1, :])
    fe, rims, mid = Pair(fe_m, fe_e), Pair(rims_m, rims_e), Pair(mid_m, mid_e)
    part, kept_rim = Pair(part_m, part_e), Pair(kept_rim_m, kept_rim_e)
    forces, forces_rim = Pair(forces_m, forces_e), Pair(forces_rim_m, forces_rim_e)
    rest = 1.0 - 1.0 / RELAXATION[2]
    at_rim = grid.at_rim()
    sign = rim_sign(grid)
    outward = grid.outward()

    def edge_steps(tile):
        adj, fl = Pair(None, edge), Pair(None, fl_e)
        hold, ab, kept = Pair(None, hold_e), Pair(None, ab_e), Pair(None, kept_e)
        hold_rim, ab_rim = Pair(None, hold_rim_e), Pair(None, ab_rim_e)
        rim_psis(grid, tile, rims)
        first_step(grid, tile, adj, fl, rims, hold, ab, kept, hold_rim, ab_rim, kept_rim)
        early_forces(grid, tile, fe, rims, forces, forces_rim)
        finish_first(grid, tile, fl, rims, hold, ab, kept, hold_rim, ab_rim, mid, part)

    grid.over_edge(edge_steps)

    def complete(tile):
        t = tile.index
        added = [(1.0 - tile.get(rims, LATE_PSI + s)) * near[s, t] for s in range(3)]
        alpha = [tile.get(part, s) + added[s] for s in range(3)]
        beta = [tile.get(part, 3 + d) for d in range(3)]
        far = [near[3 + s, t] + tile.get(part, 6 + s) for s in range(2)]
        far_beta = [near[5 + d, t] for d in range(2)]
        ahead = outward * beta[0]
        for s in range(3):
            change[s, t] = added[s]
        for j, yz in enumerate(CROSS):
            side = mixed(yz, beta[1:]) if j else None
            side_far = mixed(yz, far_beta) if j else None
            for s in range(3):
                v = plus(side, alpha[s] + ahead)
                if s == 2:
                    v = v + rest * tile.get(kept_rim, 9 + j)
                    rim_far[10 + j, t] = near[7 + j, t] + tile.get(part, 8)
                else:
                    rim_far[s * 5 + j, t] = plus(side_far, far[s])
                rim_mid[s * 5 + j, t] = v
        if tile.edge:
            level_row(tile, alpha, part, kept_rim, rim_level)

    grid.over(complete)

    def collide(tile):
        load = lambda c, dz: tile.get(mid, c, dz)
        after = lambda s, j, dz: tile.get(rim_far, s * 5 + j, dz)
        if tile.edge:
            moments = brick_moments(grid, tile, load, rim_mid, kept2)
            along = lambda s, i, dz: tile.get(rim_level, s * 9 + i, dz)
            moments_rim = rim_moments(grid, tile, along, after, load, None)
        else:
            for q in range(19):
                kept2[q, tile.index] = kept2_m[q, tile.index]
            moments, moments_rim = get_moments(tile, brick2_m), get_moments(tile, rim2_m)
            along = lambda s, i, dz: tile.get(change, s, dz)
            more = crossing_moments(grid, tile, rim_mid, kept2)
            more_rim = rim_moments(grid, tile, along, after, None, None)
            for s in range(3):
                moments[s] = summed(moments[s], more[s])
                moments_rim[s] = summed(moments_rim[s], more_rim[s])
        known = [[tile.get(forces, 3 * s + d) for d in range(3)] for s in range(3)]
        brick_adjoint(tile, moments, fe, known, hold2, ab2)
        known = [[tile.get(forces_rim, 3 * s + d) for d in range(3)] for s in range(3)]
        rho, u = [[tile.get(rims, EARLY + at + d) for d in range(3)] for at in (0, 3)]
        psi = [tile.get(rims, EARLY_PSI + s) for s in range(3)]
        rim_adjoint(grid, tile, moments_rim, rho, u, psi, known, hold_rim2, None)

    grid.over(collide)

    def finish(tile):
        back = spread_inside(grid, tile, hold2, fe)
        dip = [tile.get(fe, 6 + d) for d in range(3)]
        inward = hand_over(grid, tile, hold_rim2, (rims, EARLY + 6), dip, sign)
        for s in range(3):
            x = back[s] + jnp.where(at_rim, inward[s], 0.0)
            total[s, tile.index] = tile.get(ab2, s) + (1.0 - tile.get(fe, 9 + s)) * x

    grid.over(finish)
    at_side = (grid.lane < HALO) | (grid.lane >= cols - HALO)
    first_group = lax.rem(grid.lane, grid.width) < grid.group
    sources = [total.at[s] for s in range(3)] + [ab2.at[3 + d] for d in range(3)]
    sources += [kept2.at[q] for q in range(19)]
    for i, ref in enumerate(sources):
        v = ref[planes]
        patches[i] = jnp.where(first_group, pltpu.roll(v, cols - 2 * grid.group, 1), v)
    copies = []
    for p in range(planes):
        turn = (cols - p * grid.width - grid.group) % cols

        def patched(i):
            return jnp.where(at_side, pltpu.roll(patches[i], turn, 1), sources[i][p])

        alpha = [patched(s) for s in range(3)]
        beta = [patched(3 + d) for d in range(3)]
        for q in range(19):
            along = mixed(VELOCITY[q], beta) if q != 16 else None
            for s in range(3):
                v = alpha[s] if along is None else alpha[s] + along
                if s == 2:
                    v = v + rest * patched(6 + q)
                staged[s * 19 + q, p] = v
        copies.append(pltpu.make_async_copy(staged.at[:, p], out.at[:, p], sems.at[p]))
        copies[p].start()
    for copy in copies:
        copy.wait()


def call(kernel, outs, scratch, args, in_hbm=False, out_hbm=False, cost=0):
    vmem = pl.BlockSpec(memory_space=pltpu.VMEM)
    hbm = pl.BlockSpec(memory_space=pltpu.HBM)
    return pl.pallas_call(
        kernel,
        out_shape=[jax.ShapeDtypeStruct(s, F32) for s in outs],
        in_specs=[hbm if in_hbm else vmem] * len(args),
        out_specs=[hbm if out_hbm else vmem] * len(outs),
        scratch_shapes=[pltpu.VMEM(s, F32) if isinstance(s, tuple) else s for s in scratch],
        compiler_params=pltpu.CompilerParams(vmem_limit_bytes=VMEM_BYTES),
        cost_estimate=pl.CostEstimate(flops=cost, bytes_accessed=cost, transcendentals=0),
    )(*[pltpu.with_memory_space_constraint(x, pltpu.HBM) if in_hbm else x for x in args])


def swap(block, axis, offset):
    size = lax.axis_size(axis)
    route = []
    for i in range(offset, size + offset, 2):
        a, b = i % size, (i + 1) % size
        route += [(a, b), (b, a)]
    return lax.ppermute(block, axis, route)


def shards(adjoint_in, populations_early, populations_late, dipoles_early, dipoles_late):
    pops, planes, rows, cols = adjoint_in.shape
    tile = (rows, cols)
    pack = cols // planes // (2 * HALO)
    groups = -(-(pops + 18) // pack)
    groups += groups % 2

    def lines(n):
        return (-(-n // 8) * 8, cols)

    def main(*counts):
        return [(n, planes) + tile for n in counts]

    def edges(*counts):
        return [(n,) + tile for n in counts]

    def tiled(*counts):
        return [(n, planes + 1) + tile for n in counts]

    static = lines(STATIC * planes)
    second = lines(STATIC + DYNAMIC * (planes + 1))
    send_c, send_d, own_left, own_right, fl_m, fe_m, adj, send_a, send_b = call(
        pack_columns_kernel,
        edges(groups // 2, groups // 2, groups, groups) + main(12, 12, pops) + [static] * 2,
        [
            pltpu.VMEM(x.shape, x.dtype)
            for x in (populations_late, populations_early, dipoles_late, dipoles_early)
        ]
        + [(2,) + static, pltpu.SemaphoreType.DMA((4 + CHUNKS,))],
        [adjoint_in, populations_late, populations_early, dipoles_late, dipoles_early],
        in_hbm=True,
    )
    static_a, static_b = swap(send_a, "gx", 1), swap(send_b, "gx", 0)
    recv_c, recv_d = swap(send_c, "gy", 1), swap(send_d, "gy", 0)
    (sides,) = call(
        inside_kernel, main(DYNAMIC), main(9, 6, 19), [adj, fl_m], cost=INSIDE_COST
    )
    send_a, send_b, edge, fl_e, fe_e = call(
        edge_kernel,
        [second] * 2 + edges(pops, 12, 12),
        [(2,) + second] + edges(9, 6, 19, DYNAMIC),
        [own_left, own_right, recv_c, recv_d, sides],
        cost=EDGE_COST,
    )
    recv_a, recv_b = swap(send_a, "gx", 1), swap(send_b, "gx", 0)
    known = (RIMS, pops, 9, 14, 9, 9)
    mains = call(
        main_kernel,
        main(*known, 30, 30, 19),
        [(2,) + static] + main(9, 6, 19, 9, 6, 27),
        [adj, fl_m, fe_m, static_a, static_b, fl_e],
        cost=MAIN_COST,
    )
    (out,) = call(
        last_kernel,
        [(pops, planes) + tile],
        edges(*known, 9, 6, 19, 9, 6, 25)
        + [(2,) + second]
        + tiled(DYNAMIC, 3, 15, 27, 15, 9, 9, 6, 19, 3)
        + main(pops)
        + [pltpu.SemaphoreType.DMA((planes,))],
        [fe_m, *mains, edge, fl_e, fe_e, recv_a, recv_b],
        out_hbm=True,
    )
    return out


def solution(mesh):
    placed = P(None, None, "gx", "gy")
    return jax.shard_map(
        shards, mesh=mesh, in_specs=(placed,) * 5, out_specs=placed, check_vma=False
    )
```
